32 devices in a mesh: chan: 4 (over z), pix: 8 (over y, x, core).
Axes of the slice: x: 2, y: 2, z: 4, core: 2. Of those that a mesh axis runs over, the one named last changes fastest.
Arguments:
- frames_raw: float32 [16, 256, 5120], P(None, 'chan', 'pix')
- grad_out: float32 [16, 256, 4096], P(None, 'chan', 'pix'), may hold values from -6 to 6
- col_offsets: int32 [4], replicated, may hold values from 0 to 16
- flip_flags: int32 [4], replicated, may hold values from 0 to 1
- owners: int32 [138, 1], replicated, may hold values from 0 to 7; in each aligned block of 138 rows (0 to 137, 138 to 275, ...) at most 26 rows name the same one
- w_expand: float32 [256, 1024], P(None, 'chan'), may hold values from -0.375 to 0.375
- w_dw: float32 [25, 1024], P(None, 'chan'), may hold values from -1.25 to 1.25
- norm_gains: float32 [2, 1024], P(None, 'chan'), may hold values from 0.25 to 1.75
- norm_biases: float32 [2, 1024], P(None, 'chan'), may hold values from -3 to 3
- w_project: float32 [1024, 256], P('chan'), may hold values from -0.5 to 0.5
- squeeze_matrix: float32 [256, 16], P('chan'), may hold values from -1.5 to 1.5
- se_down_bias: float32 [16], replicated, may hold values from -3 to 3
- excite_matrix: float32 [16, 256], P(None, 'chan'), may hold values from -3 to 3
- excite_bias_row: float32 [256], P('chan'), may hold values from -3 to 3
- first_moment: float32 [4, 208, 1024], P('chan', 'pix'), may hold values from -512 to 512
- second_moment: float32 [4, 208, 1024], P('chan', 'pix'), may hold values from 6400 to 25600
Outputs:
- output: float32 [16, 256, 4096], P(None, 'chan', 'pix')
- grad_frames: float32 [16, 256, 5120], P(None, 'chan', 'pix')
- first_new: float32 [4, 208, 1024], P('chan', 'pix')
- second_new: float32 [4, 208, 1024], P('chan', 'pix')
- new_params: float32 [4, 140624], P('chan')
The draws below stay inside these ranges and needn't reach their ends.
Inputs may be any that keep to these rules, and one draw needn't show every extreme that they name: `owners`: an owner holds at most 26 blocks, a bound that some block reaches.
All inputs are finite; a program needn't handle non-finite values.
Results may differ from the reference program's by a relative error of at most 0.0003.
Values sent between devices are 32-bit elements; how exact they have to be, the bound alone decides.
No kernel may reach another device: no remote copies, remote signals or barrier semaphores. Data moves between devices by JAX's collectives and lax.ppermute only.
A program may use at most 128 MiB of HBM per device.

```python
import math
from functools import partial
import jax
import jax.numpy as jnp
import numpy as np
from jax import lax

C = 256
E = 1024
R = 16
K = 5
FRAME_ROWS = 64
FRAME_COLUMNS = 64
PADC = 16
CLIP_LEN = 4
MB = 4
STEP = 5
BLK = 1024
FPM = 4
FRAMES = 16
CLIPS = 4
WIN = 80
EC = 256
CC = 64
PARAMS = 140624
NBLK = 138
MOST = 26
SLOTS = 208
N_CHAN = 4
N_PIX = 8


def draw_frames_raw(key, part):
    key = jax.random.fold_in(key, 11)
    shape_all = (FRAMES, C, FRAME_ROWS * WIN)
    base_vals = jax.random.normal(key, shape_all, jnp.float32)
    rise_top = 2.0
    frame_pos = jnp.arange(FRAMES, dtype=jnp.float32) / max(FRAMES - 1, 1)
    chan_pos = jnp.arange(C, dtype=jnp.float32) / max(C - 1, 1)
    row_pos = (jnp.arange(FRAME_ROWS * WIN, dtype=jnp.int32) // WIN).astype(jnp.float32) / (FRAME_ROWS - 1)
    scale_map = jnp.sqrt((1.0 + frame_pos)[:, None, None] * (1.0 + chan_pos)[None, :, None] * (1.0 + rise_top * row_pos)[None, None, :])
    return base_vals * scale_map


def plant(drawn, rng, low, top_value):
    longest = drawn.shape.index(max(drawn.shape))
    spots = []
    for shift in (0, 1):
        where = [jax.random.randint(jax.random.fold_in(rng, axis), (), 0, length) for axis, length in enumerate(drawn.shape)]
        where[longest] = (where[longest] + shift) % drawn.shape[longest]
        spots.append(tuple(where))
    return drawn.at[spots[0]].set(low).at[spots[1]].set(top_value)


def shard_levels(stream_key, dims, pieces, smallest, high):
    def one(dim, blocks):
        steps = jax.random.uniform(jax.random.fold_in(jax.random.fold_in(stream_key, 6), dim), (blocks,), jnp.float32, smallest / len(pieces), high / len(pieces))
        return jnp.repeat(jnp.exp(steps), dims[dim] // blocks).reshape((-1,) + (1,) * (len(dims) - dim - 1))

    factor_of = one(*pieces[0])
    for cut in pieces[1:]:
        factor_of = factor_of * one(*cut)
    return factor_of


def deal_out(stream_key, own, number, rows, count, top, bound, slope):
    ranking = jax.random.permutation(stream_key, count)
    heavy_load, ordinary = load_shares(count, rows * top, bound, slope, True), load_shares(count, rows * top, bound, slope, False)
    places = jnp.arange(count)

    def named(sizes, turn):
        used = int((sizes > 0).sum())
        fixed = max(1, used // 4)
        passed = fixed + (places - fixed + turn * (used - fixed)) % max(1, count - fixed)
        return jnp.zeros((count,), jnp.int32).at[ranking[jnp.where(places < fixed, places, passed)]].set(jnp.asarray(sizes, jnp.int32))

    sizes = jnp.where(number % 4 == 0, named(heavy_load, number // 4), named(ordinary, number - number // 4 - 1))
    mixed = jax.random.permutation(jax.random.fold_in(own, 3), count)
    source_of, receiver = mixed[0:count // 2 * 2:2], mixed[1:count // 2 * 2:2]
    room = jnp.minimum(sizes[source_of] - 1, bound - sizes[receiver]) // 2
    room = jnp.where((source_of == ranking[0]) | (receiver == ranking[0]) | (sizes[receiver] == 0), 0, jnp.maximum(room, 0))
    passed = jax.random.randint(jax.random.fold_in(own, 4), (count // 2,), 0, 1 << 20) % (room + 1)
    sizes = sizes.at[source_of].add(-passed).at[receiver].add(passed)
    labels = jnp.searchsorted(jnp.cumsum(sizes), jnp.arange(rows * top), side="right").astype(jnp.int32)
    table = labels.reshape(top, rows).T
    table = table[jax.random.permutation(jax.random.fold_in(own, 1), rows)]
    turn = jax.random.randint(jax.random.fold_in(own, 2), (rows, 1), 0, top)
    return jnp.take_along_axis(table, (jnp.arange(top)[None, :] + turn) % top, axis=1)


def load_shares(number_of, total, limit, lean, full):
    loads = [(1 << 20) // math.isqrt(rank ** lean) + 1 for rank in range(1, number_of + 1)]
    largest = limit if full else min(limit, max(-(-total // number_of), total * loads[0] // sum(loads)))
    least = 1 if total - largest >= number_of - 1 else 0
    counts, surplus = [largest] + [least] * (number_of - 1), total - largest - least * (number_of - 1)
    while surplus > 0:
        candidates = [i for i in range(1, number_of) if counts[i] < largest] or [i for i in range(1, number_of) if counts[i] < limit]
        mass, left = sum([loads[i] for i in candidates]), surplus
        for i in candidates:
            more = min(limit - counts[i], max(1, left * loads[i] // mass), surplus)
            counts[i] = counts[i] + more
            surplus = surplus - more
    return np.array(counts)


def gaussian(rng, shape, scale, bound, pieces=(), kind=jnp.bfloat16):
    array = jax.random.normal(rng, shape, jnp.float32) * scale
    if len(pieces) > 0:
        array = shard_levels(rng, shape, pieces, -0.22, 0.18) * array
    return jnp.clip(array, min=-bound, max=bound).astype(kind)


def setup_inputs(seed: int = 0) -> dict:
    seeds = jax.random.split(jax.random.key(seed), 17)
    frames_raw = draw_frames_raw(jax.random.fold_in(seeds[16], 71), 0)
    grad_out = gaussian(seeds[1], (FRAMES, C, FRAME_ROWS * FRAME_COLUMNS), 1.0, 6.0, ((1, 4), (2, 8)), jnp.float32)
    col_offsets = plant(jax.random.randint(seeds[2], (CLIPS,), 0, PADC + 1), jax.random.fold_in(seeds[2], 1), 0, PADC).astype(jnp.int32)
    flip_flags = plant(jax.random.randint(seeds[3], (CLIPS,), 0, 2), jax.random.fold_in(seeds[3], 1), 0, 1).astype(jnp.int32)
    owners_keys = jax.random.split(jax.random.fold_in(seeds[4], 1), NBLK // NBLK)
    owners_turns = jax.random.permutation(jax.random.fold_in(seeds[4], 3), NBLK // NBLK)
    owners = jax.vmap(lambda own, number: deal_out(jax.random.fold_in(seeds[4], 2), own, number, NBLK, N_PIX, 1, MOST, 1))(owners_keys, owners_turns).reshape((NBLK, 1))
    w_expand = gaussian(seeds[5], (C, E), C ** -0.5, 0.375, ((1, 4),), jnp.float32)
    w_dw = gaussian(seeds[6], (K * K, E), (K * K) ** -0.5, 1.25, ((1, 4),), jnp.float32)
    norm_gains = jnp.clip(1.0 + 0.15 * jax.random.normal(seeds[7], (2, E), jnp.float32), 0.25, 1.75)
    norm_biases = gaussian(seeds[8], (2, E), 0.5, 3.0, ((1, 4),), jnp.float32)
    w_project = gaussian(seeds[9], (E, C), (E // 8) ** -0.5, 0.5, ((0, 4),), jnp.float32)
    squeeze_matrix = gaussian(seeds[10], (C, R), (C // 16) ** -0.5, 1.5, ((0, 4),), jnp.float32)
    se_down_bias = gaussian(seeds[11], (R,), 0.5, 3.0, (), jnp.float32)
    excite_matrix = gaussian(seeds[12], (R, C), (R // 4) ** -0.5, 3.0, ((1, 4),), jnp.float32)
    excite_bias_row = gaussian(seeds[13], (C,), 0.5, 3.0, ((0, 4),), jnp.float32)
    first_moment = gaussian(seeds[14], (N_CHAN, SLOTS, BLK), (20 * FRAMES ** 0.5), 512.0, ((0, 4), (1, 8)), jnp.float32)
    second_moment = jnp.clip(jnp.exp(math.log(25600.0) - 1.3862944 * jax.random.uniform(seeds[15], (N_CHAN, SLOTS, BLK), jnp.float32) ** shard_levels(seeds[15], (N_CHAN, SLOTS, BLK), ((0, 4), (1, 8)), -0.2, 0.2)), 6400.0, 25600.0)
    return {"frames_raw": frames_raw, "grad_out": grad_out, "col_offsets": col_offsets, "flip_flags": flip_flags, "owners": owners, "w_expand": w_expand, "w_dw": w_dw, "norm_gains": norm_gains, "norm_biases": norm_biases, "w_project": w_project, "squeeze_matrix": squeeze_matrix, "se_down_bias": se_down_bias, "excite_matrix": excite_matrix, "excite_bias_row": excite_bias_row, "first_moment": first_moment, "second_moment": second_moment}


precise_setting = lax.Precision.HIGHEST
norm_eps = 1e-05
beta_first = 0.5
beta_second = 0.6
adam_eps = 1e-08
weight_decay = 0.1

@jax.custom_vjp
def low(v):
    return lax.optimization_barrier(v.astype(jnp.bfloat16)).astype(jnp.float32)

@jax.custom_vjp
def low_back(v):
    return v

def low_keep(v):
    return (low(v), None)

def low_pass(kept, grad):
    return (grad,)

def back_keep(v):
    return (v, None)

def back_low(kept, grad):
    return (low(grad),)
low.defvjp(low_keep, low_pass)
low_back.defvjp(back_keep, back_low)

def swish_act(values):
    return values * jax.nn.sigmoid(values)

def batch_norm(hidden, gain_row, bias_row):
    pixel_count = hidden.shape[0] * hidden.shape[1] * hidden.shape[2]
    mean_value = lax.optimization_barrier(jnp.sum(hidden, axis=(0, 1, 2))) / pixel_count
    mean_square = lax.optimization_barrier(jnp.sum(hidden * hidden, axis=(0, 1, 2))) / pixel_count
    inverse = lax.rsqrt(mean_square - mean_value * mean_value + norm_eps)
    return (hidden - mean_value) * inverse * gain_row + bias_row

def depthwise(field_in, kernel):
    half_width = K // 2
    row_count = field_in.shape[1]
    col_count = field_in.shape[2]
    padded = jnp.pad(field_in, ((0, 0), (half_width, half_width), (half_width, half_width), (0, 0)))
    accum_sum = jnp.zeros_like(field_in)
    for row_tap in range(K):
        for col_tap in range(K):
            accum_sum = accum_sum + padded[:, row_tap:row_tap + row_count, col_tap:col_tap + col_count, :] * kernel[row_tap * K + col_tap]
    return accum_sum

def micro_batch(crops, weights):
    w_expand, w_dw, norm_gains, norm_biases, w_project, squeeze_matrix, se_down_bias, excite_matrix, excite_bias_row = weights
    expanded = jnp.einsum('fhwc,ce->fhwe', crops, w_expand, precision=precise_setting)
    first_act = swish_act(batch_norm(expanded, norm_gains[0], norm_biases[0]))
    spatial = depthwise(first_act, w_dw)
    second_act = swish_act(batch_norm(spatial, norm_gains[1], norm_biases[1]))
    projected = jnp.einsum('fhwe,ec->fhwc', second_act, w_project, precision=precise_setting)
    pooled = lax.optimization_barrier(jnp.mean(projected, axis=(1, 2)))
    squeezed_features = swish_act(jnp.dot(pooled, squeeze_matrix, precision=precise_setting) + se_down_bias)
    excite = jax.nn.sigmoid(jnp.dot(squeezed_features, excite_matrix, precision=precise_setting) + excite_bias_row)
    return crops + projected * excite[:, None, None, :]

def crop_one(frame, left_col, flipped):
    piece_out = lax.dynamic_slice(frame, (jnp.int32(0), jnp.int32(0), left_col), (frame.shape[0], FRAME_ROWS, FRAME_COLUMNS))
    piece_out = jnp.where(flipped == 1, piece_out[:, :, ::-1], piece_out)
    return piece_out.transpose(1, 2, 0)

def forward(frames_in, weights, left_cols, flip_each):
    stored = frames_in.reshape(FRAMES, C, FRAME_ROWS, WIN)
    crops = jax.vmap(crop_one)(stored, left_cols, flip_each)
    grouped = crops.reshape(MB, FPM, FRAME_ROWS, FRAME_COLUMNS, C)
    step_fn = jax.checkpoint(partial(micro_batch, weights=weights))

    def scan_step(carry, block_in):
        return (carry, step_fn(block_in))
    carry_end, outputs = lax.scan(scan_step, jnp.float32(0.0), grouped)
    return outputs.reshape(FRAMES, FRAME_ROWS, FRAME_COLUMNS, C).transpose(0, 3, 1, 2).reshape(FRAMES, C, FRAME_ROWS * FRAME_COLUMNS)

def segments(chan_in, hidden_dev, chan_dev, reduced, tap_count, hidden_all):
    seg_sizes = [chan_in * hidden_dev, tap_count * hidden_dev, 2 * hidden_dev, 2 * hidden_dev, hidden_dev * chan_in, chan_dev * reduced, reduced, reduced * chan_dev, chan_dev]
    seg_rates = [0.5 / math.sqrt(chan_in), 0.5 / math.sqrt(tap_count), 0.3, 0.3, 0.5 * math.sqrt(8.0 / hidden_all), 2.0 / math.sqrt(chan_in), 0.3, 1.0 / math.sqrt(reduced), 0.3]
    return (seg_sizes, seg_rates)

def rate_blocks(seg_sizes, seg_rates, block_count, block_len):
    filled = jnp.concatenate([jnp.full((length,), rate_val, jnp.float32) for length, rate_val in zip(seg_sizes, seg_rates)])
    return jnp.pad(filled, (0, block_count * block_len - filled.shape[0])).reshape(block_count, block_len)

def flatten_blocks(members, block_count, block_len):
    flat_vec = jnp.concatenate([member.reshape(-1) for member in members])
    return jnp.pad(flat_vec, (0, block_count * block_len - flat_vec.shape[0])).reshape(block_count, block_len)

def group_members(weights, group_idx):
    w_expand, w_dw, norm_gains, norm_biases, w_project, squeeze_matrix, se_down_bias, excite_matrix, excite_bias_row = weights
    hid_lo = group_idx * EC
    chan_lo = group_idx * CC
    return [w_expand[:, hid_lo:hid_lo + EC], w_dw[:, hid_lo:hid_lo + EC], norm_gains[:, hid_lo:hid_lo + EC], norm_biases[:, hid_lo:hid_lo + EC], w_project[hid_lo:hid_lo + EC, :], squeeze_matrix[chan_lo:chan_lo + CC, :], se_down_bias, excite_matrix[:, chan_lo:chan_lo + CC], excite_bias_row[chan_lo:chan_lo + CC]]

def slot_rows(owners, capacity):
    owner_col = owners[:, 0]
    position = jnp.arange(owner_col.shape[0], dtype=jnp.int32)
    earlier = (owner_col[None, :] == owner_col[:, None]) & (position[None, :] < position[:, None])
    return (owner_col * capacity + lax.optimization_barrier(jnp.sum(earlier.astype(jnp.int32), axis=1))).astype(jnp.int32)

def adam_step(grad_blk, first_old, second_old, weight_old, rate_blk):
    first_next = beta_first * first_old + (1.0 - beta_first) * grad_blk
    second_next = beta_second * second_old + (1.0 - beta_second) * grad_blk * grad_blk
    first_hat = first_next / (1.0 - beta_first ** STEP)
    second_hat = second_next / (1.0 - beta_second ** STEP)
    weight_next = weight_old * (1.0 - rate_blk * weight_decay) - rate_blk * first_hat / (jnp.sqrt(second_hat) + adam_eps)
    return (first_next, second_next, weight_next)

def reference(frames_raw, grad_out, col_offsets, flip_flags, owners, w_expand, w_dw, norm_gains, norm_biases, w_project, squeeze_matrix, se_down_bias, excite_matrix, excite_bias_row, first_moment, second_moment):
    left_cols = jnp.repeat(col_offsets, CLIP_LEN)
    flip_each = jnp.repeat(flip_flags, CLIP_LEN)
    weights = (w_expand, w_dw, norm_gains, norm_biases, w_project, squeeze_matrix, se_down_bias, excite_matrix, excite_bias_row)

    def whole_cell(frames_in, *params):
        return forward(frames_in, params, left_cols, flip_each)
    output, pullback = jax.vjp(whole_cell, frames_raw, *weights)
    all_grads = pullback(grad_out)
    grad_frames = all_grads[0]
    weight_grads = all_grads[1:]
    seg_sizes, seg_rates = segments(C, EC, CC, R, K * K, E)
    rate_table = rate_blocks(seg_sizes, seg_rates, NBLK, BLK)
    slot_index = slot_rows(owners, MOST)
    firsts = []
    seconds = []
    new_rows = []
    for group_idx in range(N_CHAN):
        grad_flat = flatten_blocks(group_members(weight_grads, group_idx), NBLK, BLK)
        weight_flat = flatten_blocks(group_members(weights, group_idx), NBLK, BLK)
        empty_slots = jnp.zeros((SLOTS, BLK), jnp.float32)
        packed_grad = empty_slots.at[slot_index].set(grad_flat)
        packed_weight = empty_slots.at[slot_index].set(weight_flat)
        packed_rate = empty_slots.at[slot_index].set(rate_table)
        first_next, second_next, weight_next = adam_step(packed_grad, first_moment[group_idx], second_moment[group_idx], packed_weight, packed_rate)
        firsts.append(first_next)
        seconds.append(second_next)
        new_rows.append(weight_next[slot_index].reshape(-1)[:PARAMS])
    return (output, grad_frames, jnp.stack(firsts), jnp.stack(seconds), jnp.stack(new_rows))
```

```python
from functools import partial
import math

import jax
import jax.numpy as jnp
from jax import lax
from jax.experimental import pallas as pl
from jax.experimental.pallas import tpu as pltpu
from jax.sharding import Mesh, PartitionSpec as P

K = 5
FRAME_ROWS = 64
FRAME_COLUMNS = 64
CLIP_LEN = 4
MB = 4
STEP = 5
WIN = 80
SUB = 8
TAPS = K * K
HALO_IN = 4
HALO_OUT = 2

norm_eps = 1e-05
beta_first = 0.5
beta_second = 0.6
adam_eps = 1e-08
weight_decay = 0.1

F32 = jnp.float32
BF16 = jnp.bfloat16
ALL = ("chan", "hi", "lo")
PIX = ("hi", "lo")
SPREAD = ("chan", "lo")
MIB = 2**20


def params(mib, dims=1):
    return pltpu.CompilerParams(vmem_limit_bytes=mib * MIB, dimension_semantics=("arbitrary",) * dims)


def cost(flops, moved):
    return pl.CostEstimate(flops=int(flops), bytes_accessed=int(moved), transcendentals=0)


def sigmoid(v):
    return 0.5 * jnp.tanh(0.5 * v) + 0.5


def split(v):
    high = v.astype(BF16)
    return high, (v - high.astype(F32)).astype(BF16)


def dot(a, b):
    return jnp.dot(a, b, preferred_element_type=F32)


def dot3(a, b):
    return dot(a[0], b[0]) + (dot(a[0], b[1]) + dot(a[1], b[0]))


def exact_dot(a, b):
    return jnp.dot(a, b, preferred_element_type=F32, precision=lax.Precision.HIGHEST)


def total(refs):
    value = refs[0][...]
    for ref in refs[1:]:
        value = value + ref[...]
    return value


def norm_terms(sums, count, gain, bias):
    mean = sums[0:1] / count
    inverse = lax.rsqrt(sums[1:2] / count - mean * mean + norm_eps)
    scale = gain * inverse
    return mean, inverse, scale, bias - mean * scale


def back_terms(sums, back, count, gain):
    mean = sums[0:1] / count
    inverse = lax.rsqrt(sums[1:2] / count - mean * mean + norm_eps)
    a = gain * inverse
    b = -a * inverse * (back[1:2] / count)
    return a, b, -a * (back[0:1] / count) - b * mean


def exchange(x, stride):
    n = lax.axis_size(ALL)
    return lax.ppermute(x, ALL, [(i, i ^ stride) for i in range(n)])


def shares(x, base, size):
    bits = size.bit_length() - 1
    parts = [x]
    if bits % 2:
        parts = [x, exchange(x, base)]
        base, bits = base * 2, bits - 1
    while bits:
        x = sum(parts[1:], parts[0])
        parts = [x] + [exchange(x, base * k) for k in (1, 2, 3)]
        base, bits = base * 4, bits - 2
    return parts


def deal(x):
    return lax.all_to_all(x, SPREAD, 0, 0, tiled=True)


def edge(x, rows, band, first):
    if rows >= band:
        n = rows // band
        return x[:, :n] if first else x[:, x.shape[1] - n :]
    width = rows * FRAME_COLUMNS
    return x[:, :1, :, :width] if first else x[:, -1:, :, x.shape[3] - width :]


def rims(x, rows, band):
    n = lax.axis_size("hi")
    down = [(i, i + 1) for i in range(n - 1)]
    up = [(i + 1, i) for i in range(n - 1)]
    top = lax.ppermute(edge(x, rows, band, False), "hi", down)
    low = lax.ppermute(edge(x, rows, band, True), "hi", up)
    return top, low


def source_column(p, left, flip):
    row, c, s = p // FRAME_COLUMNS, (p // SUB) % SUB, p % SUB
    j = s * SUB + c
    return row * WIN + left + jnp.where(flip == 1, FRAME_COLUMNS - 1 - j, j)


def plain_place(p):
    row, c, s = p // FRAME_COLUMNS, (p // SUB) % SUB, p % SUB
    return row * FRAME_COLUMNS + s * SUB + c


def pick(x, chosen):
    rows = x.shape[0] * x.shape[1]
    high, low = split(x.reshape(rows, x.shape[2]))
    return (dot(high, chosen) + dot(low, chosen)).reshape(x.shape[0], x.shape[1], chosen.shape[1])


def crop_kernel(left_ref, flip_ref, raw_ref, out_ref):
    k = pl.program_id(0)
    width, area = raw_ref.shape[2], out_ref.shape[2]
    p = lax.broadcasted_iota(jnp.int32, (1, area), 1)
    place = source_column(p, left_ref[k], flip_ref[k])
    q = lax.broadcasted_iota(jnp.int32, (width, area), 0)
    out_ref[...] = pick(raw_ref[...], (q == place).astype(F32).astype(BF16))


def crop(raw, left, flip):
    frames, chans, width = raw.shape
    area = width // WIN * FRAME_COLUMNS
    return pl.pallas_call(
        crop_kernel,
        grid=(frames // CLIP_LEN,),
        in_specs=[
            pl.BlockSpec(memory_space=pltpu.SMEM),
            pl.BlockSpec(memory_space=pltpu.SMEM),
            pl.BlockSpec((CLIP_LEN, chans, width), lambda k: (k, 0, 0)),
        ],
        out_specs=pl.BlockSpec((CLIP_LEN, chans, area), lambda k: (k, 0, 0)),
        out_shape=jax.ShapeDtypeStruct((frames, chans, area), F32),
        compiler_params=params(32),
        cost_estimate=cost(4 * frames * chans * width * area, 4 * frames * chans * (width + area)),
        name="crop",
    )(left, flip, raw)


def order_kernel(x_ref, out_ref):
    area = x_ref.shape[2]
    p = lax.broadcasted_iota(jnp.int32, (1, area), 1)
    q = lax.broadcasted_iota(jnp.int32, (area, area), 0)
    out_ref[...] = pick(x_ref[...], (q == plain_place(p)).astype(F32).astype(BF16))


def order(x):
    frames, chans, area = x.shape
    return pl.pallas_call(
        order_kernel,
        grid=(frames // CLIP_LEN,),
        in_specs=[pl.BlockSpec((CLIP_LEN, chans, area), lambda k: (k, 0, 0))],
        out_specs=pl.BlockSpec((CLIP_LEN, chans, area), lambda k: (k, 0, 0)),
        out_shape=jax.ShapeDtypeStruct((frames, chans, area), F32),
        compiler_params=params(32),
        cost_estimate=cost(4 * frames * chans * area * area, 8 * frames * chans * area),
        name="order",
    )(x)


def restore_kernel(x_ref, out_ref):
    area = x_ref.shape[2]
    p = lax.broadcasted_iota(jnp.int32, (area, 1), 0)
    q = lax.broadcasted_iota(jnp.int32, (area, area), 1)
    out_ref[...] = pick(x_ref[...], (q == plain_place(p)).astype(F32).astype(BF16))


def restore(x):
    frames, chans, area = x.shape
    return pl.pallas_call(
        restore_kernel,
        grid=(frames // CLIP_LEN,),
        in_specs=[pl.BlockSpec((CLIP_LEN, chans, area), lambda k: (k, 0, 0))],
        out_specs=pl.BlockSpec((CLIP_LEN, chans, area), lambda k: (k, 0, 0)),
        out_shape=jax.ShapeDtypeStruct((frames, chans, area), F32),
        compiler_params=params(32),
        cost_estimate=cost(4 * frames * chans * area * area, 8 * frames * chans * area),
        name="restore",
    )(x)


def uncrop_kernel(left_ref, flip_ref, x_ref, out_ref):
    k = pl.program_id(0)
    area, width = x_ref.shape[2], out_ref.shape[2]
    p = lax.broadcasted_iota(jnp.int32, (area, 1), 0)
    place = source_column(p, left_ref[k], flip_ref[k])
    q = lax.broadcasted_iota(jnp.int32, (area, width), 1)
    out_ref[...] = pick(x_ref[...], (q == place).astype(F32).astype(BF16))


def uncrop(x, left, flip):
    frames, chans, area = x.shape
    width = area // FRAME_COLUMNS * WIN
    return pl.pallas_call(
        uncrop_kernel,
        grid=(frames // CLIP_LEN,),
        in_specs=[
            pl.BlockSpec(memory_space=pltpu.SMEM),
            pl.BlockSpec(memory_space=pltpu.SMEM),
            pl.BlockSpec((CLIP_LEN, chans, area), lambda k: (k, 0, 0)),
        ],
        out_specs=pl.BlockSpec((CLIP_LEN, chans, width), lambda k: (k, 0, 0)),
        out_shape=jax.ShapeDtypeStruct((frames, chans, width), F32),
        compiler_params=params(32),
        cost_estimate=cost(4 * frames * chans * width * area, 4 * frames * chans * (width + area)),
        name="uncrop",
    )(left, flip, x)


def chunks(width):
    step = 256 if width % 256 == 0 else width
    return [slice(i, i + step) for i in range(0, width, step)]


def expand_kernel(x_ref, top_ref, low_ref, w_ref, own_ref, halo_ref, sum_ref, w_high, w_low):
    t, n = pl.program_id(0), pl.num_programs(0) - 1
    chan_all, hidden = w_ref.shape

    @pl.when(t == 0)
    def _():
        w_high[...], w_low[...] = split(w_ref[...])
        sum_ref[...] = jnp.zeros_like(sum_ref)

    @pl.when(t < n)
    def _():
        x = split(x_ref[:, 0].reshape(chan_all, x_ref.shape[3]).T)
        for cut in chunks(hidden):
            y = dot3(x, (w_high[:, cut], w_low[:, cut]))
            own_ref[0, :, cut] = y
            sum_ref[0:1, cut] += jnp.sum(y, axis=0, keepdims=True)
            sum_ref[1:2, cut] += jnp.sum(y * y, axis=0, keepdims=True)

    @pl.when(t == n)
    def _():
        width = top_ref.shape[3]
        for side, ref in enumerate((top_ref, low_ref)):
            for k in range(ref.shape[1]):
                x = split(ref[:, k].reshape(chan_all, width).T)
                for cut in chunks(hidden):
                    halo_ref[side, k * width : (k + 1) * width, cut] = dot3(x, (w_high[:, cut], w_low[:, cut]))


def whole(shape):
    return pl.BlockSpec(shape, lambda *_: (0,) * len(shape))


def expand(x, top, low, w):
    nz, bands, chans, area = x.shape
    hidden = w.shape[1]
    halo = HALO_IN * FRAME_COLUMNS
    last = bands - 1
    return pl.pallas_call(
        expand_kernel,
        grid=(bands + 1,),
        in_specs=[
            pl.BlockSpec((nz, 1, chans, area), lambda t: (0, jnp.minimum(t, last), 0, 0)),
            whole(top.shape),
            whole(low.shape),
            whole(w.shape),
        ],
        out_specs=[
            pl.BlockSpec((1, area, hidden), lambda t: (jnp.minimum(t, last), 0, 0)),
            whole((2, halo, hidden)),
            whole((2, hidden)),
        ],
        out_shape=[
            jax.ShapeDtypeStruct((bands, area, hidden), F32),
            jax.ShapeDtypeStruct((2, halo, hidden), F32),
            jax.ShapeDtypeStruct((2, hidden), F32),
        ],
        scratch_shapes=[pltpu.VMEM(w.shape, BF16), pltpu.VMEM(w.shape, BF16)],
        compiler_params=params(40),
        cost_estimate=cost(6 * (bands * area + 2 * halo) * hidden * nz * chans, 4 * bands * area * hidden),
        name="expand",
    )(x, top, low, w)


def fill_sides(pad, row):
    s = lax.broadcasted_iota(jnp.int32, (SUB, 128), 0)
    for k in range(2):
        left = pltpu.roll(pad[row, SUB + k], 1, 0)
        pad[row, k] = jnp.where(s == 0, 0.0, left)
        right = pltpu.roll(pad[row, 2 + k], SUB - 1, 0)
        pad[row, SUB + 2 + k] = jnp.where(s == SUB - 1, 0.0, right)


def clear_rows(pad, start, count):
    for row in range(start, start + count):
        pad[row] = jnp.zeros(pad.shape[1:], F32)


def tap_rows(pad, w_ref, start, count, c, flipped=False):
    acc = [None] * count
    for b in range(K):
        for row in range(count + K - 1):
            value = pad[start + row, c + b]
            for a in range(K):
                o = row - a
                if 0 <= o < count:
                    tap = a * K + b
                    term = value * w_ref[TAPS - 1 - tap if flipped else tap]
                    acc[o] = term if acc[o] is None else acc[o] + term
    return acc


def spread_kernel(parts, count, side_ref, own_ref, halo_ref, gain_ref, bias_ref, w_ref, *rest):
    sums, (out_ref, edge_ref, sum_ref, pad, terms) = rest[:parts], rest[parts:]
    rows = own_ref.shape[0]
    _, _, scale, shift = norm_terms(total(sums), count, gain_ref[0:1], bias_ref[0:1])
    terms[0] = jnp.broadcast_to(scale, (SUB, 128))
    terms[1] = jnp.broadcast_to(shift, (SUB, 128))

    def act(value):
        v = value * terms[0] + terms[1]
        return v * sigmoid(v)

    def own_row(r, _):
        for c in range(SUB):
            pad[r + HALO_IN, c + 2] = act(own_ref[r, c])
        fill_sides(pad, r + HALO_IN)
        return 0

    lax.fori_loop(0, rows, own_row, 0)
    for side, start in ((0, 0), (1, rows + HALO_IN)):

        @pl.when(side_ref[side] == 1)
        def _(side=side, start=start):
            for r in range(HALO_IN):
                for c in range(SUB):
                    pad[start + r, c + 2] = act(halo_ref[side, r, c])
                fill_sides(pad, start + r)

        @pl.when(side_ref[side] == 0)
        def _(start=start):
            clear_rows(pad, start, HALO_IN)

    def group(i, carry):
        one, two = carry
        r = i * SUB
        for c in range(SUB):
            acc = tap_rows(pad, w_ref, r + 2, SUB, c)
            for o in range(SUB):
                out_ref[r + o, c] = acc[o]
                one = one + acc[o]
                two = two + acc[o] * acc[o]
        return one, two

    zero = jnp.zeros((SUB, 128), F32)
    one, two = lax.fori_loop(0, rows // SUB, group, (zero, zero))
    sum_ref[0:1] = jnp.sum(one, axis=0, keepdims=True)
    sum_ref[1:2] = jnp.sum(two, axis=0, keepdims=True)
    for side, start in ((0, 0), (1, rows + 2)):

        @pl.when(side_ref[side] == 1)
        def _(side=side, start=start):
            for c in range(SUB):
                acc = tap_rows(pad, w_ref, start, HALO_OUT, c)
                for o in range(HALO_OUT):
                    edge_ref[side, o, c] = acc[o]

        @pl.when(side_ref[side] == 0)
        def _(side=side):
            edge_ref[side] = jnp.zeros(edge_ref.shape[1:], F32)


def lanes(shape):
    lead = len(shape) - 1
    return pl.BlockSpec(tuple(shape[:-1]) + (128,), lambda e: (0,) * lead + (e,))


def spread(count, side, own, halo, gains, biases, taps, sums):
    rows, hidden = own.shape[0], own.shape[-1]
    arrays = [own, halo, gains, biases, taps, *sums]
    return pl.pallas_call(
        partial(spread_kernel, len(sums), count),
        grid=(hidden // 128,),
        in_specs=[pl.BlockSpec(memory_space=pltpu.SMEM)] + [lanes(a.shape) for a in arrays],
        out_specs=[
            lanes((rows, SUB, SUB, hidden)),
            lanes((2, HALO_OUT, SUB, SUB, hidden)),
            lanes((2, hidden)),
        ],
        out_shape=[
            jax.ShapeDtypeStruct((rows, SUB, SUB, hidden), F32),
            jax.ShapeDtypeStruct((2, HALO_OUT, SUB, SUB, hidden), F32),
            jax.ShapeDtypeStruct((2, hidden), F32),
        ],
        scratch_shapes=[
            pltpu.VMEM((rows + 2 * HALO_IN, SUB + 4, SUB, 128), F32),
            pltpu.VMEM((2, SUB, 128), F32),
        ],
        compiler_params=params(40),
        cost_estimate=cost(rows * 64 * hidden * 800, 8 * rows * 64 * hidden),
        name="spread",
    )(side, *arrays)


def as_row(columns):
    width = columns.shape[1]
    folded = columns[:, 0:128]
    for i in range(128, width, 128):
        folded = folded + columns[:, i : i + 128]
    return jnp.sum(folded.T, axis=0, keepdims=True)


def gather_kernel(parts, count, own_ref, gout_ref, gain_ref, bias_ref, wt_ref, *rest):
    sums, (m_ref, s_ref, se_ref) = rest[:parts], rest[parts:]
    t = pl.program_id(0)
    chan_all, hidden = wt_ref.shape

    @pl.when(t == 0)
    def _():
        m_ref[...] = jnp.zeros_like(m_ref)
        s_ref[...] = jnp.zeros_like(s_ref)

    _, _, scale, shift = norm_terms(total(sums), count, gain_ref[1:2], bias_ref[1:2])
    gout = split(gout_ref[:, 0].reshape(chan_all, gout_ref.shape[3]))
    for cut in chunks(hidden):
        v = own_ref[0, :, cut] * scale[:, cut] + shift[:, cut]
        act = v * sigmoid(v)
        s_ref[0:1, cut] += jnp.sum(act, axis=0, keepdims=True)
        m_ref[:, cut] += dot3(gout, split(act))

    @pl.when(t == pl.num_programs(0) - 1)
    def _():
        wt = wt_ref[...]
        se_ref[0:1] = as_row(s_ref[...] * wt)
        se_ref[1:2] = as_row(m_ref[...] * wt)


def gather(count, own, gout, gains, biases, wt, sums):
    nz, bands, chans, area = gout.shape
    hidden = wt.shape[1]
    chan_all = nz * chans
    return pl.pallas_call(
        partial(gather_kernel, len(sums), count),
        grid=(bands,),
        in_specs=[
            pl.BlockSpec((1, area, hidden), lambda t: (t, 0, 0)),
            pl.BlockSpec((nz, 1, chans, area), lambda t: (0, t, 0, 0)),
            whole(gains.shape),
            whole(biases.shape),
            whole(wt.shape),
        ]
        + [whole(s.shape) for s in sums],
        out_specs=[whole((chan_all, hidden)), whole((1, hidden)), whole((2, chan_all))],
        out_shape=[
            jax.ShapeDtypeStruct((chan_all, hidden), F32),
            jax.ShapeDtypeStruct((1, hidden), F32),
            jax.ShapeDtypeStruct((2, chan_all), F32),
        ],
        compiler_params=params(40),
        cost_estimate=cost(6 * bands * area * hidden * chan_all, 4 * bands * area * hidden),
        name="gather",
    )(own, gout, gains, biases, wt, *sums)


def column(row):
    return jnp.broadcast_to(row, (SUB, row.shape[1])).T[:, 0:1]


def padded_dot(row, matrix):
    return exact_dot(jnp.broadcast_to(row, (SUB, row.shape[1])), matrix)[0:1]


def proj_back_kernel(
    pairs,
    parts,
    count,
    side_ref,
    own_ref,
    halo_ref,
    gout_ref,
    top_ref,
    low_ref,
    gain_ref,
    bias_ref,
    wt_ref,
    sq_ref,
    sqt_ref,
    down_ref,
    ex_ref,
    ext_ref,
    exb_ref,
    *rest,
):
    ses, sums = rest[:pairs], rest[pairs : pairs + parts]
    q_ref, edge_ref, sum_ref, val_ref, w_high, w_low, k_row = rest[pairs + parts :]
    t, n = pl.program_id(0), pl.num_programs(0) - 1
    chan_all, hidden = wt_ref.shape
    reduced = ex_ref.shape[0]

    @pl.when(t == 0)
    def _():
        se = total(ses)
        pooled = se[0:1] / (FRAME_ROWS * FRAME_COLUMNS)
        pre = padded_dot(pooled, sq_ref[...]) + down_ref[...]
        gate = sigmoid(pre)
        squeezed = pre * gate
        excite = sigmoid(padded_dot(squeezed, ex_ref[...]) + exb_ref[...])
        logit = se[1:2] * excite * (1.0 - excite)
        slope = gate * (1.0 + pre * (1.0 - gate))
        grad_sq = padded_dot(logit, ext_ref[...]) * slope
        pool_grad = padded_dot(grad_sq, sqt_ref[...]) / (FRAME_ROWS * FRAME_COLUMNS)
        val_ref[...] = jnp.zeros_like(val_ref)
        val_ref[0:1] = excite
        val_ref[1:2] = pool_grad
        val_ref[2:3] = logit
        val_ref[3:4] = pooled
        val_ref[4:5, 0:reduced] = squeezed
        val_ref[5:6, 0:reduced] = grad_sq
        wt = wt_ref[...]
        w_high[...], w_low[...] = split(wt * column(excite))
        k_row[...] = jnp.sum(wt * column(pool_grad), axis=0, keepdims=True)
        sum_ref[...] = jnp.zeros_like(sum_ref)

    mean, inverse, _, _ = norm_terms(total(sums), count, gain_ref[1:2], bias_ref[1:2])
    gain, bias = gain_ref[1:2], bias_ref[1:2]

    def back(gout, value, cut):
        grad = dot3(gout, (w_high[:, cut], w_low[:, cut])) + k_row[:, cut]
        centered = (value - mean[:, cut]) * inverse[:, cut]
        v = centered * gain[:, cut] + bias[:, cut]
        s = sigmoid(v)
        return grad * (s + v * s * (1.0 - s)), centered

    @pl.when(t < n)
    def _():
        gout = split(gout_ref[:, 0].reshape(chan_all, gout_ref.shape[3]).T)
        for cut in chunks(hidden):
            q, centered = back(gout, own_ref[0, :, cut], cut)
            q_ref[0, :, cut] = q
            sum_ref[0:1, cut] += jnp.sum(q, axis=0, keepdims=True)
            sum_ref[1:2, cut] += jnp.sum(q * centered, axis=0, keepdims=True)

    for side, ref in enumerate((top_ref, low_ref)):

        @pl.when((t == n) & (side_ref[side] == 1))
        def _(side=side, ref=ref):
            width = ref.shape[3]
            for k in range(ref.shape[1]):
                here = slice(k * width, (k + 1) * width)
                gout = split(ref[:, k].reshape(chan_all, width).T)
                for cut in chunks(hidden):
                    edge_ref[side, here, cut] = back(gout, halo_ref[side, here, cut], cut)[0]


def proj_back(count, side, own, halo, gout, top, low, gains, biases, wt, se_weights, ses, sums):
    nz, bands, chans, area = gout.shape
    hidden = wt.shape[1]
    chan_all = nz * chans
    last = bands - 1
    fixed = [top, low, gains, biases, wt, *se_weights, *ses, *sums]
    edge_px = HALO_OUT * FRAME_COLUMNS
    return pl.pallas_call(
        partial(proj_back_kernel, len(ses), len(sums), count),
        grid=(bands + 1,),
        in_specs=[
            pl.BlockSpec(memory_space=pltpu.SMEM),
            pl.BlockSpec((1, area, hidden), lambda t: (jnp.minimum(t, last), 0, 0)),
            whole(halo.shape),
            pl.BlockSpec((nz, 1, chans, area), lambda t: (0, jnp.minimum(t, last), 0, 0)),
        ]
        + [whole(a.shape) for a in fixed],
        out_specs=[
            pl.BlockSpec((1, area, hidden), lambda t: (jnp.minimum(t, last), 0, 0)),
            whole((2, edge_px, hidden)),
            whole((2, hidden)),
            whole((SUB, chan_all)),
        ],
        out_shape=[
            jax.ShapeDtypeStruct((bands, area, hidden), F32),
            jax.ShapeDtypeStruct((2, edge_px, hidden), F32),
            jax.ShapeDtypeStruct((2, hidden), F32),
            jax.ShapeDtypeStruct((SUB, chan_all), F32),
        ],
        scratch_shapes=[
            pltpu.VMEM(wt.shape, BF16),
            pltpu.VMEM(wt.shape, BF16),
            pltpu.VMEM((1, hidden), F32),
        ],
        compiler_params=params(48),
        cost_estimate=cost(6 * (bands * area + 2 * edge_px) * hidden * chan_all, 8 * bands * area * hidden),
        name="proj_back",
    )(side, own, halo, gout, *fixed)


def project_kernel(parts, count, own_ref, x_ref, gain_ref, bias_ref, w_ref, val_ref, m_ref, s_ref, *rest):
    sums, (out_ref, grad_ref, w_high, w_low) = rest[:parts], rest[parts:]
    t = pl.program_id(0)
    nz, _, chans, area = x_ref.shape
    hidden, chan_all = w_ref.shape

    @pl.when(t == 0)
    def _():
        w_high[...], w_low[...] = split(w_ref[...])
        grad_ref[...] = column(val_ref[0:1]) * m_ref[...] + column(val_ref[1:2]) * s_ref[...]

    _, _, scale, shift = norm_terms(total(sums), count, gain_ref[1:2], bias_ref[1:2])
    out = None
    for cut in chunks(hidden):
        v = own_ref[0, :, cut] * scale[:, cut] + shift[:, cut]
        term = dot3(split(v * sigmoid(v)), (w_high[cut], w_low[cut]))
        out = term if out is None else out + term
    out = (out * val_ref[0:1]).T
    out_ref[:, 0] = x_ref[:, 0] + out.reshape(nz, chans, area)


def project(count, own, x, gains, biases, w, values, m, s, sums):
    nz, bands, chans, area = x.shape
    hidden = w.shape[0]
    chan_all = nz * chans
    fixed = [gains, biases, w, values, m, s, *sums]
    return pl.pallas_call(
        partial(project_kernel, len(sums), count),
        grid=(bands,),
        in_specs=[
            pl.BlockSpec((1, area, hidden), lambda t: (t, 0, 0)),
            pl.BlockSpec((nz, 1, chans, area), lambda t: (0, t, 0, 0)),
        ]
        + [whole(a.shape) for a in fixed],
        out_specs=[pl.BlockSpec((nz, 1, chans, area), lambda t: (0, t, 0, 0)), whole(m.shape)],
        out_shape=[
            jax.ShapeDtypeStruct((nz, bands, chans, area), F32),
            jax.ShapeDtypeStruct(m.shape, F32),
        ],
        scratch_shapes=[pltpu.VMEM(w.shape, BF16), pltpu.VMEM(w.shape, BF16)],
        compiler_params=params(40),
        cost_estimate=cost(6 * bands * area * hidden * chan_all, 4 * bands * area * hidden),
        name="project",
    )(own, x, *fixed)


def spread_back_kernel(
    parts,
    count,
    side_ref,
    hid_ref,
    hid_halo_ref,
    own_ref,
    halo_ref,
    q_ref,
    q_halo_ref,
    gain_ref,
    bias_ref,
    w_ref,
    *rest,
):
    sums_one, sums_two, backs = (rest[i * parts : (i + 1) * parts] for i in range(3))
    out_ref, sum_ref, tap_ref, pad, grad, terms = rest[3 * parts :]
    rows = own_ref.shape[0]
    mean, inverse, scale, shift = norm_terms(total(sums_one), count, gain_ref[0:1], bias_ref[0:1])
    a, b, c0 = back_terms(total(sums_two), total(backs), count, gain_ref[1:2])
    for i, row in enumerate((scale, shift, a, b, c0, mean, inverse)):
        terms[i] = jnp.broadcast_to(row, (SUB, 128))

    def act(value):
        v = value * terms[0] + terms[1]
        return v * sigmoid(v)

    def grad_in(q, value):
        return q * terms[2] + (value * terms[3] + terms[4])

    def own_row(r, _):
        for c in range(SUB):
            pad[r + HALO_OUT, c + 2] = act(hid_ref[r, c])
            grad[r + HALO_OUT, c + 2] = grad_in(q_ref[r, c], own_ref[r, c])
        fill_sides(pad, r + HALO_OUT)
        fill_sides(grad, r + HALO_OUT)
        return 0

    lax.fori_loop(0, rows, own_row, 0)
    for side, start, first in ((0, 0, HALO_IN - HALO_OUT), (1, rows + HALO_OUT, 0)):

        @pl.when(side_ref[side] == 1)
        def _(side=side, start=start, first=first):
            for r in range(HALO_OUT):
                for c in range(SUB):
                    pad[start + r, c + 2] = act(hid_halo_ref[side, first + r, c])
                    grad[start + r, c + 2] = grad_in(q_halo_ref[side, r, c], halo_ref[side, r, c])
                fill_sides(pad, start + r)
                fill_sides(grad, start + r)

        @pl.when(side_ref[side] == 0)
        def _(start=start):
            clear_rows(pad, start, HALO_OUT)
            clear_rows(grad, start, HALO_OUT)

    def weight_group(i, acc):
        acc = list(acc)
        r = i // SUB * SUB
        c = i % SUB
        mine = [grad[r + HALO_OUT + o, c + 2] for o in range(SUB)]
        for bb in range(K):
            for row in range(SUB + K - 1):
                value = pad[r + row, c + bb]
                for aa in range(K):
                    o = row - aa
                    if 0 <= o < SUB:
                        acc[aa * K + bb] = acc[aa * K + bb] + value * mine[o]
        return tuple(acc)

    zero = jnp.zeros((SUB, 128), F32)
    acc = lax.fori_loop(0, rows, weight_group, (zero,) * TAPS)
    for tap in range(TAPS):
        tap_ref[tap : tap + 1] = jnp.sum(acc[tap], axis=0, keepdims=True)

    def group(i, carry):
        one, two = carry
        r = i * SUB
        for c in range(SUB):
            acc = tap_rows(grad, w_ref, r, SUB, c, flipped=True)
            for o in range(SUB):
                hidden = hid_ref[r + o, c]
                v = hidden * terms[0] + terms[1]
                s = sigmoid(v)
                value = acc[o] * (s + v * s * (1.0 - s))
                out_ref[r + o, c] = value
                one = one + value
                two = two + value * ((hidden - terms[5]) * terms[6])
        return one, two

    one, two = lax.fori_loop(0, rows // SUB, group, (zero, zero))
    sum_ref[0:1] = jnp.sum(one, axis=0, keepdims=True)
    sum_ref[1:2] = jnp.sum(two, axis=0, keepdims=True)


def spread_back(count, side, hid, hid_halo, own, halo, q, q_halo, gains, biases, taps, sums_one, sums_two, backs):
    rows, hidden = own.shape[0], own.shape[-1]
    arrays = [hid, hid_halo, own, halo, q, q_halo, gains, biases, taps, *sums_one, *sums_two, *backs]
    return pl.pallas_call(
        partial(spread_back_kernel, len(backs), count),
        grid=(hidden // 128,),
        in_specs=[pl.BlockSpec(memory_space=pltpu.SMEM)] + [lanes(a.shape) for a in arrays],
        out_specs=[lanes((rows, SUB, SUB, hidden)), lanes((2, hidden)), lanes((TAPS, hidden))],
        out_shape=[
            jax.ShapeDtypeStruct((rows, SUB, SUB, hidden), F32),
            jax.ShapeDtypeStruct((2, hidden), F32),
            jax.ShapeDtypeStruct((TAPS, hidden), F32),
        ],
        scratch_shapes=[
            pltpu.VMEM((rows + 2 * HALO_OUT, SUB + 4, SUB, 128), F32),
            pltpu.VMEM((rows + 2 * HALO_OUT, SUB + 4, SUB, 128), F32),
            pltpu.VMEM((7, SUB, 128), F32),
        ],
        compiler_params=params(48),
        cost_estimate=cost(rows * 64 * hidden * 1600, 16 * rows * 64 * hidden),
        name="spread_back",
    )(side, *arrays)


def expand_back_kernel(parts, count, q_ref, hid_ref, x_ref, gout_ref, gain_ref, wt_ref, *rest):
    sums, backs = rest[:parts], rest[parts : 2 * parts]
    grad_ref, out_ref, w_high, w_low = rest[2 * parts :]
    t = pl.program_id(0)
    nz, _, chans, area = x_ref.shape
    hidden, chan_all = wt_ref.shape

    @pl.when(t == 0)
    def _():
        w_high[...], w_low[...] = split(wt_ref[...])
        grad_ref[...] = jnp.zeros_like(grad_ref)

    a, b, c = back_terms(total(sums), total(backs), count, gain_ref[0:1])
    x = split(x_ref[:, 0].reshape(chan_all, area))
    out = None
    for cut in chunks(hidden):
        grad = split(q_ref[0, :, cut] * a[:, cut] + (hid_ref[0, :, cut] * b[:, cut] + c[:, cut]))
        grad_ref[:, cut] += dot3(x, grad)
        term = dot3(grad, (w_high[cut], w_low[cut]))
        out = term if out is None else out + term
    out_ref[:, 0] = gout_ref[:, 0] + out.T.reshape(nz, chans, area)


def expand_back(count, q, hid, x, gout, gains, wt, sums, backs):
    nz, bands, chans, area = x.shape
    hidden = wt.shape[0]
    chan_all = nz * chans
    fixed = [gains, wt, *sums, *backs]
    return pl.pallas_call(
        partial(expand_back_kernel, len(sums), count),
        grid=(bands,),
        in_specs=[
            pl.BlockSpec((1, area, hidden), lambda t: (t, 0, 0)),
            pl.BlockSpec((1, area, hidden), lambda t: (t, 0, 0)),
            pl.BlockSpec((nz, 1, chans, area), lambda t: (0, t, 0, 0)),
            pl.BlockSpec((nz, 1, chans, area), lambda t: (0, t, 0, 0)),
        ]
        + [whole(v.shape) for v in fixed],
        out_specs=[whole((chan_all, hidden)), pl.BlockSpec((nz, 1, chans, area), lambda t: (0, t, 0, 0))],
        out_shape=[
            jax.ShapeDtypeStruct((chan_all, hidden), F32),
            jax.ShapeDtypeStruct((nz, bands, chans, area), F32),
        ],
        scratch_shapes=[pltpu.VMEM(wt.shape, BF16), pltpu.VMEM(wt.shape, BF16)],
        compiler_params=params(40),
        cost_estimate=cost(12 * bands * area * hidden * chan_all, 8 * bands * area * hidden),
        name="expand_back",
    )(q, hid, x, gout, *fixed)


def segments(chan_in, hidden_dev, chan_dev, reduced, tap_count, hidden_all):
    seg_sizes = [
        chan_in * hidden_dev,
        tap_count * hidden_dev,
        2 * hidden_dev,
        2 * hidden_dev,
        hidden_dev * chan_in,
        chan_dev * reduced,
        reduced,
        reduced * chan_dev,
        chan_dev,
    ]
    seg_rates = [
        0.5 / math.sqrt(chan_in),
        0.5 / math.sqrt(tap_count),
        0.3,
        0.3,
        0.5 * math.sqrt(8.0 / hidden_all),
        2.0 / math.sqrt(chan_in),
        0.3,
        1.0 / math.sqrt(reduced),
        0.3,
    ]
    return (seg_sizes, seg_rates)


def in_blocks(pieces, block_len):
    flat = jnp.concatenate([piece.reshape(-1) for piece in pieces])
    blocks = -(-flat.shape[0] // block_len)
    return jnp.pad(flat, (0, blocks * block_len - flat.shape[0])).reshape(blocks, block_len)


def thirds(v):
    high = v.astype(BF16)
    rest = v - high.astype(F32)
    mid = rest.astype(BF16)
    return high, mid, (rest - mid.astype(F32)).astype(BF16)


def choose(chosen, v):
    high, mid, low = thirds(v)
    return (dot(chosen, high) + dot(chosen, mid)) + dot(chosen, low)


def adam_kernel(
    bounds,
    rates,
    capacity,
    me_ref,
    row_ref,
    col_ref,
    grad_ref,
    weight_ref,
    first_all_ref,
    second_all_ref,
    first_ref,
    second_ref,
    first_out,
    second_out,
    new_ref,
):
    blocks, length = grad_ref.shape
    slots = first_all_ref.shape[0]
    own_row, own_col = row_ref[...], col_ref[...]
    i = lax.broadcasted_iota(jnp.int32, (blocks, blocks), 0)
    j = lax.broadcasted_iota(jnp.int32, (blocks, blocks), 1)
    same = own_row == own_col
    before = jnp.sum(jnp.where(same & (j < i), 1.0, 0.0), axis=1, keepdims=True)
    slot_col = own_col * capacity + before.astype(jnp.int32)
    behind = jnp.sum(jnp.where(same & (i < j), 1.0, 0.0), axis=0, keepdims=True)
    slot_row = own_row * capacity + behind.astype(jnp.int32)
    grad = grad_ref[...]

    mine = lax.broadcasted_iota(jnp.int32, (capacity, blocks), 0) + me_ref[0] * capacity
    owned = choose((mine == slot_row).astype(F32).astype(BF16), grad)
    first_out[0] = beta_first * first_ref[0] + (1.0 - beta_first) * owned
    second_out[0] = beta_second * second_ref[0] + (1.0 - beta_second) * owned * owned

    pick_slot = lax.broadcasted_iota(jnp.int32, (blocks, slots), 1) == slot_col
    chosen = pick_slot.astype(F32).astype(BF16)
    first = beta_first * choose(chosen, first_all_ref[...]) + (1.0 - beta_first) * grad
    second = beta_second * choose(chosen, second_all_ref[...]) + (1.0 - beta_second) * grad * grad
    first_hat = first / (1.0 - beta_first**STEP)
    second_hat = second / (1.0 - beta_second**STEP)
    place = lax.broadcasted_iota(jnp.int32, (blocks, length), 0) * length + lax.broadcasted_iota(
        jnp.int32, (blocks, length), 1
    )
    rate = jnp.zeros((blocks, length), F32)
    for bound, value in zip(reversed(bounds), reversed(rates)):
        rate = jnp.where(place < bound, jnp.float32(value), rate)
    new = weight_ref[...] * (1.0 - rate * weight_decay) - rate * first_hat / (
        jnp.sqrt(second_hat) + adam_eps
    )
    new_ref[...] = new


def adam(me, owners, grads, weights, first_all, second_all, first, second, bounds, rates):
    capacity = first.shape[1]
    arrays = [owners.reshape(1, -1), owners, grads, weights, first_all, second_all, first, second]
    return pl.pallas_call(
        partial(adam_kernel, bounds, rates, capacity),
        grid=(1,),
        in_specs=[pl.BlockSpec(memory_space=pltpu.SMEM)] + [whole(a.shape) for a in arrays],
        out_specs=[whole(first.shape), whole(second.shape), whole(grads.shape)],
        out_shape=[
            jax.ShapeDtypeStruct(first.shape, F32),
            jax.ShapeDtypeStruct(second.shape, F32),
            jax.ShapeDtypeStruct(grads.shape, F32),
        ],
        compiler_params=params(40),
        cost_estimate=cost(10**8, 4 * 6 * grads.size),
        name="adam",
    )(me, *arrays)


def sum_to_group(rows):
    n_pix = lax.axis_size(PIX)
    nz = lax.axis_size("chan")
    n, hidden = rows.shape
    dealt = lax.all_to_all(rows.reshape(n_pix, n // n_pix, hidden), PIX, 0, 0, tiled=True)
    mine = jnp.sum(dealt, axis=0).reshape(n // n_pix, nz, hidden // nz).transpose(1, 0, 2)
    return jnp.sum(lax.all_to_all(mine, "chan", 0, 0, tiled=True), axis=0)


def local(
    frames_raw,
    grad_out,
    col_offsets,
    flip_flags,
    owners,
    w_expand,
    w_dw,
    norm_gains,
    norm_biases,
    w_project,
    squeeze_matrix,
    se_down_bias,
    excite_matrix,
    excite_bias_row,
    first_moment,
    second_moment,
):
    nz, nhi, nlo = (lax.axis_size(axis) for axis in ALL)
    frames, chans, stored = frames_raw.shape
    band = stored // WIN
    area = band * FRAME_COLUMNS
    rows = nlo * band
    chan_in, hidden_dev = w_expand.shape
    hidden = hidden_dev * nz
    reduced = squeeze_matrix.shape[1]
    group = nz // MB * nhi * nlo
    count = float(frames // MB * FRAME_ROWS * FRAME_COLUMNS)
    hi = lax.axis_index("hi")
    side = jnp.stack([(hi > 0).astype(jnp.int32), (hi < nhi - 1).astype(jnp.int32)])

    crops = crop(frames_raw, col_offsets, flip_flags)
    x = deal(crops).reshape(nz, nlo, chans, area)
    gout = deal(order(grad_out)).reshape(nz, nlo, chans, area)

    w_expand_all = lax.all_gather(w_expand, "chan", axis=1, tiled=True)
    w_project_all = lax.all_gather(w_project, "chan", axis=0, tiled=True)
    hidden_rows = jnp.concatenate([w_dw, norm_gains, norm_biases], axis=0)
    hidden_rows = lax.all_gather(hidden_rows, "chan", axis=1, tiled=True)
    taps = jnp.broadcast_to(hidden_rows[:TAPS, None, :], (TAPS, SUB, hidden))
    gains = hidden_rows[TAPS : TAPS + 2]
    biases = hidden_rows[TAPS + 2 : TAPS + 4]
    se_rows = jnp.concatenate([squeeze_matrix.T, excite_matrix, excite_bias_row[None]], axis=0)
    se_rows = lax.all_gather(se_rows, "chan", axis=0)
    se_rows = se_rows.transpose(1, 0, 2).reshape(2 * reduced + 1, chan_in)
    sq_t, ex_all, ex_bias = se_rows[:reduced], se_rows[reduced : 2 * reduced], se_rows[2 * reduced :]
    se_weights = [sq_t.T, sq_t, se_down_bias[None], ex_all, ex_all.T, ex_bias]
    w_project_t = w_project_all.T
    w_expand_t = w_expand_all.T

    first_all = lax.all_gather(first_moment[0], PIX, axis=0, tiled=True)
    second_all = lax.all_gather(second_moment[0], PIX, axis=0, tiled=True)

    top, low = rims(x, HALO_IN, band)
    g_top, g_low = rims(gout, HALO_OUT, band)

    def as_rows(v):
        return v.reshape(rows, SUB, SUB, hidden)

    def as_bands(v):
        return v.reshape(nlo, area, hidden)

    def as_sides(v, n):
        return v.reshape(2, n, SUB, SUB, hidden)

    hid, hid_halo, sums_one = expand(x, top, low, w_expand_all)
    hid_halo = as_sides(hid_halo, HALO_IN)
    sums_one = shares(sums_one, 1, group)
    spatial, spatial_halo, sums_two = spread(count, side, as_rows(hid), hid_halo, gains, biases, taps, sums_one)
    sums_two = shares(sums_two, 1, group)
    m, s, se_part = gather(count, as_bands(spatial), gout, gains, biases, w_project_t, sums_two)
    ses = shares(se_part, nlo, nhi)
    q, q_halo, back_two, values = proj_back(
        count,
        side,
        as_bands(spatial),
        spatial_halo.reshape(2, -1, hidden),
        gout,
        g_top,
        g_low,
        gains,
        biases,
        w_project_t,
        se_weights,
        ses,
        sums_two,
    )
    backs_two = shares(back_two, 1, group)
    out, g_project = project(count, as_bands(spatial), x, gains, biases, w_project_all, values, m, s, sums_two)
    output = restore(deal(out.reshape(frames, chans, area)))
    q1, back_one, g_dw = spread_back(
        count,
        side,
        as_rows(hid),
        hid_halo,
        spatial,
        spatial_halo,
        as_rows(q),
        as_sides(q_halo, HALO_OUT),
        gains,
        biases,
        taps,
        sums_one,
        sums_two,
        backs_two,
    )
    backs_one = shares(back_one, 1, group)
    g_expand, grad_x = expand_back(count, as_bands(q1), hid, x, gout, gains, w_expand_t, sums_one, backs_one)
    grad_frames = uncrop(deal(grad_x.reshape(frames, chans, area)), col_offsets, flip_flags)

    lead = (hi == 0).astype(F32)
    excite_row, logit, pooled = values[0:1], values[2:3], values[3:4]
    squeezed, grad_sq = values[4, :reduced], values[5, :reduced]
    logit, grad_sq = logit * lead, grad_sq * lead
    g_sq_t = grad_sq[:, None] * pooled
    g_ex = squeezed[:, None] * logit
    spare = jnp.zeros((reduced, nz, chans), F32)
    spare = spare.at[0].set(logit.reshape(nz, chans))
    spare = spare.at[1, :, :reduced].set(jnp.broadcast_to(grad_sq, (nz, reduced)))
    se_grads = jnp.concatenate(
        [
            g_sq_t.reshape(reduced, nz, chans),
            g_ex.reshape(reduced, nz, chans),
            spare,
            jnp.zeros((reduced, nz, hidden_dev - 3 * chans), F32),
        ],
        axis=2,
    ).reshape(reduced, hidden)
    small = jnp.concatenate(
        [
            g_dw,
            back_one[1:2],
            back_two[1:2],
            back_one[0:1],
            back_two[0:1],
            jnp.zeros((3, hidden), F32),
            se_grads,
            jnp.zeros((16, hidden), F32),
        ],
        axis=0,
    )
    n_pix = nhi * nlo

    def everywhere(v):
        return lax.all_gather(v, PIX, axis=0, tiled=True)

    g_project = everywhere(sum_to_group(g_project))
    small = everywhere(sum_to_group(small))
    g_expand = everywhere(sum_to_group(g_expand))
    se_block = small[32 : 32 + reduced]
    block_len = first_moment.shape[2]
    grads = in_blocks(
        [
            g_expand,
            small[: TAPS + 4],
            g_project.T,
            se_block[:, :chans].T,
            se_block[1, 2 * chans : 2 * chans + reduced],
            se_block[:, chans : 2 * chans],
            se_block[0, 2 * chans : 3 * chans],
        ],
        block_len,
    )
    weights = in_blocks(
        [
            w_expand,
            w_dw,
            norm_gains,
            norm_biases,
            w_project,
            squeeze_matrix,
            se_down_bias,
            excite_matrix,
            excite_bias_row,
        ],
        block_len,
    )
    seg_sizes, seg_rates = segments(chan_in, hidden_dev, chans, reduced, TAPS, hidden)
    bounds = [sum(seg_sizes[: i + 1]) for i in range(len(seg_sizes))]
    me = (hi * nlo + lax.axis_index("lo")).astype(jnp.int32).reshape(1)
    first_next, second_next, new = adam(
        me, owners, grads, weights, first_all, second_all, first_moment, second_moment, bounds, seg_rates
    )
    new_params = new.reshape(-1)[: bounds[-1]][None, :]
    return (output, grad_frames, first_next, second_next, new_params)


def solution(mesh):
    nz, n_pix = mesh.shape["chan"], mesh.shape["pix"]
    placed = (
        P(None, "chan", PIX),
        P(None, "chan", PIX),
        P(),
        P(),
        P(),
        P(None, "chan"),
        P(None, "chan"),
        P(None, "chan"),
        P(None, "chan"),
        P("chan", None),
        P("chan", None),
        P(),
        P(None, "chan"),
        P("chan"),
        P("chan", PIX, None),
        P("chan", PIX, None),
    )

    def run(*arrays):
        nlo = arrays[0].shape[0] // nz
        return jax.shard_map(
            local,
            mesh=Mesh(mesh.devices.reshape(nz, n_pix // nlo, nlo), ALL),
            in_specs=placed,
            out_specs=(
                P(None, "chan", PIX),
                P(None, "chan", PIX),
                P("chan", PIX, None),
                P("chan", PIX, None),
                P("chan", None),
            ),
            check_vma=False,
        )(*arrays)

    return run
```

```python
from functools import partial
import math

import jax
import jax.numpy as jnp
from jax import lax
from jax.experimental import pallas as pl
from jax.experimental.pallas import tpu as pltpu
from jax.sharding import Mesh, PartitionSpec as P

K = 5
FRAME_ROWS = 64
FRAME_COLUMNS = 64
CLIP_LEN = 4
MB = 4
STEP = 5
WIN = 80
SUB = 8
TAPS = K * K
HALO_IN = 4
SMALL = 64
HALO_OUT = 2

norm_eps = 1e-05
beta_first = 0.5
beta_second = 0.6
adam_eps = 1e-08
weight_decay = 0.1

F32 = jnp.float32
BF16 = jnp.bfloat16
ALL = ("chan", "hi", "lo")
PIX = ("hi", "lo")
SPREAD = ("chan", "lo")
VMEM_BYTES = 60 * 2**20


def params(dims=1):
    return pltpu.CompilerParams(vmem_limit_bytes=VMEM_BYTES, dimension_semantics=("arbitrary",) * dims)


def cost(us):
    return pl.CostEstimate(flops=int(us * 1.1e9), bytes_accessed=int(us * 3.5e6), transcendentals=0)


def sigmoid(v):
    return 0.5 * jnp.tanh(0.5 * v) + 0.5


def split(v):
    high = v.astype(BF16)
    return high, (v - high.astype(F32)).astype(BF16)


def dot(a, b):
    return jnp.dot(a, b, preferred_element_type=F32)


def dot3(a, b):
    return dot(a[0], b[0]) + (dot(a[0], b[1]) + dot(a[1], b[0]))


def exact_dot(a, b):
    return jnp.dot(a, b, preferred_element_type=F32, precision=lax.Precision.HIGHEST)


def total(refs):
    value = refs[0][...]
    for ref in refs[1:]:
        value = value + ref[...]
    return value


def norm_terms(sums, count, gain, bias):
    mean = sums[0:1] / count
    inverse = lax.rsqrt(sums[1:2] / count - mean * mean + norm_eps)
    scale = gain * inverse
    return mean, inverse, scale, bias - mean * scale


def back_terms(sums, back, count, gain):
    mean = sums[0:1] / count
    inverse = lax.rsqrt(sums[1:2] / count - mean * mean + norm_eps)
    a = gain * inverse
    b = -a * inverse * (back[1:2] / count)
    return a, b, -a * (back[0:1] / count) - b * mean


def exchange(x, stride):
    n = lax.axis_size(ALL)
    return lax.ppermute(x, ALL, [(i, i ^ stride) for i in range(n)])


def shares(x, base, size):
    bits = size.bit_length() - 1
    parts = [x]
    if bits % 2:
        parts = [x, exchange(x, base)]
        base, bits = base * 2, bits - 1
    while bits:
        x = sum(parts[1:], parts[0])
        parts = [x] + [exchange(x, base * k) for k in (1, 2, 3)]
        base, bits = base * 4, bits - 2
    return parts


def deal(x):
    return lax.all_to_all(x, SPREAD, 0, 0, tiled=True)


def edge(x, rows, band, first):
    if rows >= band:
        n = rows // band
        return x[:, :n] if first else x[:, x.shape[1] - n :]
    width = rows * FRAME_COLUMNS
    return x[:, :1, :, :width] if first else x[:, -1:, :, x.shape[3] - width :]


def rims(x, rows, band):
    n = lax.axis_size("hi")
    if n == 2:
        mine = jnp.where(lax.axis_index("hi") == 0, edge(x, rows, band, False), edge(x, rows, band, True))
        other = lax.ppermute(mine, "hi", [(0, 1), (1, 0)])
        return other, other
    down = [(i, i + 1) for i in range(n - 1)]
    up = [(i + 1, i) for i in range(n - 1)]
    top = lax.ppermute(edge(x, rows, band, False), "hi", down)
    low = lax.ppermute(edge(x, rows, band, True), "hi", up)
    return top, low


def near(n_pix):
    return n_pix == 8


def gather_pix(x):
    n_pix = lax.axis_size(PIX)
    if not near(n_pix):
        return [lax.all_gather(x, PIX, axis=0)], [list(range(n_pix))]
    b = x[None]
    b = jnp.concatenate([b, exchange(b, 2)])
    b = jnp.concatenate([b, exchange(b, 4)])
    return [b, exchange(b, 1)], [[0, 2, 4, 6], [1, 3, 5, 7]]


def gather_chan(x):
    nz, n_pix = lax.axis_size("chan"), lax.axis_size(PIX)
    if not near(n_pix):
        return list(lax.all_gather(x, "chan", axis=0))
    return [x] + [exchange(x, k * n_pix) for k in range(1, nz)]


def source_column(p, left, flip):
    row, c, s = p // FRAME_COLUMNS, (p // SUB) % SUB, p % SUB
    j = s * SUB + c
    return row * WIN + left + jnp.where(flip == 1, FRAME_COLUMNS - 1 - j, j)


def plain_place(p):
    row, c, s = p // FRAME_COLUMNS, (p // SUB) % SUB, p % SUB
    return row * FRAME_COLUMNS + s * SUB + c


def pick(x, chosen):
    rows = x.shape[0] * x.shape[1]
    high, low = split(x.reshape(rows, x.shape[2]))
    return (dot(high, chosen) + dot(low, chosen)).reshape(x.shape[0], x.shape[1], chosen.shape[1])


def crop_kernel(left_ref, flip_ref, raw_ref, out_ref):
    k = pl.program_id(0)
    width, area = raw_ref.shape[2], out_ref.shape[2]
    p = lax.broadcasted_iota(jnp.int32, (1, area), 1)
    place = source_column(p, left_ref[k], flip_ref[k])
    q = lax.broadcasted_iota(jnp.int32, (width, area), 0)
    out_ref[...] = pick(raw_ref[...], (q == place).astype(F32).astype(BF16))


def crop(raw, left, flip):
    frames, chans, width = raw.shape
    area = width // WIN * FRAME_COLUMNS
    return pl.pallas_call(
        crop_kernel,
        grid=(frames // CLIP_LEN,),
        in_specs=[
            pl.BlockSpec(memory_space=pltpu.SMEM),
            pl.BlockSpec(memory_space=pltpu.SMEM),
            pl.BlockSpec((CLIP_LEN, chans, width), lambda k: (k, 0, 0)),
        ],
        out_specs=pl.BlockSpec((CLIP_LEN, chans, area), lambda k: (k, 0, 0)),
        out_shape=jax.ShapeDtypeStruct((frames, chans, area), F32),
        compiler_params=params(),
        cost_estimate=cost(5),
        name="crop",
    )(left, flip, raw)


def order_kernel(x_ref, out_ref):
    area = x_ref.shape[2]
    p = lax.broadcasted_iota(jnp.int32, (1, area), 1)
    q = lax.broadcasted_iota(jnp.int32, (area, area), 0)
    out_ref[...] = pick(x_ref[...], (q == plain_place(p)).astype(F32).astype(BF16))


def order(x):
    frames, chans, area = x.shape
    return pl.pallas_call(
        order_kernel,
        grid=(frames // CLIP_LEN,),
        in_specs=[pl.BlockSpec((CLIP_LEN, chans, area), lambda k: (k, 0, 0))],
        out_specs=pl.BlockSpec((CLIP_LEN, chans, area), lambda k: (k, 0, 0)),
        out_shape=jax.ShapeDtypeStruct((frames, chans, area), F32),
        compiler_params=params(),
        cost_estimate=cost(1),
        name="order",
    )(x)


def restore_kernel(x_ref, out_ref):
    area = x_ref.shape[2]
    p = lax.broadcasted_iota(jnp.int32, (area, 1), 0)
    q = lax.broadcasted_iota(jnp.int32, (area, area), 1)
    out_ref[...] = pick(x_ref[...], (q == plain_place(p)).astype(F32).astype(BF16))


def restore(x):
    frames, chans, area = x.shape
    return pl.pallas_call(
        restore_kernel,
        grid=(frames // CLIP_LEN,),
        in_specs=[pl.BlockSpec((CLIP_LEN, chans, area), lambda k: (k, 0, 0))],
        out_specs=pl.BlockSpec((CLIP_LEN, chans, area), lambda k: (k, 0, 0)),
        out_shape=jax.ShapeDtypeStruct((frames, chans, area), F32),
        compiler_params=params(),
        cost_estimate=cost(5),
        name="restore",
    )(x)


def uncrop_kernel(left_ref, flip_ref, x_ref, y_ref, out_ref):
    k = pl.program_id(0)
    area, width = x_ref.shape[2], out_ref.shape[2]
    q = lax.broadcasted_iota(jnp.int32, (area, width), 1)
    out = None
    for half, ref in enumerate((x_ref, y_ref)):
        p = lax.broadcasted_iota(jnp.int32, (area, 1), 0) + half * area
        place = source_column(p, left_ref[k], flip_ref[k])
        term = pick(ref[...], (q == place).astype(F32).astype(BF16))
        out = term if out is None else out + term
    out_ref[...] = out


def uncrop(x, y, left, flip):
    frames, chans, area = x.shape
    width = 2 * area // FRAME_COLUMNS * WIN
    return pl.pallas_call(
        uncrop_kernel,
        grid=(frames // CLIP_LEN,),
        in_specs=[
            pl.BlockSpec(memory_space=pltpu.SMEM),
            pl.BlockSpec(memory_space=pltpu.SMEM),
            pl.BlockSpec((CLIP_LEN, chans, area), lambda k: (k, 0, 0)),
            pl.BlockSpec((CLIP_LEN, chans, area), lambda k: (k, 0, 0)),
        ],
        out_specs=pl.BlockSpec((CLIP_LEN, chans, width), lambda k: (k, 0, 0)),
        out_shape=jax.ShapeDtypeStruct((frames, chans, width), F32),
        compiler_params=params(),
        cost_estimate=cost(5),
        name="uncrop",
    )(left, flip, x, y)


def chunks(width):
    step = 256 if width % 256 == 0 else width
    return [slice(i, i + step) for i in range(0, width, step)]


def expand_kernel(x_ref, high_ref, low_ref, own_ref, sum_ref, gram_ref):
    @pl.when(pl.program_id(0) == 0)
    def _():
        sum_ref[...] = jnp.zeros_like(sum_ref)
        gram_ref[...] = jnp.zeros_like(gram_ref)

    chan_all, hidden = high_ref.shape
    plain = x_ref[:, 0].reshape(chan_all, x_ref.shape[3])
    turned = plain.T
    x = split(turned)
    for cut in chunks(hidden):
        y = dot3(x, (high_ref[:, cut], low_ref[:, cut]))
        own_ref[0, :, cut] = y
        sum_ref[0:1, cut] += jnp.sum(y, axis=0, keepdims=True)
        sum_ref[1:2, cut] += jnp.sum(y * y, axis=0, keepdims=True)
    gram_ref[:, 0:chan_all] += dot3(split(plain), x)
    gram_ref[:, chan_all:] += jnp.broadcast_to(jnp.sum(plain, axis=1, keepdims=True), (chan_all, 128))


def whole(shape):
    return pl.BlockSpec(shape, lambda *_: (0,) * len(shape))


def expand(x, high, low):
    nz, bands, chans, area = x.shape
    hidden = high.shape[1]
    return pl.pallas_call(
        expand_kernel,
        grid=(bands,),
        in_specs=[
            pl.BlockSpec((nz, 1, chans, area), lambda t: (0, t, 0, 0)),
            whole(high.shape),
            whole(low.shape),
        ],
        out_specs=[
            pl.BlockSpec((1, area, hidden), lambda t: (t, 0, 0)),
            whole((2, hidden)),
            whole((nz * chans, nz * chans + 128)),
        ],
        out_shape=[
            jax.ShapeDtypeStruct((bands, area, hidden), F32),
            jax.ShapeDtypeStruct((2, hidden), F32),
            jax.ShapeDtypeStruct((nz * chans, nz * chans + 128), F32),
        ],
        compiler_params=params(),
        cost_estimate=cost(8),
        name="expand",
    )(x, high, low)


def fill_sides(pad, row):
    s = lax.broadcasted_iota(jnp.int32, (SUB, 128), 0)
    for k in range(2):
        left = pltpu.roll(pad[row, SUB + k], 1, 0)
        pad[row, k] = jnp.where(s == 0, 0.0, left)
        right = pltpu.roll(pad[row, 2 + k], SUB - 1, 0)
        pad[row, SUB + 2 + k] = jnp.where(s == SUB - 1, 0.0, right)


def clear_rows(pad, start, count):
    for row in range(start, start + count):
        pad[row] = jnp.zeros(pad.shape[1:], F32)


def tap_rows(pad, w_ref, start, count, c, flipped=False):
    acc = [None] * count
    for b in range(K):
        for row in range(count + K - 1):
            value = pad[start + row, c + b]
            for a in range(K):
                o = row - a
                if 0 <= o < count:
                    tap = a * K + b
                    term = value * w_ref[TAPS - 1 - tap if flipped else tap]
                    acc[o] = term if acc[o] is None else acc[o] + term
    return acc


def turn_rims(refs, side_ref, high, low):
    for side, ref in enumerate(refs):
        chan_all, width = ref.shape[0] * ref.shape[2], ref.shape[3]

        @pl.when(side_ref[side] == 1)
        def _(side=side, ref=ref, chan_all=chan_all, width=width):
            for k in range(ref.shape[1]):
                here = slice(k * width, (k + 1) * width)
                high[side, here], low[side, here] = split(ref[:, k].reshape(chan_all, width).T)


def spread_kernel(
    parts, count, side_ref, top_ref, low_ref, own_ref, high_ref, lower_ref, gain_ref, bias_ref, w_ref, *rest
):
    sums = rest[:parts]
    out_ref, edge_ref, hid_ref, sum_ref, pad, terms, rim_high, rim_low = rest[parts:]
    rows = own_ref.shape[0]
    _, _, scale, shift = norm_terms(total(sums), count, gain_ref[0:1], bias_ref[0:1])
    terms[0] = jnp.broadcast_to(scale, (SUB, 128))
    terms[1] = jnp.broadcast_to(shift, (SUB, 128))

    @pl.when(pl.program_id(0) == 0)
    def _():
        turn_rims((top_ref, low_ref), side_ref, rim_high, rim_low)

    def act(value):
        v = value * terms[0] + terms[1]
        return v * sigmoid(v)

    def own_row(r, _):
        for c in range(SUB):
            pad[r + HALO_IN, c + 2] = act(own_ref[r, c])
        fill_sides(pad, r + HALO_IN)
        return 0

    lax.fori_loop(0, rows, own_row, 0)
    for side, start, first in ((0, 0, HALO_IN - HALO_OUT), (1, rows + HALO_IN, 0)):

        @pl.when(side_ref[side] == 1)
        def _(side=side, start=start, first=first):
            halo = dot3((rim_high[side], rim_low[side]), (high_ref[...], lower_ref[...]))
            halo = halo.reshape(HALO_IN, SUB, SUB, 128)
            hid_ref[side] = halo[first : first + HALO_OUT]
            pad[start : start + HALO_IN, 2 : SUB + 2] = act(halo)
            for r in range(HALO_IN):
                fill_sides(pad, start + r)

        @pl.when(side_ref[side] == 0)
        def _(side=side, start=start):
            clear_rows(pad, start, HALO_IN)
            hid_ref[side] = jnp.zeros(hid_ref.shape[1:], F32)

    def group(i, carry):
        one, two = carry
        r = i * SUB
        for c in range(SUB):
            acc = tap_rows(pad, w_ref, r + 2, SUB, c)
            for o in range(SUB):
                out_ref[r + o, c] = acc[o]
                one = one + acc[o]
                two = two + acc[o] * acc[o]
        return one, two

    zero = jnp.zeros((SUB, 128), F32)
    one, two = lax.fori_loop(0, rows // SUB, group, (zero, zero))
    sum_ref[0:1] = jnp.sum(one, axis=0, keepdims=True)
    sum_ref[1:2] = jnp.sum(two, axis=0, keepdims=True)
    for side, start in ((0, 0), (1, rows + 2)):

        @pl.when(side_ref[side] == 1)
        def _(side=side, start=start):
            for c in range(SUB):
                acc = tap_rows(pad, w_ref, start, HALO_OUT, c)
                for o in range(HALO_OUT):
                    edge_ref[side, o, c] = acc[o]

        @pl.when(side_ref[side] == 0)
        def _(side=side):
            edge_ref[side] = jnp.zeros(edge_ref.shape[1:], F32)


def lanes(shape):
    lead = len(shape) - 1
    return pl.BlockSpec(tuple(shape[:-1]) + (128,), lambda e: (0,) * lead + (e,))


def spread(count, side, top, low, own, w_high, w_low, gains, biases, taps, sums):
    rows, hidden = own.shape[0], own.shape[-1]
    chan_all = w_high.shape[0]
    arrays = [own, w_high, w_low, gains, biases, taps, *sums]
    edge_shape = (2, HALO_OUT, SUB, SUB, hidden)
    rim_shape = (2, HALO_IN * FRAME_COLUMNS, chan_all)
    return pl.pallas_call(
        partial(spread_kernel, len(sums), count),
        grid=(hidden // 128,),
        in_specs=[pl.BlockSpec(memory_space=pltpu.SMEM), whole(top.shape), whole(low.shape)]
        + [lanes(a.shape) for a in arrays],
        out_specs=[
            lanes((rows, SUB, SUB, hidden)),
            lanes(edge_shape),
            lanes(edge_shape),
            lanes((2, hidden)),
        ],
        out_shape=[
            jax.ShapeDtypeStruct((rows, SUB, SUB, hidden), F32),
            jax.ShapeDtypeStruct(edge_shape, F32),
            jax.ShapeDtypeStruct(edge_shape, F32),
            jax.ShapeDtypeStruct((2, hidden), F32),
        ],
        scratch_shapes=[
            pltpu.VMEM((rows + 2 * HALO_IN, SUB + 4, SUB, 128), F32),
            pltpu.VMEM((2, SUB, 128), F32),
            pltpu.VMEM(rim_shape, BF16),
            pltpu.VMEM(rim_shape, BF16),
        ],
        compiler_params=params(),
        cost_estimate=cost(25),
        name="spread",
    )(side, top, low, *arrays)


def as_row(columns):
    width = columns.shape[1]
    folded = columns[:, 0:128]
    for i in range(128, width, 128):
        folded = folded + columns[:, i : i + 128]
    return jnp.sum(folded.T, axis=0, keepdims=True)


def gather_kernel(parts, count, own_ref, gout_ref, gain_ref, bias_ref, wt_ref, high_ref, low_ref, *rest):
    sums, (m_ref, s_ref, se_ref, proj_ref) = rest[:parts], rest[parts:]
    t = pl.program_id(0)
    chan_all, hidden = wt_ref.shape

    @pl.when(t == 0)
    def _():
        m_ref[...] = jnp.zeros_like(m_ref)
        s_ref[...] = jnp.zeros_like(s_ref)

    _, _, scale, shift = norm_terms(total(sums), count, gain_ref[1:2], bias_ref[1:2])
    gout = split(gout_ref[:, 0].reshape(chan_all, gout_ref.shape[3]))
    proj = None
    for cut in chunks(hidden):
        v = own_ref[0, :, cut] * scale[:, cut] + shift[:, cut]
        act = v * sigmoid(v)
        s_ref[0:1, cut] += jnp.sum(act, axis=0, keepdims=True)
        act = split(act)
        m_ref[:, cut] += dot3(gout, act)
        term = dot3(act, (high_ref[cut], low_ref[cut]))
        proj = term if proj is None else proj + term
    proj_ref[0] = proj

    @pl.when(t == pl.num_programs(0) - 1)
    def _():
        wt = wt_ref[...]
        se_ref[0:1] = as_row(s_ref[...] * wt)
        se_ref[1:2] = as_row(m_ref[...] * wt)


def gather(count, own, gout, gains, biases, wt, w_high, w_low, sums):
    nz, bands, chans, area = gout.shape
    hidden = wt.shape[1]
    chan_all = nz * chans
    return pl.pallas_call(
        partial(gather_kernel, len(sums), count),
        grid=(bands,),
        in_specs=[
            pl.BlockSpec((1, area, hidden), lambda t: (t, 0, 0)),
            pl.BlockSpec((nz, 1, chans, area), lambda t: (0, t, 0, 0)),
            whole(gains.shape),
            whole(biases.shape),
            whole(wt.shape),
            whole(w_high.shape),
            whole(w_low.shape),
        ]
        + [whole(s.shape) for s in sums],
        out_specs=[
            whole((chan_all, hidden)),
            whole((1, hidden)),
            whole((2, chan_all)),
            pl.BlockSpec((1, area, chan_all), lambda t: (t, 0, 0)),
        ],
        out_shape=[
            jax.ShapeDtypeStruct((chan_all, hidden), F32),
            jax.ShapeDtypeStruct((1, hidden), F32),
            jax.ShapeDtypeStruct((2, chan_all), F32),
            jax.ShapeDtypeStruct((bands, area, chan_all), F32),
        ],
        compiler_params=params(),
        cost_estimate=cost(13),
        name="gather",
    )(own, gout, gains, biases, wt, w_high, w_low, *sums)


def column(row):
    return jnp.broadcast_to(row, (SUB, row.shape[1])).T[:, 0:1]


def padded_dot(row, matrix):
    return exact_dot(jnp.broadcast_to(row, (SUB, row.shape[1])), matrix)[0:1]


def slope_terms(sums, count, gain_ref, bias_ref):
    mean, inverse, _, _ = norm_terms(sums, count, gain_ref[1:2], bias_ref[1:2])
    return mean, inverse, gain_ref[1:2], bias_ref[1:2]


def second_grad(gout, weights, k_row, value, terms, cut):
    mean, inverse, gain, bias = terms
    grad = dot3(gout, (weights[0][:, cut], weights[1][:, cut])) + k_row[:, cut]
    centered = (value - mean[:, cut]) * inverse[:, cut]
    v = centered * gain[:, cut] + bias[:, cut]
    s = sigmoid(v)
    return grad * (s + v * s * (1.0 - s)), centered


def proj_back_kernel(
    pairs,
    parts,
    count,
    own_ref,
    gout_ref,
    gain_ref,
    bias_ref,
    wt_ref,
    sq_ref,
    sqt_ref,
    down_ref,
    ex_ref,
    ext_ref,
    exb_ref,
    *rest,
):
    ses, sums = rest[:pairs], rest[pairs : pairs + parts]
    q_ref, sum_ref, val_ref, w_high, w_low, k_row = rest[pairs + parts :]
    chan_all, hidden = wt_ref.shape
    reduced = ex_ref.shape[0]

    @pl.when(pl.program_id(0) == 0)
    def _():
        se = total(ses)
        pooled = se[0:1] / (FRAME_ROWS * FRAME_COLUMNS)
        pre = padded_dot(pooled, sq_ref[...]) + down_ref[...]
        gate = sigmoid(pre)
        squeezed = pre * gate
        excite = sigmoid(padded_dot(squeezed, ex_ref[...]) + exb_ref[...])
        logit = se[1:2] * excite * (1.0 - excite)
        slope = gate * (1.0 + pre * (1.0 - gate))
        grad_sq = padded_dot(logit, ext_ref[...]) * slope
        pool_grad = padded_dot(grad_sq, sqt_ref[...]) / (FRAME_ROWS * FRAME_COLUMNS)
        val_ref[...] = jnp.zeros_like(val_ref)
        val_ref[0:1] = excite
        val_ref[1:2] = pool_grad
        val_ref[2:3] = logit
        val_ref[3:4] = pooled
        val_ref[4:5, 0:reduced] = squeezed
        val_ref[5:6, 0:reduced] = grad_sq
        wt = wt_ref[...]
        w_high[...], w_low[...] = split(wt * column(excite))
        k_row[...] = jnp.sum(wt * column(pool_grad), axis=0, keepdims=True)
        sum_ref[...] = jnp.zeros_like(sum_ref)

    terms = slope_terms(total(sums), count, gain_ref, bias_ref)
    gout = split(gout_ref[:, 0].reshape(chan_all, gout_ref.shape[3]).T)
    for cut in chunks(hidden):
        q, centered = second_grad(gout, (w_high, w_low), k_row, own_ref[0, :, cut], terms, cut)
        q_ref[0, :, cut] = q
        sum_ref[0:1, cut] += jnp.sum(q, axis=0, keepdims=True)
        sum_ref[1:2, cut] += jnp.sum(q * centered, axis=0, keepdims=True)


def proj_back(count, own, gout, gains, biases, wt, se_weights, ses, sums):
    nz, bands, chans, area = gout.shape
    hidden = wt.shape[1]
    chan_all = nz * chans
    fixed = [gains, biases, wt, *se_weights, *ses, *sums]
    return pl.pallas_call(
        partial(proj_back_kernel, len(ses), len(sums), count),
        grid=(bands,),
        in_specs=[
            pl.BlockSpec((1, area, hidden), lambda t: (t, 0, 0)),
            pl.BlockSpec((nz, 1, chans, area), lambda t: (0, t, 0, 0)),
        ]
        + [whole(a.shape) for a in fixed],
        out_specs=[
            pl.BlockSpec((1, area, hidden), lambda t: (t, 0, 0)),
            whole((2, hidden)),
            whole((SUB, chan_all)),
            whole(wt.shape),
            whole(wt.shape),
            whole((1, hidden)),
        ],
        out_shape=[
            jax.ShapeDtypeStruct((bands, area, hidden), F32),
            jax.ShapeDtypeStruct((2, hidden), F32),
            jax.ShapeDtypeStruct((SUB, chan_all), F32),
            jax.ShapeDtypeStruct(wt.shape, BF16),
            jax.ShapeDtypeStruct(wt.shape, BF16),
            jax.ShapeDtypeStruct((1, hidden), F32),
        ],
        compiler_params=params(),
        cost_estimate=cost(12),
        name="proj_back",
    )(own, gout, *fixed)


def project_kernel(proj_ref, x_ref, val_ref, m_ref, s_ref, out_ref, grad_ref):
    nz, _, chans, area = x_ref.shape

    @pl.when(pl.program_id(0) == 0)
    def _():
        grad_ref[...] = column(val_ref[0:1]) * m_ref[...] + column(val_ref[1:2]) * s_ref[...]

    out = (proj_ref[0] * val_ref[0:1]).T
    out_ref[:, 0] = x_ref[:, 0] + out.reshape(nz, chans, area)


def project(proj, x, values, m, s):
    nz, bands, chans, area = x.shape
    fixed = [values, m, s]
    return pl.pallas_call(
        project_kernel,
        grid=(bands,),
        in_specs=[
            pl.BlockSpec((1, area, nz * chans), lambda t: (t, 0, 0)),
            pl.BlockSpec((nz, 1, chans, area), lambda t: (0, t, 0, 0)),
        ]
        + [whole(a.shape) for a in fixed],
        out_specs=[pl.BlockSpec((nz, 1, chans, area), lambda t: (0, t, 0, 0)), whole(m.shape)],
        out_shape=[
            jax.ShapeDtypeStruct((nz, bands, chans, area), F32),
            jax.ShapeDtypeStruct(m.shape, F32),
        ],
        compiler_params=params(),
        cost_estimate=cost(4),
        name="project",
    )(proj, x, *fixed)


def spread_back_kernel(
    parts,
    count,
    side_ref,
    top_ref,
    low_ref,
    hid_ref,
    hid_halo_ref,
    own_ref,
    halo_ref,
    q_ref,
    high_ref,
    lower_ref,
    k_ref,
    gain_ref,
    bias_ref,
    w_ref,
    *rest,
):
    sums_one, sums_two, backs = (rest[i * parts : (i + 1) * parts] for i in range(3))
    out_ref, sum_ref, tap_ref, pad, grad, terms, rim_high, rim_low = rest[3 * parts :]
    rows = own_ref.shape[0]

    @pl.when(pl.program_id(0) == 0)
    def _():
        turn_rims((top_ref, low_ref), side_ref, rim_high, rim_low)

    mean, inverse, scale, shift = norm_terms(total(sums_one), count, gain_ref[0:1], bias_ref[0:1])
    a, b, c0 = back_terms(total(sums_two), total(backs), count, gain_ref[1:2])
    for i, row in enumerate((scale, shift, a, b, c0, mean, inverse)):
        terms[i] = jnp.broadcast_to(row, (SUB, 128))

    def act(value):
        v = value * terms[0] + terms[1]
        return v * sigmoid(v)

    def grad_in(q, value):
        return q * terms[2] + (value * terms[3] + terms[4])

    def own_row(r, _):
        for c in range(SUB):
            pad[r + HALO_OUT, c + 2] = act(hid_ref[r, c])
            grad[r + HALO_OUT, c + 2] = grad_in(q_ref[r, c], own_ref[r, c])
        fill_sides(pad, r + HALO_OUT)
        fill_sides(grad, r + HALO_OUT)
        return 0

    lax.fori_loop(0, rows, own_row, 0)
    slope = slope_terms(total(sums_two), count, gain_ref, bias_ref)
    for side, start in ((0, 0), (1, rows + HALO_OUT)):

        @pl.when(side_ref[side] == 1)
        def _(side=side, start=start):
            value = halo_ref[side].reshape(HALO_OUT * FRAME_COLUMNS, 128)
            weights = (high_ref, lower_ref)
            gout = (rim_high[side], rim_low[side])
            q, _ = second_grad(gout, weights, k_ref, value, slope, slice(0, 128))
            edge = grad_in(q.reshape(HALO_OUT, SUB, SUB, 128), halo_ref[side])
            grad[start : start + HALO_OUT, 2 : SUB + 2] = edge
            pad[start : start + HALO_OUT, 2 : SUB + 2] = act(hid_halo_ref[side])
            for r in range(HALO_OUT):
                fill_sides(pad, start + r)
                fill_sides(grad, start + r)

        @pl.when(side_ref[side] == 0)
        def _(start=start):
            clear_rows(pad, start, HALO_OUT)
            clear_rows(grad, start, HALO_OUT)

    def weight_group(i, acc):
        acc = list(acc)
        r = i // SUB * SUB
        c = i % SUB
        mine = [grad[r + HALO_OUT + o, c + 2] for o in range(SUB)]
        for bb in range(K):
            for row in range(SUB + K - 1):
                value = pad[r + row, c + bb]
                for aa in range(K):
                    o = row - aa
                    if 0 <= o < SUB:
                        acc[aa * K + bb] = acc[aa * K + bb] + value * mine[o]
        return tuple(acc)

    zero = jnp.zeros((SUB, 128), F32)
    acc = lax.fori_loop(0, rows, weight_group, (zero,) * TAPS)
    for tap in range(TAPS):
        tap_ref[tap : tap + 1] = jnp.sum(acc[tap], axis=0, keepdims=True)

    def group(i, carry):
        one, two = carry
        r = i * SUB
        for c in range(SUB):
            acc = tap_rows(grad, w_ref, r, SUB, c, flipped=True)
            for o in range(SUB):
                hidden = hid_ref[r + o, c]
                v = hidden * terms[0] + terms[1]
                s = sigmoid(v)
                value = acc[o] * (s + v * s * (1.0 - s))
                out_ref[r + o, c] = value
                one = one + value
                two = two + value * ((hidden - terms[5]) * terms[6])
        return one, two

    one, two = lax.fori_loop(0, rows // SUB, group, (zero, zero))
    sum_ref[0:1] = jnp.sum(one, axis=0, keepdims=True)
    sum_ref[1:2] = jnp.sum(two, axis=0, keepdims=True)


def spread_back(
    count, side, top, low, hid, hid_halo, own, halo, q, weights, gains, biases, taps, sums_one, sums_two, backs
):
    rows, hidden = own.shape[0], own.shape[-1]
    arrays = [hid, hid_halo, own, halo, q, *weights, gains, biases, taps, *sums_one, *sums_two, *backs]
    rim_shape = (2, HALO_OUT * FRAME_COLUMNS, weights[0].shape[0])
    return pl.pallas_call(
        partial(spread_back_kernel, len(backs), count),
        grid=(hidden // 128,),
        in_specs=[pl.BlockSpec(memory_space=pltpu.SMEM), whole(top.shape), whole(low.shape)]
        + [lanes(a.shape) for a in arrays],
        out_specs=[lanes((rows, SUB, SUB, hidden)), lanes((2, hidden)), lanes((TAPS, hidden))],
        out_shape=[
            jax.ShapeDtypeStruct((rows, SUB, SUB, hidden), F32),
            jax.ShapeDtypeStruct((2, hidden), F32),
            jax.ShapeDtypeStruct((TAPS, hidden), F32),
        ],
        scratch_shapes=[
            pltpu.VMEM((rows + 2 * HALO_OUT, SUB + 4, SUB, 128), F32),
            pltpu.VMEM((rows + 2 * HALO_OUT, SUB + 4, SUB, 128), F32),
            pltpu.VMEM((7, SUB, 128), F32),
            pltpu.VMEM(rim_shape, BF16),
            pltpu.VMEM(rim_shape, BF16),
        ],
        compiler_params=params(),
        cost_estimate=cost(47),
        name="spread_back",
    )(side, top, low, *arrays)


def expand_grad(q_ref, hid_ref, terms, cut):
    a, b, c = terms
    return split(q_ref[0, :, cut] * a[:, cut] + (hid_ref[0, :, cut] * b[:, cut] + c[:, cut]))


def input_kernel(parts, count, half, q_ref, hid_ref, gout_ref, gain_ref, w_high, w_low, *rest):
    sums, backs, out_ref = rest[:parts], rest[parts : 2 * parts], rest[2 * parts]
    nz, _, chans, area = out_ref.shape
    terms = back_terms(total(sums), total(backs), count, gain_ref[0:1])
    out = None
    for cut in chunks(w_high.shape[0]):
        term = dot3(expand_grad(q_ref, hid_ref, terms, cut), (w_high[cut], w_low[cut]))
        out = term if out is None else out + term
    own = gout_ref[:, 0]
    if own.shape[2] > area:
        own = own[:, :, half * area : (half + 1) * area]
    out_ref[:, 0] = own + out.T.reshape(nz, chans, area)


def input_grad(count, half, q, hid, gout, gains, w_high, w_low, sums, backs):
    nz, bands, chans, area = gout.shape
    hidden = w_high.shape[0]
    area //= 2
    fixed = [gains, w_high, w_low, *sums, *backs]
    return pl.pallas_call(
        partial(input_kernel, len(sums), count, half),
        grid=(bands,),
        in_specs=[
            pl.BlockSpec((1, area, hidden), lambda t: (t, half, 0)),
            pl.BlockSpec((1, area, hidden), lambda t: (t, half, 0)),
            whole_half(nz, chans, area, half),
        ]
        + [whole(v.shape) for v in fixed],
        out_specs=pl.BlockSpec((nz, 1, chans, area), lambda t: (0, t, 0, 0)),
        out_shape=jax.ShapeDtypeStruct((nz, bands, chans, area), F32),
        compiler_params=params(),
        cost_estimate=cost(5),
        name="input_grad",
    )(q, hid, gout, *fixed)


def whole_half(nz, chans, area, half):
    if area % 128 == 0:
        return pl.BlockSpec((nz, 1, chans, area), lambda t: (0, t, 0, half))
    return pl.BlockSpec((nz, 1, chans, 2 * area), lambda t: (0, t, 0, 0))


def weight_kernel(chans, reduced, ids_ref, q_ref, x_ref, tap_ref, one_ref, two_ref, val_ref, *rest):
    outs, acc, small = rest[:-2], rest[-2], rest[-1]
    nz, _, _, area = x_ref.shape
    chan_all, hidden = acc.shape
    width = hidden // nz
    t = pl.program_id(0)

    @pl.when(t == 0)
    def _():
        acc[...] = jnp.zeros_like(acc)
        small[...] = jnp.zeros_like(small)
        small[0:TAPS] = tap_ref[...]
        small[TAPS : TAPS + 1] = one_ref[1:2]
        small[TAPS + 1 : TAPS + 2] = two_ref[1:2]
        small[TAPS + 2 : TAPS + 3] = one_ref[0:1]
        small[TAPS + 3 : TAPS + 4] = two_ref[0:1]
        lead = (ids_ref[1] == 0).astype(F32)
        logit, pooled = val_ref[2:3] * lead, val_ref[3:4]
        squeezed, grad_sq = val_ref[4:5, 0:reduced], val_ref[5:6, 0:reduced] * lead
        g_sq = column(grad_sq) * pooled
        g_ex = column(squeezed) * logit
        for z in range(nz):
            own, at = slice(z * chans, (z + 1) * chans), z * width
            small[32 : 32 + reduced, at : at + chans] = g_sq[:, own]
            small[32 : 32 + reduced, at + chans : at + 2 * chans] = g_ex[:, own]
            small[32:33, at + 2 * chans : at + 3 * chans] = logit[:, own]
            small[33:34, at + 2 * chans : at + 2 * chans + reduced] = grad_sq

    x = split(x_ref[:, 0].reshape(chan_all, area))
    for cut in chunks(hidden):
        acc[:, cut] += dot3(x, split(q_ref[0, :, cut]))

    @pl.when(t == pl.num_programs(0) - 1)
    def _():
        n = len(outs)
        r, m = chan_all // n, SMALL // n
        for i, out in enumerate(outs):
            p = ids_ref[0] ^ i
            out[0:r] = acc[pl.ds(pl.multiple_of(p * r, r), r), :]
            out[r : r + m] = small[pl.ds(pl.multiple_of(p * m, m), m), :]


def weight_grad(ids, pieces, q, x, taps, one, two, values, reduced):
    nz, bands, chans, area = x.shape
    hidden = q.shape[2]
    chan_all = nz * chans
    fixed = [taps, one, two, values]
    shape = ((chan_all + SMALL) // pieces, hidden)
    return pl.pallas_call(
        partial(weight_kernel, chans, reduced),
        grid=(bands,),
        in_specs=[
            pl.BlockSpec(memory_space=pltpu.SMEM),
            pl.BlockSpec((1, area, hidden), lambda t: (t, 0, 0)),
            pl.BlockSpec((nz, 1, chans, area), lambda t: (0, t, 0, 0)),
        ]
        + [whole(v.shape) for v in fixed],
        out_specs=[whole(shape)] * pieces,
        out_shape=[jax.ShapeDtypeStruct(shape, F32)] * pieces,
        scratch_shapes=[pltpu.VMEM((chan_all, hidden), F32), pltpu.VMEM((SMALL, hidden), F32)],
        compiler_params=params(),
        cost_estimate=cost(7),
        name="weight_grad",
    )(ids, q, x, *fixed)


def collect_kernel(n, nz, parts, count, ids_ref, early_ref, gram_ref, high_ref, low_ref, gain_ref, *rest):
    pieces, sums, backs = rest[:n], rest[n : n + parts], rest[n + parts : n + 2 * parts]
    outs, acc = rest[n + 2 * parts : -1], rest[-1]
    value = total(pieces)
    rows, width = value.shape[0], acc.shape[2]
    r, chan_all = early_ref.shape[0], high_ref.shape[0]
    a, b, c = back_terms(total(sums), total(backs), count, gain_ref[0:1])
    gram = gram_ref[...]
    hid = dot3(split(gram[:, 0:chan_all]), (high_ref[...], low_ref[...]))
    grad = a * value[0:r] + (b * hid + c * gram[:, chan_all : chan_all + 1])
    for z in range(nz):
        here = slice(z * width, (z + 1) * width)
        acc[z, 0:r] = grad[:, here]
        acc[z, r:rows] = value[r:, here]
        acc[z, rows:] = early_ref[:, here]
    for k, out in enumerate(outs):
        out[...] = acc[ids_ref[2] ^ k]


def collect(count, ids, nz, pieces, early, gram, w_high, w_low, gains, sums, backs):
    width = early.shape[1] // nz
    rows = pieces[0].shape[0] + early.shape[0]
    arrays = [early, gram, w_high, w_low, gains, *pieces, *sums, *backs]
    return pl.pallas_call(
        partial(collect_kernel, len(pieces), nz, len(sums), count),
        grid=(1,),
        in_specs=[pl.BlockSpec(memory_space=pltpu.SMEM)] + [whole(a.shape) for a in arrays],
        out_specs=[whole((rows, width))] * nz,
        out_shape=[jax.ShapeDtypeStruct((rows, width), F32)] * nz,
        scratch_shapes=[pltpu.VMEM((nz, rows, width), F32)],
        compiler_params=params(),
        cost_estimate=cost(3),
        name="collect",
    )(ids, *arrays)


def segments(chan_in, hidden_dev, chan_dev, reduced, tap_count, hidden_all):
    seg_sizes = [
        chan_in * hidden_dev,
        tap_count * hidden_dev,
        2 * hidden_dev,
        2 * hidden_dev,
        hidden_dev * chan_in,
        chan_dev * reduced,
        reduced,
        reduced * chan_dev,
        chan_dev,
    ]
    seg_rates = [
        0.5 / math.sqrt(chan_in),
        0.5 / math.sqrt(tap_count),
        0.3,
        0.3,
        0.5 * math.sqrt(8.0 / hidden_all),
        2.0 / math.sqrt(chan_in),
        0.3,
        1.0 / math.sqrt(reduced),
        0.3,
    ]
    return (seg_sizes, seg_rates)


def pack_kernel(at_ref, we_ref, wp_ref, dw_ref, gain_ref, bias_ref, sq_ref, ex_ref, exb_ref, out_ref, small):
    p = at_ref[0]
    chan_in, width = we_ref.shape
    chans, reduced = sq_ref.shape
    m = small.shape[0] * out_ref.shape[0] // (2 * chan_in + small.shape[0])
    r = (out_ref.shape[0] - m) // 2
    small[...] = jnp.zeros_like(small)
    small[0:TAPS] = dw_ref[...]
    small[TAPS : TAPS + 2] = gain_ref[...]
    small[TAPS + 2 : TAPS + 4] = bias_ref[...]
    small[32 : 32 + reduced, 0:chans] = sq_ref[...].T
    small[32 : 32 + reduced, chans : 2 * chans] = ex_ref[...]
    small[32:33, 2 * chans : 3 * chans] = exb_ref[...]
    out_ref[0:r] = we_ref[pl.ds(pl.multiple_of(p * r, r), r), :]
    if chan_in == width:
        out_ref[r : 2 * r] = wp_ref[pl.ds(pl.multiple_of(p * r, r), r), :]
    else:
        row, part = p * r % width, p * r // width
        out_ref[r : 2 * r] = wp_ref[
            pl.ds(pl.multiple_of(row, r), r), pl.ds(pl.multiple_of(part * width, 128), width)
        ]
    out_ref[2 * r : 2 * r + m] = small[pl.ds(pl.multiple_of(p * m, m), m), :]


def pack_weights(at, w_expand, w_dw, norm_gains, norm_biases, w_project, squeeze_matrix, excite_matrix, excite_bias_row):
    n_pix = lax.axis_size(PIX)
    chan_in, width = w_expand.shape
    arrays = [
        w_expand,
        w_project,
        w_dw,
        norm_gains,
        norm_biases,
        squeeze_matrix,
        excite_matrix,
        excite_bias_row[None],
    ]
    shape = ((2 * chan_in + SMALL) // n_pix, width)
    return pl.pallas_call(
        pack_kernel,
        grid=(1,),
        in_specs=[pl.BlockSpec(memory_space=pltpu.SMEM)] + [whole(a.shape) for a in arrays],
        out_specs=whole(shape),
        out_shape=jax.ShapeDtypeStruct(shape, F32),
        scratch_shapes=[pltpu.VMEM((SMALL, width), F32)],
        compiler_params=params(),
        cost_estimate=cost(2),
        name="pack_weights",
    )(at, *arrays)


def weights_kernel(
    chan_in,
    chans,
    orders,
    base_ref,
    *refs,
):
    slabs = refs[: len(orders)]
    (
        we_high,
        we_low,
        wet_high,
        wet_low,
        wp_high,
        wp_low,
        wpt_ref,
        tap_ref,
        gain_ref,
        bias_ref,
        sq_ref,
        sqt_ref,
        ex_ref,
        ext_ref,
        exb_ref,
        first,
        second,
        small,
    ) = refs[len(orders) :]
    nz, width = first.shape[0], first.shape[2]
    n_pix = sum(len(order) for order in orders)
    r, m = chan_in // n_pix, SMALL // n_pix
    reduced = ex_ref.shape[0]
    for ref, order in zip(slabs, orders):
        for i, p in enumerate(order):
            at = base_ref[0] ^ p
            wide = pl.ds(pl.multiple_of(at * r, r), r)
            for z in range(nz):
                here = slice(z * width, (z + 1) * width)
                group = base_ref[1] ^ z
                first[group, wide, :] = ref[i, 0:r, here]
                second[group, wide, :] = ref[i, r : 2 * r, here]
                small[group, pl.ds(pl.multiple_of(at * m, m), m), :] = ref[i, 2 * r : 2 * r + m, here]
    parts = chan_in // width
    for z in range(nz):
        here = slice(z * width, (z + 1) * width)
        own = slice(z * chans, (z + 1) * chans)
        we = first[z]
        we_high[:, here], we_low[:, here] = split(we)
        wet_high[here], wet_low[here] = split(we.T)
        for h in range(parts):
            wp = second[z, h * width : (h + 1) * width]
            cols = slice(h * width, (h + 1) * width)
            wp_high[here, cols], wp_low[here, cols] = split(wp)
            wpt_ref[cols, here] = wp.T
        for tap in range(TAPS):
            tap_ref[tap, :, here] = jnp.broadcast_to(small[z, tap : tap + 1], (SUB, width))
        gain_ref[:, here] = small[z, TAPS : TAPS + 2]
        bias_ref[:, here] = small[z, TAPS + 2 : TAPS + 4]
        sqt_ref[:, own] = small[z, 32 : 32 + reduced, 0:chans]
        ex_ref[:, own] = small[z, 32 : 32 + reduced, chans : 2 * chans]
        exb_ref[:, own] = small[z, 32:33, 2 * chans : 3 * chans]
    sq_ref[...] = sqt_ref[...].T
    ext_ref[...] = ex_ref[...].T


def order_weights(base, slabs, orders, nz, chan_in, chans, reduced):
    hidden = slabs[0].shape[2]
    width = hidden // nz
    shapes = (
        [((chan_in, hidden), BF16)] * 2
        + [((hidden, chan_in), BF16)] * 4
        + [
            ((chan_in, hidden), F32),
            ((TAPS, SUB, hidden), F32),
            ((2, hidden), F32),
            ((2, hidden), F32),
            ((chan_in, reduced), F32),
            ((reduced, chan_in), F32),
            ((reduced, chan_in), F32),
            ((chan_in, reduced), F32),
            ((1, chan_in), F32),
        ]
    )
    return pl.pallas_call(
        partial(weights_kernel, chan_in, chans, orders),
        grid=(1,),
        in_specs=[pl.BlockSpec(memory_space=pltpu.SMEM)] + [whole(a.shape) for a in slabs],
        out_specs=[whole(shape) for shape, _ in shapes],
        out_shape=[jax.ShapeDtypeStruct(shape, kind) for shape, kind in shapes],
        scratch_shapes=[
            pltpu.VMEM((nz, chan_in, width), F32),
            pltpu.VMEM((nz, chan_in, width), F32),
            pltpu.VMEM((nz, SMALL, width), F32),
        ],
        compiler_params=params(),
        cost_estimate=cost(1),
        name="order_weights",
    )(base, *slabs)


def thirds(v):
    high = v.astype(BF16)
    rest = v - high.astype(F32)
    mid = rest.astype(BF16)
    return high, mid, (rest - mid.astype(F32)).astype(BF16)


def choose(chosen, v):
    high, mid, low = thirds(v)
    return (dot(chosen, high) + dot(chosen, mid)) + dot(chosen, low)


def choose_lanes(v, chosen):
    high, mid, low = thirds(v)
    return (dot(high, chosen) + dot(mid, chosen)) + dot(low, chosen)


def ones(condition):
    return condition.astype(F32).astype(BF16)


def lay_flat(v, start, width):
    n, m = v.shape
    place = lax.broadcasted_iota(jnp.int32, (m, width), 1) - start
    column_of = lax.broadcasted_iota(jnp.int32, (m, width), 0)
    wide = choose_lanes(v, ones((place + 64 * m) % m == column_of))
    place = lax.broadcasted_iota(jnp.int32, (n, width), 1) - start
    low = lax.broadcasted_iota(jnp.int32, (n, width), 0) * m
    return jnp.sum(jnp.where((place >= low) & (place < low + m), wide, 0.0), axis=0, keepdims=True)


def fill_blocks(out, first, middle, flip, last, squeeze, down, excite, bias):
    blocks, length = out.shape
    tiles, n, _ = first.shape
    width = tiles * 128
    per = length // width
    for i in range(per):
        for u in range(tiles):
            at = i * width + u * 128
            out[0 : n // per, at : at + 128] = first[u, pl.ds(i, n // per, stride=per), :]
    for k in range(TAPS + 4):
        row = n + k
        out[row // per : row // per + 1, row % per * width : (row % per + 1) * width] = middle[k : k + 1, :]
    base = n + TAPS + 4
    parts = last // width
    step = per // parts
    for h in range(parts):
        for e in range(step):
            row = base + parts * e + h
            block, slot = row // per, row % per
            count = width // step
            for u in range(tiles):
                at = slot * width + u * 128
                out[block : block + count, at : at + 128] = flip[
                    h * tiles + u, pl.ds(e, count, stride=step), :
                ]
    start = (base + width * parts) * width
    block = start // length
    start -= block * length
    tail_width = (blocks - block) * length
    tail = lay_flat(squeeze, start, tail_width)
    start += squeeze.shape[0] * squeeze.shape[1]
    tail = tail + lay_flat(down, start, tail_width)
    start += down.shape[1]
    tail = tail + lay_flat(excite, start, tail_width)
    start += excite.shape[0] * excite.shape[1]
    tail = tail + lay_flat(bias, start, tail_width)
    inside = lax.broadcasted_iota(jnp.int32, (1, length), 1)
    kept = jnp.where(inside < (base + width * parts) * width - block * length, out[block : block + 1, :], 0.0)
    out[block : block + 1, :] = kept + tail[:, 0:length]
    for k in range(1, blocks - block):
        out[block + k : block + k + 1, :] = tail[:, k * length : (k + 1) * length]


def prepare_kernel(
    orders,
    base_ref,
    col_ref,
    we_ref,
    dw_ref,
    gain_ref,
    bias_ref,
    wp_ref,
    sq_ref,
    down_ref,
    ex_ref,
    exb_ref,
    *rest,
):
    slabs = rest[: len(orders)]
    weight, first_ref, second_ref, head, flip, middle, moments, ranked = rest[len(orders) :]
    blocks, length = weight.shape
    chan_in, width = we_ref.shape
    devices, room = moments.shape[1:3]
    middle[0:TAPS] = dw_ref[...]
    middle[TAPS : TAPS + 2] = gain_ref[...]
    middle[TAPS + 2 : TAPS + 4] = bias_ref[...]
    for u in range(width // 128):
        head[u] = we_ref[:, u * 128 : (u + 1) * 128]
    for u in range(chan_in // 128):
        flip[u] = wp_ref[:, u * 128 : (u + 1) * 128]
    fill_blocks(
        weight, head, middle, flip, chan_in, sq_ref[...], down_ref[...], ex_ref[...], exb_ref[...]
    )
    at = 0
    home = jnp.zeros(col_ref.shape, jnp.int32)
    own_col = col_ref[...]
    for ref, order in zip(slabs, orders):
        for k, p in enumerate(order):
            for m in range(2):
                moments[m, at] = ref[k, m * room : (m + 1) * room]
            home = jnp.where(own_col == base_ref[0] ^ p, at, home)
            at += 1
    ranked[...] = jnp.broadcast_to(own_col.astype(F32), ranked.shape)
    own_row = ranked[...].T[0:1].astype(jnp.int32)
    i = lax.broadcasted_iota(jnp.int32, (blocks, blocks), 0)
    j = lax.broadcasted_iota(jnp.int32, (blocks, blocks), 1)
    earlier = (own_row == own_col) & (j < i)
    rank = jnp.sum(jnp.where(earlier, 1.0, 0.0), axis=1, keepdims=True).astype(jnp.int32)
    slot = home * room + rank
    chosen = ones(lax.broadcasted_iota(jnp.int32, (blocks, devices * room), 1) == slot)
    first_ref[...] = choose(chosen, moments[0].reshape(devices * room, length))
    second_ref[...] = choose(chosen, moments[1].reshape(devices * room, length))


def prepare(base, owners, weights, slabs, orders, length):
    blocks = owners.shape[0]
    chan_in, width = weights[0].shape
    devices = sum(len(o) for o in orders)
    arrays = [owners, *weights, *slabs]
    return pl.pallas_call(
        partial(prepare_kernel, orders),
        grid=(1,),
        in_specs=[pl.BlockSpec(memory_space=pltpu.SMEM)] + [whole(a.shape) for a in arrays],
        out_specs=[whole((blocks, length))] * 3,
        out_shape=[jax.ShapeDtypeStruct((blocks, length), F32)] * 3,
        scratch_shapes=[
            pltpu.VMEM((width // 128, chan_in, 128), F32),
            pltpu.VMEM((chan_in // 128, width, 128), F32),
            pltpu.VMEM((32, width), F32),
            pltpu.VMEM((2, devices, slabs[0].shape[1] // 2, length), F32),
            pltpu.VMEM((blocks, 128), F32),
        ],
        compiler_params=params(),
        cost_estimate=cost(5),
        name="prepare",
    )(base, *arrays)


def adam_kernel(
    bounds,
    rates,
    orders,
    chans,
    reduced,
    me_ref,
    col_ref,
    weight_ref,
    old_one_ref,
    old_two_ref,
    first_ref,
    second_ref,
    *rest,
):
    grad_slabs = rest[: len(orders)]
    first_out, second_out, new_ref, grad, head, flip, tall, small, ranked = rest[len(orders) :]
    blocks, length = grad.shape
    capacity = first_ref.shape[0]
    chan_in, width = tall.shape
    devices = sum(len(order) for order in orders)
    r, m = chan_in // devices, SMALL // devices
    for ref, order in zip(grad_slabs, orders):
        for k, i in enumerate(order):
            p = me_ref[1] ^ i
            for u in range(width // 128):
                head[u, pl.ds(pl.multiple_of(p * r, r), r), :] = ref[k, 0:r, u * 128 : (u + 1) * 128]
            small[pl.ds(pl.multiple_of(p * m, m), m), :] = ref[k, r : r + m]
            tall[pl.ds(pl.multiple_of(p * r, r), r), :] = ref[k, r + m : 2 * r + m]
    for u in range(chan_in // 128):
        flip[u] = tall[u * 128 : (u + 1) * 128].T
    fill_blocks(
        grad,
        head,
        small,
        flip,
        chan_in,
        small[32 : 32 + reduced, 0:chans].T,
        small[33:34, 2 * chans : 2 * chans + reduced],
        small[32 : 32 + reduced, chans : 2 * chans],
        small[32:33, 2 * chans : 3 * chans],
    )

    own_col = col_ref[...]
    ranked[...] = jnp.broadcast_to(own_col.astype(F32), ranked.shape)
    own_row = ranked[...].T[0:1].astype(jnp.int32)
    i = lax.broadcasted_iota(jnp.int32, (blocks, blocks), 0)
    j = lax.broadcasted_iota(jnp.int32, (blocks, blocks), 1)
    earlier = (own_row == own_col) & (i < j)
    rank = jnp.sum(jnp.where(earlier, 1.0, 0.0), axis=0, keepdims=True).astype(jnp.int32)
    g = grad[...]
    mine = lax.broadcasted_iota(jnp.int32, (capacity, blocks), 0)
    owned = choose(ones((mine == rank) & (own_row == me_ref[0])), g)
    first_out[:, 0] = beta_first * first_ref[:, 0] + (1.0 - beta_first) * owned
    second_out[:, 0] = beta_second * second_ref[:, 0] + (1.0 - beta_second) * owned * owned

    first = beta_first * old_one_ref[...] + (1.0 - beta_first) * g
    second = beta_second * old_two_ref[...] + (1.0 - beta_second) * g * g
    first_hat = first / (1.0 - beta_first**STEP)
    second_hat = second / (1.0 - beta_second**STEP)
    place = lax.broadcasted_iota(jnp.int32, (blocks, length), 0) * length + lax.broadcasted_iota(
        jnp.int32, (blocks, length), 1
    )
    rate = jnp.zeros((blocks, length), F32)
    for bound, value in zip(reversed(bounds), reversed(rates)):
        rate = jnp.where(place < bound, jnp.float32(value), rate)
    grad[...] = weight_ref[...] * (1.0 - rate * weight_decay) - rate * first_hat / (
        jnp.sqrt(second_hat) + adam_eps
    )
    for k in range(blocks):
        end = min((k + 1) * length, new_ref.shape[1])
        new_ref[:, k * length : end] = grad[k : k + 1, 0 : end - k * length]


def adam(ids, owners, prepared, first, second, grads, orders, chan_in, chans, reduced, bounds, rates):
    blocks, length = prepared[0].shape
    width = grads[0].shape[2]
    arrays = [owners, *prepared, first, second, *grads]
    new_shape = (1, bounds[-1])
    return pl.pallas_call(
        partial(adam_kernel, bounds, rates, orders, chans, reduced),
        grid=(1,),
        in_specs=[pl.BlockSpec(memory_space=pltpu.SMEM)] + [whole(a.shape) for a in arrays],
        out_specs=[whole(first.shape), whole(second.shape), whole(new_shape)],
        out_shape=[
            jax.ShapeDtypeStruct(first.shape, F32),
            jax.ShapeDtypeStruct(second.shape, F32),
            jax.ShapeDtypeStruct(new_shape, F32),
        ],
        scratch_shapes=[
            pltpu.VMEM((blocks, length), F32),
            pltpu.VMEM((width // 128, chan_in, 128), F32),
            pltpu.VMEM((chan_in // 128, width, 128), F32),
            pltpu.VMEM((chan_in, width), F32),
            pltpu.VMEM((SMALL, width), F32),
            pltpu.VMEM((blocks, 128), F32),
        ],
        compiler_params=params(),
        cost_estimate=cost(4),
        name="adam",
    )(ids, *arrays)


def deal_rows(rows):
    n_pix = lax.axis_size(PIX)
    n, hidden = rows.shape
    dealt = lax.all_to_all(rows.reshape(n_pix, n // n_pix, hidden), PIX, 0, 0, tiled=True)
    return jnp.sum(dealt, axis=0)


def together(*values):
    return lax.optimization_barrier(values)


def local(
    frames_raw,
    grad_out,
    col_offsets,
    flip_flags,
    owners,
    w_expand,
    w_dw,
    norm_gains,
    norm_biases,
    w_project,
    squeeze_matrix,
    se_down_bias,
    excite_matrix,
    excite_bias_row,
    first_moment,
    second_moment,
):
    nz, nhi, nlo = (lax.axis_size(axis) for axis in ALL)
    frames, chans, stored = frames_raw.shape
    band = stored // WIN
    area = band * FRAME_COLUMNS
    rows = nlo * band
    chan_in, hidden_dev = w_expand.shape
    hidden = hidden_dev * nz
    reduced = squeeze_matrix.shape[1]
    group = nz // MB * nhi * nlo
    count = float(frames // MB * FRAME_ROWS * FRAME_COLUMNS)
    hi = lax.axis_index("hi")
    side = jnp.stack([(hi > 0).astype(jnp.int32), (hi < nhi - 1).astype(jnp.int32)])

    n_pix = nhi * nlo
    me = hi * nlo + lax.axis_index("lo")
    relative = me if near(n_pix) else 0 * me
    z_relative = lax.axis_index("chan") if near(n_pix) else 0 * me

    slab = pack_weights(
        me.astype(jnp.int32).reshape(1),
        w_expand,
        w_dw,
        norm_gains,
        norm_biases,
        w_project,
        squeeze_matrix,
        excite_matrix,
        excite_bias_row,
    )
    crops = crop(frames_raw, col_offsets, flip_flags)
    crops, *slab = together(crops, *gather_chan(slab))
    x = deal(crops).reshape(nz, nlo, chans, area)
    slabs, orders = gather_pix(jnp.concatenate(slab, axis=1))
    (
        we_high,
        we_low,
        wet_high,
        wet_low,
        wp_high,
        wp_low,
        w_project_t,
        taps,
        gains,
        biases,
        sq_all,
        sq_t,
        ex_all,
        ex_t,
        ex_bias,
    ) = order_weights(
        jnp.stack([relative, z_relative]), slabs, orders, nz, chan_in, chans, reduced
    )
    se_weights = [sq_all, sq_t, se_down_bias[None], ex_all, ex_t, ex_bias]
    ordered = order(grad_out)
    x, ordered, we_high, we_low = together(x, ordered, we_high, we_low)

    top, low = rims(x, HALO_IN, band)

    def as_rows(v):
        return v.reshape(rows, SUB, SUB, hidden)

    def as_bands(v):
        return v.reshape(nlo, area, hidden)

    def as_sides(v, n):
        return v.reshape(2, n, SUB, SUB, hidden)

    hid, sums_one, gram = expand(x, we_high, we_low)
    hid, ordered = together(hid, ordered)
    gout = deal(ordered).reshape(nz, nlo, chans, area)
    g_top, g_low = rims(gout, HALO_OUT, band)
    sums_one = shares(sums_one, 1, group)
    spatial, spatial_halo, hid_halo, sums_two = spread(
        count, side, top, low, as_rows(hid), we_high, we_low, gains, biases, taps, sums_one
    )
    first_turned, second_turned, spatial = together(
        first_moment.transpose(1, 0, 2), second_moment.transpose(1, 0, 2), spatial
    )
    capacity = first_moment.shape[1]
    room = ((0, -capacity % SUB), (0, 0))
    moments = jnp.concatenate([jnp.pad(v[:, 0], room) for v in (first_turned, second_turned)])
    moments = lax.all_gather(moments, PIX, axis=0)
    sums_two = shares(sums_two, 1, group)
    m, s, se_part, proj = gather(
        count, as_bands(spatial), gout, gains, biases, w_project_t, wp_high, wp_low, sums_two
    )
    ses = shares(se_part, nlo, nhi)
    ses, g_top, g_low = together(ses, g_top, g_low)
    q, back_two, values, *w4 = proj_back(
        count, as_bands(spatial), gout, gains, biases, w_project_t, se_weights, ses, sums_two
    )
    backs_two = shares(back_two, 1, group)
    out, g_project = project(proj, x, values, m, s)
    backs_two, out, g_project = together(backs_two, out, g_project)
    out = deal(out.reshape(frames, chans, area))
    q1, back_one, g_dw = spread_back(
        count,
        side,
        g_top,
        g_low,
        as_rows(hid),
        hid_halo,
        spatial,
        spatial_halo,
        as_rows(q),
        w4,
        gains,
        biases,
        taps,
        sums_one,
        sums_two,
        backs_two,
    )
    backs_one = shares(back_one, 1, group)

    ids = jnp.stack([relative, hi, z_relative]).astype(jnp.int32)
    pieces = weight_grad(
        ids, n_pix if near(n_pix) else 1, as_bands(q1), x, g_dw, back_one, back_two, values, reduced
    )
    if near(n_pix):
        early = lax.psum_scatter(g_project, PIX, scatter_dimension=0, tiled=True)
        gram = lax.psum_scatter(gram, PIX, scatter_dimension=0, tiled=True)
    else:
        early, gram = deal_rows(g_project), deal_rows(gram)
    q1, out, early, gram, *pieces = together(q1, out, early, gram, *pieces)

    def input_half(half, q1):
        grad = input_grad(count, half, as_bands(q1), hid, gout, gains, wet_high, wet_low, sums_one, backs_one)
        return grad.reshape(frames, chans, area // 2)

    grad_one = input_half(0, q1)
    grad_one, q1, *pieces = together(grad_one, q1, *pieces)
    if near(n_pix):
        pieces = [pieces[0]] + [exchange(pieces[i], i) for i in range(1, n_pix)]
        moments, out, pieces[1] = together(moments, out, pieces[1])
    else:
        pieces = [jnp.concatenate([deal_rows(pieces[0][:chan_in]), deal_rows(pieces[0][chan_in:])])]
    grad_two = input_half(1, q1)
    output = restore(out)
    weights = [
        w_expand,
        w_dw,
        norm_gains,
        norm_biases,
        w_project,
        squeeze_matrix,
        se_down_bias[None],
        excite_matrix,
        excite_bias_row[None],
    ]
    block_len = first_moment.shape[2]
    natural = [list(range(n_pix))]
    base = jnp.zeros((1,), jnp.int32)
    prepared = prepare(base, owners, weights, [moments], natural, block_len)
    grad_two, output, prepared, *pieces = together(grad_two, output, prepared, *pieces)
    groups = collect(count, ids, nz, pieces, early, gram, we_high, we_low, gains, sums_one, backs_one)
    if near(n_pix):
        others = [groups[0]] + [exchange(groups[k], k * n_pix) for k in range(1, nz)]
    else:
        others = list(lax.all_to_all(jnp.stack(groups), "chan", 0, 0, tiled=True))
    grad_one = deal(grad_one)
    grad_one, grad_two, *others = together(grad_one, grad_two, *others)
    summed = sum(others[1:], others[0])
    grad_two = deal(grad_two)
    grads, _ = gather_pix(summed)
    seg_sizes, seg_rates = segments(chan_in, hidden_dev, chans, reduced, TAPS, hidden)
    bounds = [sum(seg_sizes[: i + 1]) for i in range(len(seg_sizes))]
    first_next, second_next, new_params = adam(
        jnp.stack([me, relative]).astype(jnp.int32),
        owners,
        prepared,
        first_turned,
        second_turned,
        grads,
        orders,
        chan_in,
        chans,
        reduced,
        bounds,
        seg_rates,
    )
    first_next, second_next = first_next.transpose(1, 0, 2), second_next.transpose(1, 0, 2)
    grad_frames = uncrop(grad_one, grad_two, col_offsets, flip_flags)
    return (output, grad_frames, first_next, second_next, new_params)


def solution(mesh):
    nz, n_pix = mesh.shape["chan"], mesh.shape["pix"]
    placed = (
        P(None, "chan", PIX),
        P(None, "chan", PIX),
        P(),
        P(),
        P(),
        P(None, "chan"),
        P(None, "chan"),
        P(None, "chan"),
        P(None, "chan"),
        P("chan", None),
        P("chan", None),
        P(),
        P(None, "chan"),
        P("chan"),
        P("chan", PIX, None),
        P("chan", PIX, None),
    )

    def run(*arrays):
        nlo = arrays[0].shape[0] // nz
        return jax.shard_map(
            local,
            mesh=Mesh(mesh.devices.reshape(nz, n_pix // nlo, nlo), ALL),
            in_specs=placed,
            out_specs=(
                P(None, "chan", PIX),
                P(None, "chan", PIX),
                P("chan", PIX, None),
                P("chan", PIX, None),
                P("chan", None),
            ),
            check_vma=False,
        )(*arrays)

    return run
```

```python
from functools import partial
import math

import jax
import jax.numpy as jnp
from jax import lax
from jax.experimental import pallas as pl
from jax.experimental.pallas import tpu as pltpu
from jax.sharding import Mesh, PartitionSpec as P

K = 5
FRAME_ROWS = 64
FRAME_COLUMNS = 64
CLIP_LEN = 4
MB = 4
STEP = 5
WIN = 80
SUB = 8
TAPS = K * K
HALO_IN = 4
SMALL = 64
HALO_OUT = 2

norm_eps = 1e-05
beta_first = 0.5
beta_second = 0.6
adam_eps = 1e-08
weight_decay = 0.1

F32 = jnp.float32
BF16 = jnp.bfloat16
ALL = ("chan", "hi", "lo")
PIX = ("hi", "lo")
SPREAD = ("chan", "lo")
VMEM_BYTES = 62 * 2**20


def params(dims=1):
    return pltpu.CompilerParams(vmem_limit_bytes=VMEM_BYTES, dimension_semantics=("arbitrary",) * dims)


def cost(us):
    return pl.CostEstimate(flops=int(us * 1.1e9), bytes_accessed=int(us * 3.5e6), transcendentals=0)


def sigmoid(v):
    return 0.5 * jnp.tanh(0.5 * v) + 0.5


def swish_half(h):
    return h + h * jnp.tanh(h)


def slope_half(h):
    t = jnp.tanh(h)
    return 1.0 + (t + h * (1.0 - t * t))


def split(v):
    high = v.astype(BF16)
    return high, (v - high.astype(F32)).astype(BF16)


def dot(a, b):
    return jnp.dot(a, b, preferred_element_type=F32)


def dot3(a, b):
    return dot(a[0], b[0]) + (dot(a[0], b[1]) + dot(a[1], b[0]))


def total(refs):
    value = refs[0][...]
    for ref in refs[1:]:
        value = value + ref[...]
    return value


def norm_terms(sums, count, gain, bias):
    mean = sums[0:1] / count
    inverse = lax.rsqrt(sums[1:2] / count - mean * mean + norm_eps)
    scale = gain * inverse
    return mean, inverse, scale, bias - mean * scale


def back_terms(sums, back, count, gain):
    mean = sums[0:1] / count
    inverse = lax.rsqrt(sums[1:2] / count - mean * mean + norm_eps)
    a = gain * inverse
    b = -a * inverse * (back[1:2] / count)
    return a, b, -a * (back[0:1] / count) - b * mean


def exchange(x, stride):
    n = lax.axis_size(ALL)
    return lax.ppermute(x, ALL, [(i, i ^ stride) for i in range(n)])


def shares(x, base, size, after=()):
    bits = size.bit_length() - 1
    parts = [x]
    if bits % 2:
        parts = [x, exchange(x, base)]
        base, bits = base * 2, bits - 1
    while bits:
        x = sum(parts[1:], parts[0])
        if after:
            x, *kept = together(x, *after)
            after[:] = kept
            after = ()
        parts = [x] + [exchange(x, base * k) for k in (1, 2, 3)]
        base, bits = base * 4, bits - 2
    return parts


def deal(x):
    return lax.all_to_all(x, SPREAD, 0, 0, tiled=True)


def edge(x, rows, band, first):
    if rows >= band:
        n = rows // band
        return x[:, :n] if first else x[:, x.shape[1] - n :]
    width = rows * FRAME_COLUMNS
    return x[:, :1, :, :width] if first else x[:, -1:, :, x.shape[3] - width :]


def rims(x, rows, band):
    n = lax.axis_size("hi")
    if n == 2:
        mine = jnp.where(lax.axis_index("hi") == 0, edge(x, rows, band, False), edge(x, rows, band, True))
        other = lax.ppermute(mine, "hi", [(0, 1), (1, 0)])
        return other, other
    down = [(i, i + 1) for i in range(n - 1)]
    up = [(i + 1, i) for i in range(n - 1)]
    top = lax.ppermute(edge(x, rows, band, False), "hi", down)
    low = lax.ppermute(edge(x, rows, band, True), "hi", up)
    return top, low


def near(n_pix):
    return n_pix == 8


def gather_pix(x, beside=None):
    n_pix = lax.axis_size(PIX)
    if not near(n_pix):
        return [lax.all_gather(x, PIX, axis=0)], [list(range(n_pix))], beside
    b = x[None]
    b = jnp.concatenate([b, exchange(b, 2)])
    if beside is not None:
        b, beside = together(b, beside)
    b = jnp.concatenate([b, exchange(b, 4)])
    return [b, exchange(b, 1)], [[0, 2, 4, 6], [1, 3, 5, 7]], beside


def gather_chan(x):
    nz, n_pix = lax.axis_size("chan"), lax.axis_size(PIX)
    if not near(n_pix):
        return list(lax.all_gather(x, "chan", axis=0))
    return [x] + [exchange(x, k * n_pix) for k in range(1, nz)]


def source_column(p, left, flip):
    row, c, s = p // FRAME_COLUMNS, (p // SUB) % SUB, p % SUB
    j = s * SUB + c
    return row * WIN + left + jnp.where(flip == 1, FRAME_COLUMNS - 1 - j, j)


def plain_place(p):
    row, c, s = p // FRAME_COLUMNS, (p // SUB) % SUB, p % SUB
    return row * FRAME_COLUMNS + s * SUB + c


def pick(x, chosen):
    rows = x.shape[0] * x.shape[1]
    high, low = split(x.reshape(rows, x.shape[2]))
    return (dot(high, chosen) + dot(low, chosen)).reshape(x.shape[0], x.shape[1], chosen.shape[1])


def crop_kernel(left_ref, flip_ref, raw_ref, out_ref):
    k = pl.program_id(0)
    width, area = raw_ref.shape[2], out_ref.shape[2]
    p = lax.broadcasted_iota(jnp.int32, (1, area), 1)
    place = source_column(p, left_ref[k], flip_ref[k])
    q = lax.broadcasted_iota(jnp.int32, (width, area), 0)
    out_ref[...] = pick(raw_ref[...], (q == place).astype(F32).astype(BF16))


def crop(raw, left, flip):
    frames, chans, width = raw.shape
    area = width // WIN * FRAME_COLUMNS
    return pl.pallas_call(
        crop_kernel,
        grid=(frames // CLIP_LEN,),
        in_specs=[
            pl.BlockSpec(memory_space=pltpu.SMEM),
            pl.BlockSpec(memory_space=pltpu.SMEM),
            pl.BlockSpec((CLIP_LEN, chans, width), lambda k: (k, 0, 0)),
        ],
        out_specs=pl.BlockSpec((CLIP_LEN, chans, area), lambda k: (k, 0, 0)),
        out_shape=jax.ShapeDtypeStruct((frames, chans, area), F32),
        compiler_params=params(),
        cost_estimate=cost(5),
        name="crop",
    )(left, flip, raw)


def order_kernel(x_ref, out_ref):
    area = x_ref.shape[2]
    p = lax.broadcasted_iota(jnp.int32, (1, area), 1)
    q = lax.broadcasted_iota(jnp.int32, (area, area), 0)
    out_ref[...] = pick(x_ref[...], (q == plain_place(p)).astype(F32).astype(BF16))


def order(x):
    frames, chans, area = x.shape
    return pl.pallas_call(
        order_kernel,
        grid=(frames // CLIP_LEN,),
        in_specs=[pl.BlockSpec((CLIP_LEN, chans, area), lambda k: (k, 0, 0))],
        out_specs=pl.BlockSpec((CLIP_LEN, chans, area), lambda k: (k, 0, 0)),
        out_shape=jax.ShapeDtypeStruct((frames, chans, area), F32),
        compiler_params=params(),
        cost_estimate=cost(25),
        name="order",
    )(x)


def restore_kernel(x_ref, out_ref):
    area = x_ref.shape[2]
    p = lax.broadcasted_iota(jnp.int32, (area, 1), 0)
    q = lax.broadcasted_iota(jnp.int32, (area, area), 1)
    out_ref[...] = pick(x_ref[...], (q == plain_place(p)).astype(F32).astype(BF16))


def restore(x):
    frames, chans, area = x.shape
    return pl.pallas_call(
        restore_kernel,
        grid=(frames // CLIP_LEN,),
        in_specs=[pl.BlockSpec((CLIP_LEN, chans, area), lambda k: (k, 0, 0))],
        out_specs=pl.BlockSpec((CLIP_LEN, chans, area), lambda k: (k, 0, 0)),
        out_shape=jax.ShapeDtypeStruct((frames, chans, area), F32),
        compiler_params=params(),
        cost_estimate=cost(1),
        name="restore",
    )(x)


def uncrop_kernel(left_ref, flip_ref, x_ref, y_ref, out_ref):
    k = pl.program_id(0)
    width = out_ref.shape[2]
    out = None
    for start, ref in ((0, x_ref), (x_ref.shape[2], y_ref)):
        area = ref.shape[2]
        q = lax.broadcasted_iota(jnp.int32, (area, width), 1)
        p = lax.broadcasted_iota(jnp.int32, (area, 1), 0) + start
        place = source_column(p, left_ref[k], flip_ref[k])
        term = pick(ref[...], (q == place).astype(F32).astype(BF16))
        out = term if out is None else out + term
    out_ref[...] = out


def uncrop(x, y, left, flip):
    frames, chans, area = x.shape
    width = (area + y.shape[2]) // FRAME_COLUMNS * WIN
    return pl.pallas_call(
        uncrop_kernel,
        grid=(frames // CLIP_LEN,),
        in_specs=[
            pl.BlockSpec(memory_space=pltpu.SMEM),
            pl.BlockSpec(memory_space=pltpu.SMEM),
            pl.BlockSpec((CLIP_LEN, chans, area), lambda k: (k, 0, 0)),
            pl.BlockSpec((CLIP_LEN, chans, y.shape[2]), lambda k: (k, 0, 0)),
        ],
        out_specs=pl.BlockSpec((CLIP_LEN, chans, width), lambda k: (k, 0, 0)),
        out_shape=jax.ShapeDtypeStruct((frames, chans, width), F32),
        compiler_params=params(),
        cost_estimate=cost(1),
        name="uncrop",
    )(left, flip, x, y)


def chunks(width):
    step = 256 if width % 256 == 0 else width
    return [slice(i, i + step) for i in range(0, width, step)]


def expand_kernel(x_ref, high_ref, low_ref, own_ref, sum_ref, gram_ref):
    @pl.when(pl.program_id(0) == 0)
    def _():
        sum_ref[...] = jnp.zeros_like(sum_ref)
        gram_ref[...] = jnp.zeros_like(gram_ref)

    chan_all, hidden = high_ref.shape
    plain = x_ref[:, 0].reshape(chan_all, x_ref.shape[3])
    turned = plain.T
    x = split(turned)
    for cut in chunks(hidden):
        y = dot3(x, (high_ref[:, cut], low_ref[:, cut]))
        own_ref[0, :, cut] = y
        sum_ref[0:1, cut] += jnp.sum(y, axis=0, keepdims=True)
        sum_ref[1:2, cut] += jnp.sum(y * y, axis=0, keepdims=True)
    gram_ref[:, 0:chan_all] += dot3(split(plain), x)
    gram_ref[:, chan_all:] += jnp.broadcast_to(jnp.sum(plain, axis=1, keepdims=True), (chan_all, 128))


def whole(shape):
    return pl.BlockSpec(shape, lambda *_: (0,) * len(shape))


def by_steps(nz, bands, chans, area):
    run = area
    n = area // run

    def tall(hidden):
        return pl.BlockSpec((1, run, hidden), lambda t: (t // n, t % n, 0))

    def out(hidden):
        return pl.BlockSpec((1, run, hidden), lambda t: (t // n, t % n, 0))

    wide = pl.BlockSpec((nz, 1, chans, run), lambda t: (0, t // n, 0, t % n))
    return (bands * n,), tall, out, wide


def expand(x, high, low):
    nz, bands, chans, area = x.shape
    grid, _, tall, wide = by_steps(nz, bands, chans, area)
    hidden = high.shape[1]
    return pl.pallas_call(
        expand_kernel,
        grid=grid,
        in_specs=[
            wide,
            whole(high.shape),
            whole(low.shape),
        ],
        out_specs=[
            tall(hidden),
            whole((2, hidden)),
            whole((nz * chans, nz * chans + 128)),
        ],
        out_shape=[
            jax.ShapeDtypeStruct((bands, area, hidden), F32),
            jax.ShapeDtypeStruct((2, hidden), F32),
            jax.ShapeDtypeStruct((nz * chans, nz * chans + 128), F32),
        ],
        compiler_params=params(),
        cost_estimate=cost(8),
        name="expand",
    )(x, high, low)


def fill_sides(pad, row):
    s = lax.broadcasted_iota(jnp.int32, (SUB, 128), 0)
    for k in range(2):
        left = pltpu.roll(pad[row, SUB + k], 1, 0)
        pad[row, k] = jnp.where(s == 0, 0.0, left)
        right = pltpu.roll(pad[row, 2 + k], SUB - 1, 0)
        pad[row, SUB + 2 + k] = jnp.where(s == SUB - 1, 0.0, right)


def clear_rows(pad, start, count):
    for row in range(start, start + count):
        pad[row] = jnp.zeros(pad.shape[1:], F32)


def tap_rows(pad, w_ref, start, count, c, flipped=False):
    acc = [None] * count
    for b in range(K):
        for row in range(count + K - 1):
            value = pad[start + row, c + b]
            for a in range(K):
                o = row - a
                if 0 <= o < count:
                    tap = a * K + b
                    term = value * w_ref[TAPS - 1 - tap if flipped else tap]
                    acc[o] = term if acc[o] is None else acc[o] + term
    return acc


def turn_rims(refs, side_ref, high, low):
    for side, ref in enumerate(refs):
        chan_all, width = ref.shape[0] * ref.shape[2], ref.shape[3]

        @pl.when(side_ref[side] == 1)
        def _(side=side, ref=ref, chan_all=chan_all, width=width):
            for k in range(ref.shape[1]):
                here = slice(k * width, (k + 1) * width)
                high[side, here], low[side, here] = split(ref[:, k].reshape(chan_all, width).T)


def raise_rows(d):
    e1, o1 = d[2] + d[6] - 4.25 * d[4], d[1] + d[5] - 4.25 * d[3]
    e2, o2 = 0.25 * d[2] - 1.25 * d[4] + d[6], 0.5 * d[1] - 2.5 * d[3] + 2.0 * d[5]
    e3, o3 = 4.0 * d[2] - 5.0 * d[4] + d[6], 2.0 * d[1] - 2.5 * d[3] + 0.5 * d[5]
    return [
        d[0] - d[6] + 5.25 * (d[4] - d[2]),
        e1 + o1,
        e1 - o1,
        e2 + o2,
        e2 - o2,
        e3 + o3,
        e3 - o3,
        d[7] - d[1] + 5.25 * (d[3] - d[5]),
    ]


POINT_SCALES = (1.0, -2.0 / 9.0, -2.0 / 9.0, 1.0 / 90.0, 1.0 / 90.0, 32.0 / 45.0, 32.0 / 45.0)
POINT_PLACES = (0.0, 1.0, -1.0, 2.0, -2.0, 0.5, -0.5)
POINTS = 8
GROUP = 4


def tap_factors():
    rows = [[scale * place**a for a in range(K)] for scale, place in zip(POINT_SCALES, POINT_PLACES)]
    return rows + [[0.0] * (K - 1) + [1.0]]


def mix(factors, values):
    out = None
    for factor, value in zip(factors, values):
        if factor != 0.0:
            term = value if factor == 1.0 else value * factor
            out = term if out is None else out + term
    return out


def lower(m):
    s1, d1, s2, d2, s3, d3 = m[1] + m[2], m[1] - m[2], m[3] + m[4], m[3] - m[4], m[5] + m[6], m[5] - m[6]
    return [
        m[0] + s1 + (s2 + s3),
        d1 + (2.0 * d2 + 0.5 * d3),
        s1 + (4.0 * s2 + 0.25 * s3),
        d1 + m[7] + (8.0 * d2 + 0.125 * d3),
    ]


def spread_points(g):
    e1, o1 = g[0] + g[2], g[1] + g[3]
    e2, o2 = g[0] + 4.0 * g[2], 2.0 * g[1] + 8.0 * g[3]
    e3, o3 = g[0] + 0.25 * g[2], 0.5 * g[1] + 0.125 * g[3]
    return [g[0], e1 + o1, e1 - o1, e2 + o2, e2 - o2, e3 + o3, e3 - o3, g[3]]


def raise_all(pad, first, raised):
    def one(g, _):
        for c in range(SUB):
            d = [pad[first + GROUP * g + k, c + 2] for k in range(2 * GROUP)]
            for p, value in enumerate(raise_rows(d)):
                raised[g, p, c + 2] = value
        for p in range(POINTS):
            fill_sides(raised.at[g], p)
        return 0

    lax.fori_loop(0, raised.shape[0], one, 0)


def raise_taps(w_ref, taps, flipped=False, scale=1.0):
    for b in range(K):
        column_taps = []
        for a in range(K):
            tap = a * K + b
            column_taps.append(w_ref[TAPS - 1 - tap if flipped else tap])
        for p, factors in enumerate(tap_factors()):
            taps[p * K + b] = mix([scale * factor for factor in factors], column_taps)


def four_rows(raised, taps, g, columns):
    m = []
    for p in range(POINTS):
        values = {c: raised[g, p, c] for c in range(columns[0], columns[-1] + K)}
        row = []
        for c in columns:
            row.append(mix([1.0] * K, [values[c + b] * taps[p * K + b] for b in range(K)]))
        m.append(row)
    return [lower([m[p][i] for p in range(POINTS)]) for i in range(len(columns))]


def spread_kernel(
    parts, count, side_ref, top_ref, low_ref, own_ref, high_ref, lower_ref, gain_ref, bias_ref, w_ref, *rest
):
    sums = rest[:parts]
    out_ref, edge_ref, hid_ref, sum_ref, pad, terms, rim_high, rim_low, raised, taps = rest[parts:]
    rows = own_ref.shape[0]
    _, _, scale, shift = norm_terms(total(sums), count, gain_ref[0:1], bias_ref[0:1])
    terms[0] = jnp.broadcast_to(0.5 * scale, (SUB, 128))
    terms[1] = jnp.broadcast_to(0.5 * shift, (SUB, 128))

    @pl.when(pl.program_id(0) == 0)
    def _():
        turn_rims((top_ref, low_ref), side_ref, rim_high, rim_low)

    def act(value):
        return swish_half(value * terms[0] + terms[1])

    def own_rows(i, _):
        for k in range(GROUP):
            for c in range(SUB):
                pad[GROUP * i + k + HALO_IN, c + 2] = act(own_ref[GROUP * i + k, c])
        return 0

    lax.fori_loop(0, rows // GROUP, own_rows, 0)
    for side, start, first in ((0, 0, HALO_IN - HALO_OUT), (1, rows + HALO_IN, 0)):

        @pl.when(side_ref[side] == 1)
        def _(side=side, start=start, first=first):
            halo = dot3((rim_high[side], rim_low[side]), (high_ref[...], lower_ref[...]))
            halo = halo.reshape(HALO_IN, SUB, SUB, 128)
            hid_ref[side] = halo[first : first + HALO_OUT]
            pad[start : start + HALO_IN, 2 : SUB + 2] = act(halo)
            edge_row = min(start, rows + 2)
            for r in range(HALO_OUT + K - 1):
                fill_sides(pad, edge_row + r)

        @pl.when(side_ref[side] == 0)
        def _(side=side, start=start):
            clear_rows(pad, start, HALO_IN)
            hid_ref[side] = jnp.zeros(hid_ref.shape[1:], F32)

    raise_taps(w_ref, taps)
    raise_all(pad, 2, raised)

    def group(g, carry):
        one, two = carry
        for columns in (range(0, SUB // 2), range(SUB // 2, SUB)):
            for c, values in zip(columns, four_rows(raised, taps, g, columns)):
                for o, value in enumerate(values):
                    out_ref[GROUP * g + o, c] = value
                    one = one + value
                    two = two + value * value
        return one, two

    zero = jnp.zeros((SUB, 128), F32)
    one, two = lax.fori_loop(0, rows // GROUP, group, (zero, zero))
    sum_ref[0:1] = jnp.sum(one, axis=0, keepdims=True)
    sum_ref[1:2] = jnp.sum(two, axis=0, keepdims=True)
    for side, start in ((0, 0), (1, rows + 2)):

        @pl.when(side_ref[side] == 1)
        def _(side=side, start=start):
            for c in range(SUB):
                acc = tap_rows(pad, w_ref, start, HALO_OUT, c)
                for o in range(HALO_OUT):
                    edge_ref[side, o, c] = acc[o]

        @pl.when(side_ref[side] == 0)
        def _(side=side):
            edge_ref[side] = jnp.zeros(edge_ref.shape[1:], F32)


def lanes(shape):
    lead = len(shape) - 1
    return pl.BlockSpec(tuple(shape[:-1]) + (128,), lambda e: (0,) * lead + (e,))


def spread(count, side, top, low, own, w_high, w_low, gains, biases, taps, sums):
    rows, hidden = own.shape[0], own.shape[-1]
    chan_all = w_high.shape[0]
    arrays = [own, w_high, w_low, gains, biases, taps, *sums]
    edge_shape = (2, HALO_OUT, SUB, SUB, hidden)
    rim_shape = (2, HALO_IN * FRAME_COLUMNS, chan_all)
    return pl.pallas_call(
        partial(spread_kernel, len(sums), count),
        grid=(hidden // 128,),
        in_specs=[pl.BlockSpec(memory_space=pltpu.SMEM), whole(top.shape), whole(low.shape)]
        + [lanes(a.shape) for a in arrays],
        out_specs=[
            lanes((rows, SUB, SUB, hidden)),
            lanes(edge_shape),
            lanes(edge_shape),
            lanes((2, hidden)),
        ],
        out_shape=[
            jax.ShapeDtypeStruct((rows, SUB, SUB, hidden), F32),
            jax.ShapeDtypeStruct(edge_shape, F32),
            jax.ShapeDtypeStruct(edge_shape, F32),
            jax.ShapeDtypeStruct((2, hidden), F32),
        ],
        scratch_shapes=[
            pltpu.VMEM((rows + 2 * HALO_IN, SUB + 4, SUB, 128), F32),
            pltpu.VMEM((2, SUB, 128), F32),
            pltpu.VMEM(rim_shape, BF16),
            pltpu.VMEM(rim_shape, BF16),
            pltpu.VMEM((rows // GROUP, POINTS, SUB + 4, SUB, 128), F32),
            pltpu.VMEM((POINTS * K, SUB, 128), F32),
        ],
        compiler_params=params(),
        cost_estimate=cost(10),
        name="spread",
    )(side, top, low, *arrays)


def as_row(columns):
    width = columns.shape[1]
    folded = columns[:, 0:128]
    for i in range(128, width, 128):
        folded = folded + columns[:, i : i + 128]
    return jnp.sum(folded.T, axis=0, keepdims=True)


def gather_kernel(parts, count, own_ref, gout_ref, gain_ref, bias_ref, wt_ref, high_ref, low_ref, *rest):
    sums, (m_ref, s_ref, se_ref, proj_ref) = rest[:parts], rest[parts:]
    t = pl.program_id(0)
    chan_all, hidden = wt_ref.shape

    @pl.when(t == 0)
    def _():
        m_ref[...] = jnp.zeros_like(m_ref)
        s_ref[...] = jnp.zeros_like(s_ref)

    _, _, scale, shift = norm_terms(total(sums), count, gain_ref[1:2], bias_ref[1:2])
    scale, shift = 0.5 * scale, 0.5 * shift
    gout = split(gout_ref[:, 0].reshape(chan_all, gout_ref.shape[3]))
    proj = None
    for cut in chunks(hidden):
        act = swish_half(own_ref[0, :, cut] * scale[:, cut] + shift[:, cut])
        s_ref[0:1, cut] += jnp.sum(act, axis=0, keepdims=True)
        act = split(act)
        m_ref[:, cut] += dot3(gout, act)
        term = dot3(act, (high_ref[cut], low_ref[cut]))
        proj = term if proj is None else proj + term
    proj_ref[0] = proj

    @pl.when(t == pl.num_programs(0) - 1)
    def _():
        wt = wt_ref[...]
        se_ref[0:1] = as_row(s_ref[...] * wt)
        se_ref[1:2] = as_row(m_ref[...] * wt)


def gather(count, own, gout, gains, biases, wt, w_high, w_low, sums):
    nz, bands, chans, area = gout.shape
    hidden = wt.shape[1]
    chan_all = nz * chans
    grid, tall, put, wide = by_steps(nz, bands, chans, area)
    return pl.pallas_call(
        partial(gather_kernel, len(sums), count),
        grid=grid,
        in_specs=[
            tall(hidden),
            wide,
            whole(gains.shape),
            whole(biases.shape),
            whole(wt.shape),
            whole(w_high.shape),
            whole(w_low.shape),
        ]
        + [whole(s.shape) for s in sums],
        out_specs=[
            whole((chan_all, hidden)),
            whole((1, hidden)),
            whole((2, chan_all)),
            put(chan_all),
        ],
        out_shape=[
            jax.ShapeDtypeStruct((chan_all, hidden), F32),
            jax.ShapeDtypeStruct((1, hidden), F32),
            jax.ShapeDtypeStruct((2, chan_all), F32),
            jax.ShapeDtypeStruct((bands, area, chan_all), F32),
        ],
        compiler_params=params(),
        cost_estimate=cost(13),
        name="gather",
    )(own, gout, gains, biases, wt, w_high, w_low, *sums)


def column(row):
    return jnp.broadcast_to(row, (SUB, row.shape[1])).T[:, 0:1]


def slope_terms(sums, count, gain_ref, bias_ref):
    _, _, scale, shift = norm_terms(sums, count, gain_ref[1:2], bias_ref[1:2])
    return 0.5 * scale, 0.5 * shift


def second_grad(gout, weights, k_row, value, terms, cut):
    h = value * terms[0][:, cut] + terms[1][:, cut]
    return (dot3(gout, (weights[0][:, cut], weights[1][:, cut])) + k_row[:, cut]) * slope_half(h), h


def proj_back_kernel(
    pairs,
    parts,
    count,
    own_ref,
    gout_ref,
    gain_ref,
    bias_ref,
    wt_ref,
    sqt_ref,
    down_ref,
    ex_ref,
    exb_ref,
    *rest,
):
    ses, sums = rest[:pairs], rest[pairs : pairs + parts]
    q_ref, sum_ref, val_ref, col_ref, w_high, w_low, k_row = rest[pairs + parts :]
    chan_all, hidden = wt_ref.shape

    @pl.when(pl.program_id(0) == 0)
    def _():
        se = total(ses)
        pooled = se[0:1] / (FRAME_ROWS * FRAME_COLUMNS)
        sqt, ex = sqt_ref[...], ex_ref[...]
        pre = jnp.sum(sqt * pooled, axis=1, keepdims=True) + down_ref[...]
        gate = sigmoid(pre)
        squeezed = pre * gate
        excite = sigmoid(jnp.sum(ex * squeezed, axis=0, keepdims=True) + exb_ref[...])
        logit = se[1:2] * excite * (1.0 - excite)
        slope = gate * (1.0 + pre * (1.0 - gate))
        grad_sq = jnp.sum(ex * logit, axis=1, keepdims=True) * slope
        pool_grad = jnp.sum(sqt * grad_sq, axis=0, keepdims=True) / (FRAME_ROWS * FRAME_COLUMNS)
        val_ref[...] = jnp.zeros_like(val_ref)
        val_ref[0:1] = excite
        val_ref[1:2] = pool_grad
        val_ref[2:3] = logit
        val_ref[3:4] = pooled
        lane = lax.broadcasted_iota(jnp.int32, col_ref.shape, 1)
        col_ref[...] = jnp.where(lane == 0, squeezed, jnp.where(lane == 1, grad_sq, 0.0))
        wt = 0.5 * wt_ref[...]
        w_high[...], w_low[...] = split(wt * column(excite))
        k_row[...] = jnp.sum(wt * column(pool_grad), axis=0, keepdims=True)
        sum_ref[...] = jnp.zeros_like(sum_ref)

    terms = slope_terms(total(sums), count, gain_ref, bias_ref)
    gout = split(gout_ref[:, 0].reshape(chan_all, gout_ref.shape[3]).T)
    for cut in chunks(hidden):
        q, h = second_grad(gout, (w_high, w_low), k_row, own_ref[0, :, cut], terms, cut)
        q_ref[0, :, cut] = q
        sum_ref[0:1, cut] += jnp.sum(q, axis=0, keepdims=True)
        sum_ref[1:2, cut] += jnp.sum(q * h, axis=0, keepdims=True)

    @pl.when(pl.program_id(0) == pl.num_programs(0) - 1)
    def _():
        sum_ref[1:2] = (2.0 * sum_ref[1:2] - bias_ref[1:2] * sum_ref[0:1]) / gain_ref[1:2]


def proj_back(count, own, gout, gains, biases, wt, se_weights, ses, sums):
    nz, bands, chans, area = gout.shape
    hidden = wt.shape[1]
    chan_all = nz * chans
    reduced = se_weights[0].shape[0]
    fixed = [gains, biases, wt, *se_weights, *ses, *sums]
    grid, tall, put, wide = by_steps(nz, bands, chans, area)
    return pl.pallas_call(
        partial(proj_back_kernel, len(ses), len(sums), count),
        grid=grid,
        in_specs=[
            tall(hidden),
            wide,
        ]
        + [whole(a.shape) for a in fixed],
        out_specs=[
            put(hidden),
            whole((2, hidden)),
            whole((SUB, chan_all)),
            whole((reduced, 128)),
            whole(wt.shape),
            whole(wt.shape),
            whole((1, hidden)),
        ],
        out_shape=[
            jax.ShapeDtypeStruct((bands, area, hidden), F32),
            jax.ShapeDtypeStruct((2, hidden), F32),
            jax.ShapeDtypeStruct((SUB, chan_all), F32),
            jax.ShapeDtypeStruct((reduced, 128), F32),
            jax.ShapeDtypeStruct(wt.shape, BF16),
            jax.ShapeDtypeStruct(wt.shape, BF16),
            jax.ShapeDtypeStruct((1, hidden), F32),
        ],
        compiler_params=params(),
        cost_estimate=cost(12),
        name="proj_back",
    )(own, gout, *fixed)


def project_kernel(proj_ref, x_ref, val_ref, m_ref, s_ref, out_ref, grad_ref):
    nz, _, chans, area = x_ref.shape

    @pl.when(pl.program_id(0) == 0)
    def _():
        grad_ref[...] = column(val_ref[0:1]) * m_ref[...] + column(val_ref[1:2]) * s_ref[...]

    out = (proj_ref[0] * val_ref[0:1]).T
    out_ref[:, 0] = x_ref[:, 0] + out.reshape(nz, chans, area)


def project(proj, x, values, m, s):
    nz, bands, chans, area = x.shape
    fixed = [values, m, s]
    grid, tall, put, wide = by_steps(nz, bands, chans, area)
    return pl.pallas_call(
        project_kernel,
        grid=grid,
        in_specs=[
            tall(nz * chans),
            wide,
        ]
        + [whole(a.shape) for a in fixed],
        out_specs=[wide, whole(m.shape)],
        out_shape=[
            jax.ShapeDtypeStruct((nz, bands, chans, area), F32),
            jax.ShapeDtypeStruct(m.shape, F32),
        ],
        compiler_params=params(),
        cost_estimate=cost(4),
        name="project",
    )(proj, x, *fixed)


def spread_back_kernel(
    parts,
    count,
    side_ref,
    top_ref,
    low_ref,
    hid_ref,
    hid_halo_ref,
    own_ref,
    halo_ref,
    q_ref,
    high_ref,
    lower_ref,
    k_ref,
    gain_ref,
    bias_ref,
    w_ref,
    *rest,
):
    sums_one, sums_two, backs = (rest[i * parts : (i + 1) * parts] for i in range(3))
    out_ref, sum_ref, tap_ref, pad, grad, terms, rim_high, rim_low, raised, points, taps = rest[3 * parts :]
    rows = own_ref.shape[0]

    @pl.when(pl.program_id(0) == 0)
    def _():
        turn_rims((top_ref, low_ref), side_ref, rim_high, rim_low)

    _, _, scale, shift = norm_terms(total(sums_one), count, gain_ref[0:1], bias_ref[0:1])
    a, b, c0 = back_terms(total(sums_two), total(backs), count, gain_ref[1:2])
    for i, row in enumerate((0.5 * scale, 0.5 * shift, a, b, c0)):
        terms[i] = jnp.broadcast_to(row, (SUB, 128))

    def act(value):
        return swish_half(value * terms[0] + terms[1])

    def grad_in(q, value):
        return q * terms[2] + (value * terms[3] + terms[4])

    def own_rows(i, _):
        for k in range(GROUP):
            r = GROUP * i + k
            for c in range(SUB):
                pad[r + HALO_OUT, c + 2] = act(hid_ref[r, c])
                grad[r + HALO_OUT, c + 2] = grad_in(q_ref[r, c], own_ref[r, c])
        return 0

    lax.fori_loop(0, rows // GROUP, own_rows, 0)
    slope = slope_terms(total(sums_two), count, gain_ref, bias_ref)
    for side, start in ((0, 0), (1, rows + HALO_OUT)):

        @pl.when(side_ref[side] == 1)
        def _(side=side, start=start):
            value = halo_ref[side].reshape(HALO_OUT * FRAME_COLUMNS, 128)
            weights = (high_ref, lower_ref)
            gout = (rim_high[side], rim_low[side])
            q, _ = second_grad(gout, weights, k_ref, value, slope, slice(0, 128))
            edge = grad_in(q.reshape(HALO_OUT, SUB, SUB, 128), halo_ref[side])
            grad[start : start + HALO_OUT, 2 : SUB + 2] = edge
            pad[start : start + HALO_OUT, 2 : SUB + 2] = act(hid_halo_ref[side])

        @pl.when(side_ref[side] == 0)
        def _(start=start):
            clear_rows(pad, start, HALO_OUT)
            clear_rows(grad, start, HALO_OUT)

    raise_all(pad, 0, raised)

    def point_group(g, _):
        for c in range(SUB):
            mine = [grad[GROUP * g + HALO_OUT + k, c + 2] for k in range(GROUP)]
            for p, value in enumerate(spread_points(mine)):
                points[g, p, c] = value
        return 0

    lax.fori_loop(0, rows // GROUP, point_group, 0)
    zero = jnp.zeros((SUB, 128), F32)
    factors = tap_factors()
    tap_sums = [None] * TAPS
    for p in range(0, POINTS, 2):

        def weight_group(g, acc, p=p):
            acc = list(acc)
            for k in range(2):
                values = [raised[g, p + k, c] for c in range(SUB + K - 1)]
                for c in range(SUB):
                    mine = points[g, p + k, c]
                    for b in range(K):
                        at = (k * 2 + c % 2) * K + b
                        acc[at] = acc[at] + values[c + b] * mine
            return tuple(acc)

        acc = lax.fori_loop(0, rows // GROUP, weight_group, (zero,) * (4 * K))
        for k in range(2):
            for b in range(K):
                value = jnp.sum(acc[2 * k * K + b] + acc[(2 * k + 1) * K + b], axis=0, keepdims=True)
                for a in range(K):
                    if factors[p + k][a] != 0.0:
                        term = value * factors[p + k][a]
                        old = tap_sums[a * K + b]
                        tap_sums[a * K + b] = term if old is None else old + term
    for tap in range(TAPS):
        tap_ref[tap : tap + 1] = tap_sums[tap]

    raise_taps(w_ref, taps, flipped=True, scale=0.5)
    raise_all(grad, 0, raised)

    def group(g, carry):
        one, two = carry
        for columns in (range(0, SUB // 2), range(SUB // 2, SUB)):
            for c, values in zip(columns, four_rows(raised, taps, g, columns)):
                for o, value in enumerate(values):
                    h = hid_ref[GROUP * g + o, c] * terms[0] + terms[1]
                    value = value * slope_half(h)
                    out_ref[GROUP * g + o, c] = value
                    one = one + value
                    two = two + value * h
        return one, two

    one, two = lax.fori_loop(0, rows // GROUP, group, (zero, zero))
    one, two = jnp.sum(one, axis=0, keepdims=True), jnp.sum(two, axis=0, keepdims=True)
    sum_ref[0:1] = one
    sum_ref[1:2] = (2.0 * two - bias_ref[0:1] * one) / gain_ref[0:1]


def spread_back(
    count, side, top, low, hid, hid_halo, own, halo, q, weights, gains, biases, taps, sums_one, sums_two, backs
):
    rows, hidden = own.shape[0], own.shape[-1]
    arrays = [hid, hid_halo, own, halo, q, *weights, gains, biases, taps, *sums_one, *sums_two, *backs]
    rim_shape = (2, HALO_OUT * FRAME_COLUMNS, weights[0].shape[0])
    return pl.pallas_call(
        partial(spread_back_kernel, len(backs), count),
        grid=(hidden // 128,),
        in_specs=[pl.BlockSpec(memory_space=pltpu.SMEM), whole(top.shape), whole(low.shape)]
        + [lanes(a.shape) for a in arrays],
        out_specs=[lanes((rows, SUB, SUB, hidden)), lanes((2, hidden)), lanes((TAPS, hidden))],
        out_shape=[
            jax.ShapeDtypeStruct((rows, SUB, SUB, hidden), F32),
            jax.ShapeDtypeStruct((2, hidden), F32),
            jax.ShapeDtypeStruct((TAPS, hidden), F32),
        ],
        scratch_shapes=[
            pltpu.VMEM((rows + 2 * HALO_OUT, SUB + 4, SUB, 128), F32),
            pltpu.VMEM((rows + 2 * HALO_OUT, SUB + 4, SUB, 128), F32),
            pltpu.VMEM((5, SUB, 128), F32),
            pltpu.VMEM(rim_shape, BF16),
            pltpu.VMEM(rim_shape, BF16),
            pltpu.VMEM((rows // GROUP, POINTS, SUB + 4, SUB, 128), F32),
            pltpu.VMEM((rows // GROUP, POINTS, SUB, SUB, 128), F32),
            pltpu.VMEM((POINTS * K, SUB, 128), F32),
        ],
        compiler_params=params(),
        cost_estimate=cost(150),
        name="spread_back",
    )(side, top, low, *arrays)


def expand_grad(q_ref, hid_ref, terms, cut):
    a, b, c = terms
    return split(q_ref[0, :, cut] * a[:, cut] + (hid_ref[0, :, cut] * b[:, cut] + c[:, cut]))


def input_kernel(parts, count, start, q_ref, hid_ref, gout_ref, gain_ref, w_high, w_low, *rest):
    sums, backs, out_ref = rest[:parts], rest[parts : 2 * parts], rest[2 * parts]
    nz, _, chans, area = out_ref.shape
    terms = back_terms(total(sums), total(backs), count, gain_ref[0:1])
    out = None
    for cut in chunks(w_high.shape[0]):
        term = dot3(expand_grad(q_ref, hid_ref, terms, cut), (w_high[cut], w_low[cut]))
        out = term if out is None else out + term
    own = gout_ref[:, 0]
    if own.shape[2] > area:
        own = own[:, :, start : start + area]
    out_ref[:, 0] = own + out.T.reshape(nz, chans, area)


def input_grad(count, start, width, q, hid, gout, gains, w_high, w_low, sums, backs):
    nz, bands, chans, area = gout.shape
    hidden = w_high.shape[0]
    at = start // width
    fixed = [gains, w_high, w_low, *sums, *backs]
    if width % 128 == 0:
        gout_spec = pl.BlockSpec((nz, 1, chans, width), lambda t: (0, t, 0, at))
    else:
        gout_spec = pl.BlockSpec((nz, 1, chans, area), lambda t: (0, t, 0, 0))
    return pl.pallas_call(
        partial(input_kernel, len(sums), count, start),
        grid=(bands,),
        in_specs=[
            pl.BlockSpec((1, width, hidden), lambda t: (t, at, 0)),
            pl.BlockSpec((1, width, hidden), lambda t: (t, at, 0)),
            gout_spec,
        ]
        + [whole(v.shape) for v in fixed],
        out_specs=pl.BlockSpec((nz, 1, chans, width), lambda t: (0, t, 0, 0)),
        out_shape=jax.ShapeDtypeStruct((nz, bands, chans, width), F32),
        compiler_params=params(),
        cost_estimate=cost(12),
        name="input_grad",
    )(q, hid, gout, *fixed)


def weight_kernel(chans, ids_ref, q_ref, x_ref, tap_ref, one_ref, two_ref, val_ref, col_ref, *rest):
    outs, acc, small = rest[:-2], rest[-2], rest[-1]
    nz, _, _, area = x_ref.shape
    chan_all, hidden = acc.shape
    width = hidden // nz
    t = pl.program_id(0)

    @pl.when(t == 0)
    def _():
        acc[...] = jnp.zeros_like(acc)
        small[...] = jnp.zeros_like(small)
        small[0:TAPS] = tap_ref[...]
        small[TAPS : TAPS + 1] = one_ref[1:2]
        small[TAPS + 1 : TAPS + 2] = two_ref[1:2]
        small[TAPS + 2 : TAPS + 3] = one_ref[0:1]
        small[TAPS + 3 : TAPS + 4] = two_ref[0:1]
        lead = (ids_ref[1] == 0).astype(F32)
        logit, pooled = val_ref[2:3] * lead, val_ref[3:4]
        reduced = col_ref.shape[0]
        grad_sq = col_ref[:, 1:2] * lead
        g_sq = grad_sq * pooled
        g_ex = col_ref[:, 0:1] * logit
        grad_row = jnp.broadcast_to(grad_sq, (reduced, 128)).T[0:1]
        for z in range(nz):
            own, at = slice(z * chans, (z + 1) * chans), z * width
            small[32 : 32 + reduced, at : at + chans] = g_sq[:, own]
            small[32 : 32 + reduced, at + chans : at + 2 * chans] = g_ex[:, own]
            small[32:33, at + 2 * chans : at + 3 * chans] = logit[:, own]
            small[33:34, at + 2 * chans : at + 2 * chans + reduced] = grad_row

    x = split(x_ref[:, 0].reshape(chan_all, area))
    for cut in chunks(hidden):
        acc[:, cut] += dot3(x, split(q_ref[0, :, cut]))

    @pl.when(t == pl.num_programs(0) - 1)
    def _():
        n = sum(out.shape[0] for out in outs)
        r, m = chan_all // n, SMALL // n
        for core, out in enumerate(outs):
            for i in range(out.shape[0]):
                p = ids_ref[0] ^ (i * len(outs) + core)
                out[i, 0:r] = acc[pl.ds(pl.multiple_of(p * r, r), r), :]
                out[i, r : r + m] = small[pl.ds(pl.multiple_of(p * m, m), m), :]


def weight_grad(ids, shape, q, x, taps, one, two, values, columns):
    nz, bands, chans, area = x.shape
    hidden = q.shape[2]
    chan_all = nz * chans
    fixed = [taps, one, two, values, columns]
    pieces, chips = shape
    shape = (chips, (chan_all + SMALL) // (pieces * chips), hidden)
    grid, tall, put, wide = by_steps(nz, bands, chans, area)
    return pl.pallas_call(
        partial(weight_kernel, chans),
        grid=grid,
        in_specs=[
            pl.BlockSpec(memory_space=pltpu.SMEM),
            tall(hidden),
            wide,
        ]
        + [whole(v.shape) for v in fixed],
        out_specs=[whole(shape)] * pieces,
        out_shape=[jax.ShapeDtypeStruct(shape, F32)] * pieces,
        scratch_shapes=[pltpu.VMEM((chan_all, hidden), F32), pltpu.VMEM((SMALL, hidden), F32)],
        compiler_params=params(),
        cost_estimate=cost(7),
        name="weight_grad",
    )(ids, q, x, *fixed)


def merge_kernel(one_ref, two_ref, *outs):
    for i, out in enumerate(outs):
        out[...] = one_ref[i] + two_ref[i]


def merge(one, two):
    n = one.shape[0]
    return pl.pallas_call(
        merge_kernel,
        grid=(1,),
        in_specs=[whole(one.shape), whole(two.shape)],
        out_specs=[whole(one.shape[1:])] * n,
        out_shape=[jax.ShapeDtypeStruct(one.shape[1:], F32)] * n,
        compiler_params=params(),
        cost_estimate=cost(2),
        name="merge",
    )(one, two)


def collect_kernel(n, nz, parts, count, ids_ref, early_ref, gram_ref, high_ref, low_ref, gain_ref, *rest):
    pieces, sums, backs = rest[:n], rest[n : n + parts], rest[n + parts : n + 2 * parts]
    outs, acc = rest[n + 2 * parts : -1], rest[-1]
    value = total(pieces)
    rows, width = value.shape[0], acc.shape[2]
    r, chan_all = early_ref.shape[0], high_ref.shape[0]
    a, b, c = back_terms(total(sums), total(backs), count, gain_ref[0:1])
    gram = gram_ref[...]
    hid = dot3(split(gram[:, 0:chan_all]), (high_ref[...], low_ref[...]))
    grad = a * value[0:r] + (b * hid + c * gram[:, chan_all : chan_all + 1])
    for z in range(nz):
        here = slice(z * width, (z + 1) * width)
        acc[z, 0:r] = grad[:, here]
        acc[z, r:rows] = value[r:, here]
        acc[z, rows:] = early_ref[:, here]
    for k, out in enumerate(outs):
        out[...] = acc[ids_ref[2] ^ k]


def collect(count, ids, nz, pieces, early, gram, w_high, w_low, gains, sums, backs):
    width = early.shape[1] // nz
    rows = pieces[0].shape[0] + early.shape[0]
    arrays = [early, gram, w_high, w_low, gains, *pieces, *sums, *backs]
    return pl.pallas_call(
        partial(collect_kernel, len(pieces), nz, len(sums), count),
        grid=(1,),
        in_specs=[pl.BlockSpec(memory_space=pltpu.SMEM)] + [whole(a.shape) for a in arrays],
        out_specs=[whole((rows, width))] * nz,
        out_shape=[jax.ShapeDtypeStruct((rows, width), F32)] * nz,
        scratch_shapes=[pltpu.VMEM((nz, rows, width), F32)],
        compiler_params=params(),
        cost_estimate=cost(3),
        name="collect",
    )(ids, *arrays)


def segments(chan_in, hidden_dev, chan_dev, reduced, tap_count, hidden_all):
    seg_sizes = [
        chan_in * hidden_dev,
        tap_count * hidden_dev,
        2 * hidden_dev,
        2 * hidden_dev,
        hidden_dev * chan_in,
        chan_dev * reduced,
        reduced,
        reduced * chan_dev,
        chan_dev,
    ]
    seg_rates = [
        0.5 / math.sqrt(chan_in),
        0.5 / math.sqrt(tap_count),
        0.3,
        0.3,
        0.5 * math.sqrt(8.0 / hidden_all),
        2.0 / math.sqrt(chan_in),
        0.3,
        1.0 / math.sqrt(reduced),
        0.3,
    ]
    return (seg_sizes, seg_rates)


def pack_kernel(at_ref, we_ref, wp_ref, dw_ref, gain_ref, bias_ref, sq_ref, ex_ref, exb_ref, out_ref, small):
    p = at_ref[0]
    chan_in, width = we_ref.shape
    reduced, chans = sq_ref.shape
    m = small.shape[0] * out_ref.shape[0] // (2 * chan_in + small.shape[0])
    r = (out_ref.shape[0] - m) // 2
    small[...] = jnp.zeros_like(small)
    small[0:TAPS] = dw_ref[...]
    small[TAPS : TAPS + 2] = gain_ref[...]
    small[TAPS + 2 : TAPS + 4] = bias_ref[...]
    small[32 : 32 + reduced, 0:chans] = sq_ref[...]
    small[32 : 32 + reduced, chans : 2 * chans] = ex_ref[...]
    small[32:33, 2 * chans : 3 * chans] = exb_ref[...]
    out_ref[0:r] = we_ref[pl.ds(pl.multiple_of(p * r, r), r), :]
    if chan_in == width:
        out_ref[r : 2 * r] = wp_ref[pl.ds(pl.multiple_of(p * r, r), r), :]
    else:
        row, part = p * r % width, p * r // width
        out_ref[r : 2 * r] = wp_ref[
            pl.ds(pl.multiple_of(row, r), r), pl.ds(pl.multiple_of(part * width, 128), width)
        ]
    out_ref[2 * r : 2 * r + m] = small[pl.ds(pl.multiple_of(p * m, m), m), :]


def pack_weights(at, w_expand, w_dw, norm_gains, norm_biases, w_project, squeeze_matrix, excite_matrix, excite_bias_row):
    n_pix = lax.axis_size(PIX)
    chan_in, width = w_expand.shape
    arrays = [
        w_expand,
        w_project,
        w_dw,
        norm_gains,
        norm_biases,
        squeeze_matrix.T,
        excite_matrix,
        excite_bias_row[None],
    ]
    shape = ((2 * chan_in + SMALL) // n_pix, width)
    return pl.pallas_call(
        pack_kernel,
        grid=(1,),
        in_specs=[pl.BlockSpec(memory_space=pltpu.SMEM)] + [whole(a.shape) for a in arrays],
        out_specs=whole(shape),
        out_shape=jax.ShapeDtypeStruct(shape, F32),
        scratch_shapes=[pltpu.VMEM((SMALL, width), F32)],
        compiler_params=params(),
        cost_estimate=cost(2),
        name="pack_weights",
    )(at, *arrays)


def weights_kernel(
    chan_in,
    chans,
    orders,
    base_ref,
    *refs,
):
    slabs = refs[: len(orders)]
    (
        we_high,
        we_low,
        wet_high,
        wet_low,
        wp_high,
        wp_low,
        wpt_ref,
        tap_ref,
        gain_ref,
        bias_ref,
        sqt_ref,
        ex_ref,
        exb_ref,
        first,
        second,
        small,
    ) = refs[len(orders) :]
    nz, width = first.shape[0], first.shape[2]
    n_pix = sum(len(order) for order in orders)
    r, m = chan_in // n_pix, SMALL // n_pix
    reduced = ex_ref.shape[0]
    for ref, order in zip(slabs, orders):
        for i, p in enumerate(order):
            at = base_ref[0] ^ p
            wide = pl.ds(pl.multiple_of(at * r, r), r)
            for z in range(nz):
                here = slice(z * width, (z + 1) * width)
                group = base_ref[1] ^ z
                first[group, wide, :] = ref[i, 0:r, here]
                second[group, wide, :] = ref[i, r : 2 * r, here]
                small[group, pl.ds(pl.multiple_of(at * m, m), m), :] = ref[i, 2 * r : 2 * r + m, here]
    parts = chan_in // width
    for z in range(nz):
        here = slice(z * width, (z + 1) * width)
        own = slice(z * chans, (z + 1) * chans)
        we = first[z]
        we_high[:, here], we_low[:, here] = split(we)
        wet_high[here], wet_low[here] = split(we.T)
        for h in range(parts):
            wp = second[z, h * width : (h + 1) * width]
            cols = slice(h * width, (h + 1) * width)
            wp_high[here, cols], wp_low[here, cols] = split(wp)
            wpt_ref[cols, here] = wp.T
        for tap in range(TAPS):
            tap_ref[tap, :, here] = jnp.broadcast_to(small[z, tap : tap + 1], (SUB, width))
        gain_ref[:, here] = small[z, TAPS : TAPS + 2]
        bias_ref[:, here] = small[z, TAPS + 2 : TAPS + 4]
        sqt_ref[:, own] = small[z, 32 : 32 + reduced, 0:chans]
        ex_ref[:, own] = small[z, 32 : 32 + reduced, chans : 2 * chans]
        exb_ref[:, own] = small[z, 32:33, 2 * chans : 3 * chans]


def order_weights(base, slabs, orders, nz, chan_in, chans, reduced):
    hidden = slabs[0].shape[2]
    width = hidden // nz
    shapes = (
        [((chan_in, hidden), BF16)] * 2
        + [((hidden, chan_in), BF16)] * 4
        + [
            ((chan_in, hidden), F32),
            ((TAPS, SUB, hidden), F32),
            ((2, hidden), F32),
            ((2, hidden), F32),
            ((reduced, chan_in), F32),
            ((reduced, chan_in), F32),
            ((1, chan_in), F32),
        ]
    )
    return pl.pallas_call(
        partial(weights_kernel, chan_in, chans, orders),
        grid=(1,),
        in_specs=[pl.BlockSpec(memory_space=pltpu.SMEM)] + [whole(a.shape) for a in slabs],
        out_specs=[whole(shape) for shape, _ in shapes],
        out_shape=[jax.ShapeDtypeStruct(shape, kind) for shape, kind in shapes],
        scratch_shapes=[
            pltpu.VMEM((nz, chan_in, width), F32),
            pltpu.VMEM((nz, chan_in, width), F32),
            pltpu.VMEM((nz, SMALL, width), F32),
        ],
        compiler_params=params(),
        cost_estimate=cost(3),
        name="order_weights",
    )(base, *slabs)


def thirds(v):
    high = v.astype(BF16)
    rest = v - high.astype(F32)
    mid = rest.astype(BF16)
    return high, mid, (rest - mid.astype(F32)).astype(BF16)


def choose(chosen, v):
    high, mid, low = thirds(v)
    return (dot(chosen, high) + dot(chosen, mid)) + dot(chosen, low)


def choose_lanes(v, chosen):
    high, mid, low = thirds(v)
    return (dot(high, chosen) + dot(mid, chosen)) + dot(low, chosen)


def ones(condition):
    return condition.astype(F32).astype(BF16)


def lay_flat(v, start, width):
    n, m = v.shape
    place = lax.broadcasted_iota(jnp.int32, (m, width), 1) - start
    column_of = lax.broadcasted_iota(jnp.int32, (m, width), 0)
    wide = choose_lanes(v, ones((place + 64 * m) % m == column_of))
    place = lax.broadcasted_iota(jnp.int32, (n, width), 1) - start
    low = lax.broadcasted_iota(jnp.int32, (n, width), 0) * m
    return jnp.sum(jnp.where((place >= low) & (place < low + m), wide, 0.0), axis=0, keepdims=True)


def fill_blocks(out, first, middle, flip, last, squeeze, down, excite, bias):
    blocks, length = out.shape
    tiles, n, _ = first.shape
    width = tiles * 128
    per = length // width
    for i in range(per):
        for u in range(tiles):
            at = i * width + u * 128
            out[0 : n // per, at : at + 128] = first[u, pl.ds(i, n // per, stride=per), :]
    for k in range(TAPS + 4):
        row = n + k
        out[row // per : row // per + 1, row % per * width : (row % per + 1) * width] = middle[k : k + 1, :]
    base = n + TAPS + 4
    parts = last // width
    step = per // parts
    for h in range(parts):
        for e in range(step):
            row = base + parts * e + h
            block, slot = row // per, row % per
            count = width // step
            for u in range(tiles):
                at = slot * width + u * 128
                out[block : block + count, at : at + 128] = flip[
                    h * tiles + u, pl.ds(e, count, stride=step), :
                ]
    start = (base + width * parts) * width
    block = start // length
    start -= block * length
    tail_width = (blocks - block) * length
    tail = lay_flat(squeeze, start, tail_width)
    start += squeeze.shape[0] * squeeze.shape[1]
    tail = tail + lay_flat(down, start, tail_width)
    start += down.shape[1]
    tail = tail + lay_flat(excite, start, tail_width)
    start += excite.shape[0] * excite.shape[1]
    tail = tail + lay_flat(bias, start, tail_width)
    inside = lax.broadcasted_iota(jnp.int32, (1, length), 1)
    kept = jnp.where(inside < (base + width * parts) * width - block * length, out[block : block + 1, :], 0.0)
    out[block : block + 1, :] = kept + tail[:, 0:length]
    for k in range(1, blocks - block):
        out[block + k : block + k + 1, :] = tail[:, k * length : (k + 1) * length]


def prepare_kernel(
    orders,
    base_ref,
    col_ref,
    we_ref,
    dw_ref,
    gain_ref,
    bias_ref,
    wp_ref,
    sq_ref,
    down_ref,
    ex_ref,
    exb_ref,
    *rest,
):
    slabs = rest[: len(orders)]
    weight, first_ref, second_ref, head, flip, middle, moments, ranked = rest[len(orders) :]
    blocks, length = weight.shape
    chan_in, width = we_ref.shape
    devices, room = moments.shape[1:3]
    middle[0:TAPS] = dw_ref[...]
    middle[TAPS : TAPS + 2] = gain_ref[...]
    middle[TAPS + 2 : TAPS + 4] = bias_ref[...]
    for u in range(width // 128):
        head[u] = we_ref[:, u * 128 : (u + 1) * 128]
    for u in range(chan_in // 128):
        flip[u] = wp_ref[:, u * 128 : (u + 1) * 128]
    fill_blocks(
        weight, head, middle, flip, chan_in, sq_ref[...].T, down_ref[...], ex_ref[...], exb_ref[...]
    )
    at = 0
    home = jnp.zeros(col_ref.shape, jnp.int32)
    own_col = col_ref[...]
    for ref, order in zip(slabs, orders):
        for k, p in enumerate(order):
            for m in range(2):
                moments[m, at] = ref[k, m * room : (m + 1) * room]
            home = jnp.where(own_col == base_ref[0] ^ p, at, home)
            at += 1
    ranked[...] = jnp.broadcast_to(own_col.astype(F32), ranked.shape)
    own_row = ranked[...].T[0:1].astype(jnp.int32)
    i = lax.broadcasted_iota(jnp.int32, (blocks, blocks), 0)
    j = lax.broadcasted_iota(jnp.int32, (blocks, blocks), 1)
    earlier = (own_row == own_col) & (j < i)
    rank = jnp.sum(jnp.where(earlier, 1.0, 0.0), axis=1, keepdims=True).astype(jnp.int32)
    slot = home * room + rank
    chosen = ones(lax.broadcasted_iota(jnp.int32, (blocks, devices * room), 1) == slot)
    first_ref[...] = choose(chosen, moments[0].reshape(devices * room, length))
    second_ref[...] = choose(chosen, moments[1].reshape(devices * room, length))


def prepare(base, owners, weights, slabs, orders, length):
    blocks = owners.shape[0]
    chan_in, width = weights[0].shape
    devices = sum(len(o) for o in orders)
    arrays = [owners, *weights, *slabs]
    return pl.pallas_call(
        partial(prepare_kernel, orders),
        grid=(1,),
        in_specs=[pl.BlockSpec(memory_space=pltpu.SMEM)] + [whole(a.shape) for a in arrays],
        out_specs=[whole((blocks, length))] * 3,
        out_shape=[jax.ShapeDtypeStruct((blocks, length), F32)] * 3,
        scratch_shapes=[
            pltpu.VMEM((width // 128, chan_in, 128), F32),
            pltpu.VMEM((chan_in // 128, width, 128), F32),
            pltpu.VMEM((32, width), F32),
            pltpu.VMEM((2, devices, slabs[0].shape[1] // 2, length), F32),
            pltpu.VMEM((blocks, 128), F32),
        ],
        compiler_params=params(),
        cost_estimate=cost(1),
        name="prepare",
    )(base, *arrays)


def adam_kernel(
    bounds,
    rates,
    orders,
    chans,
    reduced,
    me_ref,
    col_ref,
    weight_ref,
    old_one_ref,
    old_two_ref,
    first_ref,
    second_ref,
    *rest,
):
    grad_slabs = rest[: len(orders)]
    first_out, second_out, new_ref, grad, head, flip, tall, small, ranked = rest[len(orders) :]
    blocks, length = grad.shape
    capacity = first_ref.shape[0]
    chan_in, width = tall.shape
    devices = sum(len(order) for order in orders)
    r, m = chan_in // devices, SMALL // devices
    for ref, order in zip(grad_slabs, orders):
        for k, i in enumerate(order):
            p = me_ref[1] ^ i
            for u in range(width // 128):
                head[u, pl.ds(pl.multiple_of(p * r, r), r), :] = ref[k, 0:r, u * 128 : (u + 1) * 128]
            small[pl.ds(pl.multiple_of(p * m, m), m), :] = ref[k, r : r + m]
            tall[pl.ds(pl.multiple_of(p * r, r), r), :] = ref[k, r + m : 2 * r + m]
    for u in range(chan_in // 128):
        flip[u] = tall[u * 128 : (u + 1) * 128].T
    fill_blocks(
        grad,
        head,
        small,
        flip,
        chan_in,
        small[32 : 32 + reduced, 0:chans].T,
        small[33:34, 2 * chans : 2 * chans + reduced],
        small[32 : 32 + reduced, chans : 2 * chans],
        small[32:33, 2 * chans : 3 * chans],
    )

    own_col = col_ref[...]
    ranked[...] = jnp.broadcast_to(own_col.astype(F32), ranked.shape)
    own_row = ranked[...].T[0:1].astype(jnp.int32)
    i = lax.broadcasted_iota(jnp.int32, (blocks, blocks), 0)
    j = lax.broadcasted_iota(jnp.int32, (blocks, blocks), 1)
    earlier = (own_row == own_col) & (i < j)
    rank = jnp.sum(jnp.where(earlier, 1.0, 0.0), axis=0, keepdims=True).astype(jnp.int32)
    g = grad[...]
    mine = lax.broadcasted_iota(jnp.int32, (capacity, blocks), 0)
    owned = choose(ones((mine == rank) & (own_row == me_ref[0])), g)
    first_out[:, 0] = beta_first * first_ref[:, 0] + (1.0 - beta_first) * owned
    second_out[:, 0] = beta_second * second_ref[:, 0] + (1.0 - beta_second) * owned * owned

    first = beta_first * old_one_ref[...] + (1.0 - beta_first) * g
    second = beta_second * old_two_ref[...] + (1.0 - beta_second) * g * g
    first_hat = first / (1.0 - beta_first**STEP)
    second_hat = second / (1.0 - beta_second**STEP)
    place = lax.broadcasted_iota(jnp.int32, (blocks, length), 0) * length + lax.broadcasted_iota(
        jnp.int32, (blocks, length), 1
    )
    rate = jnp.zeros((blocks, length), F32)
    for bound, value in zip(reversed(bounds), reversed(rates)):
        rate = jnp.where(place < bound, jnp.float32(value), rate)
    grad[...] = weight_ref[...] * (1.0 - rate * weight_decay) - rate * first_hat / (
        jnp.sqrt(second_hat) + adam_eps
    )
    for k in range(blocks):
        end = min((k + 1) * length, new_ref.shape[1])
        new_ref[:, k * length : end] = grad[k : k + 1, 0 : end - k * length]


def adam(ids, owners, prepared, first, second, grads, orders, chan_in, chans, reduced, bounds, rates):
    blocks, length = prepared[0].shape
    width = grads[0].shape[2]
    arrays = [owners, *prepared, first, second, *grads]
    new_shape = (1, bounds[-1])
    return pl.pallas_call(
        partial(adam_kernel, bounds, rates, orders, chans, reduced),
        grid=(1,),
        in_specs=[pl.BlockSpec(memory_space=pltpu.SMEM)] + [whole(a.shape) for a in arrays],
        out_specs=[whole(first.shape), whole(second.shape), whole(new_shape)],
        out_shape=[
            jax.ShapeDtypeStruct(first.shape, F32),
            jax.ShapeDtypeStruct(second.shape, F32),
            jax.ShapeDtypeStruct(new_shape, F32),
        ],
        scratch_shapes=[
            pltpu.VMEM((blocks, length), F32),
            pltpu.VMEM((width // 128, chan_in, 128), F32),
            pltpu.VMEM((chan_in // 128, width, 128), F32),
            pltpu.VMEM((chan_in, width), F32),
            pltpu.VMEM((SMALL, width), F32),
            pltpu.VMEM((blocks, 128), F32),
        ],
        compiler_params=params(),
        cost_estimate=cost(10),
        name="adam",
    )(ids, *arrays)


def deal_rows(rows):
    n_pix = lax.axis_size(PIX)
    n, hidden = rows.shape
    dealt = lax.all_to_all(rows.reshape(n_pix, n // n_pix, hidden), PIX, 0, 0, tiled=True)
    return jnp.sum(dealt, axis=0)


def together(*values):
    return lax.optimization_barrier(values)


def local(
    frames_raw,
    grad_out,
    col_offsets,
    flip_flags,
    owners,
    w_expand,
    w_dw,
    norm_gains,
    norm_biases,
    w_project,
    squeeze_matrix,
    se_down_bias,
    excite_matrix,
    excite_bias_row,
    first_moment,
    second_moment,
):
    nz, nhi, nlo = (lax.axis_size(axis) for axis in ALL)
    frames, chans, stored = frames_raw.shape
    band = stored // WIN
    area = band * FRAME_COLUMNS
    rows = nlo * band
    chan_in, hidden_dev = w_expand.shape
    hidden = hidden_dev * nz
    reduced = squeeze_matrix.shape[1]
    group = nz // MB * nhi * nlo
    count = float(frames // MB * FRAME_ROWS * FRAME_COLUMNS)
    hi = lax.axis_index("hi")
    side = jnp.stack([(hi > 0).astype(jnp.int32), (hi < nhi - 1).astype(jnp.int32)])

    n_pix = nhi * nlo
    me = hi * nlo + lax.axis_index("lo")
    relative = me if near(n_pix) else 0 * me
    z_relative = lax.axis_index("chan") if near(n_pix) else 0 * me

    slab = pack_weights(
        me.astype(jnp.int32).reshape(1),
        w_expand,
        w_dw,
        norm_gains,
        norm_biases,
        w_project,
        squeeze_matrix,
        excite_matrix,
        excite_bias_row,
    )
    crops = crop(frames_raw, col_offsets, flip_flags)
    crops, *slab = together(crops, *gather_chan(slab))
    x = deal(crops).reshape(nz, nlo, chans, area)
    ordered = order(grad_out)
    slabs, orders, ordered = gather_pix(jnp.concatenate(slab, axis=1), ordered)
    (
        we_high,
        we_low,
        wet_high,
        wet_low,
        wp_high,
        wp_low,
        w_project_t,
        taps,
        gains,
        biases,
        sq_t,
        ex_all,
        ex_bias,
    ) = order_weights(
        jnp.stack([relative, z_relative]), slabs, orders, nz, chan_in, chans, reduced
    )
    se_weights = [sq_t, se_down_bias[:, None], ex_all, ex_bias]
    x, ordered, we_high, we_low = together(x, ordered, we_high, we_low)

    def as_rows(v):
        return v.reshape(rows, SUB, SUB, hidden)

    def as_bands(v):
        return v.reshape(nlo, area, hidden)

    def as_sides(v, n):
        return v.reshape(2, n, SUB, SUB, hidden)

    hid, sums_one, gram = expand(x, we_high, we_low)
    later = [x]
    sums_one = shares(sums_one, 1, group, later)
    [x] = later
    top, low = rims(x, HALO_IN, band)
    gout = deal(ordered).reshape(nz, nlo, chans, area)
    g_top, g_low = rims(gout, HALO_OUT, band)
    spatial, spatial_halo, hid_halo, sums_two = spread(
        count, side, top, low, as_rows(hid), we_high, we_low, gains, biases, taps, sums_one
    )
    first_turned, second_turned, spatial = together(
        first_moment.transpose(1, 0, 2), second_moment.transpose(1, 0, 2), spatial
    )
    capacity = first_moment.shape[1]
    room = ((0, -capacity % SUB), (0, 0))
    moments = jnp.concatenate([jnp.pad(v[:, 0], room) for v in (first_turned, second_turned)])
    moments = lax.all_gather(moments, PIX, axis=0)
    sums_two = shares(sums_two, 1, group)
    m, s, se_part, proj = gather(
        count, as_bands(spatial), gout, gains, biases, w_project_t, wp_high, wp_low, sums_two
    )
    ses = shares(se_part, nlo, nhi)
    ses, g_top, g_low = together(ses, g_top, g_low)
    q, back_two, values, columns, *w4 = proj_back(
        count, as_bands(spatial), gout, gains, biases, w_project_t, se_weights, ses, sums_two
    )
    backs_two = shares(back_two, 1, group)
    out, g_project = project(proj, x, values, m, s)
    out = deal(out.reshape(frames, chans, area))
    q1, back_one, g_dw = spread_back(
        count,
        side,
        g_top,
        g_low,
        as_rows(hid),
        hid_halo,
        spatial,
        spatial_halo,
        as_rows(q),
        w4,
        gains,
        biases,
        taps,
        sums_one,
        sums_two,
        backs_two,
    )
    later = [q1]
    backs_one = shares(back_one, 1, group, later)
    [q1] = later

    ids = jnp.stack([relative, hi, z_relative]).astype(jnp.int32)
    pieces = weight_grad(
        ids, (2, n_pix // 2) if near(n_pix) else (1, 1), as_bands(q1), x, g_dw, back_one, back_two, values, columns
    )
    if near(n_pix):
        early = lax.psum_scatter(g_project, PIX, scatter_dimension=0, tiled=True)
        gram = lax.psum_scatter(gram, PIX, scatter_dimension=0, tiled=True)
    else:
        early, gram = deal_rows(g_project), deal_rows(gram)
    q1, out, early, gram, moments, *pieces = together(q1, out, early, gram, moments, *pieces)

    def input_part(start, width, q1):
        grad = input_grad(
            count, start, width, as_bands(q1), hid, gout, gains, wet_high, wet_low, sums_one, backs_one
        )
        return grad.reshape(frames, chans, width)

    most = area // 2
    grad_one = input_part(0, most, q1)
    if near(n_pix):
        pieces = [pieces[0], exchange(pieces[1], 1)]
    grad_one, q1, *pieces = together(grad_one, q1, *pieces)
    if near(n_pix):
        pieces = list(merge(*pieces))
        pieces[0], out = together(pieces[0], out)
        pieces = [pieces[0]] + [exchange(pieces[i], 2 * i) for i in range(1, n_pix // 2)]
    else:
        whole_rows = pieces[0][0]
        pieces = [jnp.concatenate([deal_rows(whole_rows[:chan_in]), deal_rows(whole_rows[chan_in:])])]
    grad_two = input_part(most, area - most, q1)
    output = restore(out)
    weights = [
        w_expand,
        w_dw,
        norm_gains,
        norm_biases,
        w_project,
        squeeze_matrix.T,
        se_down_bias[None],
        excite_matrix,
        excite_bias_row[None],
    ]
    block_len = first_moment.shape[2]
    natural = [list(range(n_pix))]
    base = jnp.zeros((1,), jnp.int32)
    prepared = prepare(base, owners, weights, [moments], natural, block_len)
    grad_two, output, *pieces = together(grad_two, output, *pieces)
    groups = collect(count, ids, nz, pieces, early, gram, we_high, we_low, gains, sums_one, backs_one)
    if near(n_pix):
        others = [groups[0]] + [exchange(groups[k], k * n_pix) for k in range(1, nz)]
    else:
        others = list(lax.all_to_all(jnp.stack(groups), "chan", 0, 0, tiled=True))
    grad_one = deal(grad_one)
    grad_one, grad_two, *groups = together(grad_one, grad_two, *groups)
    summed = sum(others[1:], others[0])
    grad_two = deal(grad_two)
    grads, _, prepared = gather_pix(summed, prepared)
    seg_sizes, seg_rates = segments(chan_in, hidden_dev, chans, reduced, TAPS, hidden)
    bounds = [sum(seg_sizes[: i + 1]) for i in range(len(seg_sizes))]
    first_next, second_next, new_params = adam(
        jnp.stack([me, relative]).astype(jnp.int32),
        owners,
        prepared,
        first_turned,
        second_turned,
        grads,
        orders,
        chan_in,
        chans,
        reduced,
        bounds,
        seg_rates,
    )
    first_next, second_next = first_next.transpose(1, 0, 2), second_next.transpose(1, 0, 2)
    grad_frames = uncrop(grad_one, grad_two, col_offsets, flip_flags)
    return (output, grad_frames, first_next, second_next, new_params)


def solution(mesh):
    nz, n_pix = mesh.shape["chan"], mesh.shape["pix"]
    placed = (
        P(None, "chan", PIX),
        P(None, "chan", PIX),
        P(),
        P(),
        P(),
        P(None, "chan"),
        P(None, "chan"),
        P(None, "chan"),
        P(None, "chan"),
        P("chan", None),
        P("chan", None),
        P(),
        P(None, "chan"),
        P("chan"),
        P("chan", PIX, None),
        P("chan", PIX, None),
    )

    def run(*arrays):
        nlo = arrays[0].shape[0] // nz
        return jax.shard_map(
            local,
            mesh=Mesh(mesh.devices.reshape(nz, n_pix // nlo, nlo), ALL),
            in_specs=placed,
            out_specs=(
                P(None, "chan", PIX),
                P(None, "chan", PIX),
                P("chan", PIX, None),
                P("chan", PIX, None),
                P("chan", None),
            ),
            check_vma=False,
        )(*arrays)

    return run
```

```python
from functools import partial
import math

import jax
import jax.numpy as jnp
from jax import lax
from jax.experimental import pallas as pl
from jax.experimental.pallas import tpu as pltpu
from jax.sharding import Mesh, PartitionSpec as P

K = 5
FRAME_ROWS = 64
FRAME_COLUMNS = 64
CLIP_LEN = 4
MB = 4
STEP = 5
WIN = 80
SUB = 8
TAPS = K * K
HALO_IN = 4
SMALL = 64
HALO_OUT = 2

norm_eps = 1e-05
beta_first = 0.5
beta_second = 0.6
adam_eps = 1e-08
weight_decay = 0.1

F32 = jnp.float32
BF16 = jnp.bfloat16
ALL = ("chan", "hi", "lo")
PIX = ("hi", "lo")
SPREAD = ("chan", "lo")
VMEM_BYTES = 62 * 2**20


def params(dims=1):
    return pltpu.CompilerParams(vmem_limit_bytes=VMEM_BYTES, dimension_semantics=("arbitrary",) * dims)


def cost(us):
    return pl.CostEstimate(flops=int(us * 1.1e9), bytes_accessed=int(us * 3.5e6), transcendentals=0)


def sigmoid(v):
    return 0.5 * jnp.tanh(0.5 * v) + 0.5


def swish_half(h):
    return h + h * jnp.tanh(h)


def slope_half(h):
    t = jnp.tanh(h)
    return 1.0 + (t + h * (1.0 - t * t))


def split(v):
    high = v.astype(BF16)
    return high, (v - high.astype(F32)).astype(BF16)


def dot(a, b):
    return jnp.dot(a, b, preferred_element_type=F32)


def dot3(a, b):
    return dot(a[0], b[0]) + (dot(a[0], b[1]) + dot(a[1], b[0]))


def total(refs):
    value = refs[0][...]
    for ref in refs[1:]:
        value = value + ref[...]
    return value


def norm_terms(sums, count, gain, bias):
    mean = sums[0:1] / count
    inverse = lax.rsqrt(sums[1:2] / count - mean * mean + norm_eps)
    scale = gain * inverse
    return mean, inverse, scale, bias - mean * scale


def back_terms(sums, back, count, gain):
    mean = sums[0:1] / count
    inverse = lax.rsqrt(sums[1:2] / count - mean * mean + norm_eps)
    a = gain * inverse
    b = -a * inverse * (back[1:2] / count)
    return a, b, -a * (back[0:1] / count) - b * mean


def exchange(x, stride):
    n = lax.axis_size(ALL)
    return lax.ppermute(x, ALL, [(i, i ^ stride) for i in range(n)])


def shares(x, base, size, after=()):
    bits = size.bit_length() - 1
    parts = [x]
    if bits % 2:
        parts = [x, exchange(x, base)]
        base, bits = base * 2, bits - 1
    while bits:
        x = sum(parts[1:], parts[0])
        if after:
            x, *kept = together(x, *after)
            after[:] = kept
            after = ()
        parts = [x] + [exchange(x, base * k) for k in (1, 2, 3)]
        base, bits = base * 4, bits - 2
    return parts


def deal(x):
    return lax.all_to_all(x, SPREAD, 0, 0, tiled=True)


def edge(x, rows, band, first):
    if rows >= band:
        n = rows // band
        return x[:, :n] if first else x[:, x.shape[1] - n :]
    width = rows * FRAME_COLUMNS
    return x[:, :1, :, :width] if first else x[:, -1:, :, x.shape[3] - width :]


def rims(x, rows, band):
    n = lax.axis_size("hi")
    if n == 2:
        mine = jnp.where(lax.axis_index("hi") == 0, edge(x, rows, band, False), edge(x, rows, band, True))
        other = lax.ppermute(mine, "hi", [(0, 1), (1, 0)])
        return other, other
    down = [(i, i + 1) for i in range(n - 1)]
    up = [(i + 1, i) for i in range(n - 1)]
    top = lax.ppermute(edge(x, rows, band, False), "hi", down)
    low = lax.ppermute(edge(x, rows, band, True), "hi", up)
    return top, low


def near(n_pix):
    return n_pix == 8


def gather_pix(x, beside=None):
    n_pix = lax.axis_size(PIX)
    if not near(n_pix):
        return [lax.all_gather(x, PIX, axis=0)], [list(range(n_pix))], beside
    b = x[None]
    b = jnp.concatenate([b, exchange(b, 2)])
    if beside is not None:
        b, beside = together(b, beside)
    b = jnp.concatenate([b, exchange(b, 4)])
    return [b, exchange(b, 1)], [[0, 2, 4, 6], [1, 3, 5, 7]], beside


def gather_chan(x):
    nz, n_pix = lax.axis_size("chan"), lax.axis_size(PIX)
    if not near(n_pix):
        return list(lax.all_gather(x, "chan", axis=0))
    return [x] + [exchange(x, k * n_pix) for k in range(1, nz)]


def source_column(p, left, flip):
    row, c, s = p // FRAME_COLUMNS, (p // SUB) % SUB, p % SUB
    j = s * SUB + c
    return row * WIN + left + jnp.where(flip == 1, FRAME_COLUMNS - 1 - j, j)


def plain_place(p):
    row, c, s = p // FRAME_COLUMNS, (p // SUB) % SUB, p % SUB
    return row * FRAME_COLUMNS + s * SUB + c


def pick(x, chosen):
    rows = x.shape[0] * x.shape[1]
    high, low = split(x.reshape(rows, x.shape[2]))
    return (dot(high, chosen) + dot(low, chosen)).reshape(x.shape[0], x.shape[1], chosen.shape[1])


def crop_kernel(left_ref, flip_ref, raw_ref, out_ref):
    k = pl.program_id(0)
    width, area = raw_ref.shape[2], out_ref.shape[2]
    p = lax.broadcasted_iota(jnp.int32, (1, area), 1)
    place = source_column(p, left_ref[k], flip_ref[k])
    q = lax.broadcasted_iota(jnp.int32, (width, area), 0)
    out_ref[...] = pick(raw_ref[...], (q == place).astype(F32).astype(BF16))


def crop(raw, left, flip):
    frames, chans, width = raw.shape
    area = width // WIN * FRAME_COLUMNS
    return pl.pallas_call(
        crop_kernel,
        grid=(frames // CLIP_LEN,),
        in_specs=[
            pl.BlockSpec(memory_space=pltpu.SMEM),
            pl.BlockSpec(memory_space=pltpu.SMEM),
            pl.BlockSpec((CLIP_LEN, chans, width), lambda k: (k, 0, 0)),
        ],
        out_specs=pl.BlockSpec((CLIP_LEN, chans, area), lambda k: (k, 0, 0)),
        out_shape=jax.ShapeDtypeStruct((frames, chans, area), F32),
        compiler_params=params(),
        cost_estimate=cost(5),
        name="crop",
    )(left, flip, raw)


def order_kernel(x_ref, out_ref):
    area = x_ref.shape[2]
    p = lax.broadcasted_iota(jnp.int32, (1, area), 1)
    q = lax.broadcasted_iota(jnp.int32, (area, area), 0)
    out_ref[...] = pick(x_ref[...], (q == plain_place(p)).astype(F32).astype(BF16))


def order(x):
    frames, chans, area = x.shape
    return pl.pallas_call(
        order_kernel,
        grid=(frames // CLIP_LEN,),
        in_specs=[pl.BlockSpec((CLIP_LEN, chans, area), lambda k: (k, 0, 0))],
        out_specs=pl.BlockSpec((CLIP_LEN, chans, area), lambda k: (k, 0, 0)),
        out_shape=jax.ShapeDtypeStruct((frames, chans, area), F32),
        compiler_params=params(),
        cost_estimate=cost(25),
        name="order",
    )(x)


def restore_kernel(x_ref, out_ref):
    area = x_ref.shape[2]
    p = lax.broadcasted_iota(jnp.int32, (area, 1), 0)
    q = lax.broadcasted_iota(jnp.int32, (area, area), 1)
    out_ref[...] = pick(x_ref[...], (q == plain_place(p)).astype(F32).astype(BF16))


def restore(x):
    frames, chans, area = x.shape
    return pl.pallas_call(
        restore_kernel,
        grid=(frames // CLIP_LEN,),
        in_specs=[pl.BlockSpec((CLIP_LEN, chans, area), lambda k: (k, 0, 0))],
        out_specs=pl.BlockSpec((CLIP_LEN, chans, area), lambda k: (k, 0, 0)),
        out_shape=jax.ShapeDtypeStruct((frames, chans, area), F32),
        compiler_params=params(),
        cost_estimate=cost(1),
        name="restore",
    )(x)


def uncrop_kernel(left_ref, flip_ref, x_ref, y_ref, out_ref):
    k = pl.program_id(0)
    width = out_ref.shape[2]
    out = None
    for start, ref in ((0, x_ref), (x_ref.shape[2], y_ref)):
        area = ref.shape[2]
        q = lax.broadcasted_iota(jnp.int32, (area, width), 1)
        p = lax.broadcasted_iota(jnp.int32, (area, 1), 0) + start
        place = source_column(p, left_ref[k], flip_ref[k])
        term = pick(ref[...], (q == place).astype(F32).astype(BF16))
        out = term if out is None else out + term
    out_ref[...] = out


def uncrop(x, y, left, flip):
    frames, chans, area = x.shape
    width = (area + y.shape[2]) // FRAME_COLUMNS * WIN
    return pl.pallas_call(
        uncrop_kernel,
        grid=(frames // CLIP_LEN,),
        in_specs=[
            pl.BlockSpec(memory_space=pltpu.SMEM),
            pl.BlockSpec(memory_space=pltpu.SMEM),
            pl.BlockSpec((CLIP_LEN, chans, area), lambda k: (k, 0, 0)),
            pl.BlockSpec((CLIP_LEN, chans, y.shape[2]), lambda k: (k, 0, 0)),
        ],
        out_specs=pl.BlockSpec((CLIP_LEN, chans, width), lambda k: (k, 0, 0)),
        out_shape=jax.ShapeDtypeStruct((frames, chans, width), F32),
        compiler_params=params(),
        cost_estimate=cost(1),
        name="uncrop",
    )(left, flip, x, y)


def chunks(width):
    step = 256 if width % 256 == 0 else width
    return [slice(i, i + step) for i in range(0, width, step)]


def expand_kernel(x_ref, high_ref, low_ref, own_ref, sum_ref, gram_ref):
    @pl.when(pl.program_id(0) == 0)
    def _():
        sum_ref[...] = jnp.zeros_like(sum_ref)
        gram_ref[...] = jnp.zeros_like(gram_ref)

    chan_all, hidden = high_ref.shape
    plain = x_ref[:, 0].reshape(chan_all, x_ref.shape[3])
    turned = plain.T
    x = split(turned)
    for cut in chunks(hidden):
        y = dot3(x, (high_ref[:, cut], low_ref[:, cut]))
        own_ref[0, :, cut] = y
        sum_ref[0:1, cut] += jnp.sum(y, axis=0, keepdims=True)
        sum_ref[1:2, cut] += jnp.sum(y * y, axis=0, keepdims=True)
    gram_ref[:, 0:chan_all] += dot3(split(plain), x)
    gram_ref[:, chan_all:] += jnp.broadcast_to(jnp.sum(plain, axis=1, keepdims=True), (chan_all, 128))


def whole(shape):
    return pl.BlockSpec(shape, lambda *_: (0,) * len(shape))


def by_steps(nz, bands, chans, area):
    run = area
    n = area // run

    def tall(hidden):
        return pl.BlockSpec((1, run, hidden), lambda t: (t // n, t % n, 0))

    def out(hidden):
        return pl.BlockSpec((1, run, hidden), lambda t: (t // n, t % n, 0))

    wide = pl.BlockSpec((nz, 1, chans, run), lambda t: (0, t // n, 0, t % n))
    return (bands * n,), tall, out, wide


def expand(x, high, low):
    nz, bands, chans, area = x.shape
    grid, _, tall, wide = by_steps(nz, bands, chans, area)
    hidden = high.shape[1]
    return pl.pallas_call(
        expand_kernel,
        grid=grid,
        in_specs=[
            wide,
            whole(high.shape),
            whole(low.shape),
        ],
        out_specs=[
            tall(hidden),
            whole((2, hidden)),
            whole((nz * chans, nz * chans + 128)),
        ],
        out_shape=[
            jax.ShapeDtypeStruct((bands, area, hidden), F32),
            jax.ShapeDtypeStruct((2, hidden), F32),
            jax.ShapeDtypeStruct((nz * chans, nz * chans + 128), F32),
        ],
        compiler_params=params(),
        cost_estimate=cost(8),
        name="expand",
    )(x, high, low)


def fill_sides(pad, row):
    s = lax.broadcasted_iota(jnp.int32, (SUB, 128), 0)
    for k in range(2):
        left = pltpu.roll(pad[row, SUB + k], 1, 0)
        pad[row, k] = jnp.where(s == 0, 0.0, left)
        right = pltpu.roll(pad[row, 2 + k], SUB - 1, 0)
        pad[row, SUB + 2 + k] = jnp.where(s == SUB - 1, 0.0, right)


def clear_rows(pad, start, count):
    for row in range(start, start + count):
        pad[row] = jnp.zeros(pad.shape[1:], F32)


def tap_rows(pad, w_ref, start, count, c, flipped=False):
    acc = [None] * count
    for b in range(K):
        for row in range(count + K - 1):
            value = pad[start + row, c + b]
            for a in range(K):
                o = row - a
                if 0 <= o < count:
                    tap = a * K + b
                    term = value * w_ref[TAPS - 1 - tap if flipped else tap]
                    acc[o] = term if acc[o] is None else acc[o] + term
    return acc


def turn_rims(refs, side_ref, high, low):
    for side, ref in enumerate(refs):
        chan_all, width = ref.shape[0] * ref.shape[2], ref.shape[3]

        @pl.when(side_ref[side] == 1)
        def _(side=side, ref=ref, chan_all=chan_all, width=width):
            for k in range(ref.shape[1]):
                here = slice(k * width, (k + 1) * width)
                high[side, here], low[side, here] = split(ref[:, k].reshape(chan_all, width).T)


def raise_rows(d):
    e1, o1 = d[2] + d[6] - 4.25 * d[4], d[1] + d[5] - 4.25 * d[3]
    e2, o2 = 0.25 * d[2] - 1.25 * d[4] + d[6], 0.5 * d[1] - 2.5 * d[3] + 2.0 * d[5]
    e3, o3 = 4.0 * d[2] - 5.0 * d[4] + d[6], 2.0 * d[1] - 2.5 * d[3] + 0.5 * d[5]
    return [
        d[0] - d[6] + 5.25 * (d[4] - d[2]),
        e1 + o1,
        e1 - o1,
        e2 + o2,
        e2 - o2,
        e3 + o3,
        e3 - o3,
        d[7] - d[1] + 5.25 * (d[3] - d[5]),
    ]


POINT_SCALES = (1.0, -2.0 / 9.0, -2.0 / 9.0, 1.0 / 90.0, 1.0 / 90.0, 32.0 / 45.0, 32.0 / 45.0)
POINT_PLACES = (0.0, 1.0, -1.0, 2.0, -2.0, 0.5, -0.5)
POINTS = 8
GROUP = 4


def tap_factors():
    rows = [[scale * place**a for a in range(K)] for scale, place in zip(POINT_SCALES, POINT_PLACES)]
    return rows + [[0.0] * (K - 1) + [1.0]]


def mix(factors, values):
    out = None
    for factor, value in zip(factors, values):
        if factor != 0.0:
            term = value if factor == 1.0 else value * factor
            out = term if out is None else out + term
    return out


def lower(m):
    s1, d1, s2, d2, s3, d3 = m[1] + m[2], m[1] - m[2], m[3] + m[4], m[3] - m[4], m[5] + m[6], m[5] - m[6]
    return [
        m[0] + s1 + (s2 + s3),
        d1 + (2.0 * d2 + 0.5 * d3),
        s1 + (4.0 * s2 + 0.25 * s3),
        d1 + m[7] + (8.0 * d2 + 0.125 * d3),
    ]


def spread_points(g):
    e1, o1 = g[0] + g[2], g[1] + g[3]
    e2, o2 = g[0] + 4.0 * g[2], 2.0 * g[1] + 8.0 * g[3]
    e3, o3 = g[0] + 0.25 * g[2], 0.5 * g[1] + 0.125 * g[3]
    return [g[0], e1 + o1, e1 - o1, e2 + o2, e2 - o2, e3 + o3, e3 - o3, g[3]]


def raise_all(pad, first, raised):
    def two(i, _):
        for k in range(2):
            g = 2 * i + k
            for c in range(SUB):
                d = [pad[first + GROUP * g + n, c + 2] for n in range(2 * GROUP)]
                for p, value in enumerate(raise_rows(d)):
                    raised[g, p, c + 2] = value
            for p in range(POINTS):
                fill_sides(raised.at[g], p)
        return 0

    lax.fori_loop(0, raised.shape[0] // 2, two, 0)


def raise_taps(w_ref, taps, flipped=False, scale=1.0):
    for b in range(K):
        column_taps = []
        for a in range(K):
            tap = a * K + b
            column_taps.append(w_ref[TAPS - 1 - tap if flipped else tap])
        for p, factors in enumerate(tap_factors()):
            taps[p * K + b] = mix([scale * factor for factor in factors], column_taps)


def four_rows(raised, taps, g, columns):
    m = []
    for p in range(POINTS):
        values = {c: raised[g, p, c] for c in range(columns[0], columns[-1] + K)}
        row = []
        for c in columns:
            row.append(mix([1.0] * K, [values[c + b] * taps[p * K + b] for b in range(K)]))
        m.append(row)
    return [lower([m[p][i] for p in range(POINTS)]) for i in range(len(columns))]


def spread_kernel(
    parts, count, side_ref, top_ref, low_ref, own_ref, high_ref, lower_ref, gain_ref, bias_ref, w_ref, *rest
):
    sums = rest[:parts]
    out_ref, edge_ref, hid_ref, sum_ref, pad, terms, rim_high, rim_low, raised, taps = rest[parts:]
    rows = own_ref.shape[0]
    _, _, scale, shift = norm_terms(total(sums), count, gain_ref[0:1], bias_ref[0:1])
    terms[0] = jnp.broadcast_to(0.5 * scale, (SUB, 128))
    terms[1] = jnp.broadcast_to(0.5 * shift, (SUB, 128))

    @pl.when(pl.program_id(0) == 0)
    def _():
        turn_rims((top_ref, low_ref), side_ref, rim_high, rim_low)

    def act(value):
        return swish_half(value * terms[0] + terms[1])

    def own_rows(i, _):
        for k in range(GROUP):
            for c in range(SUB):
                pad[GROUP * i + k + HALO_IN, c + 2] = act(own_ref[GROUP * i + k, c])
        return 0

    lax.fori_loop(0, rows // GROUP, own_rows, 0)
    for side, start, first in ((0, 0, HALO_IN - HALO_OUT), (1, rows + HALO_IN, 0)):

        @pl.when(side_ref[side] == 1)
        def _(side=side, start=start, first=first):
            halo = dot3((rim_high[side], rim_low[side]), (high_ref[...], lower_ref[...]))
            halo = halo.reshape(HALO_IN, SUB, SUB, 128)
            hid_ref[side] = halo[first : first + HALO_OUT]
            pad[start : start + HALO_IN, 2 : SUB + 2] = act(halo)
            edge_row = min(start, rows + 2)
            for r in range(HALO_OUT + K - 1):
                fill_sides(pad, edge_row + r)

        @pl.when(side_ref[side] == 0)
        def _(side=side, start=start):
            clear_rows(pad, start, HALO_IN)
            hid_ref[side] = jnp.zeros(hid_ref.shape[1:], F32)

    raise_taps(w_ref, taps)
    raise_all(pad, 2, raised)

    def group(g, carry):
        one, two = carry
        for columns in (range(0, SUB // 2), range(SUB // 2, SUB)):
            for c, values in zip(columns, four_rows(raised, taps, g, columns)):
                for o, value in enumerate(values):
                    out_ref[GROUP * g + o, c] = value
                    one = one + value
                    two = two + value * value
        return one, two

    zero = jnp.zeros((SUB, 128), F32)
    one, two = lax.fori_loop(0, rows // GROUP, group, (zero, zero))
    sum_ref[0:1] = jnp.sum(one, axis=0, keepdims=True)
    sum_ref[1:2] = jnp.sum(two, axis=0, keepdims=True)
    for side, start in ((0, 0), (1, rows + 2)):

        @pl.when(side_ref[side] == 1)
        def _(side=side, start=start):
            for c in range(SUB):
                acc = tap_rows(pad, w_ref, start, HALO_OUT, c)
                for o in range(HALO_OUT):
                    edge_ref[side, o, c] = acc[o]

        @pl.when(side_ref[side] == 0)
        def _(side=side):
            edge_ref[side] = jnp.zeros(edge_ref.shape[1:], F32)


def lanes(shape):
    lead = len(shape) - 1
    return pl.BlockSpec(tuple(shape[:-1]) + (128,), lambda e: (0,) * lead + (e,))


def spread(count, side, top, low, own, w_high, w_low, gains, biases, taps, sums):
    rows, hidden = own.shape[0], own.shape[-1]
    chan_all = w_high.shape[0]
    arrays = [own, w_high, w_low, gains, biases, taps, *sums]
    edge_shape = (2, HALO_OUT, SUB, SUB, hidden)
    rim_shape = (2, HALO_IN * FRAME_COLUMNS, chan_all)
    return pl.pallas_call(
        partial(spread_kernel, len(sums), count),
        grid=(hidden // 128,),
        in_specs=[pl.BlockSpec(memory_space=pltpu.SMEM), whole(top.shape), whole(low.shape)]
        + [lanes(a.shape) for a in arrays],
        out_specs=[
            lanes((rows, SUB, SUB, hidden)),
            lanes(edge_shape),
            lanes(edge_shape),
            lanes((2, hidden)),
        ],
        out_shape=[
            jax.ShapeDtypeStruct((rows, SUB, SUB, hidden), F32),
            jax.ShapeDtypeStruct(edge_shape, F32),
            jax.ShapeDtypeStruct(edge_shape, F32),
            jax.ShapeDtypeStruct((2, hidden), F32),
        ],
        scratch_shapes=[
            pltpu.VMEM((rows + 2 * HALO_IN, SUB + 4, SUB, 128), F32),
            pltpu.VMEM((2, SUB, 128), F32),
            pltpu.VMEM(rim_shape, BF16),
            pltpu.VMEM(rim_shape, BF16),
            pltpu.VMEM((rows // GROUP, POINTS, SUB + 4, SUB, 128), F32),
            pltpu.VMEM((POINTS * K, SUB, 128), F32),
        ],
        compiler_params=params(),
        cost_estimate=cost(10),
        name="spread",
    )(side, top, low, *arrays)


def as_row(columns):
    width = columns.shape[1]
    folded = columns[:, 0:128]
    for i in range(128, width, 128):
        folded = folded + columns[:, i : i + 128]
    return jnp.sum(folded.T, axis=0, keepdims=True)


def gather_kernel(parts, count, own_ref, gout_ref, gain_ref, bias_ref, wt_ref, high_ref, low_ref, *rest):
    sums, (m_ref, s_ref, se_ref, proj_ref) = rest[:parts], rest[parts:]
    t = pl.program_id(0)
    chan_all, hidden = wt_ref.shape

    @pl.when(t == 0)
    def _():
        m_ref[...] = jnp.zeros_like(m_ref)
        s_ref[...] = jnp.zeros_like(s_ref)

    _, _, scale, shift = norm_terms(total(sums), count, gain_ref[1:2], bias_ref[1:2])
    scale, shift = 0.5 * scale, 0.5 * shift
    gout = split(gout_ref[:, 0].reshape(chan_all, gout_ref.shape[3]))
    proj = None
    for cut in chunks(hidden):
        act = swish_half(own_ref[0, :, cut] * scale[:, cut] + shift[:, cut])
        s_ref[0:1, cut] += jnp.sum(act, axis=0, keepdims=True)
        act = split(act)
        m_ref[:, cut] += dot3(gout, act)
        term = dot3(act, (high_ref[cut], low_ref[cut]))
        proj = term if proj is None else proj + term
    proj_ref[0] = proj

    @pl.when(t == pl.num_programs(0) - 1)
    def _():
        wt = wt_ref[...]
        se_ref[0:1] = as_row(s_ref[...] * wt)
        se_ref[1:2] = as_row(m_ref[...] * wt)


def gather(count, own, gout, gains, biases, wt, w_high, w_low, sums):
    nz, bands, chans, area = gout.shape
    hidden = wt.shape[1]
    chan_all = nz * chans
    grid, tall, put, wide = by_steps(nz, bands, chans, area)
    return pl.pallas_call(
        partial(gather_kernel, len(sums), count),
        grid=grid,
        in_specs=[
            tall(hidden),
            wide,
            whole(gains.shape),
            whole(biases.shape),
            whole(wt.shape),
            whole(w_high.shape),
            whole(w_low.shape),
        ]
        + [whole(s.shape) for s in sums],
        out_specs=[
            whole((chan_all, hidden)),
            whole((1, hidden)),
            whole((2, chan_all)),
            put(chan_all),
        ],
        out_shape=[
            jax.ShapeDtypeStruct((chan_all, hidden), F32),
            jax.ShapeDtypeStruct((1, hidden), F32),
            jax.ShapeDtypeStruct((2, chan_all), F32),
            jax.ShapeDtypeStruct((bands, area, chan_all), F32),
        ],
        compiler_params=params(),
        cost_estimate=cost(13),
        name="gather",
    )(own, gout, gains, biases, wt, w_high, w_low, *sums)


def column(row):
    return jnp.broadcast_to(row, (SUB, row.shape[1])).T[:, 0:1]


def slope_terms(sums, count, gain_ref, bias_ref):
    _, _, scale, shift = norm_terms(sums, count, gain_ref[1:2], bias_ref[1:2])
    return 0.5 * scale, 0.5 * shift


def second_grad(gout, weights, k_row, value, terms, cut):
    h = value * terms[0][:, cut] + terms[1][:, cut]
    return (dot3(gout, (weights[0][:, cut], weights[1][:, cut])) + k_row[:, cut]) * slope_half(h), h


def proj_back_kernel(
    pairs,
    parts,
    count,
    own_ref,
    gout_ref,
    proj_ref,
    x_ref,
    gain_ref,
    bias_ref,
    wt_ref,
    m_ref,
    s_ref,
    sqt_ref,
    down_ref,
    ex_ref,
    exb_ref,
    *rest,
):
    ses, sums = rest[:pairs], rest[pairs : pairs + parts]
    q_ref, sum_ref, val_ref, col_ref, w_high, w_low, k_row, out_ref, grad_ref = rest[pairs + parts :]
    chan_all, hidden = wt_ref.shape

    @pl.when(pl.program_id(0) == 0)
    def _():
        se = total(ses)
        pooled = se[0:1] / (FRAME_ROWS * FRAME_COLUMNS)
        sqt, ex = sqt_ref[...], ex_ref[...]
        pre = jnp.sum(sqt * pooled, axis=1, keepdims=True) + down_ref[...]
        gate = sigmoid(pre)
        squeezed = pre * gate
        excite = sigmoid(jnp.sum(ex * squeezed, axis=0, keepdims=True) + exb_ref[...])
        logit = se[1:2] * excite * (1.0 - excite)
        slope = gate * (1.0 + pre * (1.0 - gate))
        grad_sq = jnp.sum(ex * logit, axis=1, keepdims=True) * slope
        pool_grad = jnp.sum(sqt * grad_sq, axis=0, keepdims=True) / (FRAME_ROWS * FRAME_COLUMNS)
        val_ref[...] = jnp.zeros_like(val_ref)
        val_ref[0:1] = excite
        val_ref[1:2] = pool_grad
        val_ref[2:3] = logit
        val_ref[3:4] = pooled
        lane = lax.broadcasted_iota(jnp.int32, col_ref.shape, 1)
        col_ref[...] = jnp.where(lane == 0, squeezed, jnp.where(lane == 1, grad_sq, 0.0))
        wt = 0.5 * wt_ref[...]
        tall_excite, tall_pool = column(excite), column(pool_grad)
        w_high[...], w_low[...] = split(wt * tall_excite)
        k_row[...] = jnp.sum(wt * tall_pool, axis=0, keepdims=True)
        grad_ref[...] = tall_excite * m_ref[...] + tall_pool * s_ref[...]
        sum_ref[...] = jnp.zeros_like(sum_ref)

    terms = slope_terms(total(sums), count, gain_ref, bias_ref)
    gout = split(gout_ref[:, 0].reshape(chan_all, gout_ref.shape[3]).T)
    for cut in chunks(hidden):
        q, h = second_grad(gout, (w_high, w_low), k_row, own_ref[0, :, cut], terms, cut)
        q_ref[0, :, cut] = q
        sum_ref[0:1, cut] += jnp.sum(q, axis=0, keepdims=True)
        sum_ref[1:2, cut] += jnp.sum(q * h, axis=0, keepdims=True)

    nz, _, chans, area = x_ref.shape
    out_ref[:, 0] = x_ref[:, 0] + (proj_ref[0] * val_ref[0:1]).T.reshape(nz, chans, area)

    @pl.when(pl.program_id(0) == pl.num_programs(0) - 1)
    def _():
        sum_ref[1:2] = (2.0 * sum_ref[1:2] - bias_ref[1:2] * sum_ref[0:1]) / gain_ref[1:2]


def proj_back(count, own, gout, proj, x, gains, biases, wt, m, s, se_weights, ses, sums):
    nz, bands, chans, area = gout.shape
    hidden = wt.shape[1]
    chan_all = nz * chans
    reduced = se_weights[0].shape[0]
    fixed = [gains, biases, wt, m, s, *se_weights, *ses, *sums]
    grid, tall, put, wide = by_steps(nz, bands, chans, area)
    return pl.pallas_call(
        partial(proj_back_kernel, len(ses), len(sums), count),
        grid=grid,
        in_specs=[
            tall(hidden),
            wide,
            tall(chan_all),
            wide,
        ]
        + [whole(a.shape) for a in fixed],
        out_specs=[
            put(hidden),
            whole((2, hidden)),
            whole((SUB, chan_all)),
            whole((reduced, 128)),
            whole(wt.shape),
            whole(wt.shape),
            whole((1, hidden)),
            wide,
            whole(m.shape),
        ],
        out_shape=[
            jax.ShapeDtypeStruct((bands, area, hidden), F32),
            jax.ShapeDtypeStruct((2, hidden), F32),
            jax.ShapeDtypeStruct((SUB, chan_all), F32),
            jax.ShapeDtypeStruct((reduced, 128), F32),
            jax.ShapeDtypeStruct(wt.shape, BF16),
            jax.ShapeDtypeStruct(wt.shape, BF16),
            jax.ShapeDtypeStruct((1, hidden), F32),
            jax.ShapeDtypeStruct(x.shape, F32),
            jax.ShapeDtypeStruct(m.shape, F32),
        ],
        compiler_params=params(),
        cost_estimate=cost(12),
        name="proj_back",
    )(own, gout, proj, x, *fixed)


def spread_back_kernel(
    parts,
    count,
    side_ref,
    top_ref,
    low_ref,
    hid_ref,
    hid_halo_ref,
    own_ref,
    halo_ref,
    q_ref,
    high_ref,
    lower_ref,
    k_ref,
    gain_ref,
    bias_ref,
    w_ref,
    *rest,
):
    sums_one, sums_two, backs = (rest[i * parts : (i + 1) * parts] for i in range(3))
    out_ref, sum_ref, tap_ref, pad, grad, terms, rim_high, rim_low, raised, points, taps = rest[3 * parts :]
    rows = own_ref.shape[0]

    @pl.when(pl.program_id(0) == 0)
    def _():
        turn_rims((top_ref, low_ref), side_ref, rim_high, rim_low)

    _, _, scale, shift = norm_terms(total(sums_one), count, gain_ref[0:1], bias_ref[0:1])
    a, b, c0 = back_terms(total(sums_two), total(backs), count, gain_ref[1:2])
    for i, row in enumerate((0.5 * scale, 0.5 * shift, a, b, c0)):
        terms[i] = jnp.broadcast_to(row, (SUB, 128))

    def act(value):
        return swish_half(value * terms[0] + terms[1])

    def grad_in(q, value):
        return q * terms[2] + (value * terms[3] + terms[4])

    def own_rows(i, _):
        for k in range(GROUP):
            r = GROUP * i + k
            for c in range(SUB):
                pad[r + HALO_OUT, c + 2] = act(hid_ref[r, c])
                grad[r + HALO_OUT, c + 2] = grad_in(q_ref[r, c], own_ref[r, c])
        return 0

    lax.fori_loop(0, rows // GROUP, own_rows, 0)
    slope = slope_terms(total(sums_two), count, gain_ref, bias_ref)
    for side, start in ((0, 0), (1, rows + HALO_OUT)):

        @pl.when(side_ref[side] == 1)
        def _(side=side, start=start):
            value = halo_ref[side].reshape(HALO_OUT * FRAME_COLUMNS, 128)
            weights = (high_ref, lower_ref)
            gout = (rim_high[side], rim_low[side])
            q, _ = second_grad(gout, weights, k_ref, value, slope, slice(0, 128))
            edge = grad_in(q.reshape(HALO_OUT, SUB, SUB, 128), halo_ref[side])
            grad[start : start + HALO_OUT, 2 : SUB + 2] = edge
            pad[start : start + HALO_OUT, 2 : SUB + 2] = act(hid_halo_ref[side])

        @pl.when(side_ref[side] == 0)
        def _(start=start):
            clear_rows(pad, start, HALO_OUT)
            clear_rows(grad, start, HALO_OUT)

    raise_all(pad, 0, raised)

    def point_groups(i, _):
        for g in (2 * i, 2 * i + 1):
            for c in range(SUB):
                mine = [grad[GROUP * g + HALO_OUT + k, c + 2] for k in range(GROUP)]
                for p, value in enumerate(spread_points(mine)):
                    points[g, p, c] = value
        return 0

    lax.fori_loop(0, rows // GROUP // 2, point_groups, 0)
    zero = jnp.zeros((SUB, 128), F32)
    factors = tap_factors()
    tap_sums = [None] * TAPS
    for p in range(0, POINTS, 2):

        def weight_groups(i, acc, p=p):
            acc = list(acc)
            for g in (2 * i, 2 * i + 1):
                for k in range(2):
                    values = [raised[g, p + k, c] for c in range(SUB + K - 1)]
                    for c in range(SUB):
                        mine = points[g, p + k, c]
                        for b in range(K):
                            at = (k * 2 + c % 2) * K + b
                            acc[at] = acc[at] + values[c + b] * mine
            return tuple(acc)

        acc = lax.fori_loop(0, rows // GROUP // 2, weight_groups, (zero,) * (4 * K))
        for k in range(2):
            for b in range(K):
                value = jnp.sum(acc[2 * k * K + b] + acc[(2 * k + 1) * K + b], axis=0, keepdims=True)
                for a in range(K):
                    if factors[p + k][a] != 0.0:
                        term = value * factors[p + k][a]
                        old = tap_sums[a * K + b]
                        tap_sums[a * K + b] = term if old is None else old + term
    for tap in range(TAPS):
        tap_ref[tap : tap + 1] = tap_sums[tap]

    raise_taps(w_ref, taps, flipped=True, scale=0.5)
    raise_all(grad, 0, raised)

    def group(g, carry):
        one, two = carry
        for columns in (range(0, SUB // 2), range(SUB // 2, SUB)):
            for c, values in zip(columns, four_rows(raised, taps, g, columns)):
                for o, value in enumerate(values):
                    h = hid_ref[GROUP * g + o, c] * terms[0] + terms[1]
                    value = value * slope_half(h)
                    out_ref[GROUP * g + o, c] = value
                    one = one + value
                    two = two + value * h
        return one, two

    one, two = lax.fori_loop(0, rows // GROUP, group, (zero, zero))
    one, two = jnp.sum(one, axis=0, keepdims=True), jnp.sum(two, axis=0, keepdims=True)
    sum_ref[0:1] = one
    sum_ref[1:2] = (2.0 * two - bias_ref[0:1] * one) / gain_ref[0:1]


def spread_back(
    count, side, top, low, hid, hid_halo, own, halo, q, weights, gains, biases, taps, sums_one, sums_two, backs
):
    rows, hidden = own.shape[0], own.shape[-1]
    arrays = [hid, hid_halo, own, halo, q, *weights, gains, biases, taps, *sums_one, *sums_two, *backs]
    rim_shape = (2, HALO_OUT * FRAME_COLUMNS, weights[0].shape[0])
    return pl.pallas_call(
        partial(spread_back_kernel, len(backs), count),
        grid=(hidden // 128,),
        in_specs=[pl.BlockSpec(memory_space=pltpu.SMEM), whole(top.shape), whole(low.shape)]
        + [lanes(a.shape) for a in arrays],
        out_specs=[lanes((rows, SUB, SUB, hidden)), lanes((2, hidden)), lanes((TAPS, hidden))],
        out_shape=[
            jax.ShapeDtypeStruct((rows, SUB, SUB, hidden), F32),
            jax.ShapeDtypeStruct((2, hidden), F32),
            jax.ShapeDtypeStruct((TAPS, hidden), F32),
        ],
        scratch_shapes=[
            pltpu.VMEM((rows + 2 * HALO_OUT, SUB + 4, SUB, 128), F32),
            pltpu.VMEM((rows + 2 * HALO_OUT, SUB + 4, SUB, 128), F32),
            pltpu.VMEM((5, SUB, 128), F32),
            pltpu.VMEM(rim_shape, BF16),
            pltpu.VMEM(rim_shape, BF16),
            pltpu.VMEM((rows // GROUP, POINTS, SUB + 4, SUB, 128), F32),
            pltpu.VMEM((rows // GROUP, POINTS, SUB, SUB, 128), F32),
            pltpu.VMEM((POINTS * K, SUB, 128), F32),
        ],
        compiler_params=params(),
        cost_estimate=cost(150),
        name="spread_back",
    )(side, top, low, *arrays)


def expand_grad(q_ref, hid_ref, terms, cut):
    a, b, c = terms
    return split(q_ref[0, :, cut] * a[:, cut] + (hid_ref[0, :, cut] * b[:, cut] + c[:, cut]))


def input_kernel(parts, count, start, q_ref, hid_ref, gout_ref, gain_ref, w_high, w_low, *rest):
    sums, backs, out_ref = rest[:parts], rest[parts : 2 * parts], rest[2 * parts]
    nz, _, chans, area = out_ref.shape
    terms = back_terms(total(sums), total(backs), count, gain_ref[0:1])
    out = None
    for cut in chunks(w_high.shape[0]):
        term = dot3(expand_grad(q_ref, hid_ref, terms, cut), (w_high[cut], w_low[cut]))
        out = term if out is None else out + term
    own = gout_ref[:, 0]
    if own.shape[2] > area:
        own = own[:, :, start : start + area]
    out_ref[:, 0] = own + out.T.reshape(nz, chans, area)


def input_grad(count, start, width, q, hid, gout, gains, w_high, w_low, sums, backs):
    nz, bands, chans, area = gout.shape
    hidden = w_high.shape[0]
    at = start // width
    fixed = [gains, w_high, w_low, *sums, *backs]
    if width % 128 == 0:
        gout_spec = pl.BlockSpec((nz, 1, chans, width), lambda t: (0, t, 0, at))
    else:
        gout_spec = pl.BlockSpec((nz, 1, chans, area), lambda t: (0, t, 0, 0))
    return pl.pallas_call(
        partial(input_kernel, len(sums), count, start),
        grid=(bands,),
        in_specs=[
            pl.BlockSpec((1, width, hidden), lambda t: (t, at, 0)),
            pl.BlockSpec((1, width, hidden), lambda t: (t, at, 0)),
            gout_spec,
        ]
        + [whole(v.shape) for v in fixed],
        out_specs=pl.BlockSpec((nz, 1, chans, width), lambda t: (0, t, 0, 0)),
        out_shape=jax.ShapeDtypeStruct((nz, bands, chans, width), F32),
        compiler_params=params(),
        cost_estimate=cost(12),
        name="input_grad",
    )(q, hid, gout, *fixed)


def weight_kernel(chans, ids_ref, q_ref, x_ref, tap_ref, one_ref, two_ref, val_ref, col_ref, *rest):
    outs, acc, small = rest[:-2], rest[-2], rest[-1]
    nz, _, _, area = x_ref.shape
    chan_all, hidden = acc.shape
    width = hidden // nz
    t = pl.program_id(0)

    @pl.when(t == 0)
    def _():
        acc[...] = jnp.zeros_like(acc)
        small[...] = jnp.zeros_like(small)
        small[0:TAPS] = tap_ref[...]
        small[TAPS : TAPS + 1] = one_ref[1:2]
        small[TAPS + 1 : TAPS + 2] = two_ref[1:2]
        small[TAPS + 2 : TAPS + 3] = one_ref[0:1]
        small[TAPS + 3 : TAPS + 4] = two_ref[0:1]
        lead = (ids_ref[1] == 0).astype(F32)
        logit, pooled = val_ref[2:3] * lead, val_ref[3:4]
        reduced = col_ref.shape[0]
        grad_sq = col_ref[:, 1:2] * lead
        g_sq = grad_sq * pooled
        g_ex = col_ref[:, 0:1] * logit
        grad_row = jnp.broadcast_to(grad_sq, (reduced, 128)).T[0:1]
        for z in range(nz):
            own, at = slice(z * chans, (z + 1) * chans), z * width
            small[32 : 32 + reduced, at : at + chans] = g_sq[:, own]
            small[32 : 32 + reduced, at + chans : at + 2 * chans] = g_ex[:, own]
            small[32:33, at + 2 * chans : at + 3 * chans] = logit[:, own]
            small[33:34, at + 2 * chans : at + 2 * chans + reduced] = grad_row

    x = split(x_ref[:, 0].reshape(chan_all, area))
    for cut in chunks(hidden):
        acc[:, cut] += dot3(x, split(q_ref[0, :, cut]))

    @pl.when(t == pl.num_programs(0) - 1)
    def _():
        n = sum(out.shape[0] for out in outs)
        r, m = chan_all // n, SMALL // n
        for core, out in enumerate(outs):
            for i in range(out.shape[0]):
                p = ids_ref[0] ^ (i * len(outs) + core)
                out[i, 0:r] = acc[pl.ds(pl.multiple_of(p * r, r), r), :]
                out[i, r : r + m] = small[pl.ds(pl.multiple_of(p * m, m), m), :]


def weight_grad(ids, shape, q, x, taps, one, two, values, columns):
    nz, bands, chans, area = x.shape
    hidden = q.shape[2]
    chan_all = nz * chans
    fixed = [taps, one, two, values, columns]
    pieces, chips = shape
    shape = (chips, (chan_all + SMALL) // (pieces * chips), hidden)
    grid, tall, put, wide = by_steps(nz, bands, chans, area)
    return pl.pallas_call(
        partial(weight_kernel, chans),
        grid=grid,
        in_specs=[
            pl.BlockSpec(memory_space=pltpu.SMEM),
            tall(hidden),
            wide,
        ]
        + [whole(v.shape) for v in fixed],
        out_specs=[whole(shape)] * pieces,
        out_shape=[jax.ShapeDtypeStruct(shape, F32)] * pieces,
        scratch_shapes=[pltpu.VMEM((chan_all, hidden), F32), pltpu.VMEM((SMALL, hidden), F32)],
        compiler_params=params(),
        cost_estimate=cost(7),
        name="weight_grad",
    )(ids, q, x, *fixed)


def merge_kernel(one_ref, two_ref, *outs):
    for i, out in enumerate(outs):
        out[...] = one_ref[i] + two_ref[i]


def merge(one, two):
    n = one.shape[0]
    return pl.pallas_call(
        merge_kernel,
        grid=(1,),
        in_specs=[whole(one.shape), whole(two.shape)],
        out_specs=[whole(one.shape[1:])] * n,
        out_shape=[jax.ShapeDtypeStruct(one.shape[1:], F32)] * n,
        compiler_params=params(),
        cost_estimate=cost(2),
        name="merge",
    )(one, two)


def collect_kernel(n, nz, parts, count, ids_ref, early_ref, gram_ref, high_ref, low_ref, gain_ref, *rest):
    pieces, sums, backs = rest[:n], rest[n : n + parts], rest[n + parts : n + 2 * parts]
    outs, acc = rest[n + 2 * parts : -1], rest[-1]
    value = total(pieces)
    rows, width = value.shape[0], acc.shape[2]
    r, chan_all = early_ref.shape[0], high_ref.shape[0]
    a, b, c = back_terms(total(sums), total(backs), count, gain_ref[0:1])
    gram = gram_ref[...]
    hid = dot3(split(gram[:, 0:chan_all]), (high_ref[...], low_ref[...]))
    grad = a * value[0:r] + (b * hid + c * gram[:, chan_all : chan_all + 1])
    for z in range(nz):
        here = slice(z * width, (z + 1) * width)
        acc[z, 0:r] = grad[:, here]
        acc[z, r:rows] = value[r:, here]
        acc[z, rows:] = early_ref[:, here]
    for k, out in enumerate(outs):
        out[...] = acc[ids_ref[2] ^ k]


def collect(count, ids, nz, pieces, early, gram, w_high, w_low, gains, sums, backs):
    width = early.shape[1] // nz
    rows = pieces[0].shape[0] + early.shape[0]
    arrays = [early, gram, w_high, w_low, gains, *pieces, *sums, *backs]
    return pl.pallas_call(
        partial(collect_kernel, len(pieces), nz, len(sums), count),
        grid=(1,),
        in_specs=[pl.BlockSpec(memory_space=pltpu.SMEM)] + [whole(a.shape) for a in arrays],
        out_specs=[whole((rows, width))] * nz,
        out_shape=[jax.ShapeDtypeStruct((rows, width), F32)] * nz,
        scratch_shapes=[pltpu.VMEM((nz, rows, width), F32)],
        compiler_params=params(),
        cost_estimate=cost(3),
        name="collect",
    )(ids, *arrays)


def segments(chan_in, hidden_dev, chan_dev, reduced, tap_count, hidden_all):
    seg_sizes = [
        chan_in * hidden_dev,
        tap_count * hidden_dev,
        2 * hidden_dev,
        2 * hidden_dev,
        hidden_dev * chan_in,
        chan_dev * reduced,
        reduced,
        reduced * chan_dev,
        chan_dev,
    ]
    seg_rates = [
        0.5 / math.sqrt(chan_in),
        0.5 / math.sqrt(tap_count),
        0.3,
        0.3,
        0.5 * math.sqrt(8.0 / hidden_all),
        2.0 / math.sqrt(chan_in),
        0.3,
        1.0 / math.sqrt(reduced),
        0.3,
    ]
    return (seg_sizes, seg_rates)


def pack_kernel(at_ref, we_ref, wp_ref, dw_ref, gain_ref, bias_ref, sq_ref, ex_ref, exb_ref, out_ref, small):
    p = at_ref[0]
    chan_in, width = we_ref.shape
    reduced, chans = sq_ref.shape
    m = small.shape[0] * out_ref.shape[0] // (2 * chan_in + small.shape[0])
    r = (out_ref.shape[0] - m) // 2
    small[...] = jnp.zeros_like(small)
    small[0:TAPS] = dw_ref[...]
    small[TAPS : TAPS + 2] = gain_ref[...]
    small[TAPS + 2 : TAPS + 4] = bias_ref[...]
    small[32 : 32 + reduced, 0:chans] = sq_ref[...]
    small[32 : 32 + reduced, chans : 2 * chans] = ex_ref[...]
    small[32:33, 2 * chans : 3 * chans] = exb_ref[...]
    out_ref[0:r] = we_ref[pl.ds(pl.multiple_of(p * r, r), r), :]
    if chan_in == width:
        out_ref[r : 2 * r] = wp_ref[pl.ds(pl.multiple_of(p * r, r), r), :]
    else:
        row, part = p * r % width, p * r // width
        out_ref[r : 2 * r] = wp_ref[
            pl.ds(pl.multiple_of(row, r), r), pl.ds(pl.multiple_of(part * width, 128), width)
        ]
    out_ref[2 * r : 2 * r + m] = small[pl.ds(pl.multiple_of(p * m, m), m), :]


def pack_weights(at, w_expand, w_dw, norm_gains, norm_biases, w_project, squeeze_matrix, excite_matrix, excite_bias_row):
    n_pix = lax.axis_size(PIX)
    chan_in, width = w_expand.shape
    arrays = [
        w_expand,
        w_project,
        w_dw,
        norm_gains,
        norm_biases,
        squeeze_matrix.T,
        excite_matrix,
        excite_bias_row[None],
    ]
    shape = ((2 * chan_in + SMALL) // n_pix, width)
    return pl.pallas_call(
        pack_kernel,
        grid=(1,),
        in_specs=[pl.BlockSpec(memory_space=pltpu.SMEM)] + [whole(a.shape) for a in arrays],
        out_specs=whole(shape),
        out_shape=jax.ShapeDtypeStruct(shape, F32),
        scratch_shapes=[pltpu.VMEM((SMALL, width), F32)],
        compiler_params=params(),
        cost_estimate=cost(2),
        name="pack_weights",
    )(at, *arrays)


def weights_kernel(
    chan_in,
    chans,
    orders,
    base_ref,
    *refs,
):
    slabs = refs[: len(orders)]
    (
        we_high,
        we_low,
        wet_high,
        wet_low,
        wp_high,
        wp_low,
        wpt_ref,
        tap_ref,
        gain_ref,
        bias_ref,
        sqt_ref,
        ex_ref,
        exb_ref,
        first,
        second,
        small,
    ) = refs[len(orders) :]
    nz, width = first.shape[0], first.shape[2]
    n_pix = sum(len(order) for order in orders)
    r, m = chan_in // n_pix, SMALL // n_pix
    reduced = ex_ref.shape[0]
    for ref, order in zip(slabs, orders):
        for i, p in enumerate(order):
            at = base_ref[0] ^ p
            wide = pl.ds(pl.multiple_of(at * r, r), r)
            for z in range(nz):
                here = slice(z * width, (z + 1) * width)
                group = base_ref[1] ^ z
                first[group, wide, :] = ref[i, 0:r, here]
                second[group, wide, :] = ref[i, r : 2 * r, here]
                small[group, pl.ds(pl.multiple_of(at * m, m), m), :] = ref[i, 2 * r : 2 * r + m, here]
    parts = chan_in // width
    for z in range(nz):
        here = slice(z * width, (z + 1) * width)
        own = slice(z * chans, (z + 1) * chans)
        we = first[z]
        we_high[:, here], we_low[:, here] = split(we)
        wet_high[here], wet_low[here] = split(we.T)
        for h in range(parts):
            wp = second[z, h * width : (h + 1) * width]
            cols = slice(h * width, (h + 1) * width)
            wp_high[here, cols], wp_low[here, cols] = split(wp)
            wpt_ref[cols, here] = wp.T
        for tap in range(TAPS):
            tap_ref[tap, :, here] = jnp.broadcast_to(small[z, tap : tap + 1], (SUB, width))
        gain_ref[:, here] = small[z, TAPS : TAPS + 2]
        bias_ref[:, here] = small[z, TAPS + 2 : TAPS + 4]
        sqt_ref[:, own] = small[z, 32 : 32 + reduced, 0:chans]
        ex_ref[:, own] = small[z, 32 : 32 + reduced, chans : 2 * chans]
        exb_ref[:, own] = small[z, 32:33, 2 * chans : 3 * chans]


def order_weights(base, slabs, orders, nz, chan_in, chans, reduced):
    hidden = slabs[0].shape[2]
    width = hidden // nz
    shapes = (
        [((chan_in, hidden), BF16)] * 2
        + [((hidden, chan_in), BF16)] * 4
        + [
            ((chan_in, hidden), F32),
            ((TAPS, SUB, hidden), F32),
            ((2, hidden), F32),
            ((2, hidden), F32),
            ((reduced, chan_in), F32),
            ((reduced, chan_in), F32),
            ((1, chan_in), F32),
        ]
    )
    return pl.pallas_call(
        partial(weights_kernel, chan_in, chans, orders),
        grid=(1,),
        in_specs=[pl.BlockSpec(memory_space=pltpu.SMEM)] + [whole(a.shape) for a in slabs],
        out_specs=[whole(shape) for shape, _ in shapes],
        out_shape=[jax.ShapeDtypeStruct(shape, kind) for shape, kind in shapes],
        scratch_shapes=[
            pltpu.VMEM((nz, chan_in, width), F32),
            pltpu.VMEM((nz, chan_in, width), F32),
            pltpu.VMEM((nz, SMALL, width), F32),
        ],
        compiler_params=params(),
        cost_estimate=cost(3),
        name="order_weights",
    )(base, *slabs)


def thirds(v):
    high = v.astype(BF16)
    rest = v - high.astype(F32)
    mid = rest.astype(BF16)
    return high, mid, (rest - mid.astype(F32)).astype(BF16)


def choose(chosen, v):
    high, mid, low = thirds(v)
    return (dot(chosen, high) + dot(chosen, mid)) + dot(chosen, low)


def choose_lanes(v, chosen):
    high, mid, low = thirds(v)
    return (dot(high, chosen) + dot(mid, chosen)) + dot(low, chosen)


def ones(condition):
    return condition.astype(F32).astype(BF16)


def lay_flat(v, start, width):
    n, m = v.shape
    place = lax.broadcasted_iota(jnp.int32, (m, width), 1) - start
    column_of = lax.broadcasted_iota(jnp.int32, (m, width), 0)
    wide = choose_lanes(v, ones((place + 64 * m) % m == column_of))
    place = lax.broadcasted_iota(jnp.int32, (n, width), 1) - start
    low = lax.broadcasted_iota(jnp.int32, (n, width), 0) * m
    return jnp.sum(jnp.where((place >= low) & (place < low + m), wide, 0.0), axis=0, keepdims=True)


def fill_blocks(out, first, middle, flip, last, squeeze, down, excite, bias):
    blocks, length = out.shape
    tiles, n, _ = first.shape
    width = tiles * 128
    per = length // width
    for i in range(per):
        for u in range(tiles):
            at = i * width + u * 128
            out[0 : n // per, at : at + 128] = first[u, pl.ds(i, n // per, stride=per), :]
    for k in range(TAPS + 4):
        row = n + k
        out[row // per : row // per + 1, row % per * width : (row % per + 1) * width] = middle[k : k + 1, :]
    base = n + TAPS + 4
    parts = last // width
    step = per // parts
    for h in range(parts):
        for e in range(step):
            row = base + parts * e + h
            block, slot = row // per, row % per
            count = width // step
            for u in range(tiles):
                at = slot * width + u * 128
                out[block : block + count, at : at + 128] = flip[
                    h * tiles + u, pl.ds(e, count, stride=step), :
                ]
    start = (base + width * parts) * width
    block = start // length
    start -= block * length
    tail_width = (blocks - block) * length
    tail = lay_flat(squeeze, start, tail_width)
    start += squeeze.shape[0] * squeeze.shape[1]
    tail = tail + lay_flat(down, start, tail_width)
    start += down.shape[1]
    tail = tail + lay_flat(excite, start, tail_width)
    start += excite.shape[0] * excite.shape[1]
    tail = tail + lay_flat(bias, start, tail_width)
    inside = lax.broadcasted_iota(jnp.int32, (1, length), 1)
    kept = jnp.where(inside < (base + width * parts) * width - block * length, out[block : block + 1, :], 0.0)
    out[block : block + 1, :] = kept + tail[:, 0:length]
    for k in range(1, blocks - block):
        out[block + k : block + k + 1, :] = tail[:, k * length : (k + 1) * length]


def prepare_kernel(
    orders,
    base_ref,
    col_ref,
    we_ref,
    dw_ref,
    gain_ref,
    bias_ref,
    wp_ref,
    sq_ref,
    down_ref,
    ex_ref,
    exb_ref,
    *rest,
):
    slabs = rest[: len(orders)]
    weight, first_ref, second_ref, head, flip, middle, moments, ranked = rest[len(orders) :]
    blocks, length = weight.shape
    chan_in, width = we_ref.shape
    devices, room = moments.shape[1:3]
    middle[0:TAPS] = dw_ref[...]
    middle[TAPS : TAPS + 2] = gain_ref[...]
    middle[TAPS + 2 : TAPS + 4] = bias_ref[...]
    for u in range(width // 128):
        head[u] = we_ref[:, u * 128 : (u + 1) * 128]
    for u in range(chan_in // 128):
        flip[u] = wp_ref[:, u * 128 : (u + 1) * 128]
    fill_blocks(
        weight, head, middle, flip, chan_in, sq_ref[...].T, down_ref[...], ex_ref[...], exb_ref[...]
    )
    at = 0
    home = jnp.zeros(col_ref.shape, jnp.int32)
    own_col = col_ref[...]
    for ref, order in zip(slabs, orders):
        for k, p in enumerate(order):
            for m in range(2):
                moments[m, at] = ref[k, m * room : (m + 1) * room]
            home = jnp.where(own_col == base_ref[0] ^ p, at, home)
            at += 1
    ranked[...] = jnp.broadcast_to(own_col.astype(F32), ranked.shape)
    own_row = ranked[...].T[0:1].astype(jnp.int32)
    i = lax.broadcasted_iota(jnp.int32, (blocks, blocks), 0)
    j = lax.broadcasted_iota(jnp.int32, (blocks, blocks), 1)
    earlier = (own_row == own_col) & (j < i)
    rank = jnp.sum(jnp.where(earlier, 1.0, 0.0), axis=1, keepdims=True).astype(jnp.int32)
    slot = home * room + rank
    chosen = ones(lax.broadcasted_iota(jnp.int32, (blocks, devices * room), 1) == slot)
    first_ref[...] = choose(chosen, moments[0].reshape(devices * room, length))
    second_ref[...] = choose(chosen, moments[1].reshape(devices * room, length))


def prepare(base, owners, weights, slabs, orders, length):
    blocks = owners.shape[0]
    chan_in, width = weights[0].shape
    devices = sum(len(o) for o in orders)
    arrays = [owners, *weights, *slabs]
    return pl.pallas_call(
        partial(prepare_kernel, orders),
        grid=(1,),
        in_specs=[pl.BlockSpec(memory_space=pltpu.SMEM)] + [whole(a.shape) for a in arrays],
        out_specs=[whole((blocks, length))] * 3,
        out_shape=[jax.ShapeDtypeStruct((blocks, length), F32)] * 3,
        scratch_shapes=[
            pltpu.VMEM((width // 128, chan_in, 128), F32),
            pltpu.VMEM((chan_in // 128, width, 128), F32),
            pltpu.VMEM((32, width), F32),
            pltpu.VMEM((2, devices, slabs[0].shape[1] // 2, length), F32),
            pltpu.VMEM((blocks, 128), F32),
        ],
        compiler_params=params(),
        cost_estimate=cost(1),
        name="prepare",
    )(base, *arrays)


def adam_kernel(
    bounds,
    rates,
    orders,
    chans,
    reduced,
    me_ref,
    col_ref,
    weight_ref,
    old_one_ref,
    old_two_ref,
    first_ref,
    second_ref,
    *rest,
):
    grad_slabs = rest[: len(orders)]
    first_out, second_out, new_ref, grad, head, flip, tall, small, ranked = rest[len(orders) :]
    blocks, length = grad.shape
    capacity = first_ref.shape[0]
    chan_in, width = tall.shape
    devices = sum(len(order) for order in orders)
    r, m = chan_in // devices, SMALL // devices
    for ref, order in zip(grad_slabs, orders):
        for k, i in enumerate(order):
            p = me_ref[1] ^ i
            for u in range(width // 128):
                head[u, pl.ds(pl.multiple_of(p * r, r), r), :] = ref[k, 0:r, u * 128 : (u + 1) * 128]
            small[pl.ds(pl.multiple_of(p * m, m), m), :] = ref[k, r : r + m]
            tall[pl.ds(pl.multiple_of(p * r, r), r), :] = ref[k, r + m : 2 * r + m]
    for u in range(chan_in // 128):
        flip[u] = tall[u * 128 : (u + 1) * 128].T
    fill_blocks(
        grad,
        head,
        small,
        flip,
        chan_in,
        small[32 : 32 + reduced, 0:chans].T,
        small[33:34, 2 * chans : 2 * chans + reduced],
        small[32 : 32 + reduced, chans : 2 * chans],
        small[32:33, 2 * chans : 3 * chans],
    )

    own_col = col_ref[...]
    ranked[...] = jnp.broadcast_to(own_col.astype(F32), ranked.shape)
    own_row = ranked[...].T[0:1].astype(jnp.int32)
    i = lax.broadcasted_iota(jnp.int32, (blocks, blocks), 0)
    j = lax.broadcasted_iota(jnp.int32, (blocks, blocks), 1)
    earlier = (own_row == own_col) & (i < j)
    rank = jnp.sum(jnp.where(earlier, 1.0, 0.0), axis=0, keepdims=True).astype(jnp.int32)
    g = grad[...]
    mine = lax.broadcasted_iota(jnp.int32, (capacity, blocks), 0)
    owned = choose(ones((mine == rank) & (own_row == me_ref[0])), g)
    first_out[:, 0] = beta_first * first_ref[:, 0] + (1.0 - beta_first) * owned
    second_out[:, 0] = beta_second * second_ref[:, 0] + (1.0 - beta_second) * owned * owned

    first = beta_first * old_one_ref[...] + (1.0 - beta_first) * g
    second = beta_second * old_two_ref[...] + (1.0 - beta_second) * g * g
    first_hat = first / (1.0 - beta_first**STEP)
    second_hat = second / (1.0 - beta_second**STEP)
    place = lax.broadcasted_iota(jnp.int32, (blocks, length), 0) * length + lax.broadcasted_iota(
        jnp.int32, (blocks, length), 1
    )
    rate = jnp.zeros((blocks, length), F32)
    for bound, value in zip(reversed(bounds), reversed(rates)):
        rate = jnp.where(place < bound, jnp.float32(value), rate)
    grad[...] = weight_ref[...] * (1.0 - rate * weight_decay) - rate * first_hat / (
        jnp.sqrt(second_hat) + adam_eps
    )
    for k in range(blocks):
        end = min((k + 1) * length, new_ref.shape[1])
        new_ref[:, k * length : end] = grad[k : k + 1, 0 : end - k * length]


def adam(ids, owners, prepared, first, second, grads, orders, chan_in, chans, reduced, bounds, rates):
    blocks, length = prepared[0].shape
    width = grads[0].shape[2]
    arrays = [owners, *prepared, first, second, *grads]
    new_shape = (1, bounds[-1])
    return pl.pallas_call(
        partial(adam_kernel, bounds, rates, orders, chans, reduced),
        grid=(1,),
        in_specs=[pl.BlockSpec(memory_space=pltpu.SMEM)] + [whole(a.shape) for a in arrays],
        out_specs=[whole(first.shape), whole(second.shape), whole(new_shape)],
        out_shape=[
            jax.ShapeDtypeStruct(first.shape, F32),
            jax.ShapeDtypeStruct(second.shape, F32),
            jax.ShapeDtypeStruct(new_shape, F32),
        ],
        scratch_shapes=[
            pltpu.VMEM((blocks, length), F32),
            pltpu.VMEM((width // 128, chan_in, 128), F32),
            pltpu.VMEM((chan_in // 128, width, 128), F32),
            pltpu.VMEM((chan_in, width), F32),
            pltpu.VMEM((SMALL, width), F32),
            pltpu.VMEM((blocks, 128), F32),
        ],
        compiler_params=params(),
        cost_estimate=cost(10),
        name="adam",
    )(ids, *arrays)


def deal_rows(rows):
    n_pix = lax.axis_size(PIX)
    n, hidden = rows.shape
    dealt = lax.all_to_all(rows.reshape(n_pix, n // n_pix, hidden), PIX, 0, 0, tiled=True)
    return jnp.sum(dealt, axis=0)


def together(*values):
    return lax.optimization_barrier(values)


def local(
    frames_raw,
    grad_out,
    col_offsets,
    flip_flags,
    owners,
    w_expand,
    w_dw,
    norm_gains,
    norm_biases,
    w_project,
    squeeze_matrix,
    se_down_bias,
    excite_matrix,
    excite_bias_row,
    first_moment,
    second_moment,
):
    nz, nhi, nlo = (lax.axis_size(axis) for axis in ALL)
    frames, chans, stored = frames_raw.shape
    band = stored // WIN
    area = band * FRAME_COLUMNS
    rows = nlo * band
    chan_in, hidden_dev = w_expand.shape
    hidden = hidden_dev * nz
    reduced = squeeze_matrix.shape[1]
    group = nz // MB * nhi * nlo
    count = float(frames // MB * FRAME_ROWS * FRAME_COLUMNS)
    hi = lax.axis_index("hi")
    side = jnp.stack([(hi > 0).astype(jnp.int32), (hi < nhi - 1).astype(jnp.int32)])

    n_pix = nhi * nlo
    me = hi * nlo + lax.axis_index("lo")
    relative = me if near(n_pix) else 0 * me
    z_relative = lax.axis_index("chan") if near(n_pix) else 0 * me

    slab = pack_weights(
        me.astype(jnp.int32).reshape(1),
        w_expand,
        w_dw,
        norm_gains,
        norm_biases,
        w_project,
        squeeze_matrix,
        excite_matrix,
        excite_bias_row,
    )
    crops = crop(frames_raw, col_offsets, flip_flags)
    crops, *slab = together(crops, *gather_chan(slab))
    x = deal(crops).reshape(nz, nlo, chans, area)
    ordered = order(grad_out)
    slabs, orders, ordered = gather_pix(jnp.concatenate(slab, axis=1), ordered)
    first_turned, second_turned = first_moment.transpose(1, 0, 2), second_moment.transpose(1, 0, 2)
    first_turned, second_turned, *slabs = together(first_turned, second_turned, *slabs)
    room = ((0, -first_moment.shape[1] % SUB), (0, 0))
    moments = jnp.concatenate([jnp.pad(v[:, 0], room) for v in (first_turned, second_turned)])
    (
        we_high,
        we_low,
        wet_high,
        wet_low,
        wp_high,
        wp_low,
        w_project_t,
        taps,
        gains,
        biases,
        sq_t,
        ex_all,
        ex_bias,
    ) = order_weights(
        jnp.stack([relative, z_relative]), slabs, orders, nz, chan_in, chans, reduced
    )
    se_weights = [sq_t, se_down_bias[:, None], ex_all, ex_bias]
    x, ordered, we_high, we_low, moments = together(x, ordered, we_high, we_low, moments)
    moments = lax.all_gather(moments, PIX, axis=0)

    def as_rows(v):
        return v.reshape(rows, SUB, SUB, hidden)

    def as_bands(v):
        return v.reshape(nlo, area, hidden)

    def as_sides(v, n):
        return v.reshape(2, n, SUB, SUB, hidden)

    hid, sums_one, gram = expand(x, we_high, we_low)
    later = [x]
    sums_one = shares(sums_one, 1, group, later)
    [x] = later
    top, low = rims(x, HALO_IN, band)
    gout = deal(ordered).reshape(nz, nlo, chans, area)
    g_top, g_low = rims(gout, HALO_OUT, band)
    spatial, spatial_halo, hid_halo, sums_two = spread(
        count, side, top, low, as_rows(hid), we_high, we_low, gains, biases, taps, sums_one
    )
    sums_two = shares(sums_two, 1, group)
    m, s, se_part, proj = gather(
        count, as_bands(spatial), gout, gains, biases, w_project_t, wp_high, wp_low, sums_two
    )
    ses = shares(se_part, nlo, nhi)
    ses, g_top, g_low = together(ses, g_top, g_low)
    q, back_two, values, columns, *w4, out, g_project = proj_back(
        count, as_bands(spatial), gout, proj, x, gains, biases, w_project_t, m, s, se_weights, ses, sums_two
    )
    backs_two = shares(back_two, 1, group)
    out = deal(out.reshape(frames, chans, area))
    q1, back_one, g_dw = spread_back(
        count,
        side,
        g_top,
        g_low,
        as_rows(hid),
        hid_halo,
        spatial,
        spatial_halo,
        as_rows(q),
        w4,
        gains,
        biases,
        taps,
        sums_one,
        sums_two,
        backs_two,
    )
    later = [q1]
    backs_one = shares(back_one, 1, group, later)
    [q1] = later

    ids = jnp.stack([relative, hi, z_relative]).astype(jnp.int32)
    pieces = weight_grad(
        ids, (2, n_pix // 2) if near(n_pix) else (1, 1), as_bands(q1), x, g_dw, back_one, back_two, values, columns
    )
    if near(n_pix):
        early = lax.psum_scatter(g_project, PIX, scatter_dimension=0, tiled=True)
        gram = lax.psum_scatter(gram, PIX, scatter_dimension=0, tiled=True)
    else:
        early, gram = deal_rows(g_project), deal_rows(gram)
    q1, out, early, gram, moments, *pieces = together(q1, out, early, gram, moments, *pieces)

    def input_part(start, width, q1):
        grad = input_grad(
            count, start, width, as_bands(q1), hid, gout, gains, wet_high, wet_low, sums_one, backs_one
        )
        return grad.reshape(frames, chans, width)

    most = area // 2
    grad_one = input_part(0, most, q1)
    if near(n_pix):
        pieces = [pieces[0], exchange(pieces[1], 1)]
    grad_one, q1, *pieces = together(grad_one, q1, *pieces)
    if near(n_pix):
        pieces = list(merge(*pieces))
        pieces[0], out = together(pieces[0], out)
        pieces = [pieces[0]] + [exchange(pieces[i], 2 * i) for i in range(1, n_pix // 2)]
    else:
        whole_rows = pieces[0][0]
        pieces = [jnp.concatenate([deal_rows(whole_rows[:chan_in]), deal_rows(whole_rows[chan_in:])])]
    grad_two = input_part(most, area - most, q1)
    output = restore(out)
    weights = [
        w_expand,
        w_dw,
        norm_gains,
        norm_biases,
        w_project,
        squeeze_matrix.T,
        se_down_bias[None],
        excite_matrix,
        excite_bias_row[None],
    ]
    block_len = first_moment.shape[2]
    natural = [list(range(n_pix))]
    base = jnp.zeros((1,), jnp.int32)
    prepared = prepare(base, owners, weights, [moments], natural, block_len)
    grad_two, output, *pieces = together(grad_two, output, *pieces)
    groups = collect(count, ids, nz, pieces, early, gram, we_high, we_low, gains, sums_one, backs_one)
    if near(n_pix):
        others = [groups[0]] + [exchange(groups[k], k * n_pix) for k in range(1, nz)]
    else:
        others = list(lax.all_to_all(jnp.stack(groups), "chan", 0, 0, tiled=True))
    grad_one = deal(grad_one)
    grad_one, grad_two, *groups = together(grad_one, grad_two, *groups)
    summed = sum(others[1:], others[0])
    grad_two = deal(grad_two)
    grads, _, prepared = gather_pix(summed, prepared)
    seg_sizes, seg_rates = segments(chan_in, hidden_dev, chans, reduced, TAPS, hidden)
    bounds = [sum(seg_sizes[: i + 1]) for i in range(len(seg_sizes))]
    first_next, second_next, new_params = adam(
        jnp.stack([me, relative]).astype(jnp.int32),
        owners,
        prepared,
        first_turned,
        second_turned,
        grads,
        orders,
        chan_in,
        chans,
        reduced,
        bounds,
        seg_rates,
    )
    first_next, second_next = first_next.transpose(1, 0, 2), second_next.transpose(1, 0, 2)
    grad_frames = uncrop(grad_one, grad_two, col_offsets, flip_flags)
    return (output, grad_frames, first_next, second_next, new_params)


def solution(mesh):
    nz, n_pix = mesh.shape["chan"], mesh.shape["pix"]
    placed = (
        P(None, "chan", PIX),
        P(None, "chan", PIX),
        P(),
        P(),
        P(),
        P(None, "chan"),
        P(None, "chan"),
        P(None, "chan"),
        P(None, "chan"),
        P("chan", None),
        P("chan", None),
        P(),
        P(None, "chan"),
        P("chan"),
        P("chan", PIX, None),
        P("chan", PIX, None),
    )

    def run(*arrays):
        nlo = arrays[0].shape[0] // nz
        return jax.shard_map(
            local,
            mesh=Mesh(mesh.devices.reshape(nz, n_pix // nlo, nlo), ALL),
            in_specs=placed,
            out_specs=(
                P(None, "chan", PIX),
                P(None, "chan", PIX),
                P("chan", PIX, None),
                P("chan", PIX, None),
                P("chan", None),
            ),
            check_vma=False,
        )(*arrays)

    return run
```

```python
from functools import partial
import math

import jax
import jax.numpy as jnp
from jax import lax
from jax.experimental import pallas as pl
from jax.experimental.pallas import tpu as pltpu
from jax.sharding import Mesh, PartitionSpec as P

K = 5
FRAME_ROWS = 64
FRAME_COLUMNS = 64
CLIP_LEN = 4
MB = 4
STEP = 5
WIN = 80
SUB = 8
TAPS = K * K
HALO_IN = 4
SMALL = 64
HALO_OUT = 2

norm_eps = 1e-05
beta_first = 0.5
beta_second = 0.6
adam_eps = 1e-08
weight_decay = 0.1

F32 = jnp.float32
BF16 = jnp.bfloat16
ALL = ("chan", "hi", "lo")
PIX = ("hi", "lo")
SPREAD = ("chan", "lo")
VMEM_BYTES = 62 * 2**20


def params(spare=0):
    return pltpu.CompilerParams(vmem_limit_bytes=VMEM_BYTES - spare * 2**20, dimension_semantics=("arbitrary",))


def keep(x):
    return pltpu.with_memory_space_constraint(x, pltpu.VMEM)


def cost(us):
    return pl.CostEstimate(flops=int(us * 1.1e9), bytes_accessed=int(us * 3.5e6), transcendentals=0)


def sigmoid(v):
    return 0.5 * jnp.tanh(0.5 * v) + 0.5


def swish_half(h):
    return h + h * jnp.tanh(h)


def slope_half(h):
    t = jnp.tanh(h)
    return 1.0 + (t + h * (1.0 - t * t))


def split(v):
    high = v.astype(BF16)
    return high, (v - high.astype(F32)).astype(BF16)


def dot(a, b):
    return jnp.dot(a, b, preferred_element_type=F32)


def dot3(a, b):
    return dot(a[0], b[0]) + (dot(a[0], b[1]) + dot(a[1], b[0]))


def total(refs):
    value = refs[0][...]
    for ref in refs[1:]:
        value = value + ref[...]
    return value


def norm_terms(sums, count, gain, bias):
    mean = sums[0:1] / count
    inverse = lax.rsqrt(sums[1:2] / count - mean * mean + norm_eps)
    scale = gain * inverse
    return mean, inverse, scale, bias - mean * scale


def back_terms(sums, back, count, gain):
    mean = sums[0:1] / count
    inverse = lax.rsqrt(sums[1:2] / count - mean * mean + norm_eps)
    a = gain * inverse
    b = -a * inverse * (back[1:2] / count)
    return a, b, -a * (back[0:1] / count) - b * mean


def exchange(x, stride):
    n = lax.axis_size(ALL)
    return lax.ppermute(x, ALL, [(i, i ^ stride) for i in range(n)])


def shares(x, base, size, after=()):
    bits = size.bit_length() - 1
    parts = [x]
    if bits % 2:
        parts = [x, exchange(x, base)]
        base, bits = base * 2, bits - 1
    while bits:
        x = sum(parts[1:], parts[0])
        if after:
            x, *kept = together(x, *after)
            after[:] = kept
            after = ()
        parts = [x] + [exchange(x, base * k) for k in (1, 2, 3)]
        base, bits = base * 4, bits - 2
    return parts


def deal(x):
    return lax.all_to_all(x, SPREAD, 0, 0, tiled=True)


def edge(x, rows, band, first):
    if rows >= band:
        n = rows // band
        return x[:, :n] if first else x[:, x.shape[1] - n :]
    width = rows * FRAME_COLUMNS
    return x[:, :1, :, :width] if first else x[:, -1:, :, x.shape[3] - width :]


def rims(x, rows, band):
    n = lax.axis_size("hi")
    if n == 2:
        mine = jnp.where(lax.axis_index("hi") == 0, edge(x, rows, band, False), edge(x, rows, band, True))
        other = lax.ppermute(mine, "hi", [(0, 1), (1, 0)])
        return other, other
    down = [(i, i + 1) for i in range(n - 1)]
    up = [(i + 1, i) for i in range(n - 1)]
    top = lax.ppermute(edge(x, rows, band, False), "hi", down)
    low = lax.ppermute(edge(x, rows, band, True), "hi", up)
    return top, low


def near(n_pix):
    return n_pix == 8


def gather_pix(x, beside=None):
    n_pix = lax.axis_size(PIX)
    if not near(n_pix):
        return [lax.all_gather(x, PIX, axis=0)], [list(range(n_pix))], beside
    b = x[None]
    b = jnp.concatenate([b, exchange(b, 2)])
    if beside is not None:
        b, beside = together(b, beside)
    b = jnp.concatenate([b, exchange(b, 4)])
    return [b, exchange(b, 1)], [[0, 2, 4, 6], [1, 3, 5, 7]], beside


def gather_chan(x):
    nz, n_pix = lax.axis_size("chan"), lax.axis_size(PIX)
    if not near(n_pix):
        return list(lax.all_gather(x, "chan", axis=0))
    return [x] + [exchange(x, k * n_pix) for k in range(1, nz)]


def source_column(p, left, flip):
    row, c, s = p // FRAME_COLUMNS, (p // SUB) % SUB, p % SUB
    j = s * SUB + c
    return row * WIN + left + jnp.where(flip == 1, FRAME_COLUMNS - 1 - j, j)


def plain_place(p):
    row, c, s = p // FRAME_COLUMNS, (p // SUB) % SUB, p % SUB
    return row * FRAME_COLUMNS + s * SUB + c


def pick(x, chosen):
    rows = x.shape[0] * x.shape[1]
    high, low = split(x.reshape(rows, x.shape[2]))
    return (dot(high, chosen) + dot(low, chosen)).reshape(x.shape[0], x.shape[1], chosen.shape[1])


def crop_kernel(left_ref, flip_ref, raw_ref, out_ref):
    k = pl.program_id(0)
    width, area = raw_ref.shape[2], out_ref.shape[2]
    p = lax.broadcasted_iota(jnp.int32, (1, area), 1)
    place = source_column(p, left_ref[k], flip_ref[k])
    q = lax.broadcasted_iota(jnp.int32, (width, area), 0)
    out_ref[...] = pick(raw_ref[...], (q == place).astype(F32).astype(BF16))


def crop(raw, left, flip):
    frames, chans, width = raw.shape
    area = width // WIN * FRAME_COLUMNS
    return pl.pallas_call(
        crop_kernel,
        grid=(frames // CLIP_LEN,),
        in_specs=[
            pl.BlockSpec(memory_space=pltpu.SMEM),
            pl.BlockSpec(memory_space=pltpu.SMEM),
            pl.BlockSpec((CLIP_LEN, chans, width), lambda k: (k, 0, 0)),
        ],
        out_specs=pl.BlockSpec((CLIP_LEN, chans, area), lambda k: (k, 0, 0)),
        out_shape=jax.ShapeDtypeStruct((frames, chans, area), F32),
        compiler_params=params(),
        cost_estimate=cost(5),
        name="crop",
    )(left, flip, raw)


def order_kernel(x_ref, out_ref):
    area = x_ref.shape[2]
    p = lax.broadcasted_iota(jnp.int32, (1, area), 1)
    q = lax.broadcasted_iota(jnp.int32, (area, area), 0)
    out_ref[...] = pick(x_ref[...], (q == plain_place(p)).astype(F32).astype(BF16))


def order(x):
    frames, chans, area = x.shape
    return pl.pallas_call(
        order_kernel,
        grid=(frames // CLIP_LEN,),
        in_specs=[pl.BlockSpec((CLIP_LEN, chans, area), lambda k: (k, 0, 0))],
        out_specs=pl.BlockSpec((CLIP_LEN, chans, area), lambda k: (k, 0, 0)),
        out_shape=jax.ShapeDtypeStruct((frames, chans, area), F32),
        compiler_params=params(),
        cost_estimate=cost(25),
        name="order",
    )(x)


def restore_kernel(x_ref, out_ref):
    area = x_ref.shape[2]
    p = lax.broadcasted_iota(jnp.int32, (area, 1), 0)
    q = lax.broadcasted_iota(jnp.int32, (area, area), 1)
    out_ref[...] = pick(x_ref[...], (q == plain_place(p)).astype(F32).astype(BF16))


def restore(x):
    frames, chans, area = x.shape
    return pl.pallas_call(
        restore_kernel,
        grid=(frames // CLIP_LEN,),
        in_specs=[pl.BlockSpec((CLIP_LEN, chans, area), lambda k: (k, 0, 0))],
        out_specs=pl.BlockSpec((CLIP_LEN, chans, area), lambda k: (k, 0, 0)),
        out_shape=jax.ShapeDtypeStruct((frames, chans, area), F32),
        compiler_params=params(),
        cost_estimate=cost(1),
        name="restore",
    )(x)


def uncrop_kernel(left_ref, flip_ref, x_ref, y_ref, out_ref):
    k = pl.program_id(0)
    width = out_ref.shape[2]
    out = None
    for start, ref in ((0, x_ref), (x_ref.shape[2], y_ref)):
        area = ref.shape[2]
        q = lax.broadcasted_iota(jnp.int32, (area, width), 1)
        p = lax.broadcasted_iota(jnp.int32, (area, 1), 0) + start
        place = source_column(p, left_ref[k], flip_ref[k])
        term = pick(ref[...], (q == place).astype(F32).astype(BF16))
        out = term if out is None else out + term
    out_ref[...] = out


def uncrop(x, y, left, flip):
    frames, chans, area = x.shape
    width = (area + y.shape[2]) // FRAME_COLUMNS * WIN
    return pl.pallas_call(
        uncrop_kernel,
        grid=(frames // CLIP_LEN,),
        in_specs=[
            pl.BlockSpec(memory_space=pltpu.SMEM),
            pl.BlockSpec(memory_space=pltpu.SMEM),
            pl.BlockSpec((CLIP_LEN, chans, area), lambda k: (k, 0, 0)),
            pl.BlockSpec((CLIP_LEN, chans, y.shape[2]), lambda k: (k, 0, 0)),
        ],
        out_specs=pl.BlockSpec((CLIP_LEN, chans, width), lambda k: (k, 0, 0)),
        out_shape=jax.ShapeDtypeStruct((frames, chans, width), F32),
        compiler_params=params(),
        cost_estimate=cost(1),
        name="uncrop",
    )(left, flip, x, y)


def chunks(width):
    step = 256 if width % 256 == 0 else width
    return [slice(i, i + step) for i in range(0, width, step)]


def expand_kernel(x_ref, high_ref, low_ref, own_ref, sum_ref, gram_ref):
    @pl.when(pl.program_id(0) == 0)
    def _():
        sum_ref[...] = jnp.zeros_like(sum_ref)
        gram_ref[...] = jnp.zeros_like(gram_ref)

    chan_all, hidden = high_ref.shape
    plain = x_ref[:, 0].reshape(chan_all, x_ref.shape[3])
    turned = plain.T
    x = split(turned)
    for cut in chunks(hidden):
        y = dot3(x, (high_ref[:, cut], low_ref[:, cut]))
        own_ref[0, :, cut] = y
        sum_ref[0:1, cut] += jnp.sum(y, axis=0, keepdims=True)
        sum_ref[1:2, cut] += jnp.sum(y * y, axis=0, keepdims=True)
    gram_ref[:, 0:chan_all] += dot3(split(plain), x)
    gram_ref[:, chan_all:] += jnp.broadcast_to(jnp.sum(plain, axis=1, keepdims=True), (chan_all, 128))


def whole(shape):
    return pl.BlockSpec(shape, lambda *_: (0,) * len(shape))


def by_steps(nz, bands, chans, area):
    run = area
    n = area // run

    def tall(hidden):
        return pl.BlockSpec((1, run, hidden), lambda t: (t // n, t % n, 0))

    def out(hidden):
        return pl.BlockSpec((1, run, hidden), lambda t: (t // n, t % n, 0))

    wide = pl.BlockSpec((nz, 1, chans, run), lambda t: (0, t // n, 0, t % n))
    return (bands * n,), tall, out, wide


def expand(x, high, low):
    nz, bands, chans, area = x.shape
    grid, _, tall, wide = by_steps(nz, bands, chans, area)
    hidden = high.shape[1]
    return pl.pallas_call(
        expand_kernel,
        grid=grid,
        in_specs=[
            wide,
            whole(high.shape),
            whole(low.shape),
        ],
        out_specs=[
            tall(hidden),
            whole((2, hidden)),
            whole((nz * chans, nz * chans + 128)),
        ],
        out_shape=[
            jax.ShapeDtypeStruct((bands, area, hidden), F32),
            jax.ShapeDtypeStruct((2, hidden), F32),
            jax.ShapeDtypeStruct((nz * chans, nz * chans + 128), F32),
        ],
        compiler_params=params(),
        cost_estimate=cost(8),
        name="expand",
    )(x, high, low)


def fill_sides(pad, row):
    s = lax.broadcasted_iota(jnp.int32, (SUB, 128), 0)
    for k in range(2):
        left = pltpu.roll(pad[row, SUB + k], 1, 0)
        pad[row, k] = jnp.where(s == 0, 0.0, left)
        right = pltpu.roll(pad[row, 2 + k], SUB - 1, 0)
        pad[row, SUB + 2 + k] = jnp.where(s == SUB - 1, 0.0, right)


def clear_rows(pad, start, count):
    for row in range(start, start + count):
        pad[row] = jnp.zeros(pad.shape[1:], F32)


def tap_rows(pad, w_ref, start, count, c, flipped=False):
    acc = [None] * count
    for b in range(K):
        for row in range(count + K - 1):
            value = pad[start + row, c + b]
            for a in range(K):
                o = row - a
                if 0 <= o < count:
                    tap = a * K + b
                    term = value * w_ref[TAPS - 1 - tap if flipped else tap]
                    acc[o] = term if acc[o] is None else acc[o] + term
    return acc


def turn_rims(refs, side_ref, high, low):
    for side, ref in enumerate(refs):
        chan_all, width = ref.shape[0] * ref.shape[2], ref.shape[3]

        @pl.when(side_ref[side] == 1)
        def _(side=side, ref=ref, chan_all=chan_all, width=width):
            for k in range(ref.shape[1]):
                here = slice(k * width, (k + 1) * width)
                high[side, here], low[side, here] = split(ref[:, k].reshape(chan_all, width).T)


def raise_rows(d):
    e1, o1 = d[2] + d[6] - 4.25 * d[4], d[1] + d[5] - 4.25 * d[3]
    e2, o2 = 0.25 * d[2] - 1.25 * d[4] + d[6], 0.5 * d[1] - 2.5 * d[3] + 2.0 * d[5]
    e3, o3 = 4.0 * d[2] - 5.0 * d[4] + d[6], 2.0 * d[1] - 2.5 * d[3] + 0.5 * d[5]
    return [
        d[0] - d[6] + 5.25 * (d[4] - d[2]),
        e1 + o1,
        e1 - o1,
        e2 + o2,
        e2 - o2,
        e3 + o3,
        e3 - o3,
        d[7] - d[1] + 5.25 * (d[3] - d[5]),
    ]


POINT_SCALES = (1.0, -2.0 / 9.0, -2.0 / 9.0, 1.0 / 90.0, 1.0 / 90.0, 32.0 / 45.0, 32.0 / 45.0)
POINT_PLACES = (0.0, 1.0, -1.0, 2.0, -2.0, 0.5, -0.5)
POINTS = 8
GROUP = 4


def tap_factors():
    rows = [[scale * place**a for a in range(K)] for scale, place in zip(POINT_SCALES, POINT_PLACES)]
    return rows + [[0.0] * (K - 1) + [1.0]]


def mix(factors, values):
    out = None
    for factor, value in zip(factors, values):
        if factor != 0.0:
            term = value if factor == 1.0 else value * factor
            out = term if out is None else out + term
    return out


def lower(m):
    s1, d1, s2, d2, s3, d3 = m[1] + m[2], m[1] - m[2], m[3] + m[4], m[3] - m[4], m[5] + m[6], m[5] - m[6]
    return [
        m[0] + s1 + (s2 + s3),
        d1 + (2.0 * d2 + 0.5 * d3),
        s1 + (4.0 * s2 + 0.25 * s3),
        d1 + m[7] + (8.0 * d2 + 0.125 * d3),
    ]


def spread_points(g):
    e1, o1 = g[0] + g[2], g[1] + g[3]
    e2, o2 = g[0] + 4.0 * g[2], 2.0 * g[1] + 8.0 * g[3]
    e3, o3 = g[0] + 0.25 * g[2], 0.5 * g[1] + 0.125 * g[3]
    return [g[0], e1 + o1, e1 - o1, e2 + o2, e2 - o2, e3 + o3, e3 - o3, g[3]]


def raise_all(pad, first, raised):
    def two(i, _):
        for k in range(2):
            g = 2 * i + k
            for c in range(SUB):
                d = [pad[first + GROUP * g + n, c + 2] for n in range(2 * GROUP)]
                for p, value in enumerate(raise_rows(d)):
                    raised[g, p, c + 2] = value
            for p in range(POINTS):
                fill_sides(raised.at[g], p)
        return 0

    lax.fori_loop(0, raised.shape[0] // 2, two, 0)


def raise_taps(w_ref, taps, flipped=False, scale=1.0):
    for b in range(K):
        column_taps = []
        for a in range(K):
            tap = a * K + b
            column_taps.append(w_ref[TAPS - 1 - tap if flipped else tap])
        for p, factors in enumerate(tap_factors()):
            taps[p * K + b] = mix([scale * factor for factor in factors], column_taps)


def four_rows(raised, taps, g, columns):
    m = []
    for p in range(POINTS):
        values = {c: raised[g, p, c] for c in range(columns[0], columns[-1] + K)}
        row = []
        for c in columns:
            row.append(mix([1.0] * K, [values[c + b] * taps[p * K + b] for b in range(K)]))
        m.append(row)
    return [lower([m[p][i] for p in range(POINTS)]) for i in range(len(columns))]


def spread_kernel(
    parts, count, side_ref, top_ref, low_ref, own_ref, high_ref, lower_ref, gain_ref, bias_ref, w_ref, *rest
):
    sums = rest[:parts]
    out_ref, edge_ref, hid_ref, sum_ref, pad, terms, rim_high, rim_low, raised, taps = rest[parts:]
    rows = own_ref.shape[0]
    _, _, scale, shift = norm_terms(total(sums), count, gain_ref[0:1], bias_ref[0:1])
    terms[0] = jnp.broadcast_to(0.5 * scale, (SUB, 128))
    terms[1] = jnp.broadcast_to(0.5 * shift, (SUB, 128))

    @pl.when(pl.program_id(0) == 0)
    def _():
        turn_rims((top_ref, low_ref), side_ref, rim_high, rim_low)

    def act(value):
        return swish_half(value * terms[0] + terms[1])

    def own_rows(i, _):
        for k in range(GROUP):
            for c in range(SUB):
                pad[GROUP * i + k + HALO_IN, c + 2] = act(own_ref[GROUP * i + k, c])
        return 0

    lax.fori_loop(0, rows // GROUP, own_rows, 0)
    for side, start, first in ((0, 0, HALO_IN - HALO_OUT), (1, rows + HALO_IN, 0)):

        @pl.when(side_ref[side] == 1)
        def _(side=side, start=start, first=first):
            halo = dot3((rim_high[side], rim_low[side]), (high_ref[...], lower_ref[...]))
            halo = halo.reshape(HALO_IN, SUB, SUB, 128)
            hid_ref[side] = halo[first : first + HALO_OUT]
            pad[start : start + HALO_IN, 2 : SUB + 2] = act(halo)
            edge_row = min(start, rows + 2)
            for r in range(HALO_OUT + K - 1):
                fill_sides(pad, edge_row + r)

        @pl.when(side_ref[side] == 0)
        def _(side=side, start=start):
            clear_rows(pad, start, HALO_IN)
            hid_ref[side] = jnp.zeros(hid_ref.shape[1:], F32)

    raise_taps(w_ref, taps)
    raise_all(pad, 2, raised)

    def group(g, carry):
        one, two = carry
        for columns in (range(0, SUB // 2), range(SUB // 2, SUB)):
            for c, values in zip(columns, four_rows(raised, taps, g, columns)):
                for o, value in enumerate(values):
                    out_ref[GROUP * g + o, c] = value
                    one = one + value
                    two = two + value * value
        return one, two

    zero = jnp.zeros((SUB, 128), F32)
    one, two = lax.fori_loop(0, rows // GROUP, group, (zero, zero))
    sum_ref[0:1] = jnp.sum(one, axis=0, keepdims=True)
    sum_ref[1:2] = jnp.sum(two, axis=0, keepdims=True)
    for side, start in ((0, 0), (1, rows + 2)):

        @pl.when(side_ref[side] == 1)
        def _(side=side, start=start):
            for c in range(SUB):
                acc = tap_rows(pad, w_ref, start, HALO_OUT, c)
                for o in range(HALO_OUT):
                    edge_ref[side, o, c] = acc[o]

        @pl.when(side_ref[side] == 0)
        def _(side=side):
            edge_ref[side] = jnp.zeros(edge_ref.shape[1:], F32)


def lanes(shape):
    lead = len(shape) - 1
    return pl.BlockSpec(tuple(shape[:-1]) + (128,), lambda e: (0,) * lead + (e,))


def spread(count, side, top, low, own, w_high, w_low, gains, biases, taps, sums):
    rows, hidden = own.shape[0], own.shape[-1]
    chan_all = w_high.shape[0]
    arrays = [own, w_high, w_low, gains, biases, taps, *sums]
    edge_shape = (2, HALO_OUT, SUB, SUB, hidden)
    rim_shape = (2, HALO_IN * FRAME_COLUMNS, chan_all)
    return pl.pallas_call(
        partial(spread_kernel, len(sums), count),
        grid=(hidden // 128,),
        in_specs=[pl.BlockSpec(memory_space=pltpu.SMEM), whole(top.shape), whole(low.shape)]
        + [lanes(a.shape) for a in arrays],
        out_specs=[
            lanes((rows, SUB, SUB, hidden)),
            lanes(edge_shape),
            lanes(edge_shape),
            lanes((2, hidden)),
        ],
        out_shape=[
            jax.ShapeDtypeStruct((rows, SUB, SUB, hidden), F32),
            jax.ShapeDtypeStruct(edge_shape, F32),
            jax.ShapeDtypeStruct(edge_shape, F32),
            jax.ShapeDtypeStruct((2, hidden), F32),
        ],
        scratch_shapes=[
            pltpu.VMEM((rows + 2 * HALO_IN, SUB + 4, SUB, 128), F32),
            pltpu.VMEM((2, SUB, 128), F32),
            pltpu.VMEM(rim_shape, BF16),
            pltpu.VMEM(rim_shape, BF16),
            pltpu.VMEM((rows // GROUP, POINTS, SUB + 4, SUB, 128), F32),
            pltpu.VMEM((POINTS * K, SUB, 128), F32),
        ],
        compiler_params=params(),
        cost_estimate=cost(10),
        name="spread",
    )(side, top, low, *arrays)


def as_row(columns):
    width = columns.shape[1]
    folded = columns[:, 0:128]
    for i in range(128, width, 128):
        folded = folded + columns[:, i : i + 128]
    return jnp.sum(folded.T, axis=0, keepdims=True)


def gather_kernel(parts, count, own_ref, gout_ref, gain_ref, bias_ref, wt_ref, high_ref, low_ref, *rest):
    sums, (m_ref, s_ref, se_ref, proj_ref) = rest[:parts], rest[parts:]
    t = pl.program_id(0)
    chan_all, hidden = wt_ref.shape

    @pl.when(t == 0)
    def _():
        m_ref[...] = jnp.zeros_like(m_ref)
        s_ref[...] = jnp.zeros_like(s_ref)

    _, _, scale, shift = norm_terms(total(sums), count, gain_ref[1:2], bias_ref[1:2])
    scale, shift = 0.5 * scale, 0.5 * shift
    gout = split(gout_ref[:, 0].reshape(chan_all, gout_ref.shape[3]))
    proj = None
    for cut in chunks(hidden):
        act = swish_half(own_ref[0, :, cut] * scale[:, cut] + shift[:, cut])
        s_ref[0:1, cut] += jnp.sum(act, axis=0, keepdims=True)
        act = split(act)
        m_ref[:, cut] += dot3(gout, act)
        term = dot3(act, (high_ref[cut], low_ref[cut]))
        proj = term if proj is None else proj + term
    proj_ref[0] = proj

    @pl.when(t == pl.num_programs(0) - 1)
    def _():
        wt = wt_ref[...]
        se_ref[0:1] = as_row(s_ref[...] * wt)
        se_ref[1:2] = as_row(m_ref[...] * wt)


def gather(count, own, gout, gains, biases, wt, w_high, w_low, sums):
    nz, bands, chans, area = gout.shape
    hidden = wt.shape[1]
    chan_all = nz * chans
    grid, tall, put, wide = by_steps(nz, bands, chans, area)
    return pl.pallas_call(
        partial(gather_kernel, len(sums), count),
        grid=grid,
        in_specs=[
            tall(hidden),
            wide,
            whole(gains.shape),
            whole(biases.shape),
            whole(wt.shape),
            whole(w_high.shape),
            whole(w_low.shape),
        ]
        + [whole(s.shape) for s in sums],
        out_specs=[
            whole((chan_all, hidden)),
            whole((1, hidden)),
            whole((2, chan_all)),
            put(chan_all),
        ],
        out_shape=[
            pltpu.VMEM((chan_all, hidden), F32),
            jax.ShapeDtypeStruct((1, hidden), F32),
            jax.ShapeDtypeStruct((2, chan_all), F32),
            pltpu.VMEM((bands, area, chan_all), F32),
        ],
        compiler_params=params(4),
        cost_estimate=cost(13),
        name="gather",
    )(own, gout, gains, biases, wt, w_high, w_low, *sums)


def column(row):
    return jnp.broadcast_to(row, (SUB, row.shape[1])).T[:, 0:1]


def slope_terms(sums, count, gain_ref, bias_ref):
    _, _, scale, shift = norm_terms(sums, count, gain_ref[1:2], bias_ref[1:2])
    return 0.5 * scale, 0.5 * shift


def second_grad(gout, weights, k_row, value, terms, cut):
    h = value * terms[0][:, cut] + terms[1][:, cut]
    return (dot3(gout, (weights[0][:, cut], weights[1][:, cut])) + k_row[:, cut]) * slope_half(h), h


def proj_back_kernel(
    pairs,
    parts,
    count,
    own_ref,
    gout_ref,
    proj_ref,
    x_ref,
    gain_ref,
    bias_ref,
    wt_ref,
    m_ref,
    s_ref,
    sqt_ref,
    down_ref,
    ex_ref,
    exb_ref,
    *rest,
):
    ses, sums = rest[:pairs], rest[pairs : pairs + parts]
    q_ref, sum_ref, val_ref, col_ref, w_high, w_low, k_row, out_ref, grad_ref = rest[pairs + parts :]
    chan_all, hidden = wt_ref.shape

    @pl.when(pl.program_id(0) == 0)
    def _():
        se = total(ses)
        pooled = se[0:1] / (FRAME_ROWS * FRAME_COLUMNS)
        sqt, ex = sqt_ref[...], ex_ref[...]
        pre = jnp.sum(sqt * pooled, axis=1, keepdims=True) + down_ref[...]
        gate = sigmoid(pre)
        squeezed = pre * gate
        excite = sigmoid(jnp.sum(ex * squeezed, axis=0, keepdims=True) + exb_ref[...])
        logit = se[1:2] * excite * (1.0 - excite)
        slope = gate * (1.0 + pre * (1.0 - gate))
        grad_sq = jnp.sum(ex * logit, axis=1, keepdims=True) * slope
        pool_grad = jnp.sum(sqt * grad_sq, axis=0, keepdims=True) / (FRAME_ROWS * FRAME_COLUMNS)
        val_ref[...] = jnp.zeros_like(val_ref)
        val_ref[0:1] = excite
        val_ref[1:2] = pool_grad
        val_ref[2:3] = logit
        val_ref[3:4] = pooled
        lane = lax.broadcasted_iota(jnp.int32, col_ref.shape, 1)
        col_ref[...] = jnp.where(lane == 0, squeezed, jnp.where(lane == 1, grad_sq, 0.0))
        wt = 0.5 * wt_ref[...]
        tall_excite, tall_pool = column(excite), column(pool_grad)
        w_high[...], w_low[...] = split(wt * tall_excite)
        k_row[...] = jnp.sum(wt * tall_pool, axis=0, keepdims=True)
        grad_ref[...] = tall_excite * m_ref[...] + tall_pool * s_ref[...]
        sum_ref[...] = jnp.zeros_like(sum_ref)

    terms = slope_terms(total(sums), count, gain_ref, bias_ref)
    gout = split(gout_ref[:, 0].reshape(chan_all, gout_ref.shape[3]).T)
    for cut in chunks(hidden):
        q, h = second_grad(gout, (w_high, w_low), k_row, own_ref[0, :, cut], terms, cut)
        q_ref[0, :, cut] = q
        sum_ref[0:1, cut] += jnp.sum(q, axis=0, keepdims=True)
        sum_ref[1:2, cut] += jnp.sum(q * h, axis=0, keepdims=True)

    nz, _, chans, area = x_ref.shape
    out_ref[:, 0] = x_ref[:, 0] + (proj_ref[0] * val_ref[0:1]).T.reshape(nz, chans, area)

    @pl.when(pl.program_id(0) == pl.num_programs(0) - 1)
    def _():
        sum_ref[1:2] = (2.0 * sum_ref[1:2] - bias_ref[1:2] * sum_ref[0:1]) / gain_ref[1:2]


def proj_back(count, own, gout, proj, x, gains, biases, wt, m, s, se_weights, ses, sums):
    nz, bands, chans, area = gout.shape
    hidden = wt.shape[1]
    chan_all = nz * chans
    reduced = se_weights[0].shape[0]
    m, proj = keep(m), keep(proj)
    fixed = [gains, biases, wt, m, s, *se_weights, *ses, *sums]
    grid, tall, put, wide = by_steps(nz, bands, chans, area)
    return pl.pallas_call(
        partial(proj_back_kernel, len(ses), len(sums), count),
        grid=grid,
        in_specs=[
            tall(hidden),
            wide,
            tall(chan_all),
            wide,
        ]
        + [whole(a.shape) for a in fixed],
        out_specs=[
            put(hidden),
            whole((2, hidden)),
            whole((SUB, chan_all)),
            whole((reduced, 128)),
            whole(wt.shape),
            whole(wt.shape),
            whole((1, hidden)),
            wide,
            whole(m.shape),
        ],
        out_shape=[
            jax.ShapeDtypeStruct((bands, area, hidden), F32),
            jax.ShapeDtypeStruct((2, hidden), F32),
            jax.ShapeDtypeStruct((SUB, chan_all), F32),
            jax.ShapeDtypeStruct((reduced, 128), F32),
            jax.ShapeDtypeStruct(wt.shape, BF16),
            jax.ShapeDtypeStruct(wt.shape, BF16),
            jax.ShapeDtypeStruct((1, hidden), F32),
            jax.ShapeDtypeStruct(x.shape, F32),
            jax.ShapeDtypeStruct(m.shape, F32),
        ],
        compiler_params=params(4),
        cost_estimate=cost(12),
        name="proj_back",
    )(own, gout, proj, x, *fixed)


def spread_back_kernel(
    parts,
    count,
    side_ref,
    top_ref,
    low_ref,
    hid_ref,
    hid_halo_ref,
    own_ref,
    halo_ref,
    q_ref,
    high_ref,
    lower_ref,
    k_ref,
    gain_ref,
    bias_ref,
    w_ref,
    *rest,
):
    sums_one, sums_two, backs = (rest[i * parts : (i + 1) * parts] for i in range(3))
    out_ref, sum_ref, tap_ref, pad, grad, terms, rim_high, rim_low, raised, points, taps = rest[3 * parts :]
    rows = own_ref.shape[0]

    @pl.when(pl.program_id(0) == 0)
    def _():
        turn_rims((top_ref, low_ref), side_ref, rim_high, rim_low)

    _, _, scale, shift = norm_terms(total(sums_one), count, gain_ref[0:1], bias_ref[0:1])
    a, b, c0 = back_terms(total(sums_two), total(backs), count, gain_ref[1:2])
    for i, row in enumerate((0.5 * scale, 0.5 * shift, a, b, c0)):
        terms[i] = jnp.broadcast_to(row, (SUB, 128))

    def act(value):
        return swish_half(value * terms[0] + terms[1])

    def grad_in(q, value):
        return q * terms[2] + (value * terms[3] + terms[4])

    def own_rows(i, _):
        for k in range(GROUP):
            r = GROUP * i + k
            for c in range(SUB):
                pad[r + HALO_OUT, c + 2] = act(hid_ref[r, c])
                grad[r + HALO_OUT, c + 2] = grad_in(q_ref[r, c], own_ref[r, c])
        return 0

    lax.fori_loop(0, rows // GROUP, own_rows, 0)
    slope = slope_terms(total(sums_two), count, gain_ref, bias_ref)
    for side, start in ((0, 0), (1, rows + HALO_OUT)):

        @pl.when(side_ref[side] == 1)
        def _(side=side, start=start):
            value = halo_ref[side].reshape(HALO_OUT * FRAME_COLUMNS, 128)
            weights = (high_ref, lower_ref)
            gout = (rim_high[side], rim_low[side])
            q, _ = second_grad(gout, weights, k_ref, value, slope, slice(0, 128))
            edge = grad_in(q.reshape(HALO_OUT, SUB, SUB, 128), halo_ref[side])
            grad[start : start + HALO_OUT, 2 : SUB + 2] = edge
            pad[start : start + HALO_OUT, 2 : SUB + 2] = act(hid_halo_ref[side])

        @pl.when(side_ref[side] == 0)
        def _(start=start):
            clear_rows(pad, start, HALO_OUT)
            clear_rows(grad, start, HALO_OUT)

    raise_all(pad, 0, raised)

    def point_groups(i, _):
        for g in (2 * i, 2 * i + 1):
            for c in range(SUB):
                mine = [grad[GROUP * g + HALO_OUT + k, c + 2] for k in range(GROUP)]
                for p, value in enumerate(spread_points(mine)):
                    points[g, p, c] = value
        return 0

    lax.fori_loop(0, rows // GROUP // 2, point_groups, 0)
    zero = jnp.zeros((SUB, 128), F32)
    factors = tap_factors()
    tap_sums = [None] * TAPS
    for p in range(0, POINTS, 2):

        def weight_groups(i, acc, p=p):
            acc = list(acc)
            for g in (2 * i, 2 * i + 1):
                for k in range(2):
                    values = [raised[g, p + k, c] for c in range(SUB + K - 1)]
                    for c in range(SUB):
                        mine = points[g, p + k, c]
                        for b in range(K):
                            at = (k * 2 + c % 2) * K + b
                            acc[at] = acc[at] + values[c + b] * mine
            return tuple(acc)

        acc = lax.fori_loop(0, rows // GROUP // 2, weight_groups, (zero,) * (4 * K))
        for k in range(2):
            for b in range(K):
                value = jnp.sum(acc[2 * k * K + b] + acc[(2 * k + 1) * K + b], axis=0, keepdims=True)
                for a in range(K):
                    if factors[p + k][a] != 0.0:
                        term = value * factors[p + k][a]
                        old = tap_sums[a * K + b]
                        tap_sums[a * K + b] = term if old is None else old + term
    for tap in range(TAPS):
        tap_ref[tap : tap + 1] = tap_sums[tap]

    raise_taps(w_ref, taps, flipped=True, scale=0.5)
    raise_all(grad, 0, raised)

    def group(g, carry):
        one, two = carry
        for columns in (range(0, SUB // 2), range(SUB // 2, SUB)):
            for c, values in zip(columns, four_rows(raised, taps, g, columns)):
                for o, value in enumerate(values):
                    h = hid_ref[GROUP * g + o, c] * terms[0] + terms[1]
                    value = value * slope_half(h)
                    out_ref[GROUP * g + o, c] = value
                    one = one + value
                    two = two + value * h
        return one, two

    one, two = lax.fori_loop(0, rows // GROUP, group, (zero, zero))
    one, two = jnp.sum(one, axis=0, keepdims=True), jnp.sum(two, axis=0, keepdims=True)
    sum_ref[0:1] = one
    sum_ref[1:2] = (2.0 * two - bias_ref[0:1] * one) / gain_ref[0:1]


def spread_back(
    count, side, top, low, hid, hid_halo, own, halo, q, weights, gains, biases, taps, sums_one, sums_two, backs
):
    rows, hidden = own.shape[0], own.shape[-1]
    arrays = [hid, hid_halo, own, halo, q, *weights, gains, biases, taps, *sums_one, *sums_two, *backs]
    rim_shape = (2, HALO_OUT * FRAME_COLUMNS, weights[0].shape[0])
    return pl.pallas_call(
        partial(spread_back_kernel, len(backs), count),
        grid=(hidden // 128,),
        in_specs=[pl.BlockSpec(memory_space=pltpu.SMEM), whole(top.shape), whole(low.shape)]
        + [lanes(a.shape) for a in arrays],
        out_specs=[lanes((rows, SUB, SUB, hidden)), lanes((2, hidden)), lanes((TAPS, hidden))],
        out_shape=[
            jax.ShapeDtypeStruct((rows, SUB, SUB, hidden), F32),
            jax.ShapeDtypeStruct((2, hidden), F32),
            jax.ShapeDtypeStruct((TAPS, hidden), F32),
        ],
        scratch_shapes=[
            pltpu.VMEM((rows + 2 * HALO_OUT, SUB + 4, SUB, 128), F32),
            pltpu.VMEM((rows + 2 * HALO_OUT, SUB + 4, SUB, 128), F32),
            pltpu.VMEM((5, SUB, 128), F32),
            pltpu.VMEM(rim_shape, BF16),
            pltpu.VMEM(rim_shape, BF16),
            pltpu.VMEM((rows // GROUP, POINTS, SUB + 4, SUB, 128), F32),
            pltpu.VMEM((rows // GROUP, POINTS, SUB, SUB, 128), F32),
            pltpu.VMEM((POINTS * K, SUB, 128), F32),
        ],
        compiler_params=params(),
        cost_estimate=cost(150),
        name="spread_back",
    )(side, top, low, *arrays)


def expand_grad(q_ref, hid_ref, terms, cut):
    a, b, c = terms
    return split(q_ref[0, :, cut] * a[:, cut] + (hid_ref[0, :, cut] * b[:, cut] + c[:, cut]))


def input_kernel(parts, count, start, q_ref, hid_ref, gout_ref, gain_ref, w_high, w_low, *rest):
    sums, backs, out_ref = rest[:parts], rest[parts : 2 * parts], rest[2 * parts]
    nz, _, chans, area = out_ref.shape
    terms = back_terms(total(sums), total(backs), count, gain_ref[0:1])
    out = None
    for cut in chunks(w_high.shape[0]):
        term = dot3(expand_grad(q_ref, hid_ref, terms, cut), (w_high[cut], w_low[cut]))
        out = term if out is None else out + term
    own = gout_ref[:, 0]
    if own.shape[2] > area:
        own = own[:, :, start : start + area]
    out_ref[:, 0] = own + out.T.reshape(nz, chans, area)


def input_grad(count, start, width, q, hid, gout, gains, w_high, w_low, sums, backs):
    nz, bands, chans, area = gout.shape
    hidden = w_high.shape[0]
    at = start // width
    fixed = [gains, w_high, w_low, *sums, *backs]
    if width % 128 == 0:
        gout_spec = pl.BlockSpec((nz, 1, chans, width), lambda t: (0, t, 0, at))
    else:
        gout_spec = pl.BlockSpec((nz, 1, chans, area), lambda t: (0, t, 0, 0))
    return pl.pallas_call(
        partial(input_kernel, len(sums), count, start),
        grid=(bands,),
        in_specs=[
            pl.BlockSpec((1, width, hidden), lambda t: (t, at, 0)),
            pl.BlockSpec((1, width, hidden), lambda t: (t, at, 0)),
            gout_spec,
        ]
        + [whole(v.shape) for v in fixed],
        out_specs=pl.BlockSpec((nz, 1, chans, width), lambda t: (0, t, 0, 0)),
        out_shape=jax.ShapeDtypeStruct((nz, bands, chans, width), F32),
        compiler_params=params(),
        cost_estimate=cost(12),
        name="input_grad",
    )(q, hid, gout, *fixed)


def weight_kernel(chans, ids_ref, q_ref, x_ref, tap_ref, one_ref, two_ref, val_ref, col_ref, *rest):
    outs, acc, small = rest[:-2], rest[-2], rest[-1]
    nz, _, _, area = x_ref.shape
    chan_all, hidden = acc.shape
    width = hidden // nz
    t = pl.program_id(0)

    @pl.when(t == 0)
    def _():
        acc[...] = jnp.zeros_like(acc)
        small[...] = jnp.zeros_like(small)
        small[0:TAPS] = tap_ref[...]
        small[TAPS : TAPS + 1] = one_ref[1:2]
        small[TAPS + 1 : TAPS + 2] = two_ref[1:2]
        small[TAPS + 2 : TAPS + 3] = one_ref[0:1]
        small[TAPS + 3 : TAPS + 4] = two_ref[0:1]
        lead = (ids_ref[1] == 0).astype(F32)
        logit, pooled = val_ref[2:3] * lead, val_ref[3:4]
        reduced = col_ref.shape[0]
        grad_sq = col_ref[:, 1:2] * lead
        g_sq = grad_sq * pooled
        g_ex = col_ref[:, 0:1] * logit
        grad_row = jnp.broadcast_to(grad_sq, (reduced, 128)).T[0:1]
        for z in range(nz):
            own, at = slice(z * chans, (z + 1) * chans), z * width
            small[32 : 32 + reduced, at : at + chans] = g_sq[:, own]
            small[32 : 32 + reduced, at + chans : at + 2 * chans] = g_ex[:, own]
            small[32:33, at + 2 * chans : at + 3 * chans] = logit[:, own]
            small[33:34, at + 2 * chans : at + 2 * chans + reduced] = grad_row

    x = split(x_ref[:, 0].reshape(chan_all, area))
    for cut in chunks(hidden):
        acc[:, cut] += dot3(x, split(q_ref[0, :, cut]))

    @pl.when(t == pl.num_programs(0) - 1)
    def _():
        n = sum(out.shape[0] for out in outs)
        r, m = chan_all // n, SMALL // n
        for core, out in enumerate(outs):
            for i in range(out.shape[0]):
                p = ids_ref[0] ^ (i * len(outs) + core)
                out[i, 0:r] = acc[pl.ds(pl.multiple_of(p * r, r), r), :]
                out[i, r : r + m] = small[pl.ds(pl.multiple_of(p * m, m), m), :]


def weight_grad(ids, shape, q, x, taps, one, two, values, columns):
    nz, bands, chans, area = x.shape
    hidden = q.shape[2]
    chan_all = nz * chans
    fixed = [taps, one, two, values, columns]
    pieces, chips = shape
    shape = (chips, (chan_all + SMALL) // (pieces * chips), hidden)
    grid, tall, put, wide = by_steps(nz, bands, chans, area)
    return pl.pallas_call(
        partial(weight_kernel, chans),
        grid=grid,
        in_specs=[
            pl.BlockSpec(memory_space=pltpu.SMEM),
            tall(hidden),
            wide,
        ]
        + [whole(v.shape) for v in fixed],
        out_specs=[whole(shape)] * pieces,
        out_shape=[jax.ShapeDtypeStruct(shape, F32)] * pieces,
        scratch_shapes=[pltpu.VMEM((chan_all, hidden), F32), pltpu.VMEM((SMALL, hidden), F32)],
        compiler_params=params(),
        cost_estimate=cost(7),
        name="weight_grad",
    )(ids, q, x, *fixed)


def merge_kernel(one_ref, two_ref, *outs):
    for i, out in enumerate(outs):
        out[...] = one_ref[i] + two_ref[i]


def merge(one, two):
    n = one.shape[0]
    return pl.pallas_call(
        merge_kernel,
        grid=(1,),
        in_specs=[whole(one.shape), whole(two.shape)],
        out_specs=[whole(one.shape[1:])] * n,
        out_shape=[jax.ShapeDtypeStruct(one.shape[1:], F32)] * n,
        compiler_params=params(),
        cost_estimate=cost(2),
        name="merge",
    )(one, two)


def collect_kernel(n, nz, parts, count, ids_ref, early_ref, gram_ref, high_ref, low_ref, gain_ref, *rest):
    pieces, sums, backs = rest[:n], rest[n : n + parts], rest[n + parts : n + 2 * parts]
    outs, acc = rest[n + 2 * parts : -1], rest[-1]
    value = total(pieces)
    rows, width = value.shape[0], acc.shape[2]
    r, chan_all = early_ref.shape[0], high_ref.shape[0]
    a, b, c = back_terms(total(sums), total(backs), count, gain_ref[0:1])
    gram = gram_ref[...]
    hid = dot3(split(gram[:, 0:chan_all]), (high_ref[...], low_ref[...]))
    grad = a * value[0:r] + (b * hid + c * gram[:, chan_all : chan_all + 1])
    for z in range(nz):
        here = slice(z * width, (z + 1) * width)
        acc[z, 0:r] = grad[:, here]
        acc[z, r:rows] = value[r:, here]
        acc[z, rows:] = early_ref[:, here]
    for k, out in enumerate(outs):
        out[...] = acc[ids_ref[2] ^ k]


def collect(count, ids, nz, pieces, early, gram, w_high, w_low, gains, sums, backs):
    width = early.shape[1] // nz
    rows = pieces[0].shape[0] + early.shape[0]
    arrays = [early, gram, w_high, w_low, gains, *pieces, *sums, *backs]
    return pl.pallas_call(
        partial(collect_kernel, len(pieces), nz, len(sums), count),
        grid=(1,),
        in_specs=[pl.BlockSpec(memory_space=pltpu.SMEM)] + [whole(a.shape) for a in arrays],
        out_specs=[whole((rows, width))] * nz,
        out_shape=[jax.ShapeDtypeStruct((rows, width), F32)] * nz,
        scratch_shapes=[pltpu.VMEM((nz, rows, width), F32)],
        compiler_params=params(),
        cost_estimate=cost(3),
        name="collect",
    )(ids, *arrays)


def segments(chan_in, hidden_dev, chan_dev, reduced, tap_count, hidden_all):
    seg_sizes = [
        chan_in * hidden_dev,
        tap_count * hidden_dev,
        2 * hidden_dev,
        2 * hidden_dev,
        hidden_dev * chan_in,
        chan_dev * reduced,
        reduced,
        reduced * chan_dev,
        chan_dev,
    ]
    seg_rates = [
        0.5 / math.sqrt(chan_in),
        0.5 / math.sqrt(tap_count),
        0.3,
        0.3,
        0.5 * math.sqrt(8.0 / hidden_all),
        2.0 / math.sqrt(chan_in),
        0.3,
        1.0 / math.sqrt(reduced),
        0.3,
    ]
    return (seg_sizes, seg_rates)


def pack_kernel(at_ref, we_ref, wp_ref, dw_ref, gain_ref, bias_ref, sq_ref, ex_ref, exb_ref, out_ref, small):
    p = at_ref[0]
    chan_in, width = we_ref.shape
    reduced, chans = sq_ref.shape
    m = small.shape[0] * out_ref.shape[0] // (2 * chan_in + small.shape[0])
    r = (out_ref.shape[0] - m) // 2
    small[...] = jnp.zeros_like(small)
    small[0:TAPS] = dw_ref[...]
    small[TAPS : TAPS + 2] = gain_ref[...]
    small[TAPS + 2 : TAPS + 4] = bias_ref[...]
    small[32 : 32 + reduced, 0:chans] = sq_ref[...]
    small[32 : 32 + reduced, chans : 2 * chans] = ex_ref[...]
    small[32:33, 2 * chans : 3 * chans] = exb_ref[...]
    out_ref[0:r] = we_ref[pl.ds(pl.multiple_of(p * r, r), r), :]
    if chan_in == width:
        out_ref[r : 2 * r] = wp_ref[pl.ds(pl.multiple_of(p * r, r), r), :]
    else:
        row, part = p * r % width, p * r // width
        out_ref[r : 2 * r] = wp_ref[
            pl.ds(pl.multiple_of(row, r), r), pl.ds(pl.multiple_of(part * width, 128), width)
        ]
    out_ref[2 * r : 2 * r + m] = small[pl.ds(pl.multiple_of(p * m, m), m), :]


def pack_weights(at, w_expand, w_dw, norm_gains, norm_biases, w_project, squeeze_matrix, excite_matrix, excite_bias_row):
    n_pix = lax.axis_size(PIX)
    chan_in, width = w_expand.shape
    arrays = [
        w_expand,
        w_project,
        w_dw,
        norm_gains,
        norm_biases,
        squeeze_matrix.T,
        excite_matrix,
        excite_bias_row[None],
    ]
    shape = ((2 * chan_in + SMALL) // n_pix, width)
    return pl.pallas_call(
        pack_kernel,
        grid=(1,),
        in_specs=[pl.BlockSpec(memory_space=pltpu.SMEM)] + [whole(a.shape) for a in arrays],
        out_specs=whole(shape),
        out_shape=jax.ShapeDtypeStruct(shape, F32),
        scratch_shapes=[pltpu.VMEM((SMALL, width), F32)],
        compiler_params=params(),
        cost_estimate=cost(2),
        name="pack_weights",
    )(at, *arrays)


def weights_kernel(
    chan_in,
    chans,
    orders,
    base_ref,
    *refs,
):
    slabs = refs[: len(orders)]
    (
        we_high,
        we_low,
        wet_high,
        wet_low,
        wp_high,
        wp_low,
        wpt_ref,
        tap_ref,
        gain_ref,
        bias_ref,
        sqt_ref,
        ex_ref,
        exb_ref,
        first,
        second,
        small,
    ) = refs[len(orders) :]
    nz, width = first.shape[0], first.shape[2]
    n_pix = sum(len(order) for order in orders)
    r, m = chan_in // n_pix, SMALL // n_pix
    reduced = ex_ref.shape[0]
    for ref, order in zip(slabs, orders):
        for i, p in enumerate(order):
            at = base_ref[0] ^ p
            wide = pl.ds(pl.multiple_of(at * r, r), r)
            for z in range(nz):
                here = slice(z * width, (z + 1) * width)
                group = base_ref[1] ^ z
                first[group, wide, :] = ref[i, 0:r, here]
                second[group, wide, :] = ref[i, r : 2 * r, here]
                small[group, pl.ds(pl.multiple_of(at * m, m), m), :] = ref[i, 2 * r : 2 * r + m, here]
    parts = chan_in // width
    for z in range(nz):
        here = slice(z * width, (z + 1) * width)
        own = slice(z * chans, (z + 1) * chans)
        we = first[z]
        we_high[:, here], we_low[:, here] = split(we)
        wet_high[here], wet_low[here] = split(we.T)
        for h in range(parts):
            wp = second[z, h * width : (h + 1) * width]
            cols = slice(h * width, (h + 1) * width)
            wp_high[here, cols], wp_low[here, cols] = split(wp)
            wpt_ref[cols, here] = wp.T
        for tap in range(TAPS):
            tap_ref[tap, :, here] = jnp.broadcast_to(small[z, tap : tap + 1], (SUB, width))
        gain_ref[:, here] = small[z, TAPS : TAPS + 2]
        bias_ref[:, here] = small[z, TAPS + 2 : TAPS + 4]
        sqt_ref[:, own] = small[z, 32 : 32 + reduced, 0:chans]
        ex_ref[:, own] = small[z, 32 : 32 + reduced, chans : 2 * chans]
        exb_ref[:, own] = small[z, 32:33, 2 * chans : 3 * chans]


def order_weights(base, slabs, orders, nz, chan_in, chans, reduced):
    hidden = slabs[0].shape[2]
    width = hidden // nz
    shapes = (
        [((chan_in, hidden), BF16)] * 2
        + [((hidden, chan_in), BF16)] * 4
        + [
            ((chan_in, hidden), F32),
            ((TAPS, SUB, hidden), F32),
            ((2, hidden), F32),
            ((2, hidden), F32),
            ((reduced, chan_in), F32),
            ((reduced, chan_in), F32),
            ((1, chan_in), F32),
        ]
    )
    return pl.pallas_call(
        partial(weights_kernel, chan_in, chans, orders),
        grid=(1,),
        in_specs=[pl.BlockSpec(memory_space=pltpu.SMEM)] + [whole(a.shape) for a in slabs],
        out_specs=[whole(shape) for shape, _ in shapes],
        out_shape=[jax.ShapeDtypeStruct(shape, kind) for shape, kind in shapes],
        scratch_shapes=[
            pltpu.VMEM((nz, chan_in, width), F32),
            pltpu.VMEM((nz, chan_in, width), F32),
            pltpu.VMEM((nz, SMALL, width), F32),
        ],
        compiler_params=params(),
        cost_estimate=cost(3),
        name="order_weights",
    )(base, *slabs)


def thirds(v):
    high = v.astype(BF16)
    rest = v - high.astype(F32)
    mid = rest.astype(BF16)
    return high, mid, (rest - mid.astype(F32)).astype(BF16)


def choose(chosen, v):
    high, mid, low = thirds(v)
    return (dot(chosen, high) + dot(chosen, mid)) + dot(chosen, low)


def choose_lanes(v, chosen):
    high, mid, low = thirds(v)
    return (dot(high, chosen) + dot(mid, chosen)) + dot(low, chosen)


def ones(condition):
    return condition.astype(F32).astype(BF16)


def lay_flat(v, start, width):
    n, m = v.shape
    place = lax.broadcasted_iota(jnp.int32, (m, width), 1) - start
    column_of = lax.broadcasted_iota(jnp.int32, (m, width), 0)
    wide = choose_lanes(v, ones((place + 64 * m) % m == column_of))
    place = lax.broadcasted_iota(jnp.int32, (n, width), 1) - start
    low = lax.broadcasted_iota(jnp.int32, (n, width), 0) * m
    return jnp.sum(jnp.where((place >= low) & (place < low + m), wide, 0.0), axis=0, keepdims=True)


def fill_blocks(out, first, middle, flip, last, squeeze, down, excite, bias):
    blocks, length = out.shape
    tiles, n, _ = first.shape
    width = tiles * 128
    per = length // width
    for i in range(per):
        for u in range(tiles):
            at = i * width + u * 128
            out[0 : n // per, at : at + 128] = first[u, pl.ds(i, n // per, stride=per), :]
    for k in range(TAPS + 4):
        row = n + k
        out[row // per : row // per + 1, row % per * width : (row % per + 1) * width] = middle[k : k + 1, :]
    base = n + TAPS + 4
    parts = last // width
    step = per // parts
    for h in range(parts):
        for e in range(step):
            row = base + parts * e + h
            block, slot = row // per, row % per
            count = width // step
            for u in range(tiles):
                at = slot * width + u * 128
                out[block : block + count, at : at + 128] = flip[
                    h * tiles + u, pl.ds(e, count, stride=step), :
                ]
    start = (base + width * parts) * width
    block = start // length
    start -= block * length
    tail_width = (blocks - block) * length
    tail = lay_flat(squeeze, start, tail_width)
    start += squeeze.shape[0] * squeeze.shape[1]
    tail = tail + lay_flat(down, start, tail_width)
    start += down.shape[1]
    tail = tail + lay_flat(excite, start, tail_width)
    start += excite.shape[0] * excite.shape[1]
    tail = tail + lay_flat(bias, start, tail_width)
    inside = lax.broadcasted_iota(jnp.int32, (1, length), 1)
    kept = jnp.where(inside < (base + width * parts) * width - block * length, out[block : block + 1, :], 0.0)
    out[block : block + 1, :] = kept + tail[:, 0:length]
    for k in range(1, blocks - block):
        out[block + k : block + k + 1, :] = tail[:, k * length : (k + 1) * length]


def prepare_kernel(
    orders,
    base_ref,
    col_ref,
    we_ref,
    dw_ref,
    gain_ref,
    bias_ref,
    wp_ref,
    sq_ref,
    down_ref,
    ex_ref,
    exb_ref,
    *rest,
):
    slabs = rest[: len(orders)]
    weight, first_ref, second_ref, head, flip, middle, moments, ranked = rest[len(orders) :]
    blocks, length = weight.shape
    chan_in, width = we_ref.shape
    devices, room = moments.shape[1:3]
    middle[0:TAPS] = dw_ref[...]
    middle[TAPS : TAPS + 2] = gain_ref[...]
    middle[TAPS + 2 : TAPS + 4] = bias_ref[...]
    for u in range(width // 128):
        head[u] = we_ref[:, u * 128 : (u + 1) * 128]
    for u in range(chan_in // 128):
        flip[u] = wp_ref[:, u * 128 : (u + 1) * 128]
    fill_blocks(
        weight, head, middle, flip, chan_in, sq_ref[...].T, down_ref[...], ex_ref[...], exb_ref[...]
    )
    at = 0
    home = jnp.zeros(col_ref.shape, jnp.int32)
    own_col = col_ref[...]
    for ref, order in zip(slabs, orders):
        for k, p in enumerate(order):
            for m in range(2):
                moments[m, at] = ref[k, m * room : (m + 1) * room]
            home = jnp.where(own_col == base_ref[0] ^ p, at, home)
            at += 1
    ranked[...] = jnp.broadcast_to(own_col.astype(F32), ranked.shape)
    own_row = ranked[...].T[0:1].astype(jnp.int32)
    i = lax.broadcasted_iota(jnp.int32, (blocks, blocks), 0)
    j = lax.broadcasted_iota(jnp.int32, (blocks, blocks), 1)
    earlier = (own_row == own_col) & (j < i)
    rank = jnp.sum(jnp.where(earlier, 1.0, 0.0), axis=1, keepdims=True).astype(jnp.int32)
    slot = home * room + rank
    chosen = ones(lax.broadcasted_iota(jnp.int32, (blocks, devices * room), 1) == slot)
    first_ref[...] = choose(chosen, moments[0].reshape(devices * room, length))
    second_ref[...] = choose(chosen, moments[1].reshape(devices * room, length))


def prepare(base, owners, weights, slabs, orders, length):
    blocks = owners.shape[0]
    chan_in, width = weights[0].shape
    devices = sum(len(o) for o in orders)
    arrays = [owners, *weights, *slabs]
    return pl.pallas_call(
        partial(prepare_kernel, orders),
        grid=(1,),
        in_specs=[pl.BlockSpec(memory_space=pltpu.SMEM)] + [whole(a.shape) for a in arrays],
        out_specs=[whole((blocks, length))] * 3,
        out_shape=[jax.ShapeDtypeStruct((blocks, length), F32)] * 3,
        scratch_shapes=[
            pltpu.VMEM((width // 128, chan_in, 128), F32),
            pltpu.VMEM((chan_in // 128, width, 128), F32),
            pltpu.VMEM((32, width), F32),
            pltpu.VMEM((2, devices, slabs[0].shape[1] // 2, length), F32),
            pltpu.VMEM((blocks, 128), F32),
        ],
        compiler_params=params(),
        cost_estimate=cost(1),
        name="prepare",
    )(base, *arrays)


def adam_kernel(
    bounds,
    rates,
    orders,
    chans,
    reduced,
    me_ref,
    col_ref,
    weight_ref,
    old_one_ref,
    old_two_ref,
    first_ref,
    second_ref,
    *rest,
):
    grad_slabs = rest[: len(orders)]
    first_out, second_out, new_ref, grad, head, flip, tall, small, ranked = rest[len(orders) :]
    blocks, length = grad.shape
    capacity = first_ref.shape[0]
    chan_in, width = tall.shape
    devices = sum(len(order) for order in orders)
    r, m = chan_in // devices, SMALL // devices
    for ref, order in zip(grad_slabs, orders):
        for k, i in enumerate(order):
            p = me_ref[1] ^ i
            for u in range(width // 128):
                head[u, pl.ds(pl.multiple_of(p * r, r), r), :] = ref[k, 0:r, u * 128 : (u + 1) * 128]
            small[pl.ds(pl.multiple_of(p * m, m), m), :] = ref[k, r : r + m]
            tall[pl.ds(pl.multiple_of(p * r, r), r), :] = ref[k, r + m : 2 * r + m]
    for u in range(chan_in // 128):
        flip[u] = tall[u * 128 : (u + 1) * 128].T
    fill_blocks(
        grad,
        head,
        small,
        flip,
        chan_in,
        small[32 : 32 + reduced, 0:chans].T,
        small[33:34, 2 * chans : 2 * chans + reduced],
        small[32 : 32 + reduced, chans : 2 * chans],
        small[32:33, 2 * chans : 3 * chans],
    )

    own_col = col_ref[...]
    ranked[...] = jnp.broadcast_to(own_col.astype(F32), ranked.shape)
    own_row = ranked[...].T[0:1].astype(jnp.int32)
    i = lax.broadcasted_iota(jnp.int32, (blocks, blocks), 0)
    j = lax.broadcasted_iota(jnp.int32, (blocks, blocks), 1)
    earlier = (own_row == own_col) & (i < j)
    rank = jnp.sum(jnp.where(earlier, 1.0, 0.0), axis=0, keepdims=True).astype(jnp.int32)
    g = grad[...]
    mine = lax.broadcasted_iota(jnp.int32, (capacity, blocks), 0)
    owned = choose(ones((mine == rank) & (own_row == me_ref[0])), g)
    first_out[:, 0] = beta_first * first_ref[:, 0] + (1.0 - beta_first) * owned
    second_out[:, 0] = beta_second * second_ref[:, 0] + (1.0 - beta_second) * owned * owned

    first = beta_first * old_one_ref[...] + (1.0 - beta_first) * g
    second = beta_second * old_two_ref[...] + (1.0 - beta_second) * g * g
    first_hat = first / (1.0 - beta_first**STEP)
    second_hat = second / (1.0 - beta_second**STEP)
    place = lax.broadcasted_iota(jnp.int32, (blocks, length), 0) * length + lax.broadcasted_iota(
        jnp.int32, (blocks, length), 1
    )
    rate = jnp.zeros((blocks, length), F32)
    for bound, value in zip(reversed(bounds), reversed(rates)):
        rate = jnp.where(place < bound, jnp.float32(value), rate)
    grad[...] = weight_ref[...] * (1.0 - rate * weight_decay) - rate * first_hat / (
        jnp.sqrt(second_hat) + adam_eps
    )
    for k in range(blocks):
        end = min((k + 1) * length, new_ref.shape[1])
        new_ref[:, k * length : end] = grad[k : k + 1, 0 : end - k * length]


def adam(ids, owners, prepared, first, second, grads, orders, chan_in, chans, reduced, bounds, rates):
    blocks, length = prepared[0].shape
    width = grads[0].shape[2]
    arrays = [owners, *prepared, first, second, *grads]
    new_shape = (1, bounds[-1])
    return pl.pallas_call(
        partial(adam_kernel, bounds, rates, orders, chans, reduced),
        grid=(1,),
        in_specs=[pl.BlockSpec(memory_space=pltpu.SMEM)] + [whole(a.shape) for a in arrays],
        out_specs=[whole(first.shape), whole(second.shape), whole(new_shape)],
        out_shape=[
            jax.ShapeDtypeStruct(first.shape, F32),
            jax.ShapeDtypeStruct(second.shape, F32),
            jax.ShapeDtypeStruct(new_shape, F32),
        ],
        scratch_shapes=[
            pltpu.VMEM((blocks, length), F32),
            pltpu.VMEM((width // 128, chan_in, 128), F32),
            pltpu.VMEM((chan_in // 128, width, 128), F32),
            pltpu.VMEM((chan_in, width), F32),
            pltpu.VMEM((SMALL, width), F32),
            pltpu.VMEM((blocks, 128), F32),
        ],
        compiler_params=params(),
        cost_estimate=cost(10),
        name="adam",
    )(ids, *arrays)


def deal_rows(rows):
    n_pix = lax.axis_size(PIX)
    n, hidden = rows.shape
    dealt = lax.all_to_all(rows.reshape(n_pix, n // n_pix, hidden), PIX, 0, 0, tiled=True)
    return jnp.sum(dealt, axis=0)


def together(*values):
    return lax.optimization_barrier(values)


def local(
    frames_raw,
    grad_out,
    col_offsets,
    flip_flags,
    owners,
    w_expand,
    w_dw,
    norm_gains,
    norm_biases,
    w_project,
    squeeze_matrix,
    se_down_bias,
    excite_matrix,
    excite_bias_row,
    first_moment,
    second_moment,
):
    nz, nhi, nlo = (lax.axis_size(axis) for axis in ALL)
    frames, chans, stored = frames_raw.shape
    band = stored // WIN
    area = band * FRAME_COLUMNS
    rows = nlo * band
    chan_in, hidden_dev = w_expand.shape
    hidden = hidden_dev * nz
    reduced = squeeze_matrix.shape[1]
    group = nz // MB * nhi * nlo
    count = float(frames // MB * FRAME_ROWS * FRAME_COLUMNS)
    hi = lax.axis_index("hi")
    side = jnp.stack([(hi > 0).astype(jnp.int32), (hi < nhi - 1).astype(jnp.int32)])

    n_pix = nhi * nlo
    me = hi * nlo + lax.axis_index("lo")
    relative = me if near(n_pix) else 0 * me
    z_relative = lax.axis_index("chan") if near(n_pix) else 0 * me

    slab = pack_weights(
        me.astype(jnp.int32).reshape(1),
        w_expand,
        w_dw,
        norm_gains,
        norm_biases,
        w_project,
        squeeze_matrix,
        excite_matrix,
        excite_bias_row,
    )
    crops = crop(frames_raw, col_offsets, flip_flags)
    crops, *slab = together(crops, *gather_chan(slab))
    x = deal(crops).reshape(nz, nlo, chans, area)
    ordered = order(grad_out)
    slabs, orders, ordered = gather_pix(jnp.concatenate(slab, axis=1), ordered)
    first_turned, second_turned = first_moment.transpose(1, 0, 2), second_moment.transpose(1, 0, 2)
    first_turned, second_turned, *slabs = together(first_turned, second_turned, *slabs)
    room = ((0, -first_moment.shape[1] % SUB), (0, 0))
    moments = jnp.concatenate([jnp.pad(v[:, 0], room) for v in (first_turned, second_turned)])
    (
        we_high,
        we_low,
        wet_high,
        wet_low,
        wp_high,
        wp_low,
        w_project_t,
        taps,
        gains,
        biases,
        sq_t,
        ex_all,
        ex_bias,
    ) = order_weights(
        jnp.stack([relative, z_relative]), slabs, orders, nz, chan_in, chans, reduced
    )
    se_weights = [sq_t, se_down_bias[:, None], ex_all, ex_bias]
    x, ordered, we_high, we_low, moments = together(x, ordered, we_high, we_low, moments)
    moments = lax.all_gather(moments, PIX, axis=0)

    def as_rows(v):
        return v.reshape(rows, SUB, SUB, hidden)

    def as_bands(v):
        return v.reshape(nlo, area, hidden)

    def as_sides(v, n):
        return v.reshape(2, n, SUB, SUB, hidden)

    hid, sums_one, gram = expand(x, we_high, we_low)
    later = [x]
    sums_one = shares(sums_one, 1, group, later)
    [x] = later
    top, low = rims(x, HALO_IN, band)
    gout = deal(ordered).reshape(nz, nlo, chans, area)
    g_top, g_low = rims(gout, HALO_OUT, band)
    spatial, spatial_halo, hid_halo, sums_two = spread(
        count, side, top, low, as_rows(hid), we_high, we_low, gains, biases, taps, sums_one
    )
    sums_two = shares(sums_two, 1, group)
    m, s, se_part, proj = gather(
        count, as_bands(spatial), gout, gains, biases, w_project_t, wp_high, wp_low, sums_two
    )
    ses = shares(se_part, nlo, nhi)
    ses, g_top, g_low = together(ses, g_top, g_low)
    q, back_two, values, columns, *w4, out, g_project = proj_back(
        count, as_bands(spatial), gout, proj, x, gains, biases, w_project_t, m, s, se_weights, ses, sums_two
    )
    backs_two = shares(back_two, 1, group)
    out = deal(out.reshape(frames, chans, area))
    q1, back_one, g_dw = spread_back(
        count,
        side,
        g_top,
        g_low,
        as_rows(hid),
        hid_halo,
        spatial,
        spatial_halo,
        as_rows(q),
        w4,
        gains,
        biases,
        taps,
        sums_one,
        sums_two,
        backs_two,
    )
    later = [q1]
    backs_one = shares(back_one, 1, group, later)
    [q1] = later

    ids = jnp.stack([relative, hi, z_relative]).astype(jnp.int32)
    pieces = weight_grad(
        ids, (2, n_pix // 2) if near(n_pix) else (1, 1), as_bands(q1), x, g_dw, back_one, back_two, values, columns
    )
    if near(n_pix):
        early = lax.psum_scatter(g_project, PIX, scatter_dimension=0, tiled=True)
        gram = lax.psum_scatter(gram, PIX, scatter_dimension=0, tiled=True)
    else:
        early, gram = deal_rows(g_project), deal_rows(gram)
    q1, out, early, gram, moments, *pieces = together(q1, out, early, gram, moments, *pieces)

    def input_part(start, width, q1):
        grad = input_grad(
            count, start, width, as_bands(q1), hid, gout, gains, wet_high, wet_low, sums_one, backs_one
        )
        return grad.reshape(frames, chans, width)

    most = area // 2
    grad_one = input_part(0, most, q1)
    if near(n_pix):
        pieces = [pieces[0], exchange(pieces[1], 1)]
    grad_one, q1, *pieces = together(grad_one, q1, *pieces)
    if near(n_pix):
        pieces = list(merge(*pieces))
        pieces[0], out = together(pieces[0], out)
        pieces = [pieces[0]] + [exchange(pieces[i], 2 * i) for i in range(1, n_pix // 2)]
    else:
        whole_rows = pieces[0][0]
        pieces = [jnp.concatenate([deal_rows(whole_rows[:chan_in]), deal_rows(whole_rows[chan_in:])])]
    grad_two = input_part(most, area - most, q1)
    output = restore(out)
    weights = [
        w_expand,
        w_dw,
        norm_gains,
        norm_biases,
        w_project,
        squeeze_matrix.T,
        se_down_bias[None],
        excite_matrix,
        excite_bias_row[None],
    ]
    block_len = first_moment.shape[2]
    natural = [list(range(n_pix))]
    base = jnp.zeros((1,), jnp.int32)
    prepared = prepare(base, owners, weights, [moments], natural, block_len)
    grad_two, output, *pieces = together(grad_two, output, *pieces)
    groups = collect(count, ids, nz, pieces, early, gram, we_high, we_low, gains, sums_one, backs_one)
    if near(n_pix):
        others = [groups[0]] + [exchange(groups[k], k * n_pix) for k in range(1, nz)]
    else:
        others = list(lax.all_to_all(jnp.stack(groups), "chan", 0, 0, tiled=True))
    grad_one = deal(grad_one)
    grad_one, grad_two, *groups = together(grad_one, grad_two, *groups)
    summed = sum(others[1:], others[0])
    grad_two = deal(grad_two)
    grads, _, prepared = gather_pix(summed, prepared)
    seg_sizes, seg_rates = segments(chan_in, hidden_dev, chans, reduced, TAPS, hidden)
    bounds = [sum(seg_sizes[: i + 1]) for i in range(len(seg_sizes))]
    first_next, second_next, new_params = adam(
        jnp.stack([me, relative]).astype(jnp.int32),
        owners,
        prepared,
        first_turned,
        second_turned,
        grads,
        orders,
        chan_in,
        chans,
        reduced,
        bounds,
        seg_rates,
    )
    first_next, second_next = first_next.transpose(1, 0, 2), second_next.transpose(1, 0, 2)
    grad_frames = uncrop(grad_one, grad_two, col_offsets, flip_flags)
    return (output, grad_frames, first_next, second_next, new_params)


def solution(mesh):
    nz, n_pix = mesh.shape["chan"], mesh.shape["pix"]
    placed = (
        P(None, "chan", PIX),
        P(None, "chan", PIX),
        P(),
        P(),
        P(),
        P(None, "chan"),
        P(None, "chan"),
        P(None, "chan"),
        P(None, "chan"),
        P("chan", None),
        P("chan", None),
        P(),
        P(None, "chan"),
        P("chan"),
        P("chan", PIX, None),
        P("chan", PIX, None),
    )

    def run(*arrays):
        nlo = arrays[0].shape[0] // nz
        return jax.shard_map(
            local,
            mesh=Mesh(mesh.devices.reshape(nz, n_pix // nlo, nlo), ALL),
            in_specs=placed,
            out_specs=(
                P(None, "chan", PIX),
                P(None, "chan", PIX),
                P("chan", PIX, None),
                P("chan", PIX, None),
                P("chan", None),
            ),
            check_vma=False,
        )(*arrays)

    return run
```

```python
from functools import partial
import math

import jax
import jax.numpy as jnp
from jax import lax
from jax.experimental import pallas as pl
from jax.experimental.pallas import tpu as pltpu
from jax.sharding import Mesh, PartitionSpec as P

K = 5
FRAME_ROWS = 64
FRAME_COLUMNS = 64
CLIP_LEN = 4
MB = 4
STEP = 5
WIN = 80
SUB = 8
TAPS = K * K
HALO_IN = 4
SMALL = 64
HALO_OUT = 2

norm_eps = 1e-05
beta_first = 0.5
beta_second = 0.6
adam_eps = 1e-08
weight_decay = 0.1

F32 = jnp.float32
BF16 = jnp.bfloat16
ALL = ("chan", "hi", "lo")
PIX = ("hi", "lo")
SPREAD = ("chan", "lo")
VMEM_BYTES = 62 * 2**20


def params(spare=0):
    return pltpu.CompilerParams(vmem_limit_bytes=VMEM_BYTES - spare * 2**20, dimension_semantics=("arbitrary",))


def keep(x):
    return pltpu.with_memory_space_constraint(x, pltpu.VMEM)


def cost(us):
    return pl.CostEstimate(flops=int(us * 1.1e9), bytes_accessed=int(us * 3.5e6), transcendentals=0)


def sigmoid(v):
    return 0.5 * jnp.tanh(0.5 * v) + 0.5


def swish_half(h):
    return h + h * jnp.tanh(h)


def slope_half(h):
    t = jnp.tanh(h)
    return 1.0 + (t + h * (1.0 - t * t))


def split(v):
    high = v.astype(BF16)
    return high, (v - high.astype(F32)).astype(BF16)


def dot(a, b):
    return jnp.dot(a, b, preferred_element_type=F32)


def dot3(a, b):
    return dot(a[0], b[0]) + (dot(a[0], b[1]) + dot(a[1], b[0]))


def total(refs):
    value = refs[0][...]
    for ref in refs[1:]:
        value = value + ref[...]
    return value


def norm_terms(sums, count, gain, bias):
    mean = sums[0:1] / count
    inverse = lax.rsqrt(sums[1:2] / count - mean * mean + norm_eps)
    scale = gain * inverse
    return mean, inverse, scale, bias - mean * scale


def back_terms(sums, back, count, gain):
    mean = sums[0:1] / count
    inverse = lax.rsqrt(sums[1:2] / count - mean * mean + norm_eps)
    a = gain * inverse
    b = -a * inverse * (back[1:2] / count)
    return a, b, -a * (back[0:1] / count) - b * mean


def exchange(x, stride):
    n = lax.axis_size(ALL)
    return lax.ppermute(x, ALL, [(i, i ^ stride) for i in range(n)])


def shares(x, base, size, after=()):
    bits = size.bit_length() - 1
    parts = [x]
    if bits % 2:
        parts = [x, exchange(x, base)]
        base, bits = base * 2, bits - 1
    while bits:
        x = sum(parts[1:], parts[0])
        if after:
            x, *kept = together(x, *after)
            after[:] = kept
            after = ()
        parts = [x] + [exchange(x, base * k) for k in (1, 2, 3)]
        base, bits = base * 4, bits - 2
    return parts


def deal(x):
    return lax.all_to_all(x, SPREAD, 0, 0, tiled=True)


def edge(x, rows, band, first):
    if rows >= band:
        n = rows // band
        return x[:, :n] if first else x[:, x.shape[1] - n :]
    width = rows * FRAME_COLUMNS
    return x[:, :1, :, :width] if first else x[:, -1:, :, x.shape[3] - width :]


def rims(x, rows, band):
    n = lax.axis_size("hi")
    if n == 2:
        mine = jnp.where(lax.axis_index("hi") == 0, edge(x, rows, band, False), edge(x, rows, band, True))
        other = lax.ppermute(mine, "hi", [(0, 1), (1, 0)])
        return other, other
    down = [(i, i + 1) for i in range(n - 1)]
    up = [(i + 1, i) for i in range(n - 1)]
    top = lax.ppermute(edge(x, rows, band, False), "hi", down)
    low = lax.ppermute(edge(x, rows, band, True), "hi", up)
    return top, low


def near(n_pix):
    return n_pix == 8


def gather_pix(x, beside=None):
    n_pix = lax.axis_size(PIX)
    if not near(n_pix):
        return [lax.all_gather(x, PIX, axis=0)], [list(range(n_pix))], beside
    b = x[None]
    b = jnp.concatenate([b, exchange(b, 2)])
    if beside is not None:
        b, beside = together(b, beside)
    b = jnp.concatenate([b, exchange(b, 4)])
    return [b, exchange(b, 1)], [[0, 2, 4, 6], [1, 3, 5, 7]], beside


def gather_chan(x):
    nz, n_pix = lax.axis_size("chan"), lax.axis_size(PIX)
    if not near(n_pix):
        return list(lax.all_gather(x, "chan", axis=0))
    return [x] + [exchange(x, k * n_pix) for k in range(1, nz)]


def source_column(p, left, flip):
    row, c, s = p // FRAME_COLUMNS, (p // SUB) % SUB, p % SUB
    j = s * SUB + c
    return row * WIN + left + jnp.where(flip == 1, FRAME_COLUMNS - 1 - j, j)


def plain_place(p):
    row, c, s = p // FRAME_COLUMNS, (p // SUB) % SUB, p % SUB
    return row * FRAME_COLUMNS + s * SUB + c


def pick(x, chosen):
    rows = x.shape[0] * x.shape[1]
    high, low = split(x.reshape(rows, x.shape[2]))
    return (dot(high, chosen) + dot(low, chosen)).reshape(x.shape[0], x.shape[1], chosen.shape[1])


def crop_kernel(left_ref, flip_ref, raw_ref, out_ref):
    k = pl.program_id(0)
    width, area = raw_ref.shape[2], out_ref.shape[2]
    p = lax.broadcasted_iota(jnp.int32, (1, area), 1)
    place = source_column(p, left_ref[k], flip_ref[k])
    q = lax.broadcasted_iota(jnp.int32, (width, area), 0)
    out_ref[...] = pick(raw_ref[...], (q == place).astype(F32).astype(BF16))


def crop(raw, left, flip):
    frames, chans, width = raw.shape
    area = width // WIN * FRAME_COLUMNS
    return pl.pallas_call(
        crop_kernel,
        grid=(frames // CLIP_LEN,),
        in_specs=[
            pl.BlockSpec(memory_space=pltpu.SMEM),
            pl.BlockSpec(memory_space=pltpu.SMEM),
            pl.BlockSpec((CLIP_LEN, chans, width), lambda k: (k, 0, 0)),
        ],
        out_specs=pl.BlockSpec((CLIP_LEN, chans, area), lambda k: (k, 0, 0)),
        out_shape=jax.ShapeDtypeStruct((frames, chans, area), F32),
        compiler_params=params(),
        cost_estimate=cost(5),
        name="crop",
    )(left, flip, raw)


def order_kernel(x_ref, out_ref):
    area = x_ref.shape[2]
    p = lax.broadcasted_iota(jnp.int32, (1, area), 1)
    q = lax.broadcasted_iota(jnp.int32, (area, area), 0)
    out_ref[...] = pick(x_ref[...], (q == plain_place(p)).astype(F32).astype(BF16))


def order(x):
    frames, chans, area = x.shape
    return pl.pallas_call(
        order_kernel,
        grid=(frames // CLIP_LEN,),
        in_specs=[pl.BlockSpec((CLIP_LEN, chans, area), lambda k: (k, 0, 0))],
        out_specs=pl.BlockSpec((CLIP_LEN, chans, area), lambda k: (k, 0, 0)),
        out_shape=jax.ShapeDtypeStruct((frames, chans, area), F32),
        compiler_params=params(),
        cost_estimate=cost(25),
        name="order",
    )(x)


def restore_kernel(x_ref, out_ref):
    area = x_ref.shape[2]
    p = lax.broadcasted_iota(jnp.int32, (area, 1), 0)
    q = lax.broadcasted_iota(jnp.int32, (area, area), 1)
    out_ref[...] = pick(x_ref[...], (q == plain_place(p)).astype(F32).astype(BF16))


def restore(x):
    frames, chans, area = x.shape
    return pl.pallas_call(
        restore_kernel,
        grid=(frames // CLIP_LEN,),
        in_specs=[pl.BlockSpec((CLIP_LEN, chans, area), lambda k: (k, 0, 0))],
        out_specs=pl.BlockSpec((CLIP_LEN, chans, area), lambda k: (k, 0, 0)),
        out_shape=jax.ShapeDtypeStruct((frames, chans, area), F32),
        compiler_params=params(),
        cost_estimate=cost(1),
        name="restore",
    )(x)


def uncrop_kernel(left_ref, flip_ref, x_ref, y_ref, out_ref):
    k = pl.program_id(0)
    width = out_ref.shape[2]
    out = None
    for start, ref in ((0, x_ref), (x_ref.shape[2], y_ref)):
        area = ref.shape[2]
        q = lax.broadcasted_iota(jnp.int32, (area, width), 1)
        p = lax.broadcasted_iota(jnp.int32, (area, 1), 0) + start
        place = source_column(p, left_ref[k], flip_ref[k])
        term = pick(ref[...], (q == place).astype(F32).astype(BF16))
        out = term if out is None else out + term
    out_ref[...] = out


def uncrop(x, y, left, flip):
    frames, chans, area = x.shape
    width = (area + y.shape[2]) // FRAME_COLUMNS * WIN
    return pl.pallas_call(
        uncrop_kernel,
        grid=(frames // CLIP_LEN,),
        in_specs=[
            pl.BlockSpec(memory_space=pltpu.SMEM),
            pl.BlockSpec(memory_space=pltpu.SMEM),
            pl.BlockSpec((CLIP_LEN, chans, area), lambda k: (k, 0, 0)),
            pl.BlockSpec((CLIP_LEN, chans, y.shape[2]), lambda k: (k, 0, 0)),
        ],
        out_specs=pl.BlockSpec((CLIP_LEN, chans, width), lambda k: (k, 0, 0)),
        out_shape=jax.ShapeDtypeStruct((frames, chans, width), F32),
        compiler_params=params(),
        cost_estimate=cost(1),
        name="uncrop",
    )(left, flip, x, y)


def chunks(width):
    step = 256 if width % 256 == 0 else width
    return [slice(i, i + step) for i in range(0, width, step)]


def expand_kernel(x_ref, high_ref, low_ref, own_ref, sum_ref, gram_ref):
    @pl.when(pl.program_id(0) == 0)
    def _():
        sum_ref[...] = jnp.zeros_like(sum_ref)
        gram_ref[...] = jnp.zeros_like(gram_ref)

    chan_all, hidden = high_ref.shape
    plain = x_ref[:, 0].reshape(chan_all, x_ref.shape[3])
    turned = plain.T
    x = split(turned)
    for cut in chunks(hidden):
        y = dot3(x, (high_ref[:, cut], low_ref[:, cut]))
        own_ref[0, :, cut] = y
        sum_ref[0:1, cut] += jnp.sum(y, axis=0, keepdims=True)
        sum_ref[1:2, cut] += jnp.sum(y * y, axis=0, keepdims=True)
    gram_ref[:, 0:chan_all] += dot3(split(plain), x)
    gram_ref[:, chan_all:] += jnp.broadcast_to(jnp.sum(plain, axis=1, keepdims=True), (chan_all, 128))


def whole(shape):
    return pl.BlockSpec(shape, lambda *_: (0,) * len(shape))


def by_steps(nz, bands, chans, area):
    run = area
    n = area // run

    def tall(hidden):
        return pl.BlockSpec((1, run, hidden), lambda t: (t // n, t % n, 0))

    def out(hidden):
        return pl.BlockSpec((1, run, hidden), lambda t: (t // n, t % n, 0))

    wide = pl.BlockSpec((nz, 1, chans, run), lambda t: (0, t // n, 0, t % n))
    return (bands * n,), tall, out, wide


def expand(x, high, low):
    nz, bands, chans, area = x.shape
    grid, _, tall, wide = by_steps(nz, bands, chans, area)
    hidden = high.shape[1]
    return pl.pallas_call(
        expand_kernel,
        grid=grid,
        in_specs=[
            wide,
            whole(high.shape),
            whole(low.shape),
        ],
        out_specs=[
            tall(hidden),
            whole((2, hidden)),
            whole((nz * chans, nz * chans + 128)),
        ],
        out_shape=[
            jax.ShapeDtypeStruct((bands, area, hidden), F32),
            jax.ShapeDtypeStruct((2, hidden), F32),
            jax.ShapeDtypeStruct((nz * chans, nz * chans + 128), F32),
        ],
        compiler_params=params(),
        cost_estimate=cost(8),
        name="expand",
    )(x, high, low)


def fill_sides(pad, row):
    s = lax.broadcasted_iota(jnp.int32, (SUB, 128), 0)
    for k in range(2):
        left = pltpu.roll(pad[row, SUB + k], 1, 0)
        pad[row, k] = jnp.where(s == 0, 0.0, left)
        right = pltpu.roll(pad[row, 2 + k], SUB - 1, 0)
        pad[row, SUB + 2 + k] = jnp.where(s == SUB - 1, 0.0, right)


def clear_rows(pad, start, count):
    for row in range(start, start + count):
        pad[row] = jnp.zeros(pad.shape[1:], F32)


def tap_rows(pad, w_ref, start, count, c, flipped=False):
    acc = [None] * count
    for b in range(K):
        for row in range(count + K - 1):
            value = pad[start + row, c + b]
            for a in range(K):
                o = row - a
                if 0 <= o < count:
                    tap = a * K + b
                    term = value * w_ref[TAPS - 1 - tap if flipped else tap]
                    acc[o] = term if acc[o] is None else acc[o] + term
    return acc


def turn_rims(refs, side_ref, high, low):
    for side, ref in enumerate(refs):
        chan_all, width = ref.shape[0] * ref.shape[2], ref.shape[3]

        @pl.when(side_ref[side] == 1)
        def _(side=side, ref=ref, chan_all=chan_all, width=width):
            for k in range(ref.shape[1]):
                here = slice(k * width, (k + 1) * width)
                high[side, here], low[side, here] = split(ref[:, k].reshape(chan_all, width).T)


def raise_rows(d):
    e1, o1 = d[2] + d[6] - 4.25 * d[4], d[1] + d[5] - 4.25 * d[3]
    e2, o2 = 0.25 * d[2] - 1.25 * d[4] + d[6], 0.5 * d[1] - 2.5 * d[3] + 2.0 * d[5]
    e3, o3 = 4.0 * d[2] - 5.0 * d[4] + d[6], 2.0 * d[1] - 2.5 * d[3] + 0.5 * d[5]
    return [
        d[0] - d[6] + 5.25 * (d[4] - d[2]),
        e1 + o1,
        e1 - o1,
        e2 + o2,
        e2 - o2,
        e3 + o3,
        e3 - o3,
        d[7] - d[1] + 5.25 * (d[3] - d[5]),
    ]


POINT_SCALES = (1.0, -2.0 / 9.0, -2.0 / 9.0, 1.0 / 90.0, 1.0 / 90.0, 32.0 / 45.0, 32.0 / 45.0)
POINT_PLACES = (0.0, 1.0, -1.0, 2.0, -2.0, 0.5, -0.5)
POINTS = 8
GROUP = 4


def tap_factors():
    rows = [[scale * place**a for a in range(K)] for scale, place in zip(POINT_SCALES, POINT_PLACES)]
    return rows + [[0.0] * (K - 1) + [1.0]]


def mix(factors, values):
    out = None
    for factor, value in zip(factors, values):
        if factor != 0.0:
            term = value if factor == 1.0 else value * factor
            out = term if out is None else out + term
    return out


def lower(m):
    s1, d1, s2, d2, s3, d3 = m[1] + m[2], m[1] - m[2], m[3] + m[4], m[3] - m[4], m[5] + m[6], m[5] - m[6]
    return [
        m[0] + s1 + (s2 + s3),
        d1 + (2.0 * d2 + 0.5 * d3),
        s1 + (4.0 * s2 + 0.25 * s3),
        d1 + m[7] + (8.0 * d2 + 0.125 * d3),
    ]


def spread_points(g):
    e1, o1 = g[0] + g[2], g[1] + g[3]
    e2, o2 = g[0] + 4.0 * g[2], 2.0 * g[1] + 8.0 * g[3]
    e3, o3 = g[0] + 0.25 * g[2], 0.5 * g[1] + 0.125 * g[3]
    return [g[0], e1 + o1, e1 - o1, e2 + o2, e2 - o2, e3 + o3, e3 - o3, g[3]]


def raise_all(pad, first, raised):
    def two(i, _):
        for k in range(2):
            g = 2 * i + k
            for c in range(SUB):
                d = [pad[first + GROUP * g + n, c + 2] for n in range(2 * GROUP)]
                for p, value in enumerate(raise_rows(d)):
                    raised[g, p, c + 2] = value
            for p in range(POINTS):
                fill_sides(raised.at[g], p)
        return 0

    lax.fori_loop(0, raised.shape[0] // 2, two, 0)


def raise_taps(w_ref, taps, flipped=False, scale=1.0):
    for b in range(K):
        column_taps = []
        for a in range(K):
            tap = a * K + b
            column_taps.append(w_ref[TAPS - 1 - tap if flipped else tap])
        for p, factors in enumerate(tap_factors()):
            taps[p * K + b] = mix([scale * factor for factor in factors], column_taps)


def four_rows(raised, taps, g, columns):
    m = []
    for p in range(POINTS):
        values = {c: raised[g, p, c] for c in range(columns[0], columns[-1] + K)}
        row = []
        for c in columns:
            row.append(mix([1.0] * K, [values[c + b] * taps[p * K + b] for b in range(K)]))
        m.append(row)
    return [lower([m[p][i] for p in range(POINTS)]) for i in range(len(columns))]


def spread_kernel(
    parts, count, side_ref, top_ref, low_ref, own_ref, high_ref, lower_ref, gain_ref, bias_ref, w_ref, *rest
):
    sums = rest[:parts]
    out_ref, edge_ref, hid_ref, sum_ref, pad, terms, rim_high, rim_low, raised, taps = rest[parts:]
    rows = own_ref.shape[0]
    _, _, scale, shift = norm_terms(total(sums), count, gain_ref[0:1], bias_ref[0:1])
    terms[0] = jnp.broadcast_to(0.5 * scale, (SUB, 128))
    terms[1] = jnp.broadcast_to(0.5 * shift, (SUB, 128))

    @pl.when(pl.program_id(0) == 0)
    def _():
        turn_rims((top_ref, low_ref), side_ref, rim_high, rim_low)

    def act(value):
        return swish_half(value * terms[0] + terms[1])

    def own_rows(i, _):
        for k in range(GROUP):
            for c in range(SUB):
                pad[GROUP * i + k + HALO_IN, c + 2] = act(own_ref[GROUP * i + k, c])
        return 0

    lax.fori_loop(0, rows // GROUP, own_rows, 0)
    for side, start, first in ((0, 0, HALO_IN - HALO_OUT), (1, rows + HALO_IN, 0)):

        @pl.when(side_ref[side] == 1)
        def _(side=side, start=start, first=first):
            halo = dot3((rim_high[side], rim_low[side]), (high_ref[...], lower_ref[...]))
            halo = halo.reshape(HALO_IN, SUB, SUB, 128)
            hid_ref[side] = halo[first : first + HALO_OUT]
            pad[start : start + HALO_IN, 2 : SUB + 2] = act(halo)
            edge_row = min(start, rows + 2)
            for r in range(HALO_OUT + K - 1):
                fill_sides(pad, edge_row + r)

        @pl.when(side_ref[side] == 0)
        def _(side=side, start=start):
            clear_rows(pad, start, HALO_IN)
            hid_ref[side] = jnp.zeros(hid_ref.shape[1:], F32)

    raise_taps(w_ref, taps)
    raise_all(pad, 2, raised)

    def group(g, carry):
        one, two = carry
        for columns in (range(0, SUB // 2), range(SUB // 2, SUB)):
            for c, values in zip(columns, four_rows(raised, taps, g, columns)):
                for o, value in enumerate(values):
                    out_ref[GROUP * g + o, c] = value
                    one = one + value
                    two = two + value * value
        return one, two

    zero = jnp.zeros((SUB, 128), F32)
    one, two = lax.fori_loop(0, rows // GROUP, group, (zero, zero))
    sum_ref[0:1] = jnp.sum(one, axis=0, keepdims=True)
    sum_ref[1:2] = jnp.sum(two, axis=0, keepdims=True)
    for side, start in ((0, 0), (1, rows + 2)):

        @pl.when(side_ref[side] == 1)
        def _(side=side, start=start):
            for c in range(SUB):
                acc = tap_rows(pad, w_ref, start, HALO_OUT, c)
                for o in range(HALO_OUT):
                    edge_ref[side, o, c] = acc[o]

        @pl.when(side_ref[side] == 0)
        def _(side=side):
            edge_ref[side] = jnp.zeros(edge_ref.shape[1:], F32)


def lanes(shape):
    lead = len(shape) - 1
    return pl.BlockSpec(tuple(shape[:-1]) + (128,), lambda e: (0,) * lead + (e,))


def spread(count, side, top, low, own, w_high, w_low, gains, biases, taps, sums):
    rows, hidden = own.shape[0], own.shape[-1]
    chan_all = w_high.shape[0]
    arrays = [own, w_high, w_low, gains, biases, taps, *sums]
    edge_shape = (2, HALO_OUT, SUB, SUB, hidden)
    rim_shape = (2, HALO_IN * FRAME_COLUMNS, chan_all)
    return pl.pallas_call(
        partial(spread_kernel, len(sums), count),
        grid=(hidden // 128,),
        in_specs=[pl.BlockSpec(memory_space=pltpu.SMEM), whole(top.shape), whole(low.shape)]
        + [lanes(a.shape) for a in arrays],
        out_specs=[
            lanes((rows, SUB, SUB, hidden)),
            lanes(edge_shape),
            lanes(edge_shape),
            lanes((2, hidden)),
        ],
        out_shape=[
            jax.ShapeDtypeStruct((rows, SUB, SUB, hidden), F32),
            jax.ShapeDtypeStruct(edge_shape, F32),
            jax.ShapeDtypeStruct(edge_shape, F32),
            jax.ShapeDtypeStruct((2, hidden), F32),
        ],
        scratch_shapes=[
            pltpu.VMEM((rows + 2 * HALO_IN, SUB + 4, SUB, 128), F32),
            pltpu.VMEM((2, SUB, 128), F32),
            pltpu.VMEM(rim_shape, BF16),
            pltpu.VMEM(rim_shape, BF16),
            pltpu.VMEM((rows // GROUP, POINTS, SUB + 4, SUB, 128), F32),
            pltpu.VMEM((POINTS * K, SUB, 128), F32),
        ],
        compiler_params=params(),
        cost_estimate=cost(10),
        name="spread",
    )(side, top, low, *arrays)


def as_row(columns):
    width = columns.shape[1]
    folded = columns[:, 0:128]
    for i in range(128, width, 128):
        folded = folded + columns[:, i : i + 128]
    return jnp.sum(folded.T, axis=0, keepdims=True)


def gather_kernel(parts, count, own_ref, gout_ref, gain_ref, bias_ref, wt_ref, high_ref, low_ref, *rest):
    sums, (m_ref, s_ref, se_ref, proj_ref, h_ref) = rest[:parts], rest[parts:]
    t = pl.program_id(0)
    chan_all, hidden = wt_ref.shape

    @pl.when(t == 0)
    def _():
        m_ref[...] = jnp.zeros_like(m_ref)
        s_ref[...] = jnp.zeros_like(s_ref)

    _, _, scale, shift = norm_terms(total(sums), count, gain_ref[1:2], bias_ref[1:2])
    scale, shift = 0.5 * scale, 0.5 * shift
    gout = split(gout_ref[:, 0].reshape(chan_all, gout_ref.shape[3]))
    proj = None
    for cut in chunks(hidden):
        h = own_ref[0, :, cut] * scale[:, cut] + shift[:, cut]
        h_ref[0, :, cut] = h
        act = swish_half(h)
        s_ref[0:1, cut] += jnp.sum(act, axis=0, keepdims=True)
        act = split(act)
        m_ref[:, cut] += dot3(gout, act)
        term = dot3(act, (high_ref[cut], low_ref[cut]))
        proj = term if proj is None else proj + term
    proj_ref[0] = proj

    @pl.when(t == pl.num_programs(0) - 1)
    def _():
        wt = wt_ref[...]
        se_ref[0:1] = as_row(s_ref[...] * wt)
        se_ref[1:2] = as_row(m_ref[...] * wt)


def gather(count, own, gout, gains, biases, wt, w_high, w_low, sums):
    nz, bands, chans, area = gout.shape
    hidden = wt.shape[1]
    chan_all = nz * chans
    grid, tall, put, wide = by_steps(nz, bands, chans, area)
    return pl.pallas_call(
        partial(gather_kernel, len(sums), count),
        grid=grid,
        in_specs=[
            tall(hidden),
            wide,
            whole(gains.shape),
            whole(biases.shape),
            whole(wt.shape),
            whole(w_high.shape),
            whole(w_low.shape),
        ]
        + [whole(s.shape) for s in sums],
        out_specs=[
            whole((chan_all, hidden)),
            whole((1, hidden)),
            whole((2, chan_all)),
            put(chan_all),
            put(hidden),
        ],
        out_shape=[
            pltpu.VMEM((chan_all, hidden), F32),
            jax.ShapeDtypeStruct((1, hidden), F32),
            jax.ShapeDtypeStruct((2, chan_all), F32),
            pltpu.VMEM((bands, area, chan_all), F32),
            pltpu.VMEM((bands, area, hidden), F32),
        ],
        compiler_params=params(13),
        cost_estimate=cost(13),
        name="gather",
    )(own, gout, gains, biases, wt, w_high, w_low, *sums)


def column(row):
    return jnp.broadcast_to(row, (SUB, row.shape[1])).T[:, 0:1]


def slope_terms(sums, count, gain_ref, bias_ref):
    _, _, scale, shift = norm_terms(sums, count, gain_ref[1:2], bias_ref[1:2])
    return 0.5 * scale, 0.5 * shift


def second_grad(gout, weights, k_row, value, terms, cut):
    h = value if terms is None else value * terms[0][:, cut] + terms[1][:, cut]
    return (dot3(gout, (weights[0][:, cut], weights[1][:, cut])) + k_row[:, cut]) * slope_half(h), h


def proj_back_kernel(
    pairs,
    parts,
    count,
    own_ref,
    gout_ref,
    proj_ref,
    x_ref,
    gain_ref,
    bias_ref,
    wt_ref,
    m_ref,
    s_ref,
    sqt_ref,
    down_ref,
    ex_ref,
    exb_ref,
    *rest,
):
    ses, sums = rest[:pairs], rest[pairs : pairs + parts]
    q_ref, sum_ref, val_ref, col_ref, w_high, w_low, k_row, out_ref, grad_ref = rest[pairs + parts :]
    chan_all, hidden = wt_ref.shape

    @pl.when(pl.program_id(0) == 0)
    def _():
        se = total(ses)
        pooled = se[0:1] / (FRAME_ROWS * FRAME_COLUMNS)
        sqt, ex = sqt_ref[...], ex_ref[...]
        n = ex.shape[0]
        same = lax.broadcasted_iota(jnp.int32, (n, n), 0) == lax.broadcasted_iota(jnp.int32, (n, n), 1)
        down = jnp.sum(jnp.where(same, down_ref[...], 0.0), axis=1, keepdims=True)
        pre = jnp.sum(sqt * pooled, axis=1, keepdims=True) + down
        gate = sigmoid(pre)
        squeezed = pre * gate
        excite = sigmoid(jnp.sum(ex * squeezed, axis=0, keepdims=True) + exb_ref[...])
        logit = se[1:2] * excite * (1.0 - excite)
        slope = gate * (1.0 + pre * (1.0 - gate))
        grad_sq = jnp.sum(ex * logit, axis=1, keepdims=True) * slope
        pool_grad = jnp.sum(sqt * grad_sq, axis=0, keepdims=True) / (FRAME_ROWS * FRAME_COLUMNS)
        val_ref[...] = jnp.zeros_like(val_ref)
        val_ref[0:1] = excite
        val_ref[1:2] = pool_grad
        val_ref[2:3] = logit
        val_ref[3:4] = pooled
        lane = lax.broadcasted_iota(jnp.int32, col_ref.shape, 1)
        col_ref[...] = jnp.where(lane == 0, squeezed, jnp.where(lane == 1, grad_sq, 0.0))
        wt = 0.5 * wt_ref[...]
        tall_excite, tall_pool = column(excite), column(pool_grad)
        w_high[...], w_low[...] = split(wt * tall_excite)
        k_row[...] = jnp.sum(wt * tall_pool, axis=0, keepdims=True)
        grad_ref[...] = tall_excite * m_ref[...] + tall_pool * s_ref[...]
        sum_ref[...] = jnp.zeros_like(sum_ref)

    gout = split(gout_ref[:, 0].reshape(chan_all, gout_ref.shape[3]).T)
    for cut in chunks(hidden):
        q, h = second_grad(gout, (w_high, w_low), k_row, own_ref[0, :, cut], None, cut)
        q_ref[0, :, cut] = q
        sum_ref[0:1, cut] += jnp.sum(q, axis=0, keepdims=True)
        sum_ref[1:2, cut] += jnp.sum(q * h, axis=0, keepdims=True)

    nz, _, chans, area = x_ref.shape
    out_ref[:, 0] = x_ref[:, 0] + (proj_ref[0] * val_ref[0:1]).T.reshape(nz, chans, area)

    @pl.when(pl.program_id(0) == pl.num_programs(0) - 1)
    def _():
        sum_ref[1:2] = (2.0 * sum_ref[1:2] - bias_ref[1:2] * sum_ref[0:1]) / gain_ref[1:2]


def proj_back(count, own, gout, proj, x, gains, biases, wt, m, s, se_weights, ses, sums):
    nz, bands, chans, area = gout.shape
    hidden = wt.shape[1]
    chan_all = nz * chans
    reduced = se_weights[0].shape[0]
    m, proj, own = keep(m), keep(proj), keep(own)
    fixed = [gains, biases, wt, m, s, *se_weights, *ses, *sums]
    grid, tall, put, wide = by_steps(nz, bands, chans, area)
    return pl.pallas_call(
        partial(proj_back_kernel, len(ses), len(sums), count),
        grid=grid,
        in_specs=[
            tall(hidden),
            wide,
            tall(chan_all),
            wide,
        ]
        + [whole(a.shape) for a in fixed],
        out_specs=[
            put(hidden),
            whole((2, hidden)),
            whole((SUB, chan_all)),
            whole((reduced, 128)),
            whole(wt.shape),
            whole(wt.shape),
            whole((1, hidden)),
            wide,
            whole(m.shape),
        ],
        out_shape=[
            jax.ShapeDtypeStruct((bands, area, hidden), F32),
            jax.ShapeDtypeStruct((2, hidden), F32),
            jax.ShapeDtypeStruct((SUB, chan_all), F32),
            jax.ShapeDtypeStruct((reduced, 128), F32),
            jax.ShapeDtypeStruct(wt.shape, BF16),
            jax.ShapeDtypeStruct(wt.shape, BF16),
            jax.ShapeDtypeStruct((1, hidden), F32),
            jax.ShapeDtypeStruct(x.shape, F32),
            jax.ShapeDtypeStruct(m.shape, F32),
        ],
        compiler_params=params(13),
        cost_estimate=cost(12),
        name="proj_back",
    )(own, gout, proj, x, *fixed)


def spread_back_kernel(
    parts,
    count,
    side_ref,
    top_ref,
    low_ref,
    hid_ref,
    hid_halo_ref,
    own_ref,
    halo_ref,
    q_ref,
    high_ref,
    lower_ref,
    k_ref,
    gain_ref,
    bias_ref,
    w_ref,
    *rest,
):
    sums_one, sums_two, backs = (rest[i * parts : (i + 1) * parts] for i in range(3))
    out_ref, sum_ref, tap_ref, pad, grad, terms, rim_high, rim_low, raised, points, taps = rest[3 * parts :]
    rows = own_ref.shape[0]

    @pl.when(pl.program_id(0) == 0)
    def _():
        turn_rims((top_ref, low_ref), side_ref, rim_high, rim_low)

    _, _, scale, shift = norm_terms(total(sums_one), count, gain_ref[0:1], bias_ref[0:1])
    a, b, c0 = back_terms(total(sums_two), total(backs), count, gain_ref[1:2])
    for i, row in enumerate((0.5 * scale, 0.5 * shift, a, b, c0)):
        terms[i] = jnp.broadcast_to(row, (SUB, 128))

    def act(value):
        return swish_half(value * terms[0] + terms[1])

    def grad_in(q, value):
        return q * terms[2] + (value * terms[3] + terms[4])

    def own_rows(i, _):
        for k in range(GROUP):
            r = GROUP * i + k
            for c in range(SUB):
                pad[r + HALO_OUT, c + 2] = act(hid_ref[r, c])
                grad[r + HALO_OUT, c + 2] = grad_in(q_ref[r, c], own_ref[r, c])
        return 0

    lax.fori_loop(0, rows // GROUP, own_rows, 0)
    slope = slope_terms(total(sums_two), count, gain_ref, bias_ref)
    for side, start in ((0, 0), (1, rows + HALO_OUT)):

        @pl.when(side_ref[side] == 1)
        def _(side=side, start=start):
            value = halo_ref[side].reshape(HALO_OUT * FRAME_COLUMNS, 128)
            weights = (high_ref, lower_ref)
            gout = (rim_high[side], rim_low[side])
            q, _ = second_grad(gout, weights, k_ref, value, slope, slice(0, 128))
            edge = grad_in(q.reshape(HALO_OUT, SUB, SUB, 128), halo_ref[side])
            grad[start : start + HALO_OUT, 2 : SUB + 2] = edge
            pad[start : start + HALO_OUT, 2 : SUB + 2] = act(hid_halo_ref[side])

        @pl.when(side_ref[side] == 0)
        def _(start=start):
            clear_rows(pad, start, HALO_OUT)
            clear_rows(grad, start, HALO_OUT)

    raise_all(pad, 0, raised)

    def point_groups(i, _):
        for g in (2 * i, 2 * i + 1):
            for c in range(SUB):
                mine = [grad[GROUP * g + HALO_OUT + k, c + 2] for k in range(GROUP)]
                for p, value in enumerate(spread_points(mine)):
                    points[g, p, c] = value
        return 0

    lax.fori_loop(0, rows // GROUP // 2, point_groups, 0)
    zero = jnp.zeros((SUB, 128), F32)
    factors = tap_factors()
    tap_sums = [None] * TAPS
    for p in range(0, POINTS, 2):

        def weight_groups(i, acc, p=p):
            acc = list(acc)
            for g in (2 * i, 2 * i + 1):
                for k in range(2):
                    values = [raised[g, p + k, c] for c in range(SUB + K - 1)]
                    for c in range(SUB):
                        mine = points[g, p + k, c]
                        for b in range(K):
                            at = (k * 2 + c % 2) * K + b
                            acc[at] = acc[at] + values[c + b] * mine
            return tuple(acc)

        acc = lax.fori_loop(0, rows // GROUP // 2, weight_groups, (zero,) * (4 * K))
        for k in range(2):
            for b in range(K):
                value = jnp.sum(acc[2 * k * K + b] + acc[(2 * k + 1) * K + b], axis=0, keepdims=True)
                for a in range(K):
                    if factors[p + k][a] != 0.0:
                        term = value * factors[p + k][a]
                        old = tap_sums[a * K + b]
                        tap_sums[a * K + b] = term if old is None else old + term
    for tap in range(TAPS):
        tap_ref[tap : tap + 1] = tap_sums[tap]

    raise_taps(w_ref, taps, flipped=True, scale=0.5)
    raise_all(grad, 0, raised)

    def group(g, carry):
        one, two = carry
        for columns in (range(0, SUB // 2), range(SUB // 2, SUB)):
            for c, values in zip(columns, four_rows(raised, taps, g, columns)):
                for o, value in enumerate(values):
                    h = hid_ref[GROUP * g + o, c] * terms[0] + terms[1]
                    value = value * slope_half(h)
                    out_ref[GROUP * g + o, c] = value
                    one = one + value
                    two = two + value * h
        return one, two

    one, two = lax.fori_loop(0, rows // GROUP, group, (zero, zero))
    one, two = jnp.sum(one, axis=0, keepdims=True), jnp.sum(two, axis=0, keepdims=True)
    sum_ref[0:1] = one
    sum_ref[1:2] = (2.0 * two - bias_ref[0:1] * one) / gain_ref[0:1]


def spread_back(
    count, side, top, low, hid, hid_halo, own, halo, q, weights, gains, biases, taps, sums_one, sums_two, backs
):
    rows, hidden = own.shape[0], own.shape[-1]
    arrays = [hid, hid_halo, own, halo, q, *weights, gains, biases, taps, *sums_one, *sums_two, *backs]
    rim_shape = (2, HALO_OUT * FRAME_COLUMNS, weights[0].shape[0])
    return pl.pallas_call(
        partial(spread_back_kernel, len(backs), count),
        grid=(hidden // 128,),
        in_specs=[pl.BlockSpec(memory_space=pltpu.SMEM), whole(top.shape), whole(low.shape)]
        + [lanes(a.shape) for a in arrays],
        out_specs=[lanes((rows, SUB, SUB, hidden)), lanes((2, hidden)), lanes((TAPS, hidden))],
        out_shape=[
            jax.ShapeDtypeStruct((rows, SUB, SUB, hidden), F32),
            jax.ShapeDtypeStruct((2, hidden), F32),
            jax.ShapeDtypeStruct((TAPS, hidden), F32),
        ],
        scratch_shapes=[
            pltpu.VMEM((rows + 2 * HALO_OUT, SUB + 4, SUB, 128), F32),
            pltpu.VMEM((rows + 2 * HALO_OUT, SUB + 4, SUB, 128), F32),
            pltpu.VMEM((5, SUB, 128), F32),
            pltpu.VMEM(rim_shape, BF16),
            pltpu.VMEM(rim_shape, BF16),
            pltpu.VMEM((rows // GROUP, POINTS, SUB + 4, SUB, 128), F32),
            pltpu.VMEM((rows // GROUP, POINTS, SUB, SUB, 128), F32),
            pltpu.VMEM((POINTS * K, SUB, 128), F32),
        ],
        compiler_params=params(),
        cost_estimate=cost(150),
        name="spread_back",
    )(side, top, low, *arrays)


def expand_grad(q_ref, hid_ref, terms, cut):
    a, b, c = terms
    return split(q_ref[0, :, cut] * a[:, cut] + (hid_ref[0, :, cut] * b[:, cut] + c[:, cut]))


def input_kernel(parts, count, start, q_ref, hid_ref, gout_ref, gain_ref, w_high, w_low, *rest):
    sums, backs, out_ref = rest[:parts], rest[parts : 2 * parts], rest[2 * parts]
    nz, _, chans, area = out_ref.shape
    terms = back_terms(total(sums), total(backs), count, gain_ref[0:1])
    out = None
    for cut in chunks(w_high.shape[0]):
        term = dot3(expand_grad(q_ref, hid_ref, terms, cut), (w_high[cut], w_low[cut]))
        out = term if out is None else out + term
    own = gout_ref[:, 0]
    if own.shape[2] > area:
        own = own[:, :, start : start + area]
    out_ref[:, 0] = own + out.T.reshape(nz, chans, area)


def input_grad(count, start, width, q, hid, gout, gains, w_high, w_low, sums, backs):
    nz, bands, chans, area = gout.shape
    hidden = w_high.shape[0]
    at = start // width
    fixed = [gains, w_high, w_low, *sums, *backs]
    if width % 128 == 0:
        gout_spec = pl.BlockSpec((nz, 1, chans, width), lambda t: (0, t, 0, at))
    else:
        gout_spec = pl.BlockSpec((nz, 1, chans, area), lambda t: (0, t, 0, 0))
    return pl.pallas_call(
        partial(input_kernel, len(sums), count, start),
        grid=(bands,),
        in_specs=[
            pl.BlockSpec((1, width, hidden), lambda t: (t, at, 0)),
            pl.BlockSpec((1, width, hidden), lambda t: (t, at, 0)),
            gout_spec,
        ]
        + [whole(v.shape) for v in fixed],
        out_specs=pl.BlockSpec((nz, 1, chans, width), lambda t: (0, t, 0, 0)),
        out_shape=jax.ShapeDtypeStruct((nz, bands, chans, width), F32),
        compiler_params=params(),
        cost_estimate=cost(12),
        name="input_grad",
    )(q, hid, gout, *fixed)


def weight_kernel(chans, ids_ref, q_ref, x_ref, tap_ref, one_ref, two_ref, val_ref, col_ref, *rest):
    outs, acc, small = rest[:-2], rest[-2], rest[-1]
    nz, _, _, area = x_ref.shape
    chan_all, hidden = acc.shape
    width = hidden // nz
    t = pl.program_id(0)

    @pl.when(t == 0)
    def _():
        acc[...] = jnp.zeros_like(acc)
        small[...] = jnp.zeros_like(small)
        small[0:TAPS] = tap_ref[...]
        small[TAPS : TAPS + 1] = one_ref[1:2]
        small[TAPS + 1 : TAPS + 2] = two_ref[1:2]
        small[TAPS + 2 : TAPS + 3] = one_ref[0:1]
        small[TAPS + 3 : TAPS + 4] = two_ref[0:1]
        lead = (ids_ref[1] == 0).astype(F32)
        logit, pooled = val_ref[2:3] * lead, val_ref[3:4]
        reduced = col_ref.shape[0]
        grad_sq = col_ref[:, 1:2] * lead
        g_sq = grad_sq * pooled
        g_ex = col_ref[:, 0:1] * logit
        grad_row = jnp.broadcast_to(grad_sq, (reduced, 128)).T[0:1]
        for z in range(nz):
            own, at = slice(z * chans, (z + 1) * chans), z * width
            small[32 : 32 + reduced, at : at + chans] = g_sq[:, own]
            small[32 : 32 + reduced, at + chans : at + 2 * chans] = g_ex[:, own]
            small[32:33, at + 2 * chans : at + 3 * chans] = logit[:, own]
            small[33:34, at + 2 * chans : at + 2 * chans + reduced] = grad_row

    x = split(x_ref[:, 0].reshape(chan_all, area))
    for cut in chunks(hidden):
        acc[:, cut] += dot3(x, split(q_ref[0, :, cut]))

    @pl.when(t == pl.num_programs(0) - 1)
    def _():
        n = sum(out.shape[0] for out in outs)
        r, m = chan_all // n, SMALL // n
        for core, out in enumerate(outs):
            for i in range(out.shape[0]):
                p = ids_ref[0] ^ (i * len(outs) + core)
                out[i, 0:r] = acc[pl.ds(pl.multiple_of(p * r, r), r), :]
                out[i, r : r + m] = small[pl.ds(pl.multiple_of(p * m, m), m), :]


def weight_grad(ids, shape, q, x, taps, one, two, values, columns):
    nz, bands, chans, area = x.shape
    hidden = q.shape[2]
    chan_all = nz * chans
    fixed = [taps, one, two, values, columns]
    pieces, chips = shape
    shape = (chips, (chan_all + SMALL) // (pieces * chips), hidden)
    grid, tall, put, wide = by_steps(nz, bands, chans, area)
    return pl.pallas_call(
        partial(weight_kernel, chans),
        grid=grid,
        in_specs=[
            pl.BlockSpec(memory_space=pltpu.SMEM),
            tall(hidden),
            wide,
        ]
        + [whole(v.shape) for v in fixed],
        out_specs=[whole(shape)] * pieces,
        out_shape=[jax.ShapeDtypeStruct(shape, F32)] * pieces,
        scratch_shapes=[pltpu.VMEM((chan_all, hidden), F32), pltpu.VMEM((SMALL, hidden), F32)],
        compiler_params=params(),
        cost_estimate=cost(7),
        name="weight_grad",
    )(ids, q, x, *fixed)


def merge_kernel(one_ref, two_ref, *outs):
    for i, out in enumerate(outs):
        out[...] = one_ref[i] + two_ref[i]


def merge(one, two):
    n = one.shape[0]
    return pl.pallas_call(
        merge_kernel,
        grid=(1,),
        in_specs=[whole(one.shape), whole(two.shape)],
        out_specs=[whole(one.shape[1:])] * n,
        out_shape=[jax.ShapeDtypeStruct(one.shape[1:], F32)] * n,
        compiler_params=params(),
        cost_estimate=cost(2),
        name="merge",
    )(one, two)


def collect_kernel(n, nz, parts, count, ids_ref, early_ref, gram_ref, high_ref, low_ref, gain_ref, *rest):
    pieces, sums, backs = rest[:n], rest[n : n + parts], rest[n + parts : n + 2 * parts]
    outs, acc = rest[n + 2 * parts : -1], rest[-1]
    value = total(pieces)
    rows, width = value.shape[0], acc.shape[2]
    r, chan_all = early_ref.shape[0], high_ref.shape[0]
    a, b, c = back_terms(total(sums), total(backs), count, gain_ref[0:1])
    gram = gram_ref[...]
    hid = dot3(split(gram[:, 0:chan_all]), (high_ref[...], low_ref[...]))
    grad = a * value[0:r] + (b * hid + c * gram[:, chan_all : chan_all + 1])
    for z in range(nz):
        here = slice(z * width, (z + 1) * width)
        acc[z, 0:r] = grad[:, here]
        acc[z, r:rows] = value[r:, here]
        acc[z, rows:] = early_ref[:, here]
    for k, out in enumerate(outs):
        out[...] = acc[ids_ref[2] ^ k]


def collect(count, ids, nz, pieces, early, gram, w_high, w_low, gains, sums, backs):
    width = early.shape[1] // nz
    rows = pieces[0].shape[0] + early.shape[0]
    arrays = [early, gram, w_high, w_low, gains, *pieces, *sums, *backs]
    return pl.pallas_call(
        partial(collect_kernel, len(pieces), nz, len(sums), count),
        grid=(1,),
        in_specs=[pl.BlockSpec(memory_space=pltpu.SMEM)] + [whole(a.shape) for a in arrays],
        out_specs=[whole((rows, width))] * nz,
        out_shape=[jax.ShapeDtypeStruct((rows, width), F32)] * nz,
        scratch_shapes=[pltpu.VMEM((nz, rows, width), F32)],
        compiler_params=params(),
        cost_estimate=cost(3),
        name="collect",
    )(ids, *arrays)


def segments(chan_in, hidden_dev, chan_dev, reduced, tap_count, hidden_all):
    seg_sizes = [
        chan_in * hidden_dev,
        tap_count * hidden_dev,
        2 * hidden_dev,
        2 * hidden_dev,
        hidden_dev * chan_in,
        chan_dev * reduced,
        reduced,
        reduced * chan_dev,
        chan_dev,
    ]
    seg_rates = [
        0.5 / math.sqrt(chan_in),
        0.5 / math.sqrt(tap_count),
        0.3,
        0.3,
        0.5 * math.sqrt(8.0 / hidden_all),
        2.0 / math.sqrt(chan_in),
        0.3,
        1.0 / math.sqrt(reduced),
        0.3,
    ]
    return (seg_sizes, seg_rates)


def pack_kernel(at_ref, we_ref, wp_ref, dw_ref, gain_ref, bias_ref, sq_ref, ex_ref, exb_ref, out_ref, small):
    p = at_ref[0]
    chan_in, width = we_ref.shape
    reduced, chans = sq_ref.shape
    m = small.shape[0] * out_ref.shape[0] // (2 * chan_in + small.shape[0])
    r = (out_ref.shape[0] - m) // 2
    small[...] = jnp.zeros_like(small)
    small[0:TAPS] = dw_ref[...]
    small[TAPS : TAPS + 2] = gain_ref[...]
    small[TAPS + 2 : TAPS + 4] = bias_ref[...]
    small[32 : 32 + reduced, 0:chans] = sq_ref[...]
    small[32 : 32 + reduced, chans : 2 * chans] = ex_ref[...]
    small[32:33, 2 * chans : 3 * chans] = exb_ref[...]
    out_ref[0:r] = we_ref[pl.ds(pl.multiple_of(p * r, r), r), :]
    if chan_in == width:
        out_ref[r : 2 * r] = wp_ref[pl.ds(pl.multiple_of(p * r, r), r), :]
    else:
        row, part = p * r % width, p * r // width
        out_ref[r : 2 * r] = wp_ref[
            pl.ds(pl.multiple_of(row, r), r), pl.ds(pl.multiple_of(part * width, 128), width)
        ]
    out_ref[2 * r : 2 * r + m] = small[pl.ds(pl.multiple_of(p * m, m), m), :]


def pack_weights(at, w_expand, w_dw, norm_gains, norm_biases, w_project, squeeze_matrix, excite_matrix, excite_bias_row):
    n_pix = lax.axis_size(PIX)
    chan_in, width = w_expand.shape
    arrays = [
        w_expand,
        w_project,
        w_dw,
        norm_gains,
        norm_biases,
        squeeze_matrix.T,
        excite_matrix,
        excite_bias_row[None],
    ]
    shape = ((2 * chan_in + SMALL) // n_pix, width)
    return pl.pallas_call(
        pack_kernel,
        grid=(1,),
        in_specs=[pl.BlockSpec(memory_space=pltpu.SMEM)] + [whole(a.shape) for a in arrays],
        out_specs=whole(shape),
        out_shape=jax.ShapeDtypeStruct(shape, F32),
        scratch_shapes=[pltpu.VMEM((SMALL, width), F32)],
        compiler_params=params(),
        cost_estimate=cost(2),
        name="pack_weights",
    )(at, *arrays)


def weights_kernel(
    chan_in,
    chans,
    orders,
    base_ref,
    *refs,
):
    slabs = refs[: len(orders)]
    (
        we_high,
        we_low,
        wet_high,
        wet_low,
        wp_high,
        wp_low,
        wpt_ref,
        tap_ref,
        gain_ref,
        bias_ref,
        sqt_ref,
        ex_ref,
        exb_ref,
        first,
        second,
        small,
    ) = refs[len(orders) :]
    nz, width = first.shape[0], first.shape[2]
    n_pix = sum(len(order) for order in orders)
    r, m = chan_in // n_pix, SMALL // n_pix
    reduced = ex_ref.shape[0]
    for ref, order in zip(slabs, orders):
        for i, p in enumerate(order):
            at = base_ref[0] ^ p
            wide = pl.ds(pl.multiple_of(at * r, r), r)
            for z in range(nz):
                here = slice(z * width, (z + 1) * width)
                group = base_ref[1] ^ z
                first[group, wide, :] = ref[i, 0:r, here]
                second[group, wide, :] = ref[i, r : 2 * r, here]
                small[group, pl.ds(pl.multiple_of(at * m, m), m), :] = ref[i, 2 * r : 2 * r + m, here]
    parts = chan_in // width
    for z in range(nz):
        here = slice(z * width, (z + 1) * width)
        own = slice(z * chans, (z + 1) * chans)
        we = first[z]
        we_high[:, here], we_low[:, here] = split(we)
        wet_high[here], wet_low[here] = split(we.T)
        for h in range(parts):
            wp = second[z, h * width : (h + 1) * width]
            cols = slice(h * width, (h + 1) * width)
            wp_high[here, cols], wp_low[here, cols] = split(wp)
            wpt_ref[cols, here] = wp.T
        for tap in range(TAPS):
            tap_ref[tap, :, here] = jnp.broadcast_to(small[z, tap : tap + 1], (SUB, width))
        gain_ref[:, here] = small[z, TAPS : TAPS + 2]
        bias_ref[:, here] = small[z, TAPS + 2 : TAPS + 4]
        sqt_ref[:, own] = small[z, 32 : 32 + reduced, 0:chans]
        ex_ref[:, own] = small[z, 32 : 32 + reduced, chans : 2 * chans]
        exb_ref[:, own] = small[z, 32:33, 2 * chans : 3 * chans]


def order_weights(base, slabs, orders, nz, chan_in, chans, reduced):
    hidden = slabs[0].shape[2]
    width = hidden // nz
    shapes = (
        [((chan_in, hidden), BF16)] * 2
        + [((hidden, chan_in), BF16)] * 4
        + [
            ((chan_in, hidden), F32),
            ((TAPS, SUB, hidden), F32),
            ((2, hidden), F32),
            ((2, hidden), F32),
            ((reduced, chan_in), F32),
            ((reduced, chan_in), F32),
            ((1, chan_in), F32),
        ]
    )
    return pl.pallas_call(
        partial(weights_kernel, chan_in, chans, orders),
        grid=(1,),
        in_specs=[pl.BlockSpec(memory_space=pltpu.SMEM)] + [whole(a.shape) for a in slabs],
        out_specs=[whole(shape) for shape, _ in shapes],
        out_shape=[jax.ShapeDtypeStruct(shape, kind) for shape, kind in shapes],
        scratch_shapes=[
            pltpu.VMEM((nz, chan_in, width), F32),
            pltpu.VMEM((nz, chan_in, width), F32),
            pltpu.VMEM((nz, SMALL, width), F32),
        ],
        compiler_params=params(),
        cost_estimate=cost(3),
        name="order_weights",
    )(base, *slabs)


def thirds(v):
    high = v.astype(BF16)
    rest = v - high.astype(F32)
    mid = rest.astype(BF16)
    return high, mid, (rest - mid.astype(F32)).astype(BF16)


def choose(chosen, v):
    high, mid, low = thirds(v)
    return (dot(chosen, high) + dot(chosen, mid)) + dot(chosen, low)


def choose_lanes(v, chosen):
    high, mid, low = thirds(v)
    return (dot(high, chosen) + dot(mid, chosen)) + dot(low, chosen)


def ones(condition):
    return condition.astype(F32).astype(BF16)


def lay_flat(v, start, width):
    n, m = v.shape
    place = lax.broadcasted_iota(jnp.int32, (m, width), 1) - start
    column_of = lax.broadcasted_iota(jnp.int32, (m, width), 0)
    wide = choose_lanes(v, ones((place + 64 * m) % m == column_of))
    place = lax.broadcasted_iota(jnp.int32, (n, width), 1) - start
    low = lax.broadcasted_iota(jnp.int32, (n, width), 0) * m
    return jnp.sum(jnp.where((place >= low) & (place < low + m), wide, 0.0), axis=0, keepdims=True)


def fill_blocks(out, first, middle, flip, last, squeeze, down, excite, bias):
    blocks, length = out.shape
    tiles, n, _ = first.shape
    width = tiles * 128
    per = length // width
    for i in range(per):
        for u in range(tiles):
            at = i * width + u * 128
            out[0 : n // per, at : at + 128] = first[u, pl.ds(i, n // per, stride=per), :]
    for k in range(TAPS + 4):
        row = n + k
        out[row // per : row // per + 1, row % per * width : (row % per + 1) * width] = middle[k : k + 1, :]
    base = n + TAPS + 4
    parts = last // width
    step = per // parts
    for h in range(parts):
        for e in range(step):
            row = base + parts * e + h
            block, slot = row // per, row % per
            count = width // step
            for u in range(tiles):
                at = slot * width + u * 128
                out[block : block + count, at : at + 128] = flip[
                    h * tiles + u, pl.ds(e, count, stride=step), :
                ]
    start = (base + width * parts) * width
    block = start // length
    start -= block * length
    tail_width = (blocks - block) * length
    tail = lay_flat(squeeze, start, tail_width)
    start += squeeze.shape[0] * squeeze.shape[1]
    tail = tail + lay_flat(down, start, tail_width)
    start += down.shape[1]
    tail = tail + lay_flat(excite, start, tail_width)
    start += excite.shape[0] * excite.shape[1]
    tail = tail + lay_flat(bias, start, tail_width)
    inside = lax.broadcasted_iota(jnp.int32, (1, length), 1)
    kept = jnp.where(inside < (base + width * parts) * width - block * length, out[block : block + 1, :], 0.0)
    out[block : block + 1, :] = kept + tail[:, 0:length]
    for k in range(1, blocks - block):
        out[block + k : block + k + 1, :] = tail[:, k * length : (k + 1) * length]


def prepare_kernel(
    orders,
    base_ref,
    col_ref,
    we_ref,
    dw_ref,
    gain_ref,
    bias_ref,
    wp_ref,
    sq_ref,
    down_ref,
    ex_ref,
    exb_ref,
    *rest,
):
    slabs = rest[: len(orders)]
    weight, first_ref, second_ref, head, flip, middle, moments, ranked = rest[len(orders) :]
    blocks, length = weight.shape
    chan_in, width = we_ref.shape
    devices, room = moments.shape[1:3]
    middle[0:TAPS] = dw_ref[...]
    middle[TAPS : TAPS + 2] = gain_ref[...]
    middle[TAPS + 2 : TAPS + 4] = bias_ref[...]
    for u in range(width // 128):
        head[u] = we_ref[:, u * 128 : (u + 1) * 128]
    for u in range(chan_in // 128):
        flip[u] = wp_ref[:, u * 128 : (u + 1) * 128]
    fill_blocks(
        weight, head, middle, flip, chan_in, sq_ref[...].T, down_ref[...], ex_ref[...], exb_ref[...]
    )
    at = 0
    home = jnp.zeros(col_ref.shape, jnp.int32)
    own_col = col_ref[...]
    for ref, order in zip(slabs, orders):
        for k, p in enumerate(order):
            for m in range(2):
                moments[m, at] = ref[k, m * room : (m + 1) * room]
            home = jnp.where(own_col == base_ref[0] ^ p, at, home)
            at += 1
    ranked[...] = jnp.broadcast_to(own_col.astype(F32), ranked.shape)
    own_row = ranked[...].T[0:1].astype(jnp.int32)
    i = lax.broadcasted_iota(jnp.int32, (blocks, blocks), 0)
    j = lax.broadcasted_iota(jnp.int32, (blocks, blocks), 1)
    earlier = (own_row == own_col) & (j < i)
    rank = jnp.sum(jnp.where(earlier, 1.0, 0.0), axis=1, keepdims=True).astype(jnp.int32)
    slot = home * room + rank
    chosen = ones(lax.broadcasted_iota(jnp.int32, (blocks, devices * room), 1) == slot)
    first_ref[...] = choose(chosen, moments[0].reshape(devices * room, length))
    second_ref[...] = choose(chosen, moments[1].reshape(devices * room, length))


def prepare(base, owners, weights, slabs, orders, length):
    blocks = owners.shape[0]
    chan_in, width = weights[0].shape
    devices = sum(len(o) for o in orders)
    arrays = [owners, *weights, *slabs]
    return pl.pallas_call(
        partial(prepare_kernel, orders),
        grid=(1,),
        in_specs=[pl.BlockSpec(memory_space=pltpu.SMEM)] + [whole(a.shape) for a in arrays],
        out_specs=[whole((blocks, length))] * 3,
        out_shape=[jax.ShapeDtypeStruct((blocks, length), F32)] * 3,
        scratch_shapes=[
            pltpu.VMEM((width // 128, chan_in, 128), F32),
            pltpu.VMEM((chan_in // 128, width, 128), F32),
            pltpu.VMEM((32, width), F32),
            pltpu.VMEM((2, devices, slabs[0].shape[1] // 2, length), F32),
            pltpu.VMEM((blocks, 128), F32),
        ],
        compiler_params=params(),
        cost_estimate=cost(1),
        name="prepare",
    )(base, *arrays)


def adam_kernel(
    bounds,
    rates,
    orders,
    chans,
    reduced,
    me_ref,
    col_ref,
    weight_ref,
    old_one_ref,
    old_two_ref,
    first_ref,
    second_ref,
    *rest,
):
    grad_slabs = rest[: len(orders)]
    first_out, second_out, new_ref, grad, head, flip, tall, small, ranked = rest[len(orders) :]
    blocks, length = grad.shape
    capacity = first_ref.shape[0]
    chan_in, width = tall.shape
    devices = sum(len(order) for order in orders)
    r, m = chan_in // devices, SMALL // devices
    for ref, order in zip(grad_slabs, orders):
        for k, i in enumerate(order):
            p = me_ref[1] ^ i
            for u in range(width // 128):
                head[u, pl.ds(pl.multiple_of(p * r, r), r), :] = ref[k, 0:r, u * 128 : (u + 1) * 128]
            small[pl.ds(pl.multiple_of(p * m, m), m), :] = ref[k, r : r + m]
            tall[pl.ds(pl.multiple_of(p * r, r), r), :] = ref[k, r + m : 2 * r + m]
    for u in range(chan_in // 128):
        flip[u] = tall[u * 128 : (u + 1) * 128].T
    fill_blocks(
        grad,
        head,
        small,
        flip,
        chan_in,
        small[32 : 32 + reduced, 0:chans].T,
        small[33:34, 2 * chans : 2 * chans + reduced],
        small[32 : 32 + reduced, chans : 2 * chans],
        small[32:33, 2 * chans : 3 * chans],
    )

    own_col = col_ref[...]
    ranked[...] = jnp.broadcast_to(own_col.astype(F32), ranked.shape)
    own_row = ranked[...].T[0:1].astype(jnp.int32)
    i = lax.broadcasted_iota(jnp.int32, (blocks, blocks), 0)
    j = lax.broadcasted_iota(jnp.int32, (blocks, blocks), 1)
    earlier = (own_row == own_col) & (i < j)
    rank = jnp.sum(jnp.where(earlier, 1.0, 0.0), axis=0, keepdims=True).astype(jnp.int32)
    g = grad[...]
    mine = lax.broadcasted_iota(jnp.int32, (capacity, blocks), 0)
    owned = choose(ones((mine == rank) & (own_row == me_ref[0])), g)
    first_out[:, 0] = beta_first * first_ref[:, 0] + (1.0 - beta_first) * owned
    second_out[:, 0] = beta_second * second_ref[:, 0] + (1.0 - beta_second) * owned * owned

    first = beta_first * old_one_ref[...] + (1.0 - beta_first) * g
    second = beta_second * old_two_ref[...] + (1.0 - beta_second) * g * g
    first_hat = first / (1.0 - beta_first**STEP)
    second_hat = second / (1.0 - beta_second**STEP)
    place = lax.broadcasted_iota(jnp.int32, (blocks, length), 0) * length + lax.broadcasted_iota(
        jnp.int32, (blocks, length), 1
    )
    rate = jnp.zeros((blocks, length), F32)
    for bound, value in zip(reversed(bounds), reversed(rates)):
        rate = jnp.where(place < bound, jnp.float32(value), rate)
    grad[...] = weight_ref[...] * (1.0 - rate * weight_decay) - rate * first_hat / (
        jnp.sqrt(second_hat) + adam_eps
    )
    for k in range(blocks):
        end = min((k + 1) * length, new_ref.shape[1])
        new_ref[:, k * length : end] = grad[k : k + 1, 0 : end - k * length]


def adam(ids, owners, prepared, first, second, grads, orders, chan_in, chans, reduced, bounds, rates):
    blocks, length = prepared[0].shape
    width = grads[0].shape[2]
    arrays = [owners, *prepared, first, second, *grads]
    new_shape = (1, bounds[-1])
    return pl.pallas_call(
        partial(adam_kernel, bounds, rates, orders, chans, reduced),
        grid=(1,),
        in_specs=[pl.BlockSpec(memory_space=pltpu.SMEM)] + [whole(a.shape) for a in arrays],
        out_specs=[whole(first.shape), whole(second.shape), whole(new_shape)],
        out_shape=[
            jax.ShapeDtypeStruct(first.shape, F32),
            jax.ShapeDtypeStruct(second.shape, F32),
            jax.ShapeDtypeStruct(new_shape, F32),
        ],
        scratch_shapes=[
            pltpu.VMEM((blocks, length), F32),
            pltpu.VMEM((width // 128, chan_in, 128), F32),
            pltpu.VMEM((chan_in // 128, width, 128), F32),
            pltpu.VMEM((chan_in, width), F32),
            pltpu.VMEM((SMALL, width), F32),
            pltpu.VMEM((blocks, 128), F32),
        ],
        compiler_params=params(),
        cost_estimate=cost(10),
        name="adam",
    )(ids, *arrays)


def deal_rows(rows):
    n_pix = lax.axis_size(PIX)
    n, hidden = rows.shape
    dealt = lax.all_to_all(rows.reshape(n_pix, n // n_pix, hidden), PIX, 0, 0, tiled=True)
    return jnp.sum(dealt, axis=0)


def together(*values):
    return lax.optimization_barrier(values)


def local(
    frames_raw,
    grad_out,
    col_offsets,
    flip_flags,
    owners,
    w_expand,
    w_dw,
    norm_gains,
    norm_biases,
    w_project,
    squeeze_matrix,
    se_down_bias,
    excite_matrix,
    excite_bias_row,
    first_moment,
    second_moment,
):
    nz, nhi, nlo = (lax.axis_size(axis) for axis in ALL)
    frames, chans, stored = frames_raw.shape
    band = stored // WIN
    area = band * FRAME_COLUMNS
    rows = nlo * band
    chan_in, hidden_dev = w_expand.shape
    hidden = hidden_dev * nz
    reduced = squeeze_matrix.shape[1]
    group = nz // MB * nhi * nlo
    count = float(frames // MB * FRAME_ROWS * FRAME_COLUMNS)
    hi = lax.axis_index("hi")
    side = jnp.stack([(hi > 0).astype(jnp.int32), (hi < nhi - 1).astype(jnp.int32)])

    n_pix = nhi * nlo
    me = hi * nlo + lax.axis_index("lo")
    relative = me if near(n_pix) else 0 * me
    z_relative = lax.axis_index("chan") if near(n_pix) else 0 * me

    slab = pack_weights(
        me.astype(jnp.int32).reshape(1),
        w_expand,
        w_dw,
        norm_gains,
        norm_biases,
        w_project,
        squeeze_matrix,
        excite_matrix,
        excite_bias_row,
    )
    crops = crop(frames_raw, col_offsets, flip_flags)
    crops, *slab = together(crops, *gather_chan(slab))
    x = deal(crops).reshape(nz, nlo, chans, area)
    ordered = order(grad_out)
    slabs, orders, ordered = gather_pix(jnp.concatenate(slab, axis=1), ordered)
    first_turned, second_turned = first_moment.transpose(1, 0, 2), second_moment.transpose(1, 0, 2)
    first_turned, second_turned, *slabs = together(first_turned, second_turned, *slabs)
    room = ((0, -first_moment.shape[1] % SUB), (0, 0))
    moments = jnp.concatenate([jnp.pad(v[:, 0], room) for v in (first_turned, second_turned)])
    (
        we_high,
        we_low,
        wet_high,
        wet_low,
        wp_high,
        wp_low,
        w_project_t,
        taps,
        gains,
        biases,
        sq_t,
        ex_all,
        ex_bias,
    ) = order_weights(
        jnp.stack([relative, z_relative]), slabs, orders, nz, chan_in, chans, reduced
    )
    se_weights = [sq_t, se_down_bias[None], ex_all, ex_bias]
    x, ordered, we_high, we_low, moments = together(x, ordered, we_high, we_low, moments)
    moments = lax.all_gather(moments, PIX, axis=0)

    def as_rows(v):
        return v.reshape(rows, SUB, SUB, hidden)

    def as_bands(v):
        return v.reshape(nlo, area, hidden)

    def as_sides(v, n):
        return v.reshape(2, n, SUB, SUB, hidden)

    hid, sums_one, gram = expand(x, we_high, we_low)
    later = [x]
    sums_one = shares(sums_one, 1, group, later)
    [x] = later
    top, low = rims(x, HALO_IN, band)
    gout = deal(ordered).reshape(nz, nlo, chans, area)
    g_top, g_low = rims(gout, HALO_OUT, band)
    spatial, spatial_halo, hid_halo, sums_two = spread(
        count, side, top, low, as_rows(hid), we_high, we_low, gains, biases, taps, sums_one
    )
    sums_two = shares(sums_two, 1, group)
    m, s, se_part, proj, normed = gather(
        count, as_bands(spatial), gout, gains, biases, w_project_t, wp_high, wp_low, sums_two
    )
    ses = shares(se_part, nlo, nhi)
    ses, g_top, g_low = together(ses, g_top, g_low)
    q, back_two, values, columns, *w4, out, g_project = proj_back(
        count, normed, gout, proj, x, gains, biases, w_project_t, m, s, se_weights, ses, sums_two
    )
    backs_two = shares(back_two, 1, group)
    out = deal(out.reshape(frames, chans, area))
    q1, back_one, g_dw = spread_back(
        count,
        side,
        g_top,
        g_low,
        as_rows(hid),
        hid_halo,
        spatial,
        spatial_halo,
        as_rows(q),
        w4,
        gains,
        biases,
        taps,
        sums_one,
        sums_two,
        backs_two,
    )
    later = [q1]
    backs_one = shares(back_one, 1, group, later)
    [q1] = later

    ids = jnp.stack([relative, hi, z_relative]).astype(jnp.int32)
    pieces = weight_grad(
        ids, (2, n_pix // 2) if near(n_pix) else (1, 1), as_bands(q1), x, g_dw, back_one, back_two, values, columns
    )
    if near(n_pix):
        early = lax.psum_scatter(g_project, PIX, scatter_dimension=0, tiled=True)
        gram = lax.psum_scatter(gram, PIX, scatter_dimension=0, tiled=True)
    else:
        early, gram = deal_rows(g_project), deal_rows(gram)
    q1, out, early, gram, moments, *pieces = together(q1, out, early, gram, moments, *pieces)

    def input_part(start, width, q1):
        grad = input_grad(
            count, start, width, as_bands(q1), hid, gout, gains, wet_high, wet_low, sums_one, backs_one
        )
        return grad.reshape(frames, chans, width)

    most = area // 2
    grad_one = input_part(0, most, q1)
    if near(n_pix):
        pieces = [pieces[0], exchange(pieces[1], 1)]
    grad_one, q1, *pieces = together(grad_one, q1, *pieces)
    if near(n_pix):
        pieces = list(merge(*pieces))
        pieces[0], out = together(pieces[0], out)
        pieces = [pieces[0]] + [exchange(pieces[i], 2 * i) for i in range(1, n_pix // 2)]
    else:
        whole_rows = pieces[0][0]
        pieces = [jnp.concatenate([deal_rows(whole_rows[:chan_in]), deal_rows(whole_rows[chan_in:])])]
    grad_two = input_part(most, area - most, q1)
    output = restore(out)
    weights = [
        w_expand,
        w_dw,
        norm_gains,
        norm_biases,
        w_project,
        squeeze_matrix.T,
        se_down_bias[None],
        excite_matrix,
        excite_bias_row[None],
    ]
    block_len = first_moment.shape[2]
    natural = [list(range(n_pix))]
    base = jnp.zeros((1,), jnp.int32)
    prepared = prepare(base, owners, weights, [moments], natural, block_len)
    grad_two, output, *pieces = together(grad_two, output, *pieces)
    groups = collect(count, ids, nz, pieces, early, gram, we_high, we_low, gains, sums_one, backs_one)
    if near(n_pix):
        others = [groups[0]] + [exchange(groups[k], k * n_pix) for k in range(1, nz)]
    else:
        others = list(lax.all_to_all(jnp.stack(groups), "chan", 0, 0, tiled=True))
    grad_one = deal(grad_one)
    grad_one, grad_two, *groups = together(grad_one, grad_two, *groups)
    summed = sum(others[1:], others[0])
    grad_two = deal(grad_two)
    grads, _, prepared = gather_pix(summed, prepared)
    seg_sizes, seg_rates = segments(chan_in, hidden_dev, chans, reduced, TAPS, hidden)
    bounds = [sum(seg_sizes[: i + 1]) for i in range(len(seg_sizes))]
    first_next, second_next, new_params = adam(
        jnp.stack([me, relative]).astype(jnp.int32),
        owners,
        prepared,
        first_turned,
        second_turned,
        grads,
        orders,
        chan_in,
        chans,
        reduced,
        bounds,
        seg_rates,
    )
    first_next, second_next = first_next.transpose(1, 0, 2), second_next.transpose(1, 0, 2)
    grad_frames = uncrop(grad_one, grad_two, col_offsets, flip_flags)
    return (output, grad_frames, first_next, second_next, new_params)


def solution(mesh):
    nz, n_pix = mesh.shape["chan"], mesh.shape["pix"]
    placed = (
        P(None, "chan", PIX),
        P(None, "chan", PIX),
        P(),
        P(),
        P(),
        P(None, "chan"),
        P(None, "chan"),
        P(None, "chan"),
        P(None, "chan"),
        P("chan", None),
        P("chan", None),
        P(),
        P(None, "chan"),
        P("chan"),
        P("chan", PIX, None),
        P("chan", PIX, None),
    )

    def run(*arrays):
        nlo = arrays[0].shape[0] // nz
        return jax.shard_map(
            local,
            mesh=Mesh(mesh.devices.reshape(nz, n_pix // nlo, nlo), ALL),
            in_specs=placed,
            out_specs=(
                P(None, "chan", PIX),
                P(None, "chan", PIX),
                P("chan", PIX, None),
                P("chan", PIX, None),
                P("chan", None),
            ),
            check_vma=False,
        )(*arrays)

    return run
```
